32 devices in a mesh: expert: 4 (over y, x), dp: 8 (over z, core).
Axes of the slice: x: 2, y: 2, z: 4, core: 2. Of those that a mesh axis runs over, the one named last changes fastest.
Arguments:
- tokens: bfloat16 [1024, 7168], P('dp', 'expert'), may hold values from -6 to 6
- grad_out: bfloat16 [1024, 7168], P('dp', 'expert'), may hold values from -6 to 6
- expert_ids: int32 [1024, 2], P('dp'), may hold values from -1 to 3, as said below
- route_weights: float32 [1024, 2], P('dp'), may hold values from 0.1 to 1
- w_gate: bfloat16 [4, 7168, 2048], P('expert', 'dp'), may hold values from -0.0625 to 0.0625
- w_up: bfloat16 [4, 7168, 2048], P('expert', 'dp'), may hold values from -0.0625 to 0.0625
- w_down: bfloat16 [4, 2048, 7168], P('expert', None, 'dp'), may hold values from -0.125 to 0.125
Outputs:
- grad_tokens: bfloat16 [1024, 7168], P('dp', 'expert')
- grad_gate: bfloat16 [4, 7168, 2048], P('expert', 'dp')
- grad_up: bfloat16 [4, 7168, 2048], P('expert', 'dp')
- grad_down: bfloat16 [4, 2048, 7168], P('expert', None, 'dp')
The draws below stay inside these ranges and needn't reach their ends.
Inputs may be any that keep to these rules, and one draw needn't show every extreme that they name: expert_ids[t, 0] is an expert; expert_ids[t, 1] is another expert or -1. Within each block of 128 rows (the tokens of one index of dp) no expert appears in more than 64 rows, and one expert, the same in every block, appears in exactly 64 rows, each of which has -1 as its second entry.
All inputs are finite; a program needn't handle non-finite values.
Results may differ from the reference program's by a relative error of at most 0.03.
Values may be sent and summed in bfloat16 or wider, within the bound.
No kernel may reach another device: no remote copies, remote signals or barrier semaphores. Data moves between devices by JAX's collectives and lax.ppermute only.
A program may use at most 128 MiB of HBM per device.

```python
import math
import jax
import jax.numpy as jnp
from jax import lax

D = 7168
FF = 2048
TOK_DEV = 128
EXPERTS = 4
CAP = 64
TOKENS = 1024
N_DP = 8


def draw_expert_ids(key, part):
    blocks = TOKENS // TOK_DEV
    keys = jax.random.split(jax.random.fold_in(key, 11), 6)
    hottest = jax.random.randint(keys[0], (), 0, EXPERTS)
    order_keys = jax.random.split(keys[1], blocks)
    orders = jax.vmap(lambda single: jax.random.permutation(single, TOK_DEV))(order_keys)
    ranks = jnp.argsort(orders, axis=1, stable=True)
    is_hot = ranks < CAP
    first_off = jnp.minimum(jax.random.randint(keys[2], (blocks, TOK_DEV), 0, EXPERTS - 1), jax.random.randint(keys[3], (blocks, TOK_DEV), 0, EXPERTS - 1))
    first = jnp.where(is_hot, hottest, (hottest + 1 + first_off) % EXPERTS)
    second_off = jax.random.randint(keys[4], (blocks, TOK_DEV), 0, EXPERTS - 2)
    second_off = jnp.where(second_off < first_off, second_off, second_off + 1)
    second = (hottest + 1 + second_off) % EXPERTS
    use_two = (jax.random.randint(keys[5], (blocks, TOK_DEV), 0, 2) == 1) & jnp.logical_not(is_hot)
    second = jnp.where(use_two, second, -1)
    return jnp.stack([first, second], axis=-1).reshape(TOKENS, 2).astype(jnp.int32)


def shard_levels(own_key, shape, shards, least, largest):
    level = 1.0
    for axis_at, shards_of in shards:
        heights = jax.random.uniform(jax.random.fold_in(jax.random.fold_in(own_key, 6), axis_at), (shards_of,), jnp.float32, least / len(shards), largest / len(shards))
        level = level * jnp.repeat(jnp.exp(heights), shape[axis_at] // shards_of).reshape((-1,) + (1,) * (len(shape) - 1 - axis_at))
    return level


def centred(key, shape, deviation, bound, shards=(), held_as=jnp.bfloat16):
    loudness = shard_levels(key, shape, shards, -0.22, 0.18) if shards else 1.0
    entries = jax.random.normal(key, shape, jnp.float32) * deviation * loudness
    return jnp.minimum(jnp.maximum(entries, -bound), bound).astype(held_as)


def setup_inputs(seed: int = 0) -> dict:
    arg_keys = jax.random.split(jax.random.key(seed), 8)
    return {
        "tokens": centred(arg_keys[0], (TOKENS, D), 1.0, 6.0, ((0, 8), (1, 4))),
        "grad_out": centred(arg_keys[1], (TOKENS, D), 1.0, 6.0, ((0, 8), (1, 4))),
        "expert_ids": draw_expert_ids(jax.random.fold_in(arg_keys[7], 71), 0),
        "route_weights": jnp.clip(jnp.exp(math.log(1.0) - 2.3025851 * jax.random.uniform(arg_keys[3], (TOKENS, 2), jnp.float32) ** shard_levels(arg_keys[3], (TOKENS, 2), ((0, 8),), -0.2, 0.2)), 0.1, 1.0),
        "w_gate": centred(arg_keys[4], (EXPERTS, D, FF), D ** -0.5, 0.0625, ((0, 4), (1, 8))),
        "w_up": centred(arg_keys[5], (EXPERTS, D, FF), D ** -0.5, 0.0625, ((0, 4), (1, 8))),
        "w_down": centred(arg_keys[6], (EXPERTS, FF, D), FF ** -0.5, 0.125, ((0, 4), (2, 8))),
    }


def blocked_sum(rows, blocks, form):
    parts = jnp.einsum(form, rows, blocks)
    rounded = lax.optimization_barrier(parts.astype(jnp.bfloat16))
    return lax.optimization_barrier(jnp.sum(rounded.astype(jnp.float32), axis=1))

def reference(tokens, grad_out, expert_ids, route_weights, w_gate, w_up, w_down):
    slots = N_DP * CAP
    width = D // N_DP
    inv_root = 1.0 / math.sqrt(TOKENS)
    flat_ids = expert_ids.reshape(-1)
    flat_token = (jnp.arange(TOKENS * 2, dtype=jnp.int32) // 2).astype(jnp.int32)
    flat_weight = route_weights.reshape(-1)
    dx_total = jnp.zeros((TOKENS, D), jnp.float32)
    grads_gate = []
    grads_up = []
    grads_down = []
    for expert in range(EXPERTS):
        chosen = flat_ids == expert
        position = jnp.cumsum(chosen.astype(jnp.int32)) - 1
        position = jnp.where(chosen, position, slots).astype(jnp.int32)
        row_index = jnp.zeros((slots,), jnp.int32).at[position].set(flat_token, mode='drop')
        filled = jnp.zeros((slots,), jnp.float32).at[position].set(1.0, mode='drop')
        weight = jnp.zeros((slots,), jnp.float32).at[position].set(flat_weight, mode='drop')
        x_rows = jnp.where(filled[:, None] > 0, tokens[row_index], 0.0).astype(jnp.bfloat16)
        g_rows = jnp.where(filled[:, None] > 0, grad_out[row_index], 0.0).astype(jnp.bfloat16)
        x_blocks = x_rows.astype(jnp.float32).reshape(slots, N_DP, width)
        g_blocks = g_rows.astype(jnp.float32).reshape(slots, N_DP, width)
        gate = blocked_sum(x_blocks, w_gate[expert].astype(jnp.float32).reshape(N_DP, width, FF), 'sbd,bdf->sbf')
        upper = blocked_sum(x_blocks, w_up[expert].astype(jnp.float32).reshape(N_DP, width, FF), 'sbd,bdf->sbf')
        back = blocked_sum(g_blocks, w_down[expert].astype(jnp.float32).reshape(FF, N_DP, width), 'sbd,fbd->sbf')
        back = back * weight[:, None]
        sigmoid_gate = jax.nn.sigmoid(gate)
        scaled = (weight[:, None] * gate * sigmoid_gate * upper).astype(jnp.bfloat16)
        d_gate = (back * upper * sigmoid_gate * (1.0 + gate * (1.0 - sigmoid_gate))).astype(jnp.bfloat16)
        d_up = (back * gate * sigmoid_gate).astype(jnp.bfloat16)
        grads_gate.append((jnp.dot(x_rows.T, d_gate, preferred_element_type=jnp.float32) * inv_root).astype(jnp.bfloat16))
        grads_up.append((jnp.dot(x_rows.T, d_up, preferred_element_type=jnp.float32) * inv_root).astype(jnp.bfloat16))
        grads_down.append((jnp.dot(scaled.T, g_rows, preferred_element_type=jnp.float32) * inv_root).astype(jnp.bfloat16))
        part = (jnp.dot(d_gate, w_gate[expert].T, preferred_element_type=jnp.float32) + jnp.dot(d_up, w_up[expert].T, preferred_element_type=jnp.float32)).astype(jnp.bfloat16)
        dx_total = dx_total.at[row_index].add(jnp.where(filled[:, None] > 0, part.astype(jnp.float32), 0.0))
    return (dx_total.astype(jnp.bfloat16), jnp.stack(grads_gate), jnp.stack(grads_up), jnp.stack(grads_down))
```

```python
import functools
import math

import jax
import jax.numpy as jnp
from jax import lax
from jax.experimental import pallas as pl
from jax.experimental.pallas import tpu as pltpu
from jax.sharding import PartitionSpec as P

F32 = jnp.float32
BF16 = jnp.bfloat16
LAST_DIMS = (((1,), (1,)), ((), ()))
ROWS_FIRST = (((0,), (0,)), ((), ()))
VMEM_LIMIT = 48 * 1024 * 1024


def forward_kernel(chunk_ref, x_ref, g_ref, wg_ref, wu_ref, wd_ref, own_ref, other_ref):
    half, width = own_ref.shape[1], wg_ref.shape[1]
    for row, out in ((0, own_ref), (half, other_ref)):
        x = x_ref[row : row + half, :]
        g = g_ref[row : row + half, :]
        gate = jnp.dot(x, wg_ref[...], preferred_element_type=F32)
        upper = jnp.dot(x, wu_ref[...], preferred_element_type=F32)
        back = lax.dot_general(g, wd_ref[...], LAST_DIMS, preferred_element_type=F32)
        out[0, :, :width] = gate.astype(BF16)
        out[0, :, width : 2 * width] = upper.astype(BF16)
        out[0, :, 2 * width :] = back.astype(BF16)


def forward_chunk(chunks, x, g, w_gate, w_up, w_down, width):
    rows, feats = x.shape
    half = rows // 2
    whole = pl.BlockSpec((rows, feats), lambda d, c: (0, 0))
    out = jax.ShapeDtypeStruct((2, half, 3 * width), BF16)
    out_spec = pl.BlockSpec((1, half, 3 * width), lambda d, c: (d, 0, 0))
    return pl.pallas_call(
        forward_kernel,
        out_shape=(out, out),
        grid_spec=pltpu.PrefetchScalarGridSpec(
            num_scalar_prefetch=1,
            grid=(2,),
            in_specs=[
                whole,
                whole,
                pl.BlockSpec((feats, width), lambda d, c: (0, c[d])),
                pl.BlockSpec((feats, width), lambda d, c: (0, c[d])),
                pl.BlockSpec((width, feats), lambda d, c: (c[d], 0)),
            ],
            out_specs=(out_spec, out_spec),
        ),
        compiler_params=pltpu.CompilerParams(vmem_limit_bytes=VMEM_LIMIT),
        cost_estimate=pl.CostEstimate(
            flops=12 * rows * feats * width,
            bytes_accessed=4 * rows * feats + 12 * feats * width + 12 * rows * width,
            transcendentals=0,
        ),
    )(chunks, x, g, w_gate, w_up, w_down)


def backward_kernel(
    scale, first, last, x_t_ref, g_ref, own_ref, sib_ref, wg_ref, wu_ref, *refs
):
    gg_ref, gu_ref, gd_ref, *dx_out = refs[3 + (0 if first else 1) :]
    if last:
        *pieces, acc = dx_out
    else:
        (acc_out, acc) = dx_out
    width = wg_ref.shape[1]
    step = pl.program_id(0)
    both = jnp.concatenate([own_ref[0], sib_ref[0]], axis=0)
    scaled = both[:, :width]
    d_gate = both[:, width : 2 * width]
    d_up = both[:, 2 * width :]
    part = lax.dot_general(d_gate, wg_ref[...], LAST_DIMS, preferred_element_type=F32)
    part += lax.dot_general(d_up, wu_ref[...], LAST_DIMS, preferred_element_type=F32)

    @pl.when(step == 0)
    def _():
        if first:
            acc[...] = part
        else:
            acc[...] = refs[3][...] + part

    @pl.when(step == 1)
    def _():
        total = acc[...] + part
        if last:
            rows = pieces[0].shape[0]
            for i, piece in enumerate(pieces):
                piece[...] = total[i * rows : (i + 1) * rows].astype(BF16)
        else:
            acc_out[...] = total

    x_t = x_t_ref[...]
    gg_ref[...] = (jnp.dot(x_t, d_gate, preferred_element_type=F32) * scale).astype(BF16)
    gu_ref[...] = (jnp.dot(x_t, d_up, preferred_element_type=F32) * scale).astype(BF16)
    gd_ref[...] = (
        lax.dot_general(scaled, g_ref[...], ROWS_FIRST, preferred_element_type=F32) * scale
    ).astype(BF16)


def backward_chunk(index, count, scale, x_t, g, own, sib, w_gate, w_up, grads, acc, pieces):
    rows, feats = g.shape
    hidden = w_gate.shape[1]
    half, width = own.shape[1], own.shape[2] // 3
    first, last = index == 0, index == count - 1
    whole = pl.BlockSpec((rows, feats), lambda d: (0, 0))
    anywhere = pl.BlockSpec(memory_space=pl.ANY)
    half_spec = pl.BlockSpec((1, half, 3 * width), lambda d: (d, 0, 0))
    column = pl.BlockSpec((feats, width), lambda d: (0, d * count + index))
    out_shape = [
        jax.ShapeDtypeStruct((feats, hidden), BF16),
        jax.ShapeDtypeStruct((feats, hidden), BF16),
        jax.ShapeDtypeStruct((hidden, feats), BF16),
    ]
    out_specs = [column, column, pl.BlockSpec((width, feats), lambda d: (d * count + index, 0))]
    in_specs = [
        pl.BlockSpec((feats, rows), lambda d: (0, 0)),
        whole,
        half_spec,
        half_spec,
        column,
        column,
    ]
    operands = [x_t, g, own, sib, w_gate, w_up]
    aliases = {}
    if first:
        grads = [jnp.zeros((8, 128), BF16)] * 3
    else:
        aliases = {6: 0, 7: 1, 8: 2}
    operands += list(grads)
    in_specs += [anywhere] * 3
    if not first:
        operands.append(acc)
        in_specs.append(whole)
    if last:
        out_shape += [jax.ShapeDtypeStruct((rows // pieces, feats), BF16)] * pieces
        out_specs += [pl.BlockSpec((rows // pieces, feats), lambda d: (0, 0))] * pieces
    else:
        out_shape += [jax.ShapeDtypeStruct((rows, feats), F32)]
        out_specs += [whole]
    return pl.pallas_call(
        functools.partial(backward_kernel, scale, first, last),
        out_shape=out_shape,
        grid=(2,),
        in_specs=in_specs,
        out_specs=out_specs,
        scratch_shapes=[pltpu.VMEM((rows, feats), F32)],
        input_output_aliases=aliases,
        compiler_params=pltpu.CompilerParams(vmem_limit_bytes=VMEM_LIMIT),
        cost_estimate=pl.CostEstimate(
            flops=20 * rows * feats * width,
            bytes_accessed=12 * rows * feats + 20 * feats * width + 12 * rows * width,
            transcendentals=0,
        ),
    )(*operands)


def activate(total):
    width = total.shape[1] // 3
    gate = total[:, :width]
    upper = total[:, width : 2 * width]
    back = total[:, 2 * width :]
    sig = jax.nn.sigmoid(gate)
    return jnp.concatenate(
        [
            gate * sig * upper,
            back * upper * sig * (1.0 + gate * (1.0 - sig)),
            back * gate * sig,
        ],
        axis=1,
    ).astype(BF16)


def body(tokens, grad_out, expert_ids, route_weights, w_gate, w_up, w_down):
    experts = lax.axis_size("expert")
    groups = lax.axis_size("dp")
    tok_rows = tokens.shape[0]
    feats = w_gate.shape[1]
    hidden = w_gate.shape[2]
    capacity = tok_rows // 2
    chips = groups // 2
    count = chips
    width = hidden // (2 * count)
    assert groups == 2 * experts and tokens.shape[1] == 2 * feats
    inv_root = 1.0 / math.sqrt(tok_rows * groups)
    block = lax.axis_index("dp")
    chip = block // 2
    w_gate, w_up, w_down = w_gate[0], w_up[0], w_down[0]

    side = block // experts
    low = block % experts
    routed = expert_ids >= 0
    matches = (
        expert_ids[:, :, None] == jnp.arange(experts, dtype=jnp.int32)[None, None, :]
    ).astype(jnp.int32)
    flat_match = matches.reshape(tok_rows * 2, experts)
    position = jnp.sum(flat_match * (jnp.cumsum(flat_match, axis=0) - 1), axis=1).reshape(
        tok_rows, 2
    )
    slot_ids = jnp.where(routed, (expert_ids ^ low) * capacity + position, -1)
    slot_match = (
        slot_ids[None, :, :] == jnp.arange(experts * capacity, dtype=jnp.int32)[:, None, None]
    ).astype(F32)
    dispatch = jnp.sum(slot_match, axis=2).astype(BF16)
    slot_weight = jnp.einsum("stk,tk->s", slot_match, route_weights)

    def send_rows(rows, scaling):
        got = []
        for at in range(2):
            start = (side ^ at) * feats
            part = lax.dynamic_slice_in_dim(rows, start, feats, axis=1)
            out = jnp.dot(dispatch, part, preferred_element_type=F32)
            if scaling is not None:
                out = out * scaling[:, None]
            out = out.astype(BF16)
            for i in range(experts):
                got.append(
                    lax.ppermute(
                        out[i * capacity : (i + 1) * capacity],
                        ("expert", "dp"),
                        out_pairs(at * experts + i),
                    )
                )
        return got

    def out_pairs(r):
        pairs = []
        for q in range(experts):
            for b in range(groups):
                e, h = (b ^ r) % experts, (b ^ r) // experts
                pairs.append((q * groups + b, e * groups + 2 * q + h))
        return pairs

    x = jnp.concatenate(send_rows(tokens, None), axis=0)
    g = jnp.concatenate(send_rows(grad_out, slot_weight), axis=0)
    x_t = x.T

    along = (chip, chips - 1 - chip)
    swap = [(j, j ^ 1) for j in range(groups)]
    own, sib = [], []
    for i in range(count):
        chunk = jnp.stack([d * count + (i - along[d]) % count for d in range(2)]).astype(jnp.int32)
        mine, other = forward_chunk(chunk, x, g, w_gate, w_up, w_down, width)
        own.append(mine)
        sib.append(lax.ppermute(other, "dp", swap))

    slots = 2 * count + chips - 2
    zero = jnp.zeros((own[0].shape[1], 3 * width), BF16)
    recv = [[], []]
    done = [[], []]
    for s in range(slots):
        last_recv = [recv[d][s - 1] if s else zero for d in range(2)]
        now_done = [None, None]
        for d in range(2):
            at = along[d]
            total = last_recv[d].astype(F32)
            i = s % count
            if s < count + chips - 1:
                summing = (at <= s) & (s - at < count)
                total = total + jnp.where(
                    summing, own[i][d].astype(F32) + sib[i][d].astype(F32), 0.0
                )
            if chips - 1 <= s < chips - 1 + count:
                now_done[d] = activate(total)
            send = total
            if s >= count and done[1 - d][s - 1] is not None:
                send = jnp.where(at == 0, done[1 - d][s - 1].astype(F32), send)
            send = send.astype(BF16)
            pairs = []
            for z in range(chips - 1):
                if 0 <= s - z < 2 * count:
                    a, b = (z, z + 1) if d == 0 else (chips - 1 - z, chips - 2 - z)
                    pairs += [(2 * a + c, 2 * b + c) for c in range(2)]
            recv[d].append(lax.ppermute(send, "dp", pairs))
        for d in range(2):
            done[d].append(now_done[d])

    grads, acc, pieces = None, None, None
    for k in range(count):
        finished = []
        for d in range(2):
            choice = done[d][chips - 1 + k]
            for hop in range(1, chips):
                choice = jnp.where(
                    along[1 - d] == hop, recv[1 - d][hop - 1 + count + k], choice
                )
            finished.append(choice)
        mine = jnp.stack(finished)
        other = lax.ppermute(mine, "dp", swap)
        out = backward_chunk(
            k, count, inv_root, x_t, g, mine, other, w_gate, w_up, grads, acc, groups
        )
        grads = out[:3]
        if k < count - 1:
            acc = out[3]
        else:
            pieces = out[3:]

    returned = [
        lax.ppermute(piece, ("expert", "dp"), [(b, a) for a, b in out_pairs(r)])
        for r, piece in enumerate(pieces)
    ]
    halves = [
        lax.dot_general(
            dispatch,
            jnp.concatenate(returned[at * experts : (at + 1) * experts], axis=0),
            ROWS_FIRST,
            preferred_element_type=F32,
        ).astype(BF16)
        for at in range(2)
    ]
    grad_tokens = jnp.where(
        side == 0,
        jnp.concatenate(halves, axis=1),
        jnp.concatenate(halves[::-1], axis=1),
    )
    return (grad_tokens, grads[0][None], grads[1][None], grads[2][None])


def solution(mesh):
    in_specs = (
        P("dp", "expert"),
        P("dp", "expert"),
        P("dp", None),
        P("dp", None),
        P("expert", "dp", None),
        P("expert", "dp", None),
        P("expert", None, "dp"),
    )
    out_specs = (
        P("dp", "expert"),
        P("expert", "dp", None),
        P("expert", "dp", None),
        P("expert", None, "dp"),
    )
    return jax.shard_map(body, mesh=mesh, in_specs=in_specs, out_specs=out_specs, check_vma=False)
```

```python
import functools
import math

import jax
import jax.numpy as jnp
from jax import lax
from jax.experimental import pallas as pl
from jax.experimental.pallas import tpu as pltpu
from jax.sharding import PartitionSpec as P

F32 = jnp.float32
BF16 = jnp.bfloat16
LAST_DIMS = (((1,), (1,)), ((), ()))
ROWS_FIRST = (((0,), (0,)), ((), ()))
PARAMS = pltpu.CompilerParams(vmem_limit_bytes=48 * 1024 * 1024)


def dot(a, b, dims=None):
    if dims is None:
        return jnp.dot(a, b, preferred_element_type=F32)
    return lax.dot_general(a, b, dims, preferred_element_type=F32)


def cost(flops, bytes_accessed):
    return pl.CostEstimate(flops=flops, bytes_accessed=bytes_accessed, transcendentals=0)


def slot_one_hot(ids_ref, experts, capacity):
    tokens = ids_ref.shape[1]
    first, second = ids_ref[0:1, :], ids_ref[1:2, :]
    expert = lax.broadcasted_iota(jnp.int32, (8 * (-(-experts // 8)), tokens), 0)
    chosen = (first == expert) | (second == expert)
    before = lax.broadcasted_iota(jnp.int32, (tokens, tokens), 0) < lax.broadcasted_iota(
        jnp.int32, (tokens, tokens), 1
    )
    place = dot(chosen.astype(F32).astype(BF16), before.astype(F32).astype(BF16))
    place = jnp.where(chosen, place, -1.0).astype(jnp.int32)
    slot = lax.broadcasted_iota(jnp.int32, (capacity, tokens), 0)
    return [slot == place[e : e + 1, :] for e in range(experts)]


def dispatch_kernel(experts, weighted, ids_ref, weights_ref, rows_ref, out_ref):
    capacity = out_ref.shape[2]
    rows = rows_ref[0] if len(rows_ref.shape) == 3 else rows_ref[...]
    for e, hit in enumerate(slot_one_hot(ids_ref, experts, capacity)):
        out = dot(hit.astype(F32).astype(BF16), rows)
        if weighted:
            weight = jnp.where(
                ids_ref[0:1, :] == e, weights_ref[0:1, :], weights_ref[1:2, :]
            )
            out = out * jnp.sum(jnp.where(hit, weight, 0.0), axis=1, keepdims=True)
        out_ref[e, 0] = out.astype(BF16)


def dispatch_rows(ids, weights, rows, experts, weighted):
    tokens, feats = rows.shape[0], rows.shape[1] // 2
    capacity = tokens // 2
    small = pl.BlockSpec((2, tokens), lambda h: (0, 0))
    if feats % 128:
        rows = rows.reshape(tokens, 2, feats).transpose(1, 0, 2)
        rows_spec = pl.BlockSpec((1, tokens, feats), lambda h: (h, 0, 0))
    else:
        rows_spec = pl.BlockSpec((tokens, feats), lambda h: (0, h))
    return pl.pallas_call(
        functools.partial(dispatch_kernel, experts, weighted),
        out_shape=jax.ShapeDtypeStruct((experts, 2, capacity, feats), BF16),
        grid=(2,),
        in_specs=[small, small, rows_spec],
        out_specs=pl.BlockSpec((experts, 1, capacity, feats), lambda h: (0, h, 0, 0)),
        compiler_params=PARAMS,
        cost_estimate=cost(
            4 * experts * capacity * tokens * feats, 4 * (tokens + experts * capacity) * feats
        ),
    )(ids, weights, rows)


def combine_kernel(experts, scalar_ref, ids_ref, *refs):
    *pieces, out_ref, hot_ref = refs
    capacity = pieces[0].shape[0]
    at = pl.program_id(0)
    low = scalar_ref[0]

    @pl.when(at == 0)
    def _():
        hits = slot_one_hot(ids_ref, experts, capacity)
        for e in range(experts):
            place = pl.multiple_of((low ^ e) * capacity, capacity)
            hot_ref[pl.ds(place, capacity), :] = hits[e].astype(F32).astype(BF16)

    for half in range(2):

        @pl.when(at == half)
        def _():
            rows = jnp.concatenate(
                [p[...] for p in pieces[half * experts : (half + 1) * experts]], axis=0
            )
            out = dot(hot_ref[...], rows, ROWS_FIRST).astype(BF16)
            out_ref[...] = out.reshape(out_ref.shape)


def combine_rows(scalars, ids, pieces, experts):
    tokens = ids.shape[1]
    capacity, feats = pieces[0].shape
    if feats % 128:
        out_shape = jax.ShapeDtypeStruct((2, tokens, feats), BF16)
        out_spec = pl.BlockSpec((1, tokens, feats), lambda a, c: (a ^ c[1], 0, 0))
    else:
        out_shape = jax.ShapeDtypeStruct((tokens, 2 * feats), BF16)
        out_spec = pl.BlockSpec((tokens, feats), lambda a, c: (0, a ^ c[1]))
    out = pl.pallas_call(
        functools.partial(combine_kernel, experts),
        out_shape=out_shape,
        grid_spec=pltpu.PrefetchScalarGridSpec(
            num_scalar_prefetch=1,
            grid=(2,),
            in_specs=[pl.BlockSpec((2, tokens), lambda a, c: (0, 0))]
            + [pl.BlockSpec((capacity, feats), lambda a, c: (0, 0))] * len(pieces),
            out_specs=out_spec,
            scratch_shapes=[pltpu.VMEM((experts * capacity, tokens), BF16)],
        ),
        compiler_params=PARAMS,
        cost_estimate=cost(
            4 * experts * capacity * tokens * feats, 4 * (tokens + experts * capacity) * feats
        ),
    )(scalars, ids, *pieces)
    if feats % 128:
        out = out.transpose(1, 0, 2).reshape(tokens, 2 * feats)
    return out


def gate_up_kernel(scalar_ref, own_x, other_x, wg_ref, wu_ref, own_ref, other_ref):
    width = wg_ref.shape[1]
    for x_ref, out in ((own_x, own_ref), (other_x, other_ref)):
        out[0, 0, :, :width] = dot(x_ref[...], wg_ref[...]).astype(BF16)
        out[0, 0, :, width:] = dot(x_ref[...], wu_ref[...]).astype(BF16)


def gate_up(scalars, x, w_gate, w_up, count, width):
    rows, feats = x.shape
    half = rows // 2
    out = jax.ShapeDtypeStruct((count, 2, half, 2 * width), BF16)
    out_spec = pl.BlockSpec((1, 1, half, 2 * width), lambda i, d, c: (i, d, 0, 0))
    column = pl.BlockSpec((feats, width), lambda i, d, c: (0, c[1 + 2 * i + d]))
    return pl.pallas_call(
        gate_up_kernel,
        out_shape=(out, out),
        grid_spec=pltpu.PrefetchScalarGridSpec(
            num_scalar_prefetch=1,
            grid=(count, 2),
            in_specs=[
                pl.BlockSpec((half, feats), lambda i, d, c: (c[0], 0)),
                pl.BlockSpec((half, feats), lambda i, d, c: (1 - c[0], 0)),
                column,
                column,
            ],
            out_specs=(out_spec, out_spec),
        ),
        compiler_params=PARAMS,
        cost_estimate=cost(
            8 * count * rows * feats * width,
            2 * rows * feats + 8 * count * width * (feats + rows),
        ),
    )(scalars, x, x, w_gate, w_up)


def back_kernel(scalar_ref, own_g, other_g, wd_ref, own_ref, other_ref):
    own_ref[0, 0] = dot(own_g[...], wd_ref[...], LAST_DIMS).astype(BF16)
    other_ref[0, 0] = dot(other_g[...], wd_ref[...], LAST_DIMS).astype(BF16)


def back_rows(scalars, g, w_down, begin, count, width):
    rows, feats = g.shape
    half = rows // 2
    out = jax.ShapeDtypeStruct((count, 2, half, width), BF16)
    out_spec = pl.BlockSpec((1, 1, half, width), lambda i, d, c: (i, d, 0, 0))
    return pl.pallas_call(
        back_kernel,
        out_shape=(out, out),
        grid_spec=pltpu.PrefetchScalarGridSpec(
            num_scalar_prefetch=1,
            grid=(count, 2),
            in_specs=[
                pl.BlockSpec((half, feats), lambda i, d, c: (c[0], 0)),
                pl.BlockSpec((half, feats), lambda i, d, c: (1 - c[0], 0)),
                pl.BlockSpec((width, feats), lambda i, d, c: (c[1 + 2 * (begin + i) + d], 0)),
            ],
            out_specs=(out_spec, out_spec),
        ),
        compiler_params=PARAMS,
        cost_estimate=cost(
            4 * count * rows * feats * width,
            2 * rows * feats + 4 * count * width * (feats + rows),
        ),
    )(scalars, g, g, w_down)


def activate(gate, upper, back):
    sig = jax.nn.sigmoid(gate)
    gated = gate * sig
    return (
        (gated * upper).astype(BF16),
        (back * upper * sig * (1.0 + gate * (1.0 - sig))).astype(BF16),
        (back * gated).astype(BF16),
    )


def hop_kernel(plan, scalar_ref, *refs):
    slot, count, chips, d, sums, finish, source, came = plan
    refs = list(refs)
    recv_ref = refs.pop(0) if came else None
    terms = [refs.pop(0) for _ in range(4)] if sums else None
    source_ref = refs.pop(0) if source else None
    send_ref = refs.pop(0)
    done_ref = refs.pop(0) if finish else None
    at = scalar_ref[d]
    width = send_ref.shape[1] // 3
    summing = (at <= slot) & (slot - at < count)

    if sums:

        @pl.when(summing)
        def _():
            own_gu, sib_gu, own_b, sib_b = terms
            gate_up_sum = own_gu[0, 0].astype(F32) + sib_gu[0, 0].astype(F32)
            back = own_b[0, 0].astype(F32) + sib_b[0, 0].astype(F32)
            if came:
                gate_up_sum += recv_ref[:, : 2 * width].astype(F32)
                back += recv_ref[:, 2 * width :].astype(F32)
            send_ref[:, : 2 * width] = gate_up_sum.astype(BF16)
            send_ref[:, 2 * width :] = back.astype(BF16)
            if finish:

                @pl.when(at == chips - 1)
                def _():
                    done = activate(gate_up_sum[:, :width], gate_up_sum[:, width:], back)
                    for n, part in enumerate(done):
                        done_ref[:, n * width : (n + 1) * width] = part

    if not came:
        return
    passing = jnp.logical_not(summing)
    if source:

        @pl.when(passing & (at == 0))
        def _():
            send_ref[...] = source_ref[...]

        passing &= at != 0

    @pl.when(passing)
    def _():
        send_ref[...] = recv_ref[...]


def hop(scalars, slot, count, chips, d, recv, terms, source):
    sums = slot < count + chips - 1
    finish = chips - 1 <= slot < chips - 1 + count
    i = slot % count
    own_gu, sib_gu, backs = terms
    half, width = own_gu.shape[2], own_gu.shape[3] // 2
    message = pl.BlockSpec((half, 3 * width), lambda n, c: (0, 0))
    out = jax.ShapeDtypeStruct((half, 3 * width), BF16)
    operands, in_specs = [], []
    if recv is not None:
        operands.append(recv)
        in_specs.append(message)
    if sums:
        begin, own_b, sib_b = next(b for b in reversed(backs) if b[0] <= i)
        operands += [own_gu, sib_gu, own_b, sib_b]
        in_specs += [pl.BlockSpec((1, 1, half, 2 * width), lambda n, c: (i, d, 0, 0))] * 2
        in_specs += [pl.BlockSpec((1, 1, half, width), lambda n, c: (i - begin, d, 0, 0))] * 2
    if source is not None:
        operands.append(source)
        in_specs.append(message)
    plan = (slot, count, chips, d, sums, finish, source is not None, recv is not None)
    outs = pl.pallas_call(
        functools.partial(hop_kernel, plan),
        out_shape=(out, out) if finish else (out,),
        grid_spec=pltpu.PrefetchScalarGridSpec(
            num_scalar_prefetch=1,
            grid=(1,),
            in_specs=in_specs,
            out_specs=(message, message) if finish else (message,),
        ),
        compiler_params=PARAMS,
        cost_estimate=cost(20 * half * width, 18 * half * width),
    )(scalars, *operands)
    return outs[0], (outs[1] if finish else None)


def choose_kernel(scalar_ref, *refs):
    *candidates, out_ref, sem = refs
    hops = len(candidates) // 2
    for d in range(2):
        for n in range(hops):

            @pl.when(scalar_ref[1 - d] == n)
            def _():
                pltpu.make_async_copy(candidates[d * hops + n], out_ref.at[d], sem.at[d]).start()

    for d in range(2):
        pltpu.make_async_copy(candidates[d * hops], out_ref.at[d], sem.at[d]).wait()


def choose(scalars, candidates):
    rows, cols = candidates[0].shape
    return pl.pallas_call(
        choose_kernel,
        out_shape=jax.ShapeDtypeStruct((2, rows, cols), BF16),
        in_specs=[pl.BlockSpec(memory_space=pltpu.SMEM)]
        + [pl.BlockSpec(memory_space=pl.ANY)] * len(candidates),
        out_specs=pl.BlockSpec(memory_space=pl.ANY),
        scratch_shapes=[pltpu.SemaphoreType.DMA((2,))],
        compiler_params=PARAMS,
        cost_estimate=cost(0, 8 * rows * cols),
    )(scalars, *candidates)


def backward_kernel(scale, first, last, experts, scalar_ref, *refs):
    own_xt, other_xt, own_g, other_g, own_ref, sib_ref, wg_ref, wu_ref, *refs = refs
    if not first:
        refs = refs[3:]
        acc_in, *refs = refs
    gg_ref, gu_ref, gd_ref, *dx_out, acc = refs
    half, width = own_ref.shape[1], wg_ref.shape[1]
    step = pl.program_id(0)
    grads = [None] * 3
    for n, (g_in, xt_in, g_rows) in enumerate(
        ((own_ref, own_xt, own_g), (sib_ref, other_xt, other_g))
    ):
        scaled = g_in[0, :, :width]
        d_gate = g_in[0, :, width : 2 * width]
        d_up = g_in[0, :, 2 * width :]
        part = dot(d_gate, wg_ref[...], LAST_DIMS) + dot(d_up, wu_ref[...], LAST_DIMS)
        rows = pl.ds(n * half, half)

        @pl.when(step == 0)
        def _():
            acc[rows, :] = part if first else acc_in[rows, :] + part

        @pl.when(step == 1)
        def _():
            if last:
                acc[rows, :] += part
            else:
                dx_out[0][rows, :] = acc[rows, :] + part

        terms = (
            dot(xt_in[...], d_gate),
            dot(xt_in[...], d_up),
            dot(scaled, g_rows[...], ROWS_FIRST),
        )
        grads = [t if old is None else old + t for old, t in zip(grads, terms)]
    for ref, value in zip((gg_ref, gu_ref, gd_ref), grads):
        ref[...] = (value * scale).astype(BF16)
    if last:

        @pl.when(step == 1)
        def _():
            size = dx_out[0].shape[0]
            for n, piece in enumerate(dx_out):
                start = pl.multiple_of((n ^ scalar_ref[1]) * size, size)
                piece[...] = acc[pl.ds(start, size), :].astype(BF16)


def backward_chunk(scalars, index, count, scale, x_t, g, own, sib, w_gate, w_up, grads, acc, pieces):
    rows, feats = g.shape
    hidden = w_gate.shape[1]
    half, width = own.shape[1], own.shape[2] // 3
    first, last = index == 0, index == count - 1
    whole = pl.BlockSpec((rows, feats), lambda d, c: (0, 0))
    half_spec = pl.BlockSpec((1, half, 3 * width), lambda d, c: (d, 0, 0))
    column = pl.BlockSpec((feats, width), lambda d, c: (0, d * count + index))
    out_shape = [
        jax.ShapeDtypeStruct((feats, hidden), BF16),
        jax.ShapeDtypeStruct((feats, hidden), BF16),
        jax.ShapeDtypeStruct((hidden, feats), BF16),
    ]
    out_specs = [column, column, pl.BlockSpec((width, feats), lambda d, c: (d * count + index, 0))]
    in_specs = [
        pl.BlockSpec((feats, half), lambda d, c: (0, c[0])),
        pl.BlockSpec((feats, half), lambda d, c: (0, 1 - c[0])),
        pl.BlockSpec((half, feats), lambda d, c: (c[0], 0)),
        pl.BlockSpec((half, feats), lambda d, c: (1 - c[0], 0)),
        half_spec,
        half_spec,
        column,
        column,
    ]
    operands = [x_t, x_t, g, g, own, sib, w_gate, w_up]
    aliases = {}
    if not first:
        aliases = {9: 0, 10: 1, 11: 2}
        operands += [*grads, acc]
        in_specs += [pl.BlockSpec(memory_space=pl.ANY)] * 3 + [whole]
    if last:
        out_shape += [jax.ShapeDtypeStruct((rows // pieces, feats), BF16)] * pieces
        out_specs += [pl.BlockSpec((rows // pieces, feats), lambda d, c: (0, 0))] * pieces
    else:
        out_shape += [jax.ShapeDtypeStruct((rows, feats), F32)]
        out_specs += [whole]
    return pl.pallas_call(
        functools.partial(backward_kernel, scale, first, last, pieces // 2),
        out_shape=out_shape,
        grid_spec=pltpu.PrefetchScalarGridSpec(
            num_scalar_prefetch=1,
            grid=(2,),
            in_specs=in_specs,
            out_specs=out_specs,
            scratch_shapes=[pltpu.VMEM((rows, feats), F32)],
        ),
        input_output_aliases=aliases,
        compiler_params=PARAMS,
        cost_estimate=cost(
            20 * rows * feats * width,
            12 * rows * feats + 20 * feats * width + 12 * rows * width,
        ),
    )(scalars, *operands)


def body(tokens, grad_out, expert_ids, route_weights, w_gate, w_up, w_down):
    experts = lax.axis_size("expert")
    groups = lax.axis_size("dp")
    tok_rows = tokens.shape[0]
    feats = w_gate.shape[1]
    hidden = w_gate.shape[2]
    capacity = tok_rows // 2
    chips = groups // 2
    count = chips
    width = hidden // (2 * count)
    assert groups == 2 * experts and tokens.shape[1] == 2 * feats
    inv_root = 1.0 / math.sqrt(tok_rows * groups)
    expert = lax.axis_index("expert").astype(jnp.int32)
    block = lax.axis_index("dp").astype(jnp.int32)
    chip, core = block // 2, block % 2
    along = (chip, chips - 1 - chip)
    w_gate, w_up, w_down = w_gate[0], w_up[0], w_down[0]
    ids, weights = expert_ids.T, route_weights.T

    def exchange(rows, weighted):
        sent = dispatch_rows(ids, weights, rows, experts, weighted)
        sent = lax.all_to_all(sent, "expert", split_axis=0, concat_axis=0, tiled=True)
        sent = sent.reshape(groups, capacity, feats)
        sent = lax.all_to_all(sent, "dp", split_axis=0, concat_axis=0, tiled=True)
        return sent.reshape(groups * capacity, feats)

    swap = [(j, j ^ 1) for j in range(groups)]
    x = exchange(tokens, False)
    g = exchange(grad_out, True)
    x_t = x.T

    order = [core]
    for i in range(count):
        order += [d * count + (i - along[d]) % count for d in range(2)]
    forward_scalars = jnp.stack(order).astype(jnp.int32)
    chain_scalars = jnp.stack(along).astype(jnp.int32)
    own_gu, other_gu = gate_up(forward_scalars, x, w_gate, w_up, count, width)
    sib_gu = lax.ppermute(other_gu, "dp", swap)
    backs = []
    for begin, size in ((0, 1), (1, count - 1)):
        own_b, other_b = back_rows(forward_scalars, g, w_down, begin, size, width)
        backs.append((begin, own_b, lax.ppermute(other_b, "dp", swap)))

    backward_scalars = jnp.stack([core, expert])
    slots = 2 * count + chips - 2
    recv = [[], []]
    done = [[], []]
    grads, acc, pieces = None, None, None

    def backward(k, grads, acc, after):
        candidates = []
        for d in range(2):
            candidates.append(done[d][chips - 1 + k])
            candidates += [recv[1 - d][n - 1 + count + k] for n in range(1, chips)]
        if after:
            *candidates, _ = lax.optimization_barrier((*candidates, after))
        mine = choose(chain_scalars, candidates)
        other = lax.ppermute(mine, "dp", swap)
        out = backward_chunk(
            backward_scalars, k, count, inv_root, x_t, g, mine, other, w_gate, w_up, grads, acc, groups
        )
        return out[:3], out[3:]

    for s in range(slots):
        sends = []
        for d in range(2):
            source = done[1 - d][s - 1] if s >= count else None
            send, finished = hop(
                chain_scalars,
                s,
                count,
                chips,
                d,
                recv[d][s - 1] if s else None,
                (own_gu, sib_gu, backs),
                source,
            )
            pairs = []
            for z in range(chips - 1):
                if 0 <= s - z < 2 * count:
                    a, b = (z, z + 1) if d == 0 else (chips - 1 - z, chips - 2 - z)
                    pairs += [(2 * a + c, 2 * b + c) for c in range(2)]
            recv[d].append(lax.ppermute(send, "dp", pairs))
            done[d].append(finished)
            sends.append(send)
        k = s - (chips - 1 + count)
        if k >= 0:
            grads, acc = backward(k, grads, acc[0] if acc else None, sends)
            recv[0][s], recv[1][s], *rest = lax.optimization_barrier(
                (recv[0][s], recv[1][s], *grads, *acc)
            )
            grads, acc = rest[:3], rest[3:]

    for k in range(slots - (chips - 1 + count), count):
        grads, acc = backward(k, grads, acc[0], None)
    pieces = acc

    def round_pairs(r):
        pairs = []
        for q in range(experts):
            for b in range(groups):
                e, h = (b ^ r) % experts, (b ^ r) // experts
                pairs.append((e * groups + 2 * q + h, q * groups + b))
        return pairs

    returned = [
        lax.ppermute(piece, ("expert", "dp"), round_pairs(r)) for r, piece in enumerate(pieces)
    ]
    combine_scalars = jnp.stack([block % experts, block // experts])
    grad_tokens = combine_rows(combine_scalars, ids, returned, experts)
    return (grad_tokens, grads[0][None], grads[1][None], grads[2][None])


def solution(mesh):
    in_specs = (
        P("dp", "expert"),
        P("dp", "expert"),
        P("dp", None),
        P("dp", None),
        P("expert", "dp", None),
        P("expert", "dp", None),
        P("expert", None, "dp"),
    )
    out_specs = (
        P("dp", "expert"),
        P("expert", "dp", None),
        P("expert", "dp", None),
        P("expert", None, "dp"),
    )
    return jax.shard_map(body, mesh=mesh, in_specs=in_specs, out_specs=out_specs, check_vma=False)
```

```python
import functools
import math

import jax
import jax.numpy as jnp
from jax import lax
from jax.experimental import pallas as pl
from jax.experimental.pallas import tpu as pltpu
from jax.sharding import PartitionSpec as P

F32 = jnp.float32
BF16 = jnp.bfloat16
LAST_DIMS = (((1,), (1,)), ((), ()))
ROWS_FIRST = (((0,), (0,)), ((), ()))
PARAMS = pltpu.CompilerParams(vmem_limit_bytes=48 * 1024 * 1024)


def dot(a, b, dims=None):
    if dims is None:
        return jnp.dot(a, b, preferred_element_type=F32)
    return lax.dot_general(a, b, dims, preferred_element_type=F32)


def cost(flops, bytes_accessed):
    return pl.CostEstimate(flops=flops, bytes_accessed=bytes_accessed, transcendentals=0)


def slot_one_hot(ids_ref, experts, capacity):
    tokens = ids_ref.shape[1]
    first, second = ids_ref[0:1, :], ids_ref[1:2, :]
    expert = lax.broadcasted_iota(jnp.int32, (8 * (-(-experts // 8)), tokens), 0)
    chosen = (first == expert) | (second == expert)
    before = lax.broadcasted_iota(jnp.int32, (tokens, tokens), 0) < lax.broadcasted_iota(
        jnp.int32, (tokens, tokens), 1
    )
    place = dot(chosen.astype(F32).astype(BF16), before.astype(F32).astype(BF16))
    place = jnp.where(chosen, place, -1.0).astype(jnp.int32)
    slot = lax.broadcasted_iota(jnp.int32, (capacity, tokens), 0)
    return [slot == place[e : e + 1, :] for e in range(experts)]


def dispatch_kernel(experts, ids_ref, weights_ref, x_ref, g_ref, out_ref):
    capacity = out_ref.shape[2] // 2
    x, g = (r[0] if len(r.shape) == 3 else r[...] for r in (x_ref, g_ref))
    for e, hit in enumerate(slot_one_hot(ids_ref, experts, capacity)):
        hot = hit.astype(F32).astype(BF16)
        out_ref[e, 0, :capacity] = dot(hot, x).astype(BF16)
        weight = jnp.where(ids_ref[0:1, :] == e, weights_ref[0:1, :], weights_ref[1:2, :])
        weight = jnp.sum(jnp.where(hit, weight, 0.0), axis=1, keepdims=True)
        out_ref[e, 0, capacity:] = (dot(hot, g) * weight).astype(BF16)


def dispatch_rows(ids, weights, x, g, experts):
    tokens, feats = x.shape[0], x.shape[1] // 2
    capacity = tokens // 2
    small = pl.BlockSpec((2, tokens), lambda h: (0, 0))
    if feats % 128:
        x, g = (r.reshape(tokens, 2, feats).transpose(1, 0, 2) for r in (x, g))
        rows_spec = pl.BlockSpec((1, tokens, feats), lambda h: (h, 0, 0))
    else:
        rows_spec = pl.BlockSpec((tokens, feats), lambda h: (0, h))
    return pl.pallas_call(
        functools.partial(dispatch_kernel, experts),
        out_shape=jax.ShapeDtypeStruct((experts, 2, 2 * capacity, feats), BF16),
        grid=(2,),
        in_specs=[small, small, rows_spec, rows_spec],
        out_specs=pl.BlockSpec((experts, 1, 2 * capacity, feats), lambda h: (0, h, 0, 0)),
        compiler_params=PARAMS,
        cost_estimate=cost(
            8 * experts * capacity * tokens * feats, 8 * (tokens + experts * capacity) * feats
        ),
    )(ids, weights, x, g)


def combine_kernel(experts, scalar_ref, ids_ref, *refs):
    *pieces, out_ref, hot_ref = refs
    capacity = pieces[0].shape[0]
    at = pl.program_id(0)
    low = scalar_ref[0]

    @pl.when(at == 0)
    def _():
        hits = slot_one_hot(ids_ref, experts, capacity)
        for e in range(experts):
            place = pl.multiple_of((low ^ e) * capacity, capacity)
            hot_ref[pl.ds(place, capacity), :] = hits[e].astype(F32).astype(BF16)

    for half in range(2):

        @pl.when(at == half)
        def _():
            rows = jnp.concatenate(
                [p[...] for p in pieces[half * experts : (half + 1) * experts]], axis=0
            )
            out = dot(hot_ref[...], rows, ROWS_FIRST).astype(BF16)
            out_ref[...] = out.reshape(out_ref.shape)


def combine_rows(scalars, ids, pieces, experts):
    tokens = ids.shape[1]
    capacity, feats = pieces[0].shape
    if feats % 128:
        out_shape = jax.ShapeDtypeStruct((2, tokens, feats), BF16)
        out_spec = pl.BlockSpec((1, tokens, feats), lambda a, c: (a ^ c[1], 0, 0))
    else:
        out_shape = jax.ShapeDtypeStruct((tokens, 2 * feats), BF16)
        out_spec = pl.BlockSpec((tokens, feats), lambda a, c: (0, a ^ c[1]))
    out = pl.pallas_call(
        functools.partial(combine_kernel, experts),
        out_shape=out_shape,
        grid_spec=pltpu.PrefetchScalarGridSpec(
            num_scalar_prefetch=1,
            grid=(2,),
            in_specs=[pl.BlockSpec((2, tokens), lambda a, c: (0, 0))]
            + [pl.BlockSpec((capacity, feats), lambda a, c: (0, 0))] * len(pieces),
            out_specs=out_spec,
            scratch_shapes=[pltpu.VMEM((experts * capacity, tokens), BF16)],
        ),
        compiler_params=PARAMS,
        cost_estimate=cost(
            4 * experts * capacity * tokens * feats, 4 * (tokens + experts * capacity) * feats
        ),
    )(scalars, ids, *pieces)
    if feats % 128:
        out = out.transpose(1, 0, 2).reshape(tokens, 2 * feats)
    return out


def forward_kernel(scalar_ref, x_ref, g_ref, wg_ref, wu_ref, wd_ref, out_ref):
    width = wg_ref.shape[1]
    blocks, _, capacity, feats = x_ref.shape
    x = x_ref[...].reshape(blocks * capacity, feats)
    g = g_ref[...].reshape(blocks * capacity, feats)
    out_ref[0, :, :width] = dot(x, wg_ref[...]).astype(BF16)
    out_ref[0, :, width : 2 * width] = dot(x, wu_ref[...]).astype(BF16)
    out_ref[0, :, 2 * width :] = dot(g, wd_ref[...], LAST_DIMS).astype(BF16)


def forward_chunks(scalars, rows, w_gate, w_up, w_down, begin, size, own, count):
    groups, _, capacity, feats = rows.shape
    width = w_gate.shape[1] // (2 * count)
    blocks = groups // 2

    def at(i, c):
        return c[own * count + begin + i]

    return pl.pallas_call(
        forward_kernel,
        out_shape=jax.ShapeDtypeStruct((size, groups * capacity, 3 * width), BF16),
        grid_spec=pltpu.PrefetchScalarGridSpec(
            num_scalar_prefetch=1,
            grid=(size, 2),
            in_specs=[
                pl.BlockSpec((blocks, 1, capacity, feats), lambda i, n, c: (n, 0, 0, 0)),
                pl.BlockSpec((blocks, 1, capacity, feats), lambda i, n, c: (n, 1, 0, 0)),
                pl.BlockSpec((feats, width), lambda i, n, c: (0, at(i, c))),
                pl.BlockSpec((feats, width), lambda i, n, c: (0, at(i, c))),
                pl.BlockSpec((width, feats), lambda i, n, c: (at(i, c), 0)),
            ],
            out_specs=pl.BlockSpec((1, blocks * capacity, 3 * width), lambda i, n, c: (i, n, 0)),
        ),
        compiler_params=PARAMS,
        cost_estimate=cost(
            6 * size * groups * capacity * feats * width,
            4 * groups * capacity * feats + 6 * size * width * (feats + groups * capacity),
        ),
    )(scalars, rows, rows, w_gate, w_up, w_down)


def activate(gate, upper, back):
    sig = jax.nn.sigmoid(gate)
    gated = gate * sig
    return (
        (gated * upper).astype(BF16),
        (back * upper * sig * (1.0 + gate * (1.0 - sig))).astype(BF16),
        (back * gated).astype(BF16),
    )


def hop_kernel(plan, scalar_ref, *refs):
    slot, count, chips, sums, came = plan
    refs = list(refs)
    recv_ref = refs.pop(0) if came else None
    own_ref, sib_ref = refs[:2] if sums else (None, None)
    send_ref = refs[-1]
    at = scalar_ref[0]
    width = send_ref.shape[1] // 3
    summing = (at <= slot) & (slot - at < count)

    def total(part):
        columns = slice(part * width, (part + 1) * width)
        value = own_ref[0, :, columns].astype(F32) + sib_ref[0, :, columns].astype(F32)
        if came:
            value += jnp.where(at > 0, recv_ref[:, columns].astype(F32), 0.0)
        return value

    if sums:

        @pl.when(summing & (at < chips - 1))
        def _():
            for part in range(3):
                send_ref[:, part * width : (part + 1) * width] = total(part).astype(BF16)

        @pl.when(summing & (at == chips - 1))
        def _():
            for part, value in enumerate(activate(total(0), total(1), total(2))):
                send_ref[:, part * width : (part + 1) * width] = value

    if came:

        @pl.when(jnp.logical_not(summing))
        def _():
            send_ref[...] = recv_ref[...]


def hop(scalars, slot, count, chips, recv, sums):
    rows, cols = sums[0][0].shape[1:]
    tile = rows // 2
    message = pl.BlockSpec((tile, cols), lambda n, c: (n, 0))
    operands, in_specs = [], []
    if recv is not None:
        operands.append(recv)
        in_specs.append(message)
    adds = slot < count + chips - 1
    if adds:
        for array, i in sums:
            operands.append(array)
            in_specs.append(pl.BlockSpec((1, tile, cols), lambda n, c, i=i: (i, n, 0)))
    plan = (slot, count, chips, adds, recv is not None)
    return pl.pallas_call(
        functools.partial(hop_kernel, plan),
        out_shape=jax.ShapeDtypeStruct((rows, cols), BF16),
        grid_spec=pltpu.PrefetchScalarGridSpec(
            num_scalar_prefetch=1,
            grid=(rows // tile,),
            in_specs=in_specs,
            out_specs=message,
        ),
        compiler_params=PARAMS,
        cost_estimate=cost(4 * rows * cols, 8 * rows * cols),
    )(scalars, *operands)


def choose_kernel(scalar_ref, *refs):
    *candidates, out_ref, sem = refs
    for n, candidate in enumerate(candidates):

        @pl.when(scalar_ref[0] == n)
        def _():
            pltpu.make_async_copy(candidate, out_ref, sem).start()

    pltpu.make_async_copy(candidates[0], out_ref, sem).wait()


def choose(scalars, candidates):
    rows, cols = candidates[0].shape
    return pl.pallas_call(
        choose_kernel,
        out_shape=jax.ShapeDtypeStruct((rows, cols), BF16),
        in_specs=[pl.BlockSpec(memory_space=pltpu.SMEM)]
        + [pl.BlockSpec(memory_space=pl.ANY)] * len(candidates),
        out_specs=pl.BlockSpec(memory_space=pl.ANY),
        scratch_shapes=[pltpu.SemaphoreType.DMA],
        compiler_params=PARAMS,
        cost_estimate=cost(0, 4 * rows * cols),
    )(scalars, *candidates)


def backward_kernel(scale, first, last, scalar_ref, *refs):
    xt_ref, g_ref, mine_ref, other_ref, wg_ref, wu_ref, *refs = refs
    if not first:
        refs = refs[3:]
        acc_in, *refs = refs
    gg_ref, gu_ref, gd_ref, *dx_out, acc = refs
    width = wg_ref.shape[1]
    step = pl.program_id(0)

    def chunk(in_ref, before, after):
        scaled = in_ref[:, :width]
        d_gate = in_ref[:, width : 2 * width]
        d_up = in_ref[:, 2 * width :]
        part = dot(d_gate, wg_ref[...], LAST_DIMS) + dot(d_up, wu_ref[...], LAST_DIMS)
        after[...] = part if before is None else before[...] + part
        gg_ref[...] = (dot(xt_ref[...], d_gate) * scale).astype(BF16)
        gu_ref[...] = (dot(xt_ref[...], d_up) * scale).astype(BF16)
        blocks, _, capacity, feats = g_ref.shape
        rows = g_ref[...].reshape(blocks * capacity, feats)
        gd_ref[...] = (dot(scaled, rows, ROWS_FIRST) * scale).astype(BF16)

    @pl.when(step == 0)
    def _():
        chunk(mine_ref, None if first else acc_in, acc)

    @pl.when(step == 1)
    def _():
        chunk(other_ref, acc, acc if last else dx_out[0])
        if last:
            size = dx_out[0].shape[0]
            for n, piece in enumerate(dx_out):
                start = pl.multiple_of((n ^ scalar_ref[1]) * size, size)
                piece[...] = acc[pl.ds(start, size), :].astype(BF16)


def backward_chunk(scalars, index, count, scale, x_t, rows, mine, other, w_gate, w_up, grads, acc):
    groups, _, capacity, feats = rows.shape
    slots = groups * capacity
    hidden = w_gate.shape[1]
    width = mine.shape[1] // 3
    first, last = index == 0, index == count - 1
    whole = pl.BlockSpec((slots, feats), lambda d, c: (0, 0))
    message = pl.BlockSpec((slots, 3 * width), lambda d, c: (0, 0))

    def at(d, c):
        return (d ^ 1 ^ c[0]) * count + index

    column = pl.BlockSpec((feats, width), lambda d, c: (0, at(d, c)))
    out_shape = [
        jax.ShapeDtypeStruct((feats, hidden), BF16),
        jax.ShapeDtypeStruct((feats, hidden), BF16),
        jax.ShapeDtypeStruct((hidden, feats), BF16),
    ]
    out_specs = [column, column, pl.BlockSpec((width, feats), lambda d, c: (at(d, c), 0))]
    in_specs = [
        pl.BlockSpec((feats, slots), lambda d, c: (0, 0)),
        pl.BlockSpec((groups, 1, capacity, feats), lambda d, c: (0, 1, 0, 0)),
        message,
        message,
        column,
        column,
    ]
    operands = [x_t, rows, mine, other, w_gate, w_up]
    aliases = {}
    if not first:
        aliases = {7: 0, 8: 1, 9: 2}
        operands += [*grads, acc]
        in_specs += [pl.BlockSpec(memory_space=pl.ANY)] * 3 + [whole]
    if last:
        out_shape += [jax.ShapeDtypeStruct((capacity, feats), BF16)] * groups
        out_specs += [pl.BlockSpec((capacity, feats), lambda d, c: (0, 0))] * groups
    else:
        out_shape += [jax.ShapeDtypeStruct((slots, feats), F32)]
        out_specs += [whole]
    return pl.pallas_call(
        functools.partial(backward_kernel, scale, first, last),
        out_shape=out_shape,
        grid_spec=pltpu.PrefetchScalarGridSpec(
            num_scalar_prefetch=1,
            grid=(2,),
            in_specs=in_specs,
            out_specs=out_specs,
            scratch_shapes=[pltpu.VMEM((slots, feats), F32)],
        ),
        input_output_aliases=aliases,
        compiler_params=PARAMS,
        cost_estimate=cost(
            20 * slots * feats * width,
            12 * slots * feats + 20 * feats * width + 12 * slots * width,
        ),
    )(scalars, *operands)


def body(tokens, grad_out, expert_ids, route_weights, w_gate, w_up, w_down):
    experts = lax.axis_size("expert")
    groups = lax.axis_size("dp")
    tok_rows = tokens.shape[0]
    feats = w_gate.shape[1]
    capacity = tok_rows // 2
    chips = groups // 2
    count = chips
    assert groups == 2 * experts and tokens.shape[1] == 2 * feats
    inv_root = 1.0 / math.sqrt(tok_rows * groups)
    expert = lax.axis_index("expert").astype(jnp.int32)
    block = lax.axis_index("dp").astype(jnp.int32)
    chip, core = block // 2, block % 2
    along = jnp.where(core == 0, chip, chips - 1 - chip)
    w_gate, w_up, w_down = w_gate[0], w_up[0], w_down[0]
    ids, weights = expert_ids.T, route_weights.T

    rows = dispatch_rows(ids, weights, tokens, grad_out, experts)
    rows = lax.all_to_all(rows, "expert", split_axis=0, concat_axis=0, tiled=True)
    rows = rows.reshape(groups, 2 * capacity, feats)
    rows = lax.all_to_all(rows, "dp", split_axis=0, concat_axis=0, tiled=True)
    rows = rows.reshape(groups, 2, capacity, feats)

    swap = [(j, j ^ 1) for j in range(groups)]
    up = [2 * z for z in range(chips)]
    circle = up + [j + 1 for j in reversed(up)]
    ring = list(zip(circle, circle[1:] + circle[:1]))
    order = [(1 - core) * count + (i - (chips - 1 - along)) % count for i in range(count)]
    order += [core * count + (i - along) % count for i in range(count)]
    forward_scalars = jnp.stack(order).astype(jnp.int32)
    chain_scalars = along.astype(jnp.int32)[None]
    backward_scalars = jnp.stack([core, expert + experts * core]).astype(jnp.int32)

    sums = []
    for begin, size in ((0, 1), (1, 1), (2, count - 2)):
        other, mine = (
            forward_chunks(forward_scalars, rows, w_gate, w_up, w_down, begin, size, own, count)
            for own in range(2)
        )
        sib = lax.ppermute(other, "dp", swap)
        sums += [((mine, i), (sib, i)) for i in range(size)]
    x_t = rows[:, 0].reshape(groups * capacity, feats).T

    slots = 2 * count + chips - 2
    recv = []
    grads, acc = None, None

    def backward(k, grads, acc, after):
        candidates = [recv[n - 1 + count + k] for n in range(chips)]
        if after is not None:
            *candidates, _ = lax.optimization_barrier((*candidates, after))
        mine = choose(chain_scalars, candidates)
        other = lax.ppermute(mine, "dp", swap)
        out = backward_chunk(
            backward_scalars, k, count, inv_root, x_t, rows, mine, other, w_gate, w_up, grads, acc
        )
        return out[:3], out[3:]

    for s in range(slots):
        send = hop(chain_scalars, s, count, chips, recv[s - 1] if s else None, sums[s % count])
        recv.append(lax.ppermute(send, "dp", ring))
        k = s - (chips - 1 + count)
        if k >= 0:
            grads, acc = backward(k, grads, acc[0] if acc else None, send)
            recv[s], *rest = lax.optimization_barrier((recv[s], *grads, *acc))
            grads, acc = rest[:3], rest[3:]

    for k in range(slots - (chips - 1 + count), count):
        grads, acc = backward(k, grads, acc[0], None)
    pieces = acc

    def round_pairs(r):
        pairs = []
        for q in range(experts):
            for b in range(groups):
                e, h = (b ^ r) % experts, (b ^ r) // experts
                pairs.append((e * groups + 2 * q + h, q * groups + b))
        return pairs

    returned = [
        lax.ppermute(piece, ("expert", "dp"), round_pairs(r)) for r, piece in enumerate(pieces)
    ]
    combine_scalars = jnp.stack([block % experts, block // experts])
    grad_tokens = combine_rows(combine_scalars, ids, returned, experts)
    return (grad_tokens, grads[0][None], grads[1][None], grads[2][None])


def solution(mesh):
    in_specs = (
        P("dp", "expert"),
        P("dp", "expert"),
        P("dp", None),
        P("dp", None),
        P("expert", "dp", None),
        P("expert", "dp", None),
        P("expert", None, "dp"),
    )
    out_specs = (
        P("dp", "expert"),
        P("expert", "dp", None),
        P("expert", "dp", None),
        P("expert", None, "dp"),
    )
    return jax.shard_map(body, mesh=mesh, in_specs=in_specs, out_specs=out_specs, check_vma=False)
```

```python
import functools
import math

import jax
import jax.numpy as jnp
from jax import lax
from jax.experimental import pallas as pl
from jax.experimental.pallas import tpu as pltpu
from jax.sharding import PartitionSpec as P

F32 = jnp.float32
BF16 = jnp.bfloat16
LAST_DIMS = (((1,), (1,)), ((), ()))
ROWS_FIRST = (((0,), (0,)), ((), ()))
PARTS = 2
PARAMS = pltpu.CompilerParams(vmem_limit_bytes=48 * 1024 * 1024)


def dot(a, b, dims=None):
    if dims is None:
        return jnp.dot(a, b, preferred_element_type=F32)
    return lax.dot_general(a, b, dims, preferred_element_type=F32)


def cost(flops, bytes_accessed):
    return pl.CostEstimate(flops=flops, bytes_accessed=bytes_accessed, transcendentals=0)


def slot_one_hot(ids_ref, experts, capacity):
    tokens = ids_ref.shape[1]
    first, second = ids_ref[0:1, :], ids_ref[1:2, :]
    expert = lax.broadcasted_iota(jnp.int32, (8 * (-(-experts // 8)), tokens), 0)
    chosen = (first == expert) | (second == expert)
    before = lax.broadcasted_iota(jnp.int32, (tokens, tokens), 0) < lax.broadcasted_iota(
        jnp.int32, (tokens, tokens), 1
    )
    place = dot(chosen.astype(F32).astype(BF16), before.astype(F32).astype(BF16))
    place = jnp.where(chosen, place, -1.0).astype(jnp.int32)
    slot = lax.broadcasted_iota(jnp.int32, (capacity, tokens), 0)
    return [slot == place[e : e + 1, :] for e in range(experts)]


def dispatch_kernel(experts, ids_ref, weights_ref, x_ref, g_ref, out_ref):
    capacity = out_ref.shape[2] // 2
    x, g = (r[0] if len(r.shape) == 3 else r[...] for r in (x_ref, g_ref))
    for e, hit in enumerate(slot_one_hot(ids_ref, experts, capacity)):
        hot = hit.astype(F32).astype(BF16)
        out_ref[e, 0, :capacity] = dot(hot, x).astype(BF16)
        weight = jnp.where(ids_ref[0:1, :] == e, weights_ref[0:1, :], weights_ref[1:2, :])
        weight = jnp.sum(jnp.where(hit, weight, 0.0), axis=1, keepdims=True)
        out_ref[e, 0, capacity:] = (dot(hot, g) * weight).astype(BF16)


def dispatch_rows(ids, weights, x, g, experts):
    tokens, feats = x.shape[0], x.shape[1] // 2
    capacity = tokens // 2
    small = pl.BlockSpec((2, tokens), lambda h: (0, 0))
    if feats % 128:
        x, g = (r.reshape(tokens, 2, feats).transpose(1, 0, 2) for r in (x, g))
        rows_spec = pl.BlockSpec((1, tokens, feats), lambda h: (h, 0, 0))
    else:
        rows_spec = pl.BlockSpec((tokens, feats), lambda h: (0, h))
    return pl.pallas_call(
        functools.partial(dispatch_kernel, experts),
        out_shape=jax.ShapeDtypeStruct((experts, 2, 2 * capacity, feats), BF16),
        grid=(2,),
        in_specs=[small, small, rows_spec, rows_spec],
        out_specs=pl.BlockSpec((experts, 1, 2 * capacity, feats), lambda h: (0, h, 0, 0)),
        compiler_params=PARAMS,
        cost_estimate=cost(
            8 * experts * capacity * tokens * feats, 8 * (tokens + experts * capacity) * feats
        ),
    )(ids, weights, x, g)


def combine_kernel(experts, scalar_ref, ids_ref, *refs):
    *pieces, out_ref, hot_ref = refs
    capacity = pieces[0].shape[0]
    at = pl.program_id(0)
    low = scalar_ref[0]

    @pl.when(at == 0)
    def _():
        hits = slot_one_hot(ids_ref, experts, capacity)
        for e in range(experts):
            place = pl.multiple_of((low ^ e) * capacity, capacity)
            hot_ref[pl.ds(place, capacity), :] = hits[e].astype(F32).astype(BF16)

    for half in range(2):

        @pl.when(at == half)
        def _():
            rows = jnp.concatenate(
                [p[...] for p in pieces[half * experts : (half + 1) * experts]], axis=0
            )
            out = dot(hot_ref[...], rows, ROWS_FIRST).astype(BF16)
            out_ref[...] = out.reshape(out_ref.shape)


def combine_rows(scalars, ids, pieces, experts):
    tokens = ids.shape[1]
    capacity, feats = pieces[0].shape
    if feats % 128:
        out_shape = jax.ShapeDtypeStruct((2, tokens, feats), BF16)
        out_spec = pl.BlockSpec((1, tokens, feats), lambda a, c: (a ^ c[1], 0, 0))
    else:
        out_shape = jax.ShapeDtypeStruct((tokens, 2 * feats), BF16)
        out_spec = pl.BlockSpec((tokens, feats), lambda a, c: (0, a ^ c[1]))
    out = pl.pallas_call(
        functools.partial(combine_kernel, experts),
        out_shape=out_shape,
        grid_spec=pltpu.PrefetchScalarGridSpec(
            num_scalar_prefetch=1,
            grid=(2,),
            in_specs=[pl.BlockSpec((2, tokens), lambda a, c: (0, 0))]
            + [pl.BlockSpec((capacity, feats), lambda a, c: (0, 0))] * len(pieces),
            out_specs=out_spec,
            scratch_shapes=[pltpu.VMEM((experts * capacity, tokens), BF16)],
        ),
        compiler_params=PARAMS,
        cost_estimate=cost(
            4 * experts * capacity * tokens * feats, 4 * (tokens + experts * capacity) * feats
        ),
    )(scalars, ids, *pieces)
    if feats % 128:
        out = out.transpose(1, 0, 2).reshape(tokens, 2 * feats)
    return out


def forward_kernel(scalar_ref, x_ref, g_ref, wg_ref, wu_ref, wd_ref, out_ref):
    width = wg_ref.shape[1]
    blocks, _, capacity, feats = x_ref.shape
    x = x_ref[...].reshape(blocks * capacity, feats)
    g = g_ref[...].reshape(blocks * capacity, feats)
    out_ref[0, :, :width] = dot(x, wg_ref[...]).astype(BF16)
    out_ref[0, :, width : 2 * width] = dot(x, wu_ref[...]).astype(BF16)
    out_ref[0, :, 2 * width :] = dot(g, wd_ref[...], LAST_DIMS).astype(BF16)


def forward_chunks(scalars, rows, w_gate, w_up, w_down, begin, size, own, count):
    groups, _, capacity, feats = rows.shape
    width = w_gate.shape[1] // (2 * count)
    blocks = groups // 2

    def at(i, c):
        return c[own * count + begin + i]

    return pl.pallas_call(
        forward_kernel,
        out_shape=jax.ShapeDtypeStruct((size, groups * capacity, 3 * width), BF16),
        grid_spec=pltpu.PrefetchScalarGridSpec(
            num_scalar_prefetch=1,
            grid=(size, 2),
            in_specs=[
                pl.BlockSpec((blocks, 1, capacity, feats), lambda i, n, c: (n, 0, 0, 0)),
                pl.BlockSpec((blocks, 1, capacity, feats), lambda i, n, c: (n, 1, 0, 0)),
                pl.BlockSpec((feats, width), lambda i, n, c: (0, at(i, c))),
                pl.BlockSpec((feats, width), lambda i, n, c: (0, at(i, c))),
                pl.BlockSpec((width, feats), lambda i, n, c: (at(i, c), 0)),
            ],
            out_specs=pl.BlockSpec((1, blocks * capacity, 3 * width), lambda i, n, c: (i, n, 0)),
        ),
        compiler_params=PARAMS,
        cost_estimate=cost(
            6 * size * groups * capacity * feats * width,
            4 * groups * capacity * feats + 6 * size * width * (feats + groups * capacity),
        ),
    )(scalars, rows, rows, w_gate, w_up, w_down)


def activate(gate, upper, back):
    sig = jax.nn.sigmoid(gate)
    gated = gate * sig
    return (
        (gated * upper).astype(BF16),
        (back * upper * sig * (1.0 + gate * (1.0 - sig))).astype(BF16),
        (back * gated).astype(BF16),
    )


def hop_kernel(plan, scalar_ref, *refs):
    slot, count, chips, sums, came = plan
    refs = list(refs)
    recv_ref = refs.pop(0) if came else None
    own_ref, sib_ref = refs[:2] if sums else (None, None)
    send_ref = refs[-1]
    at = scalar_ref[0]
    width = send_ref.shape[1] // 3
    summing = (at <= slot) & (slot - at < count)

    def total(part):
        columns = slice(part * width, (part + 1) * width)
        value = own_ref[0, :, columns].astype(F32) + sib_ref[0, :, columns].astype(F32)
        if came:
            value += jnp.where(at > 0, recv_ref[:, columns].astype(F32), 0.0)
        return value

    if sums:

        @pl.when(summing & (at < chips - 1))
        def _():
            for part in range(3):
                send_ref[:, part * width : (part + 1) * width] = total(part).astype(BF16)

        @pl.when(summing & (at == chips - 1))
        def _():
            for part, value in enumerate(activate(total(0), total(1), total(2))):
                send_ref[:, part * width : (part + 1) * width] = value

    if came:

        @pl.when(jnp.logical_not(summing))
        def _():
            send_ref[...] = recv_ref[...]


def hop(scalars, slot, count, chips, recv, sums, part):
    rows, cols = sums[0][0].shape[1:]
    rows //= PARTS
    message = pl.BlockSpec((rows, cols), lambda n, c: (0, 0))
    operands, in_specs = [], []
    if recv is not None:
        operands.append(recv)
        in_specs.append(message)
    adds = slot < count + chips - 1
    if adds:
        for array, i in sums:
            operands.append(array)
            in_specs.append(pl.BlockSpec((1, rows, cols), lambda n, c, i=i: (i, part, 0)))
    plan = (slot, count, chips, adds, recv is not None)
    return pl.pallas_call(
        functools.partial(hop_kernel, plan),
        out_shape=jax.ShapeDtypeStruct((rows, cols), BF16),
        grid_spec=pltpu.PrefetchScalarGridSpec(
            num_scalar_prefetch=1,
            grid=(1,),
            in_specs=in_specs,
            out_specs=message,
        ),
        compiler_params=PARAMS,
        cost_estimate=cost(4 * rows * cols, 8 * rows * cols),
    )(scalars, *operands)


def choose_kernel(scalar_ref, *refs):
    *candidates, out_ref, sems = refs
    rows = candidates[0].shape[0]

    def copy(n, part):
        return pltpu.make_async_copy(
            candidates[n * PARTS + part], out_ref.at[pl.ds(part * rows, rows)], sems.at[part]
        )

    for n in range(len(candidates) // PARTS):

        @pl.when(scalar_ref[0] == n)
        def _():
            for part in range(PARTS):
                copy(n, part).start()

    for part in range(PARTS):
        copy(0, part).wait()


def choose(scalars, candidates):
    rows, cols = candidates[0].shape
    return pl.pallas_call(
        choose_kernel,
        out_shape=jax.ShapeDtypeStruct((rows * PARTS, cols), BF16),
        in_specs=[pl.BlockSpec(memory_space=pltpu.SMEM)]
        + [pl.BlockSpec(memory_space=pl.ANY)] * len(candidates),
        out_specs=pl.BlockSpec(memory_space=pl.ANY),
        scratch_shapes=[pltpu.SemaphoreType.DMA((PARTS,))],
        compiler_params=PARAMS,
        cost_estimate=cost(0, 4 * rows * PARTS * cols),
    )(scalars, *candidates)


def gradients_kernel(scale, with_rows, first, scalar_ref, *refs):
    xt_ref, g_ref, mine_ref, other_ref, *refs = refs
    if with_rows:
        wg_ref, wu_ref, *refs = refs
    if not first:
        refs = refs[3:]
    if with_rows and not first:
        acc_in, *refs = refs
    gg_ref, gu_ref, gd_ref, *refs = refs
    width = gg_ref.shape[1]

    def chunk(in_ref, before, after):
        scaled = in_ref[:, :width]
        d_gate = in_ref[:, width : 2 * width]
        d_up = in_ref[:, 2 * width :]
        if with_rows:
            part = dot(d_gate, wg_ref[...], LAST_DIMS) + dot(d_up, wu_ref[...], LAST_DIMS)
            after[...] = part if before is None else before[...] + part
        gg_ref[...] = (dot(xt_ref[...], d_gate) * scale).astype(BF16)
        gu_ref[...] = (dot(xt_ref[...], d_up) * scale).astype(BF16)
        blocks, _, capacity, feats = g_ref.shape
        rows = g_ref[...].reshape(blocks * capacity, feats)
        gd_ref[...] = (dot(scaled, rows, ROWS_FIRST) * scale).astype(BF16)

    acc_out, acc = refs if with_rows else (None, None)

    @pl.when(pl.program_id(0) == 0)
    def _():
        chunk(mine_ref, None if first else (acc_in if with_rows else None), acc)

    @pl.when(pl.program_id(0) == 1)
    def _():
        chunk(other_ref, acc, acc_out)


def chunk_at(count, index):
    return lambda d, c: (d ^ 1 ^ c[0]) * count + index


def gradients(scalars, index, count, scale, x_t, rows, mine, other, weights, grads, acc):
    groups, _, capacity, feats = rows.shape
    slots = groups * capacity
    width = mine.shape[1] // 3
    hidden = 2 * count * width
    first, with_rows = grads is None, bool(weights)
    whole = pl.BlockSpec((slots, feats), lambda d, c: (0, 0))
    message = pl.BlockSpec((slots, 3 * width), lambda d, c: (0, 0))
    at = chunk_at(count, index)
    column = pl.BlockSpec((feats, width), lambda d, c: (0, at(d, c)))
    out_shape = [
        jax.ShapeDtypeStruct((feats, hidden), BF16),
        jax.ShapeDtypeStruct((feats, hidden), BF16),
        jax.ShapeDtypeStruct((hidden, feats), BF16),
    ]
    out_specs = [column, column, pl.BlockSpec((width, feats), lambda d, c: (at(d, c), 0))]
    in_specs = [
        pl.BlockSpec((feats, slots), lambda d, c: (0, 0)),
        pl.BlockSpec((groups, 1, capacity, feats), lambda d, c: (0, 1, 0, 0)),
        message,
        message,
    ]
    operands = [x_t, rows, mine, other]
    scratch = []
    if with_rows:
        operands += list(weights)
        in_specs += [column, column]
        out_shape.append(jax.ShapeDtypeStruct((slots, feats), F32))
        out_specs.append(whole)
        scratch.append(pltpu.VMEM((slots, feats), F32))
    aliases = {}
    if not first:
        aliases = {len(operands) + 1 + n: n for n in range(3)}
        operands += grads
        in_specs += [pl.BlockSpec(memory_space=pl.ANY)] * 3
        if with_rows:
            operands.append(acc)
            in_specs.append(whole)
    out = pl.pallas_call(
        functools.partial(gradients_kernel, scale, with_rows, first),
        out_shape=out_shape,
        grid_spec=pltpu.PrefetchScalarGridSpec(
            num_scalar_prefetch=1,
            grid=(2,),
            in_specs=in_specs,
            out_specs=out_specs,
            scratch_shapes=scratch,
        ),
        input_output_aliases=aliases,
        compiler_params=PARAMS,
        cost_estimate=cost(
            (20 if with_rows else 12) * slots * feats * width,
            12 * slots * feats + 20 * feats * width + 12 * slots * width,
        ),
    )(scalars, *operands)
    return list(out[:3]), (out[3] if with_rows else None)


def last_rows_kernel(scalar_ref, mine_ref, other_ref, wg_ref, wu_ref, acc_in, *refs):
    *pieces, acc = refs
    width = wg_ref.shape[1]

    def add(in_ref, before):
        d_gate = in_ref[:, width : 2 * width]
        d_up = in_ref[:, 2 * width :]
        part = dot(d_gate, wg_ref[...], LAST_DIMS) + dot(d_up, wu_ref[...], LAST_DIMS)
        acc[...] = before[...] + part

    @pl.when(pl.program_id(0) == 0)
    def _():
        add(mine_ref, acc_in)

    @pl.when(pl.program_id(0) == 1)
    def _():
        add(other_ref, acc)
        size = pieces[0].shape[0]
        for n, piece in enumerate(pieces):
            start = pl.multiple_of((n ^ scalar_ref[1]) * size, size)
            piece[...] = acc[pl.ds(start, size), :].astype(BF16)


def last_rows(scalars, index, count, mine, other, weights, acc, groups):
    slots, feats = acc.shape
    width = mine.shape[1] // 3
    message = pl.BlockSpec((slots, 3 * width), lambda d, c: (0, 0))
    at = chunk_at(count, index)
    column = pl.BlockSpec((feats, width), lambda d, c: (0, at(d, c)))
    return pl.pallas_call(
        last_rows_kernel,
        out_shape=[jax.ShapeDtypeStruct((slots // groups, feats), BF16)] * groups,
        grid_spec=pltpu.PrefetchScalarGridSpec(
            num_scalar_prefetch=1,
            grid=(2,),
            in_specs=[
                message,
                message,
                column,
                column,
                pl.BlockSpec((slots, feats), lambda d, c: (0, 0)),
            ],
            out_specs=[pl.BlockSpec((slots // groups, feats), lambda d, c: (0, 0))] * groups,
            scratch_shapes=[pltpu.VMEM((slots, feats), F32)],
        ),
        compiler_params=PARAMS,
        cost_estimate=cost(
            8 * slots * feats * width, 6 * slots * feats + 8 * feats * width + 12 * slots * width
        ),
    )(scalars, mine, other, *weights, acc)


def body(tokens, grad_out, expert_ids, route_weights, w_gate, w_up, w_down):
    experts = lax.axis_size("expert")
    groups = lax.axis_size("dp")
    tok_rows = tokens.shape[0]
    feats = w_gate.shape[1]
    capacity = tok_rows // 2
    chips = groups // 2
    count = chips
    assert groups == 2 * experts and tokens.shape[1] == 2 * feats
    inv_root = 1.0 / math.sqrt(tok_rows * groups)
    expert = lax.axis_index("expert").astype(jnp.int32)
    block = lax.axis_index("dp").astype(jnp.int32)
    chip, core = block // 2, block % 2
    along = jnp.where(core == 0, chip, chips - 1 - chip)
    w_gate, w_up, w_down = w_gate[0], w_up[0], w_down[0]
    ids, weights = expert_ids.T, route_weights.T

    rows = dispatch_rows(ids, weights, tokens, grad_out, experts)
    rows = lax.all_to_all(rows, "expert", split_axis=0, concat_axis=0, tiled=True)
    rows = rows.reshape(groups, 2 * capacity, feats)
    rows = lax.all_to_all(rows, "dp", split_axis=0, concat_axis=0, tiled=True)
    rows = rows.reshape(groups, 2, capacity, feats)

    swap = [(j, j ^ 1) for j in range(groups)]
    up = [2 * z for z in range(chips)]
    circle = up + [j + 1 for j in reversed(up)]
    ring = list(zip(circle, circle[1:] + circle[:1]))
    order = [(1 - core) * count + (i - (chips - 1 - along)) % count for i in range(count)]
    order += [core * count + (i - along) % count for i in range(count)]
    forward_scalars = jnp.stack(order).astype(jnp.int32)
    chain_scalars = along.astype(jnp.int32)[None]
    backward_scalars = jnp.stack([core, expert + experts * core]).astype(jnp.int32)

    def after(scalars, *things):
        return lax.optimization_barrier((scalars, *things))[0]

    def forward(begin, size, scalars):
        other, mine = (
            forward_chunks(scalars, rows, w_gate, w_up, w_down, begin, size, own, count)
            for own in range(2)
        )
        sib = lax.ppermute(other, "dp", swap)
        return [((mine, i), (sib, i)) for i in range(size)]

    x_t = rows[:, 0].reshape(groups * capacity, feats).T
    slots = 2 * count + chips - 2
    sums = forward(0, 1, forward_scalars)
    recv = []
    grads, acc = None, None

    def gather(k, scalars):
        mine = choose(scalars, [r for n in range(chips) for r in recv[n - 1 + count + k]])
        return mine, lax.ppermute(mine, "dp", swap)

    def round_pairs(r):
        pairs = []
        for q in range(experts):
            for b in range(groups):
                e, h = (b ^ r) % experts, (b ^ r) // experts
                pairs.append((e * groups + 2 * q + h, q * groups + b))
        return pairs

    hop_scalars = chain_scalars
    for s in range(slots):
        came, sends = [], []
        for part in range(PARTS):
            send = hop(
                hop_scalars,
                s,
                count,
                chips,
                recv[s - 1][part] if s else None,
                sums[s % count],
                part,
            )
            came.append(lax.ppermute(send, "dp", ring))
            sends.append(send)
        recv.append(came)
        if s == 0:
            sums += forward(1, 1, after(forward_scalars, *sends))
        if s == 1:
            sums += forward(2, count - 2, after(forward_scalars, *sends))
        k = s - (chips - 1 + count)
        if 0 <= k < count - 1:
            mine, other = gather(k, after(chain_scalars, *sends))
            grads, acc = gradients(
                backward_scalars, k, count, inv_root, x_t, rows, mine, other, (w_gate, w_up), grads, acc
            )
            hop_scalars = after(chain_scalars, acc)

    for k in range(slots - (chips - 1 + count), count - 1):
        mine, other = gather(k, chain_scalars)
        grads, acc = gradients(
            backward_scalars, k, count, inv_root, x_t, rows, mine, other, (w_gate, w_up), grads, acc
        )
    k = count - 1
    mine, other = gather(k, chain_scalars)
    pieces = last_rows(backward_scalars, k, count, mine, other, (w_gate, w_up), acc, groups)
    returned = [
        lax.ppermute(piece, ("expert", "dp"), round_pairs(r)) for r, piece in enumerate(pieces)
    ]
    grads, _ = gradients(
        after(backward_scalars, *pieces),
        k,
        count,
        inv_root,
        x_t,
        rows,
        mine,
        other,
        (),
        grads,
        None,
    )
    combine_scalars = jnp.stack([block % experts, block // experts])
    grad_tokens = combine_rows(combine_scalars, ids, returned, experts)
    return (grad_tokens, grads[0][None], grads[1][None], grads[2][None])


def solution(mesh):
    in_specs = (
        P("dp", "expert"),
        P("dp", "expert"),
        P("dp", None),
        P("dp", None),
        P("expert", "dp", None),
        P("expert", "dp", None),
        P("expert", None, "dp"),
    )
    out_specs = (
        P("dp", "expert"),
        P("expert", "dp", None),
        P("expert", "dp", None),
        P("expert", None, "dp"),
    )
    return jax.shard_map(body, mesh=mesh, in_specs=in_specs, out_specs=out_specs, check_vma=False)
```

```python
import functools
import math

import jax
import jax.numpy as jnp
from jax import lax
from jax.experimental import pallas as pl
from jax.experimental.pallas import tpu as pltpu
from jax.sharding import PartitionSpec as P

F32 = jnp.float32
BF16 = jnp.bfloat16
LAST_DIMS = (((1,), (1,)), ((), ()))
ROWS_FIRST = (((0,), (0,)), ((), ()))
PARTS = 2
PARAMS = pltpu.CompilerParams(vmem_limit_bytes=48 * 1024 * 1024)


def dot(a, b, dims=None):
    if dims is None:
        return jnp.dot(a, b, preferred_element_type=F32)
    return lax.dot_general(a, b, dims, preferred_element_type=F32)


def cost():
    return pl.CostEstimate(flops=1024, bytes_accessed=1024, transcendentals=0)


def slot_one_hot(ids_ref, experts, capacity):
    tokens = ids_ref.shape[1]
    first, second = ids_ref[0:1, :], ids_ref[1:2, :]
    expert = lax.broadcasted_iota(jnp.int32, (8 * (-(-experts // 8)), tokens), 0)
    chosen = (first == expert) | (second == expert)
    before = lax.broadcasted_iota(jnp.int32, (tokens, tokens), 0) < lax.broadcasted_iota(
        jnp.int32, (tokens, tokens), 1
    )
    place = dot(chosen.astype(F32).astype(BF16), before.astype(F32).astype(BF16))
    place = jnp.where(chosen, place, -1.0).astype(jnp.int32)
    slot = lax.broadcasted_iota(jnp.int32, (capacity, tokens), 0)
    return [slot == place[e : e + 1, :] for e in range(experts)]


def dispatch_kernel(experts, scalar_ref, ids_ref, weights_ref, x_ref, g_ref, *refs):
    *messages, hot_ref, weight_ref = refs
    capacity = messages[0].shape[1]
    step = pl.program_id(0)

    @pl.when(step == 0)
    def _():
        for e, hit in enumerate(slot_one_hot(ids_ref, experts, capacity)):
            weight = jnp.where(ids_ref[0:1, :] == e, weights_ref[0:1, :], weights_ref[1:2, :])
            weight = jnp.sum(jnp.where(hit, weight, 0.0), axis=1, keepdims=True)
            place = pl.ds(pl.multiple_of((scalar_ref[0] ^ e) * capacity, capacity), capacity)
            hot_ref[place, :] = hit.astype(F32).astype(BF16)
            weight_ref[place, :] = jnp.broadcast_to(weight, (capacity, weight_ref.shape[1]))

    x, g = (r[0] if len(r.shape) == 3 else r[...] for r in (x_ref, g_ref))
    x = dot(hot_ref[...], x).astype(BF16)
    g = (dot(hot_ref[...], g) * weight_ref[:, 0:1]).astype(BF16)
    for half in range(2):

        @pl.when(step == half)
        def _():
            for t in range(experts):
                rows = slice(t * capacity, (t + 1) * capacity)
                messages[2 * t + half][0] = x[rows]
                messages[2 * t + half][1] = g[rows]


def dispatch_rows(scalars, ids, weights, x, g, experts):
    tokens, feats = x.shape[0], x.shape[1] // 2
    capacity = tokens // 2
    small = pl.BlockSpec((2, tokens), lambda h, c: (0, 0))
    if feats % 128:
        x, g = (r.reshape(tokens, 2, feats).transpose(1, 0, 2) for r in (x, g))
        rows_spec = pl.BlockSpec((1, tokens, feats), lambda h, c: (h ^ c[1], 0, 0))
    else:
        rows_spec = pl.BlockSpec((tokens, feats), lambda h, c: (0, h ^ c[1]))
    return pl.pallas_call(
        functools.partial(dispatch_kernel, experts),
        out_shape=[jax.ShapeDtypeStruct((2, capacity, feats), BF16)] * (2 * experts),
        grid_spec=pltpu.PrefetchScalarGridSpec(
            num_scalar_prefetch=1,
            grid=(2,),
            in_specs=[small, small, rows_spec, rows_spec],
            out_specs=[pl.BlockSpec((2, capacity, feats), lambda h, c: (0, 0, 0))] * (2 * experts),
            scratch_shapes=[
                pltpu.VMEM((experts * capacity, tokens), BF16),
                pltpu.VMEM((experts * capacity, 128), F32),
            ],
        ),
        compiler_params=PARAMS,
        cost_estimate=cost(),
    )(scalars, ids, weights, x, g)


def assemble_kernel(scalar_ref, *refs):
    *messages, out_ref, sems = refs

    def copy(n, message):
        return pltpu.make_async_copy(message, out_ref.at[n ^ scalar_ref[0]], sems.at[n])

    for n, message in enumerate(messages):
        copy(n, message).start()
    for n, message in enumerate(messages):
        copy(n, message).wait()


def assemble(scalars, messages):
    return pl.pallas_call(
        assemble_kernel,
        out_shape=jax.ShapeDtypeStruct((len(messages), *messages[0].shape), BF16),
        in_specs=[pl.BlockSpec(memory_space=pltpu.SMEM)]
        + [pl.BlockSpec(memory_space=pl.ANY)] * len(messages),
        out_specs=pl.BlockSpec(memory_space=pl.ANY),
        scratch_shapes=[pltpu.SemaphoreType.DMA((len(messages),))],
        compiler_params=PARAMS,
        cost_estimate=cost(),
    )(scalars, *messages)


def combine_kernel(experts, scalar_ref, ids_ref, *refs):
    *pieces, out_ref, hot_ref = refs
    capacity = pieces[0].shape[0]
    at = pl.program_id(0)
    low = scalar_ref[0]

    @pl.when(at == 0)
    def _():
        hits = slot_one_hot(ids_ref, experts, capacity)
        for e in range(experts):
            place = pl.multiple_of((low ^ e) * capacity, capacity)
            hot_ref[pl.ds(place, capacity), :] = hits[e].astype(F32).astype(BF16)

    for half in range(2):

        @pl.when(at == half)
        def _():
            rows = jnp.concatenate(
                [p[...] for p in pieces[half * experts : (half + 1) * experts]], axis=0
            )
            out = dot(hot_ref[...], rows, ROWS_FIRST).astype(BF16)
            out_ref[...] = out.reshape(out_ref.shape)


def combine_rows(scalars, ids, pieces, experts):
    tokens = ids.shape[1]
    capacity, feats = pieces[0].shape
    if feats % 128:
        out_shape = jax.ShapeDtypeStruct((2, tokens, feats), BF16)
        out_spec = pl.BlockSpec((1, tokens, feats), lambda a, c: (a ^ c[1], 0, 0))
    else:
        out_shape = jax.ShapeDtypeStruct((tokens, 2 * feats), BF16)
        out_spec = pl.BlockSpec((tokens, feats), lambda a, c: (0, a ^ c[1]))
    out = pl.pallas_call(
        functools.partial(combine_kernel, experts),
        out_shape=out_shape,
        grid_spec=pltpu.PrefetchScalarGridSpec(
            num_scalar_prefetch=1,
            grid=(2,),
            in_specs=[pl.BlockSpec((2, tokens), lambda a, c: (0, 0))]
            + [pl.BlockSpec((capacity, feats), lambda a, c: (0, 0))] * len(pieces),
            out_specs=out_spec,
            scratch_shapes=[pltpu.VMEM((experts * capacity, tokens), BF16)],
        ),
        compiler_params=PARAMS,
        cost_estimate=cost(),
    )(scalars, ids, *pieces)
    if feats % 128:
        out = out.transpose(1, 0, 2).reshape(tokens, 2 * feats)
    return out


def forward_kernel(scalar_ref, x_ref, g_ref, wg_ref, wu_ref, wd_ref, out_ref):
    width = wg_ref.shape[1]
    blocks, _, capacity, feats = x_ref.shape
    x = x_ref[...].reshape(blocks * capacity, feats)
    g = g_ref[...].reshape(blocks * capacity, feats)
    out_ref[0, :, :width] = dot(x, wg_ref[...]).astype(BF16)
    out_ref[0, :, width : 2 * width] = dot(x, wu_ref[...]).astype(BF16)
    out_ref[0, :, 2 * width :] = dot(g, wd_ref[...], LAST_DIMS).astype(BF16)


def forward_chunks(scalars, rows, w_gate, w_up, w_down, begin, size, own, count):
    groups, _, capacity, feats = rows.shape
    width = w_gate.shape[1] // (2 * count)
    blocks = groups // 2

    def at(i, c):
        return c[own * count + begin + i]

    return pl.pallas_call(
        forward_kernel,
        out_shape=jax.ShapeDtypeStruct((size, groups * capacity, 3 * width), BF16),
        grid_spec=pltpu.PrefetchScalarGridSpec(
            num_scalar_prefetch=1,
            grid=(size, 2),
            in_specs=[
                pl.BlockSpec((blocks, 1, capacity, feats), lambda i, n, c: (n, 0, 0, 0)),
                pl.BlockSpec((blocks, 1, capacity, feats), lambda i, n, c: (n, 1, 0, 0)),
                pl.BlockSpec((feats, width), lambda i, n, c: (0, at(i, c))),
                pl.BlockSpec((feats, width), lambda i, n, c: (0, at(i, c))),
                pl.BlockSpec((width, feats), lambda i, n, c: (at(i, c), 0)),
            ],
            out_specs=pl.BlockSpec((1, blocks * capacity, 3 * width), lambda i, n, c: (i, n, 0)),
        ),
        compiler_params=PARAMS,
        cost_estimate=cost(),
    )(scalars, rows, rows, w_gate, w_up, w_down)


def activate(gate, upper, back):
    sig = jax.nn.sigmoid(gate)
    gated = gate * sig
    return (
        (gated * upper).astype(BF16),
        (back * upper * sig * (1.0 + gate * (1.0 - sig))).astype(BF16),
        (back * gated).astype(BF16),
    )


def hop_kernel(plan, scalar_ref, *refs):
    slot, count, chips, sums, came = plan
    refs = list(refs)
    recv_ref = refs.pop(0) if came else None
    own_ref, sib_ref = refs[:2] if sums else (None, None)
    send_ref = refs[-1]
    at = scalar_ref[0]
    width = send_ref.shape[1] // 3
    summing = (at <= slot) & (slot - at < count)

    def total(part):
        columns = slice(part * width, (part + 1) * width)
        value = own_ref[0, :, columns].astype(F32) + sib_ref[0, :, columns].astype(F32)
        if came:
            value += jnp.where(at > 0, recv_ref[:, columns].astype(F32), 0.0)
        return value

    if sums:

        @pl.when(summing & (at < chips - 1))
        def _():
            for part in range(3):
                send_ref[:, part * width : (part + 1) * width] = total(part).astype(BF16)

        @pl.when(summing & (at == chips - 1))
        def _():
            for part, value in enumerate(activate(total(0), total(1), total(2))):
                send_ref[:, part * width : (part + 1) * width] = value

    if came:

        @pl.when(jnp.logical_not(summing))
        def _():
            send_ref[...] = recv_ref[...]


def hop(scalars, slot, count, chips, recv, sums, part):
    rows, cols = sums[0][0].shape[1:]
    rows //= PARTS
    message = pl.BlockSpec((rows, cols), lambda n, c: (0, 0))
    operands, in_specs = [], []
    if recv is not None:
        operands.append(recv)
        in_specs.append(message)
    adds = slot < count + chips - 1
    if adds:
        for array, i in sums:
            operands.append(array)
            in_specs.append(pl.BlockSpec((1, rows, cols), lambda n, c, i=i: (i, part, 0)))
    plan = (slot, count, chips, adds, recv is not None)
    return pl.pallas_call(
        functools.partial(hop_kernel, plan),
        out_shape=jax.ShapeDtypeStruct((rows, cols), BF16),
        grid_spec=pltpu.PrefetchScalarGridSpec(
            num_scalar_prefetch=1,
            grid=(1,),
            in_specs=in_specs,
            out_specs=message,
        ),
        compiler_params=PARAMS,
        cost_estimate=cost(),
    )(scalars, *operands)


def choose_kernel(scalar_ref, *refs):
    *candidates, out_ref, sems = refs
    rows = candidates[0].shape[0]

    def copy(n, part):
        return pltpu.make_async_copy(
            candidates[n * PARTS + part], out_ref.at[pl.ds(part * rows, rows)], sems.at[part]
        )

    for n in range(len(candidates) // PARTS):

        @pl.when(scalar_ref[0] == n)
        def _():
            for part in range(PARTS):
                copy(n, part).start()

    for part in range(PARTS):
        copy(0, part).wait()


def choose(scalars, candidates):
    rows, cols = candidates[0].shape
    return pl.pallas_call(
        choose_kernel,
        out_shape=jax.ShapeDtypeStruct((rows * PARTS, cols), BF16),
        in_specs=[pl.BlockSpec(memory_space=pltpu.SMEM)]
        + [pl.BlockSpec(memory_space=pl.ANY)] * len(candidates),
        out_specs=pl.BlockSpec(memory_space=pl.ANY),
        scratch_shapes=[pltpu.SemaphoreType.DMA((PARTS,))],
        compiler_params=PARAMS,
        cost_estimate=cost(),
    )(scalars, *candidates)


def gradients_kernel(scale, with_rows, first, scalar_ref, *refs):
    xt_ref, g_ref, mine_ref, other_ref, *refs = refs
    if with_rows:
        wg_ref, wu_ref, *refs = refs
    if not first:
        refs = refs[3:]
    if with_rows and not first:
        acc_in, *refs = refs
    gg_ref, gu_ref, gd_ref, *refs = refs
    width = gg_ref.shape[1]

    def chunk(in_ref, before, after):
        scaled = in_ref[:, :width]
        d_gate = in_ref[:, width : 2 * width]
        d_up = in_ref[:, 2 * width :]
        if with_rows:
            part = dot(d_gate, wg_ref[...], LAST_DIMS) + dot(d_up, wu_ref[...], LAST_DIMS)
            after[...] = part if before is None else before[...] + part
        gg_ref[...] = (dot(xt_ref[...], d_gate) * scale).astype(BF16)
        gu_ref[...] = (dot(xt_ref[...], d_up) * scale).astype(BF16)
        blocks, _, capacity, feats = g_ref.shape
        rows = g_ref[...].reshape(blocks * capacity, feats)
        gd_ref[...] = (dot(scaled, rows, ROWS_FIRST) * scale).astype(BF16)

    acc_out, acc = refs if with_rows else (None, None)

    @pl.when(pl.program_id(0) == 0)
    def _():
        chunk(mine_ref, None if first else (acc_in if with_rows else None), acc)

    @pl.when(pl.program_id(0) == 1)
    def _():
        chunk(other_ref, acc, acc_out)


def chunk_at(count, index):
    return lambda d, c: (d ^ 1 ^ c[0]) * count + index


def gradients(scalars, index, count, scale, x_t, rows, mine, other, weights, grads, acc):
    groups, _, capacity, feats = rows.shape
    slots = groups * capacity
    width = mine.shape[1] // 3
    hidden = 2 * count * width
    first, with_rows = grads is None, bool(weights)
    whole = pl.BlockSpec((slots, feats), lambda d, c: (0, 0))
    message = pl.BlockSpec((slots, 3 * width), lambda d, c: (0, 0))
    at = chunk_at(count, index)
    column = pl.BlockSpec((feats, width), lambda d, c: (0, at(d, c)))
    out_shape = [
        jax.ShapeDtypeStruct((feats, hidden), BF16),
        jax.ShapeDtypeStruct((feats, hidden), BF16),
        jax.ShapeDtypeStruct((hidden, feats), BF16),
    ]
    out_specs = [column, column, pl.BlockSpec((width, feats), lambda d, c: (at(d, c), 0))]
    in_specs = [
        pl.BlockSpec((feats, slots), lambda d, c: (0, 0)),
        pl.BlockSpec((groups, 1, capacity, feats), lambda d, c: (0, 1, 0, 0)),
        message,
        message,
    ]
    operands = [x_t, rows, mine, other]
    scratch = []
    if with_rows:
        operands += list(weights)
        in_specs += [column, column]
        out_shape.append(jax.ShapeDtypeStruct((slots, feats), F32))
        out_specs.append(whole)
        scratch.append(pltpu.VMEM((slots, feats), F32))
    aliases = {}
    if not first:
        aliases = {len(operands) + 1 + n: n for n in range(3)}
        operands += grads
        in_specs += [pl.BlockSpec(memory_space=pl.ANY)] * 3
        if with_rows:
            operands.append(acc)
            in_specs.append(whole)
    out = pl.pallas_call(
        functools.partial(gradients_kernel, scale, with_rows, first),
        out_shape=out_shape,
        grid_spec=pltpu.PrefetchScalarGridSpec(
            num_scalar_prefetch=1,
            grid=(2,),
            in_specs=in_specs,
            out_specs=out_specs,
            scratch_shapes=scratch,
        ),
        input_output_aliases=aliases,
        compiler_params=PARAMS,
        cost_estimate=cost(),
    )(scalars, *operands)
    return list(out[:3]), (out[3] if with_rows else None)


def sum_rows_kernel(units, last, scalar_ref, *refs):
    messages, (wg_ref, wu_ref, acc_in), refs = refs[:units], refs[units : units + 3], refs[units + 3 :]
    *outs, acc = refs
    width = wg_ref.shape[1]
    for u in range(units):

        @pl.when(pl.program_id(0) == u)
        def _():
            d_gate = messages[u][:, width : 2 * width]
            d_up = messages[u][:, 2 * width :]
            part = dot(d_gate, wg_ref[...], LAST_DIMS) + dot(d_up, wu_ref[...], LAST_DIMS)
            total = (acc_in if u == 0 else acc)[...] + part
            if u < units - 1 or last:
                acc[...] = total
            else:
                outs[0][...] = total
            if u == units - 1 and last:
                size = outs[0].shape[0]
                for n, piece in enumerate(outs):
                    start = pl.multiple_of((n ^ scalar_ref[1]) * size, size)
                    piece[...] = acc[pl.ds(start, size), :].astype(BF16)


def sum_rows(scalars, begin, messages, weights, acc, pieces):
    slots, feats = acc.shape
    width = messages[0].shape[1] // 3
    units = len(messages)
    column = pl.BlockSpec((feats, width), lambda u, c: (0, c[2 + begin + u]))
    whole = pl.BlockSpec((slots, feats), lambda u, c: (0, 0))
    if pieces:
        out_shape = [jax.ShapeDtypeStruct((slots // pieces, feats), BF16)] * pieces
        out_specs = [pl.BlockSpec((slots // pieces, feats), lambda u, c: (0, 0))] * pieces
    else:
        out_shape, out_specs = [jax.ShapeDtypeStruct((slots, feats), F32)], [whole]
    return pl.pallas_call(
        functools.partial(sum_rows_kernel, units, bool(pieces)),
        out_shape=out_shape,
        grid_spec=pltpu.PrefetchScalarGridSpec(
            num_scalar_prefetch=1,
            grid=(units,),
            in_specs=[pl.BlockSpec((slots, 3 * width), lambda u, c: (0, 0))] * units
            + [column, column, whole],
            out_specs=out_specs,
            scratch_shapes=[pltpu.VMEM((slots, feats), F32)],
        ),
        compiler_params=PARAMS,
        cost_estimate=cost(),
    )(scalars, *messages, *weights, acc)


def body(tokens, grad_out, expert_ids, route_weights, w_gate, w_up, w_down):
    experts = lax.axis_size("expert")
    groups = lax.axis_size("dp")
    tok_rows = tokens.shape[0]
    feats = w_gate.shape[1]
    capacity = tok_rows // 2
    chips = groups // 2
    count = chips
    assert groups == 2 * experts and tokens.shape[1] == 2 * feats
    inv_root = 1.0 / math.sqrt(tok_rows * groups)
    expert = lax.axis_index("expert").astype(jnp.int32)
    block = lax.axis_index("dp").astype(jnp.int32)
    chip, core = block // 2, block % 2
    along = jnp.where(core == 0, chip, chips - 1 - chip)
    w_gate, w_up, w_down = w_gate[0], w_up[0], w_down[0]
    ids, weights = expert_ids.T, route_weights.T

    device = lambda e, b: e * groups + b
    everyone = [(e, z, c) for e in range(experts) for z in range(chips) for c in range(2)]
    dispatch_scalars = jnp.stack([expert ^ chip, core])
    messages = dispatch_rows(dispatch_scalars, ids, weights, tokens, grad_out, experts)
    blocks = []
    for n, message in enumerate(messages):
        t, h = divmod(n, 2)
        plane = [(device(q, 2 * z + c), device(q ^ t ^ z, 2 * z + c)) for q, z, c in everyone]
        line = [
            (device(e, 2 * z + c), device(e, 2 * (e ^ t ^ z) + (c ^ h))) for e, z, c in everyone
        ]
        message = lax.ppermute(message, ("expert", "dp"), plane)
        blocks.append(lax.ppermute(message, ("expert", "dp"), line))
    rows = assemble((block ^ (2 * expert))[None], blocks)

    swap = [(j, j ^ 1) for j in range(groups)]
    up = [2 * z for z in range(chips)]
    circle = up + [j + 1 for j in reversed(up)]
    ring = list(zip(circle, circle[1:] + circle[:1]))
    order = [(1 - core) * count + (i - (chips - 1 - along)) % count for i in range(count)]
    order += [core * count + (i - along) % count for i in range(count)]
    forward_scalars = jnp.stack(order).astype(jnp.int32)
    chain_scalars = along.astype(jnp.int32)[None]
    columns = [(d ^ 1 ^ core) * count + k for k in range(count) for d in range(2)]
    backward_scalars = jnp.stack(
        [core, (expert + experts * core) ^ (2 * chip), *columns]
    ).astype(jnp.int32)

    def after(scalars, *things):
        return lax.optimization_barrier((scalars, *things))[0]

    def forward(begin, size, scalars):
        other, mine = (
            forward_chunks(scalars, rows, w_gate, w_up, w_down, begin, size, own, count)
            for own in range(2)
        )
        sib = lax.ppermute(other, "dp", swap)
        return [((mine, i), (sib, i)) for i in range(size)]

    slots = 2 * count + chips - 2
    sums = forward(0, 1, forward_scalars)
    recv = []
    grads, acc = None, None

    def gather(k, scalars):
        mine = choose(scalars, [r for n in range(chips) for r in recv[n - 1 + count + k]])
        return mine, lax.ppermute(mine, "dp", swap)

    first_back = chips - 1 + count
    hop_scalars, gradient_scalars = chain_scalars, backward_scalars
    weights_pair = (w_gate, w_up)
    chunks = []

    def add_chunk(k, with_rows, grads, acc):
        return gradients(
            gradient_scalars,
            k,
            count,
            inv_root,
            x_t,
            rows,
            *chunks[k],
            weights_pair if with_rows else (),
            grads,
            acc,
        )

    early = 0
    for s in range(slots):
        came, sends = [], []
        for part in range(PARTS):
            send = hop(
                hop_scalars,
                s,
                count,
                chips,
                recv[s - 1][part] if s else None,
                sums[s % count],
                part,
            )
            came.append(lax.ppermute(send, "dp", ring))
            sends.append(send)
        recv.append(came)
        if s == 0:
            sums += forward(1, 1, after(forward_scalars, *sends))
        if s == 1:
            sums += forward(2, count - 2, after(forward_scalars, *sends))
        if s == 3:
            x_t = rows[:, 0].reshape(groups * capacity, feats).T
            hop_scalars = after(chain_scalars, x_t)
        k = s - first_back
        if k >= 0:
            chunks.append(gather(k, after(chain_scalars, *sends)))
        if k >= 1:
            gradient_scalars = after(backward_scalars, *sends)
            grads, acc = add_chunk(k - 1, True, grads, acc)
            early = k
            hop_scalars = after(chain_scalars, acc)
    for k in range(len(chunks), count):
        chunks.append(gather(k, hop_scalars))
    units = [message for chunk in chunks for message in chunk][2 * early :]
    (acc,) = sum_rows(backward_scalars, 2 * early, units[:-1], weights_pair, acc, 0)
    pieces = sum_rows(backward_scalars, 2 * count - 1, units[-1:], weights_pair, acc, groups)

    def round_pairs(r):
        pairs = []
        for q in range(experts):
            for b in range(groups):
                h, e = divmod(b ^ r ^ (2 * q), experts)
                pairs.append((device(e, 2 * q + h), device(q, b)))
        return pairs

    returned = [
        lax.ppermute(piece, ("expert", "dp"), round_pairs(r)) for r, piece in enumerate(pieces)
    ]
    gradient_scalars = backward_scalars
    for k in range(early, count):
        grads, _ = add_chunk(k, False, grads, None)
    mixed = block ^ (2 * expert)
    combine_scalars = jnp.stack([mixed % experts, mixed // experts])
    grad_tokens = combine_rows(combine_scalars, ids, returned, experts)
    return (grad_tokens, grads[0][None], grads[1][None], grads[2][None])


def solution(mesh):
    in_specs = (
        P("dp", "expert"),
        P("dp", "expert"),
        P("dp", None),
        P("dp", None),
        P("expert", "dp", None),
        P("expert", "dp", None),
        P("expert", None, "dp"),
    )
    out_specs = (
        P("dp", "expert"),
        P("expert", "dp", None),
        P("expert", "dp", None),
        P("expert", None, "dp"),
    )
    return jax.shard_map(body, mesh=mesh, in_specs=in_specs, out_specs=out_specs, check_vma=False)
```

```python
import functools
import math

import jax
import jax.numpy as jnp
from jax import lax
from jax.experimental import pallas as pl
from jax.experimental.pallas import tpu as pltpu
from jax.sharding import PartitionSpec as P

F32 = jnp.float32
BF16 = jnp.bfloat16
LAST_DIMS = (((1,), (1,)), ((), ()))
ROWS_FIRST = (((0,), (0,)), ((), ()))
PARTS = 2
PARAMS = pltpu.CompilerParams(vmem_limit_bytes=24 * 1024 * 1024)


def dot(a, b, dims=None):
    if dims is None:
        return jnp.dot(a, b, preferred_element_type=F32)
    return lax.dot_general(a, b, dims, preferred_element_type=F32)


def cost():
    return pl.CostEstimate(flops=1024, bytes_accessed=1024, transcendentals=0)


def slot_one_hot(ids_ref, experts, capacity):
    tokens = ids_ref.shape[1]
    first, second = ids_ref[0:1, :], ids_ref[1:2, :]
    expert = lax.broadcasted_iota(jnp.int32, (8 * (-(-experts // 8)), tokens), 0)
    chosen = (first == expert) | (second == expert)
    before = lax.broadcasted_iota(jnp.int32, (tokens, tokens), 0) < lax.broadcasted_iota(
        jnp.int32, (tokens, tokens), 1
    )
    place = dot(chosen.astype(F32).astype(BF16), before.astype(F32).astype(BF16))
    place = jnp.where(chosen, place, -1.0).astype(jnp.int32)
    slot = lax.broadcasted_iota(jnp.int32, (capacity, tokens), 0)
    return [slot == place[e : e + 1, :] for e in range(experts)]


def dispatch_kernel(experts, ids_hbm, weights_hbm, x_hbm, g_hbm, out_ref, hot_ref, *scratch):
    ids_ref, weights_ref, x_ref, g_ref, sems = scratch
    feats = out_ref.shape[3]
    capacity = out_ref.shape[2] // 2

    def half(ref, h):
        return ref.at[h] if len(ref.shape) == 3 else ref.at[:, pl.ds(h * feats, feats)]

    pairs = [(ids_hbm, ids_ref), (weights_hbm, weights_ref)]
    for h in range(2):
        pairs += [(half(x_hbm, h), x_ref.at[h]), (half(g_hbm, h), g_ref.at[h])]
    copies = [pltpu.make_async_copy(a, b, sems.at[n]) for n, (a, b) in enumerate(pairs)]
    for copy in copies:
        copy.start()
    copies[0].wait()
    copies[1].wait()
    scales = []
    for e, hit in enumerate(slot_one_hot(ids_ref, experts, capacity)):
        weight = jnp.where(ids_ref[0:1, :] == e, weights_ref[0:1, :], weights_ref[1:2, :])
        scales.append(jnp.sum(jnp.where(hit, weight, 0.0), axis=1, keepdims=True))
        hot_ref[e * capacity : (e + 1) * capacity, :] = hit.astype(F32).astype(BF16)
    for h in range(2):
        copies[2 + 2 * h].wait()
        copies[3 + 2 * h].wait()
        x = dot(hot_ref[...], x_ref[h]).astype(BF16)
        g = dot(hot_ref[...], g_ref[h])
        for e in range(experts):
            rows = slice(e * capacity, (e + 1) * capacity)
            out_ref[e, h, :capacity] = x[rows]
            out_ref[e, h, capacity:] = (g[rows] * scales[e]).astype(BF16)


def dispatch_rows(ids, weights, x, g, experts):
    tokens, feats = x.shape[0], x.shape[1] // 2
    capacity = tokens // 2
    if feats % 128:
        x, g = (r.reshape(tokens, 2, feats).transpose(1, 0, 2) for r in (x, g))
    return pl.pallas_call(
        functools.partial(dispatch_kernel, experts),
        out_shape=(
            jax.ShapeDtypeStruct((experts, 2, 2 * capacity, feats), BF16),
            jax.ShapeDtypeStruct((experts * capacity, tokens), BF16),
        ),
        in_specs=[pl.BlockSpec(memory_space=pltpu.HBM)] * 4,
        scratch_shapes=[
            pltpu.VMEM((2, tokens), jnp.int32),
            pltpu.VMEM((2, tokens), F32),
            pltpu.VMEM((2, tokens, feats), BF16),
            pltpu.VMEM((2, tokens, feats), BF16),
            pltpu.SemaphoreType.DMA((6,)),
        ],
        compiler_params=PARAMS,
        cost_estimate=cost(),
    )(ids, weights, x, g)


def combine_kernel(experts, scalar_ref, hot_ref, *refs):
    pieces, (out_ref, rows_ref, sems) = refs[:-3], refs[-3:]
    capacity = pieces[0].shape[0]
    at = pl.program_id(0)

    def copy(n):
        return pltpu.make_async_copy(
            pieces[n], rows_ref.at[pl.ds(n * capacity, capacity)], sems.at[n]
        )

    @pl.when(at == 0)
    def _():
        for n in range(len(pieces)):
            copy(n).start()

    hot = jnp.concatenate(
        [
            hot_ref[pl.ds(pl.multiple_of((scalar_ref[0] ^ n) * capacity, capacity), capacity), :]
            for n in range(experts)
        ],
        axis=0,
    )
    for half in range(2):

        @pl.when(at == half)
        def _():
            for n in range(half * experts, (half + 1) * experts):
                copy(n).wait()
            rows = rows_ref[half * experts * capacity : (half + 1) * experts * capacity, :]
            out = dot(hot, rows, ROWS_FIRST).astype(BF16)
            out_ref[...] = out.reshape(out_ref.shape)


def combine_rows(scalars, hot, pieces, experts):
    tokens = hot.shape[1]
    capacity, feats = pieces[0].shape
    if feats % 128:
        out_shape = jax.ShapeDtypeStruct((2, tokens, feats), BF16)
        out_spec = pl.BlockSpec((1, tokens, feats), lambda a, c: (a ^ c[1], 0, 0))
    else:
        out_shape = jax.ShapeDtypeStruct((tokens, 2 * feats), BF16)
        out_spec = pl.BlockSpec((tokens, feats), lambda a, c: (0, a ^ c[1]))
    out = pl.pallas_call(
        functools.partial(combine_kernel, experts),
        out_shape=out_shape,
        grid_spec=pltpu.PrefetchScalarGridSpec(
            num_scalar_prefetch=1,
            grid=(2,),
            in_specs=[pl.BlockSpec((experts * capacity, tokens), lambda a, c: (0, 0))]
            + [pl.BlockSpec(memory_space=pltpu.HBM)] * len(pieces),
            out_specs=out_spec,
            scratch_shapes=[
                pltpu.VMEM((len(pieces) * capacity, feats), BF16),
                pltpu.SemaphoreType.DMA((len(pieces),)),
            ],
        ),
        compiler_params=PARAMS,
        cost_estimate=cost(),
    )(scalars, hot, *pieces)
    if feats % 128:
        out = out.transpose(1, 0, 2).reshape(tokens, 2 * feats)
    return out


def forward_kernel(scalar_ref, x_ref, g_ref, wg_ref, wu_ref, wd_ref, *outs):
    width = wg_ref.shape[1]
    blocks, _, capacity, feats = x_ref.shape
    for own in range(2):

        @pl.when(pl.program_id(1) == own)
        def _():
            x = x_ref[...].reshape(blocks * capacity, feats)
            g = g_ref[...].reshape(blocks * capacity, feats)
            outs[own][0, :, :width] = dot(x, wg_ref[...]).astype(BF16)
            outs[own][0, :, width : 2 * width] = dot(x, wu_ref[...]).astype(BF16)
            outs[own][0, :, 2 * width :] = dot(g, wd_ref[...], LAST_DIMS).astype(BF16)


def forward_chunks(scalars, rows, w_gate, w_up, w_down, begin, size, count):
    groups, _, capacity, feats = rows.shape
    width = w_gate.shape[1] // (2 * count)

    def at(i, own, c):
        return c[own * count + begin + i]

    out = jax.ShapeDtypeStruct((size, groups * capacity, 3 * width), BF16)
    out_spec = pl.BlockSpec((1, groups * capacity, 3 * width), lambda i, own, c: (i, 0, 0))
    return pl.pallas_call(
        forward_kernel,
        out_shape=(out, out),
        grid_spec=pltpu.PrefetchScalarGridSpec(
            num_scalar_prefetch=1,
            grid=(size, 2),
            in_specs=[
                pl.BlockSpec((groups, 1, capacity, feats), lambda i, own, c: (0, 0, 0, 0)),
                pl.BlockSpec((groups, 1, capacity, feats), lambda i, own, c: (0, 1, 0, 0)),
                pl.BlockSpec((feats, width), lambda i, own, c: (0, at(i, own, c))),
                pl.BlockSpec((feats, width), lambda i, own, c: (0, at(i, own, c))),
                pl.BlockSpec((width, feats), lambda i, own, c: (at(i, own, c), 0)),
            ],
            out_specs=(out_spec, out_spec),
        ),
        compiler_params=PARAMS,
        cost_estimate=cost(),
    )(scalars, rows, rows, w_gate, w_up, w_down)


def activate(gate, upper, back):
    sig = jax.nn.sigmoid(gate)
    gated = gate * sig
    return (
        (gated * upper).astype(BF16),
        (back * upper * sig * (1.0 + gate * (1.0 - sig))).astype(BF16),
        (back * gated).astype(BF16),
    )


def hop_kernel(plan, scalar_ref, *refs):
    slot, count, chips, sums, came = plan
    refs = list(refs)
    recv_ref = refs.pop(0) if came else None
    own_ref, sib_ref = refs[:2] if sums else (None, None)
    send_ref = refs[-1]
    at = scalar_ref[0]
    width = send_ref.shape[1] // 3
    summing = (at <= slot) & (slot - at < count)

    def total(part):
        columns = slice(part * width, (part + 1) * width)
        value = own_ref[0, :, columns].astype(F32) + sib_ref[0, :, columns].astype(F32)
        if came:
            value += jnp.where(at > 0, recv_ref[:, columns].astype(F32), 0.0)
        return value

    if sums:

        @pl.when(summing & (at < chips - 1))
        def _():
            for part in range(3):
                send_ref[:, part * width : (part + 1) * width] = total(part).astype(BF16)

        @pl.when(summing & (at == chips - 1))
        def _():
            for part, value in enumerate(activate(total(0), total(1), total(2))):
                send_ref[:, part * width : (part + 1) * width] = value

    if came:

        @pl.when(jnp.logical_not(summing))
        def _():
            send_ref[...] = recv_ref[...]


def hop(scalars, slot, count, chips, recv, sums, part):
    rows, cols = sums[0][0].shape[1:]
    rows //= PARTS
    message = pl.BlockSpec((rows, cols), lambda n, c: (0, 0))
    operands, in_specs = [], []
    if recv is not None:
        operands.append(recv)
        in_specs.append(message)
    adds = slot < count + chips - 1
    if adds:
        for array, i in sums:
            operands.append(array)
            in_specs.append(pl.BlockSpec((1, rows, cols), lambda n, c, i=i: (i, part, 0)))
    plan = (slot, count, chips, adds, recv is not None)
    return pl.pallas_call(
        functools.partial(hop_kernel, plan),
        out_shape=jax.ShapeDtypeStruct((rows, cols), BF16),
        grid_spec=pltpu.PrefetchScalarGridSpec(
            num_scalar_prefetch=1,
            grid=(1,),
            in_specs=in_specs,
            out_specs=message,
        ),
        compiler_params=PARAMS,
        cost_estimate=cost(),
    )(scalars, *operands)


def choose_kernel(scalar_ref, *refs):
    *candidates, out_ref, sems = refs
    rows = candidates[0].shape[0]

    def copy(n, part):
        return pltpu.make_async_copy(
            candidates[n * PARTS + part], out_ref.at[pl.ds(part * rows, rows)], sems.at[part]
        )

    for n in range(len(candidates) // PARTS):

        @pl.when(scalar_ref[0] == n)
        def _():
            for part in range(PARTS):
                copy(n, part).start()

    for part in range(PARTS):
        copy(0, part).wait()


def choose(scalars, candidates):
    rows, cols = candidates[0].shape
    return pl.pallas_call(
        choose_kernel,
        out_shape=jax.ShapeDtypeStruct((rows * PARTS, cols), BF16),
        in_specs=[pl.BlockSpec(memory_space=pltpu.SMEM)]
        + [pl.BlockSpec(memory_space=pl.ANY)] * len(candidates),
        scratch_shapes=[pltpu.SemaphoreType.DMA((PARTS,))],
        compiler_params=PARAMS,
        cost_estimate=cost(),
    )(scalars, *candidates)


def pass_on(scalar_ref, out_ref):
    for n in range(out_ref.shape[0]):
        out_ref[n] = scalar_ref[n]


def gradients_kernel(scale, with_rows, first, scalar_ref, *refs):
    xt_ref, g_ref, mine_ref, other_ref, *refs = refs
    if with_rows:
        wg_ref, wu_ref, *refs = refs
    if not first:
        refs = refs[3:]
    if with_rows and not first:
        acc_in, *refs = refs
    gg_ref, gu_ref, gd_ref, *refs = refs
    width = gg_ref.shape[1]
    if not with_rows:
        pass_on(scalar_ref, refs[0])

    def chunk(in_ref, before, after):
        scaled = in_ref[:, :width]
        d_gate = in_ref[:, width : 2 * width]
        d_up = in_ref[:, 2 * width :]
        if with_rows:
            part = dot(d_gate, wg_ref[...], LAST_DIMS) + dot(d_up, wu_ref[...], LAST_DIMS)
            after[...] = part if before is None else before[...] + part
        gg_ref[...] = (dot(xt_ref[...], d_gate) * scale).astype(BF16)
        gu_ref[...] = (dot(xt_ref[...], d_up) * scale).astype(BF16)
        blocks, _, capacity, feats = g_ref.shape
        rows = g_ref[...].reshape(blocks * capacity, feats)
        gd_ref[...] = (dot(scaled, rows, ROWS_FIRST) * scale).astype(BF16)

    acc_out, acc = refs if with_rows else (None, None)

    @pl.when(pl.program_id(0) == 0)
    def _():
        chunk(mine_ref, None if first else (acc_in if with_rows else None), acc)

    @pl.when(pl.program_id(0) == 1)
    def _():
        chunk(other_ref, acc, acc_out)


def chunk_at(count, index):
    return lambda d, c: (d ^ 1 ^ c[0]) * count + index


def gradients(scalars, index, count, scale, x_t, rows, mine, other, weights, grads, acc):
    groups, _, capacity, feats = rows.shape
    slots = groups * capacity
    width = mine.shape[1] // 3
    hidden = 2 * count * width
    first, with_rows = grads is None, bool(weights)
    whole = pl.BlockSpec((slots, feats), lambda d, c: (0, 0))
    message = pl.BlockSpec((slots, 3 * width), lambda d, c: (0, 0))
    at = chunk_at(count, index)
    column = pl.BlockSpec((feats, width), lambda d, c: (0, at(d, c)))
    out_shape = [
        jax.ShapeDtypeStruct((feats, hidden), BF16),
        jax.ShapeDtypeStruct((feats, hidden), BF16),
        jax.ShapeDtypeStruct((hidden, feats), BF16),
    ]
    out_specs = [column, column, pl.BlockSpec((width, feats), lambda d, c: (at(d, c), 0))]
    in_specs = [
        pl.BlockSpec((feats, slots), lambda d, c: (0, 0)),
        pl.BlockSpec((groups, 1, capacity, feats), lambda d, c: (0, 1, 0, 0)),
        message,
        message,
    ]
    operands = [x_t, rows, mine, other]
    scratch = []
    if with_rows:
        operands += list(weights)
        in_specs += [column, column]
        out_shape.append(jax.ShapeDtypeStruct((slots, feats), F32))
        out_specs.append(whole)
        scratch.append(pltpu.VMEM((slots, feats), F32))
    else:
        out_shape.append(jax.ShapeDtypeStruct(scalars.shape, jnp.int32))
        out_specs.append(pl.BlockSpec(memory_space=pltpu.SMEM))
    aliases = {}
    if not first:
        aliases = {len(operands) + 1 + n: n for n in range(3)}
        operands += grads
        in_specs += [pl.BlockSpec(memory_space=pl.ANY)] * 3
        if with_rows:
            operands.append(acc)
            in_specs.append(whole)
    out = pl.pallas_call(
        functools.partial(gradients_kernel, scale, with_rows, first),
        out_shape=out_shape,
        grid_spec=pltpu.PrefetchScalarGridSpec(
            num_scalar_prefetch=1,
            grid=(2,),
            in_specs=in_specs,
            out_specs=out_specs,
            scratch_shapes=scratch,
        ),
        input_output_aliases=aliases,
        compiler_params=PARAMS,
        cost_estimate=cost(),
    )(scalars, *operands)
    return list(out[:3]), out[3]


def sum_rows_kernel(units, scalar_ref, *refs):
    messages, (wg_ref, wu_ref, acc_in, out_ref, acc) = refs[:units], refs[units:]
    width = wg_ref.shape[1]
    for u in range(units):

        @pl.when(pl.program_id(0) == u)
        def _():
            d_gate = messages[u][:, width : 2 * width]
            d_up = messages[u][:, 2 * width :]
            part = dot(d_gate, wg_ref[...], LAST_DIMS) + dot(d_up, wu_ref[...], LAST_DIMS)
            (acc if u < units - 1 else out_ref)[...] = (acc_in if u == 0 else acc)[...] + part


def sum_rows(scalars, begin, messages, weights, acc):
    slots, feats = acc.shape
    width = messages[0].shape[1] // 3
    units = len(messages)
    column = pl.BlockSpec((feats, width), lambda u, c: (0, c[2 + begin + u]))
    whole = pl.BlockSpec((slots, feats), lambda u, c: (0, 0))
    return pl.pallas_call(
        functools.partial(sum_rows_kernel, units),
        out_shape=jax.ShapeDtypeStruct((slots, feats), F32),
        grid_spec=pltpu.PrefetchScalarGridSpec(
            num_scalar_prefetch=1,
            grid=(units,),
            in_specs=[pl.BlockSpec((slots, 3 * width), lambda u, c: (0, 0))] * units
            + [column, column, whole],
            out_specs=whole,
            scratch_shapes=[pltpu.VMEM((slots, feats), F32)],
        ),
        compiler_params=PARAMS,
        cost_estimate=cost(),
    )(scalars, *messages, *weights, acc)


def last_rows_kernel(scalar_ref, message_ref, wg_ref, wu_ref, acc_in, *refs):
    *pieces, token_ref, acc = refs
    width = wg_ref.shape[1]
    pass_on(scalar_ref, token_ref)
    part = dot(message_ref[:, width : 2 * width], wg_ref[...], LAST_DIMS)
    part += dot(message_ref[:, 2 * width :], wu_ref[...], LAST_DIMS)
    acc[...] = acc_in[...] + part
    size = pieces[0].shape[0]
    for n, piece in enumerate(pieces):
        start = ((scalar_ref[1] % len(pieces)) ^ n) * size
        piece[...] = acc[pl.ds(pl.multiple_of(start, size), size), :].astype(BF16)


def last_rows(scalars, unit, message, weights, acc, half, groups):
    slots, feats = acc.shape
    width = message.shape[1] // 3
    size = slots // groups
    column = pl.BlockSpec((feats, width), lambda u, c: (0, c[2 + unit]))

    def rows(u, c):
        return ((c[1] // (groups // 2)) ^ half, 0)

    *pieces, token = pl.pallas_call(
        last_rows_kernel,
        out_shape=[jax.ShapeDtypeStruct((size, feats), BF16)] * (groups // 2)
        + [jax.ShapeDtypeStruct(scalars.shape, jnp.int32)],
        grid_spec=pltpu.PrefetchScalarGridSpec(
            num_scalar_prefetch=1,
            grid=(1,),
            in_specs=[
                pl.BlockSpec((slots // 2, 3 * width), rows),
                column,
                column,
                pl.BlockSpec((slots // 2, feats), rows),
            ],
            out_specs=[pl.BlockSpec((size, feats), lambda u, c: (0, 0))] * (groups // 2)
            + [pl.BlockSpec(memory_space=pltpu.SMEM)],
            scratch_shapes=[pltpu.VMEM((slots // 2, feats), F32)],
        ),
        compiler_params=PARAMS,
        cost_estimate=cost(),
    )(scalars, message, *weights, acc)
    return pieces, token


def body(tokens, grad_out, expert_ids, route_weights, w_gate, w_up, w_down):
    experts = lax.axis_size("expert")
    groups = lax.axis_size("dp")
    tok_rows = tokens.shape[0]
    feats = w_gate.shape[1]
    capacity = tok_rows // 2
    chips = groups // 2
    count = chips
    assert groups == 2 * experts and tokens.shape[1] == 2 * feats
    inv_root = 1.0 / math.sqrt(tok_rows * groups)
    expert = lax.axis_index("expert").astype(jnp.int32)
    block = lax.axis_index("dp").astype(jnp.int32)
    chip, core = block // 2, block % 2
    along = jnp.where(core == 0, chip, chips - 1 - chip)
    w_gate, w_up, w_down = w_gate[0], w_up[0], w_down[0]
    ids, weights = expert_ids.T, route_weights.T

    rows, hot = dispatch_rows(ids, weights, tokens, grad_out, experts)
    rows = lax.all_to_all(rows, "expert", split_axis=0, concat_axis=0, tiled=True)
    rows = rows.reshape(groups, 2 * capacity, feats)
    rows = lax.all_to_all(rows, "dp", split_axis=0, concat_axis=0, tiled=True)
    rows = rows.reshape(groups, 2, capacity, feats)

    swap = [(j, j ^ 1) for j in range(groups)]
    up = [2 * z for z in range(chips)]
    circle = up + [j + 1 for j in reversed(up)]
    ring = list(zip(circle, circle[1:] + circle[:1]))
    order = [(1 - core) * count + (i - (chips - 1 - along)) % count for i in range(count)]
    order += [core * count + (i - along) % count for i in range(count)]
    forward_scalars = jnp.stack(order).astype(jnp.int32)
    chain_scalars = along.astype(jnp.int32)[None]
    columns = [(d ^ 1 ^ core) * count + k for k in range(count) for d in range(2)]
    backward_scalars = jnp.stack(
        [core, (expert + experts * core) ^ (2 * chip), *columns]
    ).astype(jnp.int32)

    def after(scalars, *things):
        return lax.optimization_barrier((scalars, *things))[0]

    def forward(begin, size, scalars):
        other, mine = forward_chunks(scalars, rows, w_gate, w_up, w_down, begin, size, count)
        sib = lax.ppermute(other, "dp", swap)
        return [((mine, i), (sib, i)) for i in range(size)]

    slots = 2 * count + chips - 2
    ahead = count // 2
    sums = forward(0, ahead, forward_scalars)
    recv = []
    grads, acc = None, None

    def gather(k, scalars):
        mine = choose(scalars, [r for n in range(chips) for r in recv[n - 1 + count + k]])
        return mine, lax.ppermute(mine, "dp", swap)

    first_back = chips - 1 + count
    hop_scalars, gradient_scalars = chain_scalars, backward_scalars
    weights_pair = (w_gate, w_up)
    chunks = []

    def add_chunk(k, with_rows, grads, acc):
        return gradients(
            gradient_scalars,
            k,
            count,
            inv_root,
            x_t,
            rows,
            *chunks[k],
            weights_pair if with_rows else (),
            grads,
            acc,
        )

    early = 0
    for s in range(slots):
        came, sends = [], []
        for part in range(PARTS):
            send = hop(
                hop_scalars,
                s,
                count,
                chips,
                recv[s - 1][part] if s else None,
                sums[s % count],
                part,
            )
            came.append(lax.ppermute(send, "dp", ring))
            sends.append(send)
        recv.append(came)
        if s == 0:
            sums += forward(ahead, count - ahead, after(forward_scalars, came[0]))
        if s == 3:
            x_t = rows[:, 0].reshape(groups * capacity, feats).T
            hop_scalars = after(chain_scalars, x_t)
        k = s - first_back
        if k >= 0:
            chunks.append(gather(k, after(chain_scalars, *sends)))
        if k >= 1:
            gradient_scalars = after(backward_scalars, *sends)
            grads, acc = add_chunk(k - 1, True, grads, acc)
            early = k
            hop_scalars = after(chain_scalars, acc)
    for k in range(len(chunks), count):
        chunks.append(gather(k, hop_scalars))
    units = [message for chunk in chunks for message in chunk][2 * early :]
    acc = sum_rows(backward_scalars, 2 * early, units[:-1], weights_pair, acc)

    def round_pairs(r):
        pairs = []
        for q in range(experts):
            for b in range(groups):
                h, e = divmod(b ^ r ^ (2 * q), experts)
                pairs.append((e * groups + 2 * q + h, q * groups + b))
        return pairs

    returned = []
    token = backward_scalars
    for half in range(2):
        pieces, token = last_rows(
            token, 2 * count - 1, units[-1], weights_pair, acc, half, groups
        )
        for n, piece in enumerate(pieces):
            pairs = round_pairs(half * (groups // 2) + n)
            returned.append(lax.ppermute(piece, ("expert", "dp"), pairs))
        left = range(early, count - 1) if half == 0 else range(count - 1, count)
        for k in left:
            gradient_scalars = token
            grads, token = add_chunk(k, False, grads, None)
    mixed = block ^ (2 * expert)
    combine_scalars = jnp.stack([mixed % experts, mixed // experts])
    grad_tokens = combine_rows(combine_scalars, hot, returned, experts)
    return (grad_tokens, grads[0][None], grads[1][None], grads[2][None])


def solution(mesh):
    in_specs = (
        P("dp", "expert"),
        P("dp", "expert"),
        P("dp", None),
        P("dp", None),
        P("expert", "dp", None),
        P("expert", "dp", None),
        P("expert", None, "dp"),
    )
    out_specs = (
        P("dp", "expert"),
        P("expert", "dp", None),
        P("expert", "dp", None),
        P("expert", None, "dp"),
    )
    return jax.shard_map(body, mesh=mesh, in_specs=in_specs, out_specs=out_specs, check_vma=False)
```

```python
import functools
import math

import jax
import jax.numpy as jnp
from jax import lax
from jax.experimental import pallas as pl
from jax.experimental.pallas import tpu as pltpu
from jax.sharding import PartitionSpec as P

F32 = jnp.float32
BF16 = jnp.bfloat16
LAST_DIMS = (((1,), (1,)), ((), ()))
ROWS_FIRST = (((0,), (0,)), ((), ()))
PARTS = 2
PARAMS = pltpu.CompilerParams(vmem_limit_bytes=48 * 1024 * 1024)


def dot(a, b, dims=None):
    if dims is None:
        return jnp.dot(a, b, preferred_element_type=F32)
    return lax.dot_general(a, b, dims, preferred_element_type=F32)


def cost():
    return pl.CostEstimate(flops=1024, bytes_accessed=1024, transcendentals=0)


def in_hbm(*arrays):
    return [pltpu.with_memory_space_constraint(a, pltpu.HBM) for a in arrays]


def pass_on(scalar_ref, out_ref):
    for n in range(out_ref.shape[0]):
        out_ref[n] = scalar_ref[n]


def slot_one_hot(ids_ref, experts, capacity):
    tokens = ids_ref.shape[1]
    first, second = ids_ref[0:1, :], ids_ref[1:2, :]
    expert = lax.broadcasted_iota(jnp.int32, (8 * (-(-experts // 8)), tokens), 0)
    chosen = (first == expert) | (second == expert)
    before = lax.broadcasted_iota(jnp.int32, (tokens, tokens), 0) < lax.broadcasted_iota(
        jnp.int32, (tokens, tokens), 1
    )
    place = dot(chosen.astype(F32).astype(BF16), before.astype(F32).astype(BF16))
    place = jnp.where(chosen, place, -1.0).astype(jnp.int32)
    slot = lax.broadcasted_iota(jnp.int32, (capacity, tokens), 0)
    return [slot == place[e : e + 1, :] for e in range(experts)]


def dispatch_kernel(experts, ids_hbm, weights_hbm, x_hbm, g_hbm, out_ref, hot_ref, *scratch):
    ids_ref, weights_ref, x_ref, g_ref, sems = scratch
    feats = out_ref.shape[3]
    capacity = out_ref.shape[2] // 2

    def half(ref, h):
        return ref.at[h] if len(ref.shape) == 3 else ref.at[:, pl.ds(h * feats, feats)]

    pairs = [(ids_hbm, ids_ref), (weights_hbm, weights_ref)]
    for h in range(2):
        pairs += [(half(x_hbm, h), x_ref.at[h]), (half(g_hbm, h), g_ref.at[h])]
    copies = [pltpu.make_async_copy(a, b, sems.at[n]) for n, (a, b) in enumerate(pairs)]
    for copy in copies:
        copy.start()
    copies[0].wait()
    copies[1].wait()
    scales = []
    for e, hit in enumerate(slot_one_hot(ids_ref, experts, capacity)):
        weight = jnp.where(ids_ref[0:1, :] == e, weights_ref[0:1, :], weights_ref[1:2, :])
        scales.append(jnp.sum(jnp.where(hit, weight, 0.0), axis=1, keepdims=True))
        hot_ref[e * capacity : (e + 1) * capacity, :] = hit.astype(F32).astype(BF16)
    for h in range(2):
        copies[2 + 2 * h].wait()
        copies[3 + 2 * h].wait()
        x = dot(hot_ref[...], x_ref[h]).astype(BF16)
        g = dot(hot_ref[...], g_ref[h])
        for e in range(experts):
            rows = slice(e * capacity, (e + 1) * capacity)
            out_ref[e, h, :capacity] = x[rows]
            out_ref[e, h, capacity:] = (g[rows] * scales[e]).astype(BF16)


def dispatch_rows(ids, weights, x, g, experts):
    tokens, feats = x.shape[0], x.shape[1] // 2
    capacity = tokens // 2
    if feats % 128:
        x, g = (r.reshape(tokens, 2, feats).transpose(1, 0, 2) for r in (x, g))
    return pl.pallas_call(
        functools.partial(dispatch_kernel, experts),
        out_shape=(
            jax.ShapeDtypeStruct((experts, 2, 2 * capacity, feats), BF16),
            jax.ShapeDtypeStruct((experts * capacity, tokens), BF16),
        ),
        in_specs=[pl.BlockSpec(memory_space=pltpu.HBM)] * 4,
        scratch_shapes=[
            pltpu.VMEM((2, tokens), jnp.int32),
            pltpu.VMEM((2, tokens), F32),
            pltpu.VMEM((2, tokens, feats), BF16),
            pltpu.VMEM((2, tokens, feats), BF16),
            pltpu.SemaphoreType.DMA((6,)),
        ],
        compiler_params=PARAMS,
        cost_estimate=cost(),
    )(*in_hbm(ids, weights, x, g))


def combine_kernel(experts, scalar_ref, hot_ref, *refs):
    pieces, (out_ref, rows_ref, sems) = refs[:-3], refs[-3:]
    capacity = pieces[0].shape[0]
    at = pl.program_id(0)

    def copy(n):
        return pltpu.make_async_copy(
            pieces[n], rows_ref.at[pl.ds(n * capacity, capacity)], sems.at[n]
        )

    @pl.when(at == 0)
    def _():
        for n in range(len(pieces)):
            copy(n).start()

    hot = jnp.concatenate(
        [
            hot_ref[pl.ds(pl.multiple_of((scalar_ref[2] ^ n) * capacity, capacity), capacity), :]
            for n in range(experts)
        ],
        axis=0,
    )
    for half in range(2):

        @pl.when(at == half)
        def _():
            for n in range(half * experts, (half + 1) * experts):
                copy(n).wait()
            rows = rows_ref[half * experts * capacity : (half + 1) * experts * capacity, :]
            out = dot(hot, rows, ROWS_FIRST).astype(BF16)
            out_ref[...] = out.reshape(out_ref.shape)


def combine_rows(scalars, hot, pieces, experts):
    tokens = hot.shape[1]
    capacity, feats = pieces[0].shape
    if feats % 128:
        out_shape = jax.ShapeDtypeStruct((2, tokens, feats), BF16)
        out_spec = pl.BlockSpec((1, tokens, feats), lambda a, c: (a ^ c[3], 0, 0))
    else:
        out_shape = jax.ShapeDtypeStruct((tokens, 2 * feats), BF16)
        out_spec = pl.BlockSpec((tokens, feats), lambda a, c: (0, a ^ c[3]))
    out = pl.pallas_call(
        functools.partial(combine_kernel, experts),
        out_shape=out_shape,
        grid_spec=pltpu.PrefetchScalarGridSpec(
            num_scalar_prefetch=1,
            grid=(2,),
            in_specs=[pl.BlockSpec((experts * capacity, tokens), lambda a, c: (0, 0))]
            + [pl.BlockSpec(memory_space=pltpu.HBM)] * len(pieces),
            out_specs=out_spec,
            scratch_shapes=[
                pltpu.VMEM((len(pieces) * capacity, feats), BF16),
                pltpu.SemaphoreType.DMA((len(pieces),)),
            ],
        ),
        compiler_params=PARAMS,
        cost_estimate=cost(),
    )(scalars, hot, *in_hbm(*pieces))
    if feats % 128:
        out = out.transpose(1, 0, 2).reshape(tokens, 2 * feats)
    return out


def forward_kernel(scalar_ref, x_ref, g_ref, wg_ref, wu_ref, wd_ref, *outs):
    width = wg_ref.shape[1]
    blocks, _, capacity, feats = x_ref.shape
    for own in range(2):

        @pl.when(pl.program_id(1) == own)
        def _():
            x = x_ref[...].reshape(blocks * capacity, feats)
            g = g_ref[...].reshape(blocks * capacity, feats)
            outs[own][0, :, :width] = dot(x, wg_ref[...]).astype(BF16)
            outs[own][0, :, width : 2 * width] = dot(x, wu_ref[...]).astype(BF16)
            outs[own][0, :, 2 * width :] = dot(g, wd_ref[...], LAST_DIMS).astype(BF16)


def forward_chunks(scalars, rows, w_gate, w_up, w_down, begin, size, count):
    groups, _, capacity, feats = rows.shape
    width = w_gate.shape[1] // (2 * count)

    def at(i, own, c):
        return c[4 + 2 * count + own * count + begin + i]

    out = jax.ShapeDtypeStruct((size, groups * capacity, 3 * width), BF16)
    out_spec = pl.BlockSpec((1, groups * capacity, 3 * width), lambda i, own, c: (i, 0, 0))
    return pl.pallas_call(
        forward_kernel,
        out_shape=(out, out),
        grid_spec=pltpu.PrefetchScalarGridSpec(
            num_scalar_prefetch=1,
            grid=(size, 2),
            in_specs=[
                pl.BlockSpec((groups, 1, capacity, feats), lambda i, own, c: (0, 0, 0, 0)),
                pl.BlockSpec((groups, 1, capacity, feats), lambda i, own, c: (0, 1, 0, 0)),
                pl.BlockSpec((feats, width), lambda i, own, c: (0, at(i, own, c))),
                pl.BlockSpec((feats, width), lambda i, own, c: (0, at(i, own, c))),
                pl.BlockSpec((width, feats), lambda i, own, c: (at(i, own, c), 0)),
            ],
            out_specs=(out_spec, out_spec),
        ),
        compiler_params=PARAMS,
        cost_estimate=cost(),
    )(scalars, rows, rows, *in_hbm(w_gate, w_up, w_down))


def activate(gate, upper, back):
    sig = jax.nn.sigmoid(gate)
    gated = gate * sig
    return (
        (gated * upper).astype(BF16),
        (back * upper * sig * (1.0 + gate * (1.0 - sig))).astype(BF16),
        (back * gated).astype(BF16),
    )


def hop_kernel(plan, scalar_ref, *refs):
    slot, count, chips, sums, came, hand_on = plan
    refs = list(refs)
    recv_ref = refs.pop(0) if came else None
    own_ref, sib_ref = refs[:2] if sums else (None, None)
    send_ref = refs[-2] if hand_on else refs[-1]
    if hand_on:
        pass_on(scalar_ref, refs[-1])
    at = scalar_ref[0]
    width = send_ref.shape[1] // 3
    summing = (at <= slot) & (slot - at < count)

    def total(part):
        columns = slice(part * width, (part + 1) * width)
        value = own_ref[0, :, columns].astype(F32) + sib_ref[0, :, columns].astype(F32)
        if came:
            value += jnp.where(at > 0, recv_ref[:, columns].astype(F32), 0.0)
        return value

    if sums:

        @pl.when(summing & (at < chips - 1))
        def _():
            for part in range(3):
                send_ref[:, part * width : (part + 1) * width] = total(part).astype(BF16)

        @pl.when(summing & (at == chips - 1))
        def _():
            for part, value in enumerate(activate(total(0), total(1), total(2))):
                send_ref[:, part * width : (part + 1) * width] = value

    if came:

        @pl.when(jnp.logical_not(summing))
        def _():
            send_ref[...] = recv_ref[...]


def hop(scalars, slot, count, chips, recv, sums, part, hand_on):
    rows, cols = sums[0][0].shape[1:]
    rows //= PARTS
    message = pl.BlockSpec((rows, cols), lambda n, c: (0, 0))
    operands, in_specs = [], []
    if recv is not None:
        operands.append(recv)
        in_specs.append(message)
    adds = slot < count + chips - 1
    if adds:
        for array, i in sums:
            operands.append(array)
            in_specs.append(pl.BlockSpec((1, rows, cols), lambda n, c, i=i: (i, part, 0)))
    plan = (slot, count, chips, adds, recv is not None, hand_on)
    out_shape, out_specs = [jax.ShapeDtypeStruct((rows, cols), BF16)], [message]
    if hand_on:
        out_shape.append(jax.ShapeDtypeStruct(scalars.shape, jnp.int32))
        out_specs.append(pl.BlockSpec(memory_space=pltpu.SMEM))
    out = pl.pallas_call(
        functools.partial(hop_kernel, plan),
        out_shape=out_shape,
        grid_spec=pltpu.PrefetchScalarGridSpec(
            num_scalar_prefetch=1,
            grid=(1,),
            in_specs=in_specs,
            out_specs=out_specs,
        ),
        compiler_params=PARAMS,
        cost_estimate=cost(),
    )(scalars, *operands)
    return out[0], (out[1] if hand_on else None)


def choose_kernel(scalar_ref, *refs):
    *candidates, out_ref, sems = refs
    rows = candidates[0].shape[0]

    def copy(n, part):
        return pltpu.make_async_copy(
            candidates[n * PARTS + part], out_ref.at[pl.ds(part * rows, rows)], sems.at[part]
        )

    for n in range(len(candidates) // PARTS):

        @pl.when(scalar_ref[0] == n)
        def _():
            for part in range(PARTS):
                copy(n, part).start()

    for part in range(PARTS):
        copy(0, part).wait()


def choose(scalars, candidates):
    rows, cols = candidates[0].shape
    return pl.pallas_call(
        choose_kernel,
        out_shape=jax.ShapeDtypeStruct((rows * PARTS, cols), BF16),
        in_specs=[pl.BlockSpec(memory_space=pltpu.SMEM)]
        + [pl.BlockSpec(memory_space=pl.ANY)] * len(candidates),
        scratch_shapes=[pltpu.SemaphoreType.DMA((PARTS,))],
        compiler_params=PARAMS,
        cost_estimate=cost(),
    )(scalars, *candidates)


def gradients_kernel(scale, first, scalar_ref, xt_ref, g_ref, *refs):
    messages, refs = refs[:2], refs[2 if first else 5 :]
    gg_ref, gu_ref, gd_ref, token_ref = refs
    width = gg_ref.shape[1]
    pass_on(scalar_ref, token_ref)
    for u in range(2):

        @pl.when(pl.program_id(0) == u)
        def _():
            scaled = messages[u][:, :width]
            d_gate = messages[u][:, width : 2 * width]
            d_up = messages[u][:, 2 * width :]
            gg_ref[...] = (dot(xt_ref[...], d_gate) * scale).astype(BF16)
            gu_ref[...] = (dot(xt_ref[...], d_up) * scale).astype(BF16)
            blocks, _, capacity, feats = g_ref.shape
            rows = g_ref[...].reshape(blocks * capacity, feats)
            gd_ref[...] = (dot(scaled, rows, ROWS_FIRST) * scale).astype(BF16)


def gradients(scalars, index, count, scale, x_t, rows, messages, grads):
    groups, _, capacity, feats = rows.shape
    slots = groups * capacity
    width = messages[0].shape[1] // 3
    hidden = 2 * count * width
    message = pl.BlockSpec((slots, 3 * width), lambda d, c: (0, 0))

    def at(d, c):
        return c[4 + 2 * index + d]

    column = pl.BlockSpec((feats, width), lambda d, c: (0, at(d, c)))
    in_specs = [
        pl.BlockSpec((feats, slots), lambda d, c: (0, 0)),
        pl.BlockSpec((groups, 1, capacity, feats), lambda d, c: (0, 1, 0, 0)),
        message,
        message,
    ]
    operands = [x_t, rows, *messages]
    aliases = {}
    if grads is not None:
        aliases = {len(operands) + 1 + n: n for n in range(3)}
        operands += grads
        in_specs += [pl.BlockSpec(memory_space=pl.ANY)] * 3
    *grads, token = pl.pallas_call(
        functools.partial(gradients_kernel, scale, grads is None),
        out_shape=[
            jax.ShapeDtypeStruct((feats, hidden), BF16),
            jax.ShapeDtypeStruct((feats, hidden), BF16),
            jax.ShapeDtypeStruct((hidden, feats), BF16),
            jax.ShapeDtypeStruct(scalars.shape, jnp.int32),
        ],
        grid_spec=pltpu.PrefetchScalarGridSpec(
            num_scalar_prefetch=1,
            grid=(2,),
            in_specs=in_specs,
            out_specs=[
                column,
                column,
                pl.BlockSpec((width, feats), lambda d, c: (at(d, c), 0)),
                pl.BlockSpec(memory_space=pltpu.SMEM),
            ],
        ),
        input_output_aliases=aliases,
        compiler_params=PARAMS,
        cost_estimate=cost(),
    )(scalars, *operands)
    return grads, token


def sum_rows_kernel(units, first, scalar_ref, *refs):
    messages, (wg_ref, wu_ref, *refs) = refs[:units], refs[units:]
    acc_in = None if first else refs[0]
    out_ref, token_ref, acc = refs[-3:]
    width = wg_ref.shape[1]
    pass_on(scalar_ref, token_ref)
    for u in range(units):

        @pl.when(pl.program_id(0) == u)
        def _():
            d_gate = messages[u][:, width : 2 * width]
            d_up = messages[u][:, 2 * width :]
            part = dot(d_gate, wg_ref[...], LAST_DIMS) + dot(d_up, wu_ref[...], LAST_DIMS)
            if u or not first:
                part += (acc if u else acc_in)[...]
            (acc if u < units - 1 else out_ref)[...] = part


def sum_rows(scalars, begin, messages, weights, acc):
    slots, width = messages[0].shape[0], messages[0].shape[1] // 3
    feats = weights[0].shape[0]
    units = len(messages)
    column = pl.BlockSpec((feats, width), lambda u, c: (0, c[4 + begin + u]))
    whole = pl.BlockSpec((slots, feats), lambda u, c: (0, 0))
    first = acc is None
    return pl.pallas_call(
        functools.partial(sum_rows_kernel, units, first),
        out_shape=(
            jax.ShapeDtypeStruct((slots, feats), F32),
            jax.ShapeDtypeStruct(scalars.shape, jnp.int32),
        ),
        grid_spec=pltpu.PrefetchScalarGridSpec(
            num_scalar_prefetch=1,
            grid=(units,),
            in_specs=[pl.BlockSpec((slots, 3 * width), lambda u, c: (0, 0))] * units
            + [column, column]
            + ([] if first else [whole]),
            out_specs=(whole, pl.BlockSpec(memory_space=pltpu.SMEM)),
            scratch_shapes=[pltpu.VMEM((slots, feats), F32)],
        ),
        compiler_params=PARAMS,
        cost_estimate=cost(),
    )(scalars, *messages, *in_hbm(*weights), *([] if first else [acc]))


def last_rows_kernel(scalar_ref, message_ref, wg_ref, wu_ref, acc_in, *refs):
    *pieces, acc = refs
    width = wg_ref.shape[1]
    part = dot(message_ref[:, width : 2 * width], wg_ref[...], LAST_DIMS)
    part += dot(message_ref[:, 2 * width :], wu_ref[...], LAST_DIMS)
    acc[...] = acc_in[...] + part
    size, each = pieces[0].shape[0], len(pieces) // 2
    for half in range(2):

        @pl.when(pl.program_id(0) == half)
        def _():
            for n in range(each):
                start = pl.multiple_of(((scalar_ref[1] % each) ^ n) * size, size)
                pieces[half * each + n][...] = acc[pl.ds(start, size), :].astype(BF16)


def last_rows(scalars, unit, message, weights, acc, groups):
    slots, feats = acc.shape
    width = message.shape[1] // 3
    size = slots // groups
    column = pl.BlockSpec((feats, width), lambda u, c: (0, c[4 + unit]))

    def rows(half, c):
        return ((c[1] // (groups // 2)) ^ half, 0)

    return pl.pallas_call(
        last_rows_kernel,
        out_shape=[jax.ShapeDtypeStruct((size, feats), BF16)] * groups,
        grid_spec=pltpu.PrefetchScalarGridSpec(
            num_scalar_prefetch=1,
            grid=(2,),
            in_specs=[
                pl.BlockSpec((slots // 2, 3 * width), rows),
                column,
                column,
                pl.BlockSpec((slots // 2, feats), rows),
            ],
            out_specs=[pl.BlockSpec((size, feats), lambda u, c: (0, 0))] * groups,
            scratch_shapes=[pltpu.VMEM((slots // 2, feats), F32)],
        ),
        compiler_params=PARAMS,
        cost_estimate=cost(),
    )(scalars, message, *in_hbm(*weights), acc)


def body(tokens, grad_out, expert_ids, route_weights, w_gate, w_up, w_down):
    experts = lax.axis_size("expert")
    groups = lax.axis_size("dp")
    tok_rows = tokens.shape[0]
    feats = w_gate.shape[1]
    capacity = tok_rows // 2
    chips = groups // 2
    count = chips
    assert groups == 2 * experts and tokens.shape[1] == 2 * feats
    inv_root = 1.0 / math.sqrt(tok_rows * groups)
    expert = lax.axis_index("expert").astype(jnp.int32)
    block = lax.axis_index("dp").astype(jnp.int32)
    chip, core = block // 2, block % 2
    along = jnp.where(core == 0, chip, chips - 1 - chip)
    w_gate, w_up, w_down = w_gate[0], w_up[0], w_down[0]
    ids, weights = expert_ids.T, route_weights.T

    rows, hot = dispatch_rows(ids, weights, tokens, grad_out, experts)
    rows = lax.all_to_all(rows, "expert", split_axis=0, concat_axis=0, tiled=True)
    rows = rows.reshape(groups, 2 * capacity, feats)
    rows = lax.all_to_all(rows, "dp", split_axis=0, concat_axis=0, tiled=True)
    rows = rows.reshape(groups, 2, capacity, feats)

    swap = [(j, j ^ 1) for j in range(groups)]
    up = [2 * z for z in range(chips)]
    circle = up + [j + 1 for j in reversed(up)]
    ring = list(zip(circle, circle[1:] + circle[:1]))
    mixed = block ^ (2 * expert)
    scalars = [along, (expert + experts * core) ^ (2 * chip), mixed % experts, mixed // experts]
    scalars += [(d ^ 1 ^ core) * count + k for k in range(count) for d in range(2)]
    scalars += [(1 - core) * count + (i - (chips - 1 - along)) % count for i in range(count)]
    scalars += [core * count + (i - along) % count for i in range(count)]
    scalars = jnp.stack(scalars).astype(jnp.int32)

    sums = []
    ahead = count // 2
    for begin, size in ((0, ahead), (ahead, count - ahead)):
        other, mine = forward_chunks(scalars, rows, w_gate, w_up, w_down, begin, size, count)
        sib = lax.ppermute(other, "dp", swap)
        sums += [((mine, i), (sib, i)) for i in range(size)]
    x_t = rows[:, 0].reshape(groups * capacity, feats).T

    slots = 2 * count + chips - 2
    first_back = chips - 1 + count
    recv, chunks = [], []
    grads, acc = None, None
    both = (w_gate, w_up)

    def gather(k, token):
        mine = choose(token, [r for n in range(chips) for r in recv[n - 1 + count + k]])
        chunks.append((mine, lax.ppermute(mine, "dp", swap)))

    token = scalars
    for s in range(slots):
        came = []
        for part in range(PARTS):
            send, handed = hop(
                token if part else scalars,
                s,
                count,
                chips,
                recv[s - 1][part] if s else None,
                sums[s % count],
                part,
                part == PARTS - 1 and s >= first_back,
            )
            came.append(lax.ppermute(send, "dp", ring))
        recv.append(came)
        k = s - first_back
        if k >= 0:
            gather(k, handed)
            if s == slots - 1 and k > 0:
                units = [message for chunk in chunks[:k] for message in chunk]
                acc, handed = sum_rows(handed, 0, units, both, None)
            grads, token = gradients(handed, k, count, inv_root, x_t, rows, chunks[k], grads)

    early = len(chunks)
    for k in range(early, count):
        gather(k, token)
    units = [message for chunk in chunks for message in chunk][2 * (early - 1) :]
    acc, _ = sum_rows(scalars, 2 * (early - 1), units[:-1], both, acc)
    pieces = last_rows(scalars, 2 * count - 1, units[-1], both, acc, groups)
    returned = []
    for r, piece in enumerate(pieces):
        pairs = []
        for q in range(experts):
            for b in range(groups):
                h, e = divmod(b ^ r ^ (2 * q), experts)
                pairs.append((e * groups + 2 * q + h, q * groups + b))
        returned.append(lax.ppermute(piece, ("expert", "dp"), pairs))
    for k in range(early, count):
        grads, _ = gradients(scalars, k, count, inv_root, x_t, rows, chunks[k], grads)
    grad_tokens = combine_rows(scalars, hot, returned, experts)
    return (grad_tokens, grads[0][None], grads[1][None], grads[2][None])


def solution(mesh):
    in_specs = (
        P("dp", "expert"),
        P("dp", "expert"),
        P("dp", None),
        P("dp", None),
        P("expert", "dp", None),
        P("expert", "dp", None),
        P("expert", None, "dp"),
    )
    out_specs = (
        P("dp", "expert"),
        P("expert", "dp", None),
        P("expert", "dp", None),
        P("expert", None, "dp"),
    )
    return jax.shard_map(body, mesh=mesh, in_specs=in_specs, out_specs=out_specs, check_vma=False)
```

```python
import functools
import math

import jax
import jax.numpy as jnp
from jax import lax
from jax.experimental import pallas as pl
from jax.experimental.pallas import tpu as pltpu
from jax.sharding import PartitionSpec as P

F32 = jnp.float32
BF16 = jnp.bfloat16
LAST_DIMS = (((1,), (1,)), ((), ()))
ROWS_FIRST = (((0,), (0,)), ((), ()))
PARTS = 2
PARAMS = pltpu.CompilerParams(vmem_limit_bytes=48 * 1024 * 1024)


def dot(a, b, dims=None):
    if dims is None:
        return jnp.dot(a, b, preferred_element_type=F32)
    return lax.dot_general(a, b, dims, preferred_element_type=F32)


def cost():
    return pl.CostEstimate(flops=1024, bytes_accessed=1024, transcendentals=0)


def in_hbm(*arrays):
    return [pltpu.with_memory_space_constraint(a, pltpu.HBM) for a in arrays]


def pass_on(scalar_ref, out_ref):
    for n in range(out_ref.shape[0]):
        out_ref[n] = scalar_ref[n]


def slot_one_hot(ids_ref, experts, capacity):
    tokens = ids_ref.shape[1]
    first, second = ids_ref[0:1, :], ids_ref[1:2, :]
    expert = lax.broadcasted_iota(jnp.int32, (8 * (-(-experts // 8)), tokens), 0)
    chosen = (first == expert) | (second == expert)
    before = lax.broadcasted_iota(jnp.int32, (tokens, tokens), 0) < lax.broadcasted_iota(
        jnp.int32, (tokens, tokens), 1
    )
    place = dot(chosen.astype(F32).astype(BF16), before.astype(F32).astype(BF16))
    place = jnp.where(chosen, place, -1.0).astype(jnp.int32)
    slot = lax.broadcasted_iota(jnp.int32, (capacity, tokens), 0)
    return [slot == place[e : e + 1, :] for e in range(experts)]


def dispatch_kernel(experts, ids_hbm, weights_hbm, x_hbm, g_hbm, out_ref, hot_ref, *scratch):
    ids_ref, weights_ref, x_ref, g_ref, sems = scratch
    feats = out_ref.shape[3]
    capacity = out_ref.shape[2] // 2

    def half(ref, h):
        return ref.at[h] if len(ref.shape) == 3 else ref.at[:, pl.ds(h * feats, feats)]

    pairs = [(ids_hbm, ids_ref), (weights_hbm, weights_ref)]
    for h in range(2):
        pairs += [(half(x_hbm, h), x_ref.at[h]), (half(g_hbm, h), g_ref.at[h])]
    copies = [pltpu.make_async_copy(a, b, sems.at[n]) for n, (a, b) in enumerate(pairs)]
    for copy in copies:
        copy.start()
    copies[0].wait()
    copies[1].wait()
    scales = []
    for e, hit in enumerate(slot_one_hot(ids_ref, experts, capacity)):
        weight = jnp.where(ids_ref[0:1, :] == e, weights_ref[0:1, :], weights_ref[1:2, :])
        scales.append(jnp.sum(jnp.where(hit, weight, 0.0), axis=1, keepdims=True))
        hot_ref[e * capacity : (e + 1) * capacity, :] = hit.astype(F32).astype(BF16)
    for h in range(2):
        copies[2 + 2 * h].wait()
        copies[3 + 2 * h].wait()
        x = dot(hot_ref[...], x_ref[h]).astype(BF16)
        g = dot(hot_ref[...], g_ref[h])
        for e in range(experts):
            rows = slice(e * capacity, (e + 1) * capacity)
            out_ref[e, h, :capacity] = x[rows]
            out_ref[e, h, capacity:] = (g[rows] * scales[e]).astype(BF16)


def dispatch_rows(ids, weights, x, g, experts):
    tokens, feats = x.shape[0], x.shape[1] // 2
    capacity = tokens // 2
    if feats % 128:
        x, g = (r.reshape(tokens, 2, feats).transpose(1, 0, 2) for r in (x, g))
    return pl.pallas_call(
        functools.partial(dispatch_kernel, experts),
        out_shape=(
            jax.ShapeDtypeStruct((experts, 2, 2 * capacity, feats), BF16),
            jax.ShapeDtypeStruct((experts * capacity, tokens), BF16),
        ),
        in_specs=[pl.BlockSpec(memory_space=pltpu.HBM)] * 4,
        scratch_shapes=[
            pltpu.VMEM((2, tokens), jnp.int32),
            pltpu.VMEM((2, tokens), F32),
            pltpu.VMEM((2, tokens, feats), BF16),
            pltpu.VMEM((2, tokens, feats), BF16),
            pltpu.SemaphoreType.DMA((6,)),
        ],
        compiler_params=PARAMS,
        cost_estimate=cost(),
    )(*in_hbm(ids, weights, x, g))


def combine_kernel(experts, scalar_ref, hot_ref, *refs):
    pieces, (out_ref, rows_ref, sems) = refs[:-3], refs[-3:]
    capacity = pieces[0].shape[0]
    at = pl.program_id(0)

    def copy(n):
        return pltpu.make_async_copy(
            pieces[n], rows_ref.at[pl.ds(n * capacity, capacity)], sems.at[n]
        )

    @pl.when(at == 0)
    def _():
        for n in range(len(pieces)):
            copy(n).start()

    hot = jnp.concatenate(
        [
            hot_ref[pl.ds(pl.multiple_of((scalar_ref[2] ^ n) * capacity, capacity), capacity), :]
            for n in range(experts)
        ],
        axis=0,
    )
    for half in range(2):

        @pl.when(at == half)
        def _():
            for n in range(half * experts, (half + 1) * experts):
                copy(n).wait()
            rows = rows_ref[half * experts * capacity : (half + 1) * experts * capacity, :]
            out = dot(hot, rows, ROWS_FIRST).astype(BF16)
            out_ref[...] = out.reshape(out_ref.shape)


def combine_rows(scalars, hot, pieces, experts):
    tokens = hot.shape[1]
    capacity, feats = pieces[0].shape
    if feats % 128:
        out_shape = jax.ShapeDtypeStruct((2, tokens, feats), BF16)
        out_spec = pl.BlockSpec((1, tokens, feats), lambda a, c: (a ^ c[3], 0, 0))
    else:
        out_shape = jax.ShapeDtypeStruct((tokens, 2 * feats), BF16)
        out_spec = pl.BlockSpec((tokens, feats), lambda a, c: (0, a ^ c[3]))
    out = pl.pallas_call(
        functools.partial(combine_kernel, experts),
        out_shape=out_shape,
        grid_spec=pltpu.PrefetchScalarGridSpec(
            num_scalar_prefetch=1,
            grid=(2,),
            in_specs=[pl.BlockSpec((experts * capacity, tokens), lambda a, c: (0, 0))]
            + [pl.BlockSpec(memory_space=pltpu.HBM)] * len(pieces),
            out_specs=out_spec,
            scratch_shapes=[
                pltpu.VMEM((len(pieces) * capacity, feats), BF16),
                pltpu.SemaphoreType.DMA((len(pieces),)),
            ],
        ),
        compiler_params=PARAMS,
        cost_estimate=cost(),
    )(scalars, hot, *in_hbm(*pieces))
    if feats % 128:
        out = out.transpose(1, 0, 2).reshape(tokens, 2 * feats)
    return out


def forward_kernel(scalar_ref, x_ref, g_ref, wg_ref, wu_ref, wd_ref, *outs):
    width = wg_ref.shape[1]
    blocks, _, capacity, feats = x_ref.shape
    if len(outs) > 2:

        @pl.when((pl.program_id(0) == 0) & (pl.program_id(1) == 0))
        def _():
            outs[2][...] = x_ref[...].reshape(blocks * capacity, feats).T

    for own in range(2):

        @pl.when(pl.program_id(1) == own)
        def _():
            x = x_ref[...].reshape(blocks * capacity, feats)
            g = g_ref[...].reshape(blocks * capacity, feats)
            outs[own][0, :, :width] = dot(x, wg_ref[...]).astype(BF16)
            outs[own][0, :, width : 2 * width] = dot(x, wu_ref[...]).astype(BF16)
            outs[own][0, :, 2 * width :] = dot(g, wd_ref[...], LAST_DIMS).astype(BF16)


def forward_chunks(scalars, rows, w_gate, w_up, w_down, begin, size, count, turned):
    groups, _, capacity, feats = rows.shape
    width = w_gate.shape[1] // (2 * count)

    def at(i, own, c):
        return c[4 + 2 * count + own * count + begin + i]

    out = jax.ShapeDtypeStruct((size, groups * capacity, 3 * width), BF16)
    out_spec = pl.BlockSpec((1, groups * capacity, 3 * width), lambda i, own, c: (i, 0, 0))
    out_shape, out_specs = [out, out], [out_spec, out_spec]
    if turned:
        out_shape.append(jax.ShapeDtypeStruct((feats, groups * capacity), BF16))
        out_specs.append(pl.BlockSpec((feats, groups * capacity), lambda i, own, c: (0, 0)))
    return pl.pallas_call(
        forward_kernel,
        out_shape=out_shape,
        grid_spec=pltpu.PrefetchScalarGridSpec(
            num_scalar_prefetch=1,
            grid=(size, 2),
            in_specs=[
                pl.BlockSpec((groups, 1, capacity, feats), lambda i, own, c: (0, 0, 0, 0)),
                pl.BlockSpec((groups, 1, capacity, feats), lambda i, own, c: (0, 1, 0, 0)),
                pl.BlockSpec((feats, width), lambda i, own, c: (0, at(i, own, c))),
                pl.BlockSpec((feats, width), lambda i, own, c: (0, at(i, own, c))),
                pl.BlockSpec((width, feats), lambda i, own, c: (at(i, own, c), 0)),
            ],
            out_specs=out_specs,
        ),
        compiler_params=PARAMS,
        cost_estimate=cost(),
    )(scalars, rows, rows, *in_hbm(w_gate, w_up, w_down))


def activate(gate, upper, back):
    sig = jax.nn.sigmoid(gate)
    gated = gate * sig
    return (
        (gated * upper).astype(BF16),
        (back * upper * sig * (1.0 + gate * (1.0 - sig))).astype(BF16),
        (back * gated).astype(BF16),
    )


def hop_kernel(plan, scalar_ref, *refs):
    slot, count, chips, came = plan
    refs = list(refs)
    recv_ref = refs.pop(0) if came else None
    own_ref, sib_ref = refs[:2]
    send_ref = refs[-1]
    at = scalar_ref[0]
    width = send_ref.shape[1] // 3
    summing = (at <= slot) & (slot - at < count)

    def total(part):
        columns = slice(part * width, (part + 1) * width)
        value = own_ref[0, :, columns].astype(F32) + sib_ref[0, :, columns].astype(F32)
        if came:
            value += jnp.where(at > 0, recv_ref[:, columns].astype(F32), 0.0)
        return value

    @pl.when(summing & (at < chips - 1))
    def _():
        for part in range(3):
            send_ref[:, part * width : (part + 1) * width] = total(part).astype(BF16)

    @pl.when(summing & (at == chips - 1))
    def _():
        for part, value in enumerate(activate(total(0), total(1), total(2))):
            send_ref[:, part * width : (part + 1) * width] = value

    if came:

        @pl.when(jnp.logical_not(summing))
        def _():
            send_ref[...] = recv_ref[...]


def hop(scalars, slot, count, chips, recv, sums, part):
    rows, cols = sums[0][0].shape[1:]
    rows //= PARTS
    message = pl.BlockSpec((rows, cols), lambda n, c: (0, 0))
    operands, in_specs = [], []
    if recv is not None:
        operands.append(recv)
        in_specs.append(message)
    for array, i in sums:
        operands.append(array)
        in_specs.append(pl.BlockSpec((1, rows, cols), lambda n, c, i=i: (i, part, 0)))
    plan = (slot, count, chips, recv is not None)
    return pl.pallas_call(
        functools.partial(hop_kernel, plan),
        out_shape=jax.ShapeDtypeStruct((rows, cols), BF16),
        grid_spec=pltpu.PrefetchScalarGridSpec(
            num_scalar_prefetch=1,
            grid=(1,),
            in_specs=in_specs,
            out_specs=message,
        ),
        compiler_params=PARAMS,
        cost_estimate=cost(),
    )(scalars, *operands)


def choose_kernel(scalar_ref, *refs):
    *candidates, out_ref, sems = refs
    rows = candidates[0].shape[0]

    def copy(n, part):
        return pltpu.make_async_copy(
            candidates[n * PARTS + part], out_ref.at[pl.ds(part * rows, rows)], sems.at[part]
        )

    for n in range(len(candidates) // PARTS):

        @pl.when(scalar_ref[0] == n)
        def _():
            for part in range(PARTS):
                copy(n, part).start()

    for part in range(PARTS):
        copy(0, part).wait()


def choose(scalars, candidates):
    rows, cols = candidates[0].shape
    return pl.pallas_call(
        choose_kernel,
        out_shape=jax.ShapeDtypeStruct((rows * PARTS, cols), BF16),
        in_specs=[pl.BlockSpec(memory_space=pltpu.SMEM)]
        + [pl.BlockSpec(memory_space=pl.ANY)] * len(candidates),
        scratch_shapes=[pltpu.SemaphoreType.DMA((PARTS,))],
        compiler_params=PARAMS,
        cost_estimate=cost(),
    )(scalars, *candidates)


def gradients_kernel(scale, first, scalar_ref, xt_ref, g_ref, *refs):
    messages, refs = refs[:2], refs[2 if first else 5 :]
    gg_ref, gu_ref, gd_ref, token_ref = refs
    width = gg_ref.shape[1]
    pass_on(scalar_ref, token_ref)
    for u in range(2):

        @pl.when(pl.program_id(0) == u)
        def _():
            scaled = messages[u][:, :width]
            d_gate = messages[u][:, width : 2 * width]
            d_up = messages[u][:, 2 * width :]
            gg_ref[...] = (dot(xt_ref[...], d_gate) * scale).astype(BF16)
            gu_ref[...] = (dot(xt_ref[...], d_up) * scale).astype(BF16)
            blocks, _, capacity, feats = g_ref.shape
            rows = g_ref[...].reshape(blocks * capacity, feats)
            gd_ref[...] = (dot(scaled, rows, ROWS_FIRST) * scale).astype(BF16)


def gradients(scalars, index, count, scale, x_t, rows, messages, grads):
    groups, _, capacity, feats = rows.shape
    slots = groups * capacity
    width = messages[0].shape[1] // 3
    hidden = 2 * count * width
    message = pl.BlockSpec((slots, 3 * width), lambda d, c: (0, 0))

    def at(d, c):
        return c[4 + 2 * index + d]

    column = pl.BlockSpec((feats, width), lambda d, c: (0, at(d, c)))
    in_specs = [
        pl.BlockSpec((feats, slots), lambda d, c: (0, 0)),
        pl.BlockSpec((groups, 1, capacity, feats), lambda d, c: (0, 1, 0, 0)),
        message,
        message,
    ]
    operands = [x_t, rows, *messages]
    aliases = {}
    if grads is not None:
        aliases = {len(operands) + 1 + n: n for n in range(3)}
        operands += grads
        in_specs += [pl.BlockSpec(memory_space=pl.ANY)] * 3
    *grads, token = pl.pallas_call(
        functools.partial(gradients_kernel, scale, grads is None),
        out_shape=[
            jax.ShapeDtypeStruct((feats, hidden), BF16),
            jax.ShapeDtypeStruct((feats, hidden), BF16),
            jax.ShapeDtypeStruct((hidden, feats), BF16),
            jax.ShapeDtypeStruct(scalars.shape, jnp.int32),
        ],
        grid_spec=pltpu.PrefetchScalarGridSpec(
            num_scalar_prefetch=1,
            grid=(2,),
            in_specs=in_specs,
            out_specs=[
                column,
                column,
                pl.BlockSpec((width, feats), lambda d, c: (at(d, c), 0)),
                pl.BlockSpec(memory_space=pltpu.SMEM),
            ],
        ),
        input_output_aliases=aliases,
        compiler_params=PARAMS,
        cost_estimate=cost(),
    )(scalars, *operands)
    return grads, token


def sum_rows_kernel(units, first, scalar_ref, *refs):
    messages, (wg_ref, wu_ref, *refs) = refs[:units], refs[units:]
    acc_in = None if first else refs[0]
    out_ref, token_ref, acc = refs[-3:]
    width = wg_ref.shape[1]
    pass_on(scalar_ref, token_ref)
    for u in range(units):

        @pl.when(pl.program_id(0) == u)
        def _():
            d_gate = messages[u][:, width : 2 * width]
            d_up = messages[u][:, 2 * width :]
            part = dot(d_gate, wg_ref[...], LAST_DIMS) + dot(d_up, wu_ref[...], LAST_DIMS)
            if u or not first:
                part += (acc if u else acc_in)[...]
            (acc if u < units - 1 else out_ref)[...] = part


def sum_rows(scalars, begin, messages, weights, acc):
    slots, width = messages[0].shape[0], messages[0].shape[1] // 3
    feats = weights[0].shape[0]
    units = len(messages)
    column = pl.BlockSpec((feats, width), lambda u, c: (0, c[4 + begin + u]))
    whole = pl.BlockSpec((slots, feats), lambda u, c: (0, 0))
    first = acc is None
    return pl.pallas_call(
        functools.partial(sum_rows_kernel, units, first),
        out_shape=(
            jax.ShapeDtypeStruct((slots, feats), F32),
            jax.ShapeDtypeStruct(scalars.shape, jnp.int32),
        ),
        grid_spec=pltpu.PrefetchScalarGridSpec(
            num_scalar_prefetch=1,
            grid=(units,),
            in_specs=[pl.BlockSpec((slots, 3 * width), lambda u, c: (0, 0))] * units
            + [column, column]
            + ([] if first else [whole]),
            out_specs=(whole, pl.BlockSpec(memory_space=pltpu.SMEM)),
            scratch_shapes=[pltpu.VMEM((slots, feats), F32)],
        ),
        compiler_params=PARAMS,
        cost_estimate=cost(),
    )(scalars, *messages, *in_hbm(*weights), *([] if first else [acc]))


def last_rows_kernel(scalar_ref, message_ref, wg_ref, wu_ref, acc_in, *refs):
    *pieces, acc = refs
    width = wg_ref.shape[1]
    part = dot(message_ref[:, width : 2 * width], wg_ref[...], LAST_DIMS)
    part += dot(message_ref[:, 2 * width :], wu_ref[...], LAST_DIMS)
    acc[...] = acc_in[...] + part
    size, each = pieces[0].shape[0], len(pieces) // 2
    for half in range(2):

        @pl.when(pl.program_id(0) == half)
        def _():
            for n in range(each):
                start = pl.multiple_of(((scalar_ref[1] % each) ^ n) * size, size)
                pieces[half * each + n][...] = acc[pl.ds(start, size), :].astype(BF16)


def last_rows(scalars, unit, message, weights, acc, groups):
    slots, feats = acc.shape
    width = message.shape[1] // 3
    size = slots // groups
    column = pl.BlockSpec((feats, width), lambda u, c: (0, c[4 + unit]))

    def rows(half, c):
        return ((c[1] // (groups // 2)) ^ half, 0)

    return pl.pallas_call(
        last_rows_kernel,
        out_shape=[jax.ShapeDtypeStruct((size, feats), BF16)] * groups,
        grid_spec=pltpu.PrefetchScalarGridSpec(
            num_scalar_prefetch=1,
            grid=(2,),
            in_specs=[
                pl.BlockSpec((slots // 2, 3 * width), rows),
                column,
                column,
                pl.BlockSpec((slots // 2, feats), rows),
            ],
            out_specs=[pl.BlockSpec((size, feats), lambda u, c: (0, 0))] * groups,
            scratch_shapes=[pltpu.VMEM((slots // 2, feats), F32)],
        ),
        compiler_params=PARAMS,
        cost_estimate=cost(),
    )(scalars, message, *in_hbm(*weights), acc)


def body(tokens, grad_out, expert_ids, route_weights, w_gate, w_up, w_down):
    experts = lax.axis_size("expert")
    groups = lax.axis_size("dp")
    tok_rows = tokens.shape[0]
    feats = w_gate.shape[1]
    capacity = tok_rows // 2
    chips = groups // 2
    count = chips
    assert groups == 2 * experts and tokens.shape[1] == 2 * feats
    inv_root = 1.0 / math.sqrt(tok_rows * groups)
    expert = lax.axis_index("expert").astype(jnp.int32)
    block = lax.axis_index("dp").astype(jnp.int32)
    chip, core = block // 2, block % 2
    along = jnp.where(core == 0, chip, chips - 1 - chip)
    w_gate, w_up, w_down = w_gate[0], w_up[0], w_down[0]
    ids, weights = expert_ids.T, route_weights.T

    rows, hot = dispatch_rows(ids, weights, tokens, grad_out, experts)
    rows = lax.all_to_all(rows, "expert", split_axis=0, concat_axis=0, tiled=True)
    rows = rows.reshape(groups, 2 * capacity, feats)
    rows = lax.all_to_all(rows, "dp", split_axis=0, concat_axis=0, tiled=True)
    rows = rows.reshape(groups, 2, capacity, feats)

    swap = [(j, j ^ 1) for j in range(groups)]
    up = [2 * z for z in range(chips)]
    circle = up + [j + 1 for j in reversed(up)]
    ring = list(zip(circle, circle[1:] + circle[:1]))
    mixed = block ^ (2 * expert)
    scalars = [along, (expert + experts * core) ^ (2 * chip), mixed % experts, mixed // experts]
    scalars += [(d ^ 1 ^ core) * count + k for k in range(count) for d in range(2)]
    scalars += [(1 - core) * count + (i - (chips - 1 - along)) % count for i in range(count)]
    scalars += [core * count + (i - along) % count for i in range(count)]
    scalars = jnp.stack(scalars).astype(jnp.int32)

    sums = []
    ahead = count // 2
    for begin, size in ((0, ahead), (ahead, count - ahead)):
        other, mine, *x_t = forward_chunks(
            scalars, rows, w_gate, w_up, w_down, begin, size, count, begin > 0
        )
        sib = lax.ppermute(other, "dp", swap)
        sums += [((mine, i), (sib, i)) for i in range(size)]
    (x_t,) = x_t

    slots = 2 * count + chips - 2
    first_back = chips - 1 + count
    recv, chunks = [], []
    grads, acc = None, None
    both = (w_gate, w_up)

    def gather(k, token):
        mine = choose(token, [r for n in range(chips) for r in recv[n - 1 + count + k]])
        chunks.append((mine, lax.ppermute(mine, "dp", swap)))

    def after(value, *things):
        return lax.optimization_barrier((value, *things))[0]

    token = scalars
    for s in range(slots):
        came = []
        k = s - first_back - 1
        for part in range(PARTS):
            if s < first_back:
                before = recv[s - 1][part] if s else None
                send = hop(scalars, s, count, chips, before, sums[s % count], part)
            else:
                send = recv[s - 1][part]
                if part == 1 and k >= 0:
                    placed = after(scalars, recv[s - 1][0])
                    grads, token = gradients(
                        placed, k, count, inv_root, x_t, rows, chunks[k], grads
                    )
                    send = after(send, token)
            came.append(lax.ppermute(send, "dp", ring))
        recv.append(came)
        if s >= first_back:
            gather(s - first_back, token)

    early = len(chunks)
    units = [message for chunk in chunks[: early - 1] for message in chunk]
    acc, token = sum_rows(token, 0, units, both, None)
    grads, token = gradients(
        token, early - 1, count, inv_root, x_t, rows, chunks[early - 1], grads
    )
    for k in range(early, count):
        gather(k, token)
    units = [message for chunk in chunks for message in chunk][2 * (early - 1) :]
    acc, _ = sum_rows(scalars, 2 * (early - 1), units[:-1], both, acc)
    pieces = last_rows(scalars, 2 * count - 1, units[-1], both, acc, groups)
    returned = []
    for r, piece in enumerate(pieces):
        pairs = []
        for q in range(experts):
            for b in range(groups):
                h, e = divmod(b ^ r ^ (2 * q), experts)
                pairs.append((e * groups + 2 * q + h, q * groups + b))
        returned.append(lax.ppermute(piece, ("expert", "dp"), pairs))
    for k in range(early, count):
        grads, _ = gradients(scalars, k, count, inv_root, x_t, rows, chunks[k], grads)
    grad_tokens = combine_rows(scalars, hot, returned, experts)
    return (grad_tokens, grads[0][None], grads[1][None], grads[2][None])


def solution(mesh):
    in_specs = (
        P("dp", "expert"),
        P("dp", "expert"),
        P("dp", None),
        P("dp", None),
        P("expert", "dp", None),
        P("expert", "dp", None),
        P("expert", None, "dp"),
    )
    out_specs = (
        P("dp", "expert"),
        P("expert", "dp", None),
        P("expert", "dp", None),
        P("expert", None, "dp"),
    )
    return jax.shard_map(body, mesh=mesh, in_specs=in_specs, out_specs=out_specs, check_vma=False)
```

```python
import functools
import math

import jax
import jax.numpy as jnp
from jax import lax
from jax.experimental import pallas as pl
from jax.experimental.pallas import tpu as pltpu
from jax.sharding import PartitionSpec as P

F32 = jnp.float32
BF16 = jnp.bfloat16
LAST_DIMS = (((1,), (1,)), ((), ()))
ROWS_FIRST = (((0,), (0,)), ((), ()))
FIXED = 5
PARTS = 2
PARAMS = pltpu.CompilerParams(vmem_limit_bytes=48 * 1024 * 1024)


def dot(a, b, dims=None):
    if dims is None:
        return jnp.dot(a, b, preferred_element_type=F32)
    return lax.dot_general(a, b, dims, preferred_element_type=F32)


def cost():
    return pl.CostEstimate(flops=1024, bytes_accessed=1024, transcendentals=0)


def in_hbm(*arrays):
    return [pltpu.with_memory_space_constraint(a, pltpu.HBM) for a in arrays]


def pass_on(scalar_ref, out_ref):
    for n in range(out_ref.shape[0]):
        out_ref[n] = scalar_ref[n]


def slot_one_hot(ids_ref, experts, capacity):
    tokens = ids_ref.shape[1]
    first, second = ids_ref[0:1, :], ids_ref[1:2, :]
    expert = lax.broadcasted_iota(jnp.int32, (8 * (-(-experts // 8)), tokens), 0)
    chosen = (first == expert) | (second == expert)
    before = lax.broadcasted_iota(jnp.int32, (tokens, tokens), 0) < lax.broadcasted_iota(
        jnp.int32, (tokens, tokens), 1
    )
    place = dot(chosen.astype(F32).astype(BF16), before.astype(F32).astype(BF16))
    place = jnp.where(chosen, place, -1.0).astype(jnp.int32)
    slot = lax.broadcasted_iota(jnp.int32, (capacity, tokens), 0)
    return [slot == place[e : e + 1, :] for e in range(experts)]


def dispatch_kernel(experts, weighted, scalar_ref, ids_hbm, weights_hbm, rows_hbm, *refs):
    *messages, hot_ref, token_ref, ids_ref, weights_ref, rows_ref, scale_ref, sems = refs
    _, capacity, feats = messages[0].shape
    pass_on(scalar_ref, token_ref)
    pairs = [(ids_hbm, ids_ref), (weights_hbm, weights_ref)]
    for h in range(2):
        whole = len(rows_hbm.shape) == 3
        half = rows_hbm.at[h] if whole else rows_hbm.at[:, pl.ds(h * feats, feats)]
        pairs.append((half, rows_ref.at[h]))
    copies = [pltpu.make_async_copy(a, b, sems.at[n]) for n, (a, b) in enumerate(pairs)]
    for copy in copies:
        copy.start()
    copies[0].wait()
    copies[1].wait()
    for e, hit in enumerate(slot_one_hot(ids_ref, experts, capacity)):
        place = slice(e * capacity, (e + 1) * capacity)
        hot_ref[place, :] = hit.astype(F32).astype(BF16)
        if weighted:
            weight = jnp.where(ids_ref[0:1, :] == e, weights_ref[0:1, :], weights_ref[1:2, :])
            weight = jnp.sum(jnp.where(hit, weight, 0.0), axis=1, keepdims=True)
            scale_ref[place, :] = jnp.broadcast_to(weight, (capacity, scale_ref.shape[1]))
    places = [
        pl.ds(pl.multiple_of((scalar_ref[4] ^ t) * capacity, capacity), capacity)
        for t in range(experts)
    ]
    hot = jnp.concatenate([hot_ref[place, :] for place in places], axis=0)
    for h in range(2):
        copies[2 + h].wait()
        out = dot(hot, rows_ref[h])
        for t, place in enumerate(places):
            part = out[t * capacity : (t + 1) * capacity]
            if weighted:
                part = part * scale_ref[place, 0:1]
            messages[t][h] = part.astype(BF16)


def dispatch_rows(scalars, ids, weights, rows, experts, weighted):
    tokens, feats = rows.shape[0], rows.shape[1] // 2
    capacity = tokens // 2
    if feats % 128:
        rows = rows.reshape(tokens, 2, feats).transpose(1, 0, 2)
    *messages, hot, token = pl.pallas_call(
        functools.partial(dispatch_kernel, experts, weighted),
        out_shape=[jax.ShapeDtypeStruct((2, capacity, feats), BF16)] * experts
        + [
            jax.ShapeDtypeStruct((experts * capacity, tokens), BF16),
            jax.ShapeDtypeStruct(scalars.shape, jnp.int32),
        ],
        in_specs=[pl.BlockSpec(memory_space=pltpu.SMEM)]
        + [pl.BlockSpec(memory_space=pltpu.HBM)] * 3,
        out_specs=[pl.BlockSpec(memory_space=pltpu.VMEM)] * (experts + 1)
        + [pl.BlockSpec(memory_space=pltpu.SMEM)],
        scratch_shapes=[
            pltpu.VMEM((2, tokens), jnp.int32),
            pltpu.VMEM((2, tokens), F32),
            pltpu.VMEM((2, tokens, feats), BF16),
            pltpu.VMEM((experts * capacity, 128), F32),
            pltpu.SemaphoreType.DMA((4,)),
        ],
        compiler_params=PARAMS,
        cost_estimate=cost(),
    )(scalars, *in_hbm(ids, weights, rows))
    return messages, hot, token


def assemble_kernel(scalar_ref, *refs):
    *messages, out_ref, sems = refs

    def copy(t, message):
        return pltpu.make_async_copy(message, out_ref.at[t ^ scalar_ref[4]], sems.at[t])

    for t, message in enumerate(messages):
        copy(t, message).start()
    for t, message in enumerate(messages):
        copy(t, message).wait()


def assemble(scalars, messages):
    return pl.pallas_call(
        assemble_kernel,
        out_shape=jax.ShapeDtypeStruct((len(messages), *messages[0].shape), BF16),
        in_specs=[pl.BlockSpec(memory_space=pltpu.SMEM)]
        + [pl.BlockSpec(memory_space=pl.ANY)] * len(messages),
        scratch_shapes=[pltpu.SemaphoreType.DMA((len(messages),))],
        compiler_params=PARAMS,
        cost_estimate=cost(),
    )(scalars, *messages)


def combine_kernel(experts, scalar_ref, hot_ref, *refs):
    pieces, (out_ref, rows_ref, sems) = refs[:-3], refs[-3:]
    capacity = pieces[0].shape[0]
    at = pl.program_id(0)

    def copy(n):
        return pltpu.make_async_copy(
            pieces[n], rows_ref.at[pl.ds(n * capacity, capacity)], sems.at[n]
        )

    @pl.when(at == 0)
    def _():
        for n in range(len(pieces)):
            copy(n).start()

    hot = jnp.concatenate(
        [
            hot_ref[pl.ds(pl.multiple_of((scalar_ref[2] ^ n) * capacity, capacity), capacity), :]
            for n in range(experts)
        ],
        axis=0,
    )
    for half in range(2):

        @pl.when(at == half)
        def _():
            for n in range(half * experts, (half + 1) * experts):
                copy(n).wait()
            rows = rows_ref[half * experts * capacity : (half + 1) * experts * capacity, :]
            out = dot(hot, rows, ROWS_FIRST).astype(BF16)
            out_ref[...] = out.reshape(out_ref.shape)


def combine_rows(scalars, hot, pieces, experts):
    tokens = hot.shape[1]
    capacity, feats = pieces[0].shape
    if feats % 128:
        out_shape = jax.ShapeDtypeStruct((2, tokens, feats), BF16)
        out_spec = pl.BlockSpec((1, tokens, feats), lambda a, c: (a ^ c[3], 0, 0))
    else:
        out_shape = jax.ShapeDtypeStruct((tokens, 2 * feats), BF16)
        out_spec = pl.BlockSpec((tokens, feats), lambda a, c: (0, a ^ c[3]))
    out = pl.pallas_call(
        functools.partial(combine_kernel, experts),
        out_shape=out_shape,
        grid_spec=pltpu.PrefetchScalarGridSpec(
            num_scalar_prefetch=1,
            grid=(2,),
            in_specs=[pl.BlockSpec((experts * capacity, tokens), lambda a, c: (0, 0))]
            + [pl.BlockSpec(memory_space=pltpu.HBM)] * len(pieces),
            out_specs=out_spec,
            scratch_shapes=[
                pltpu.VMEM((len(pieces) * capacity, feats), BF16),
                pltpu.SemaphoreType.DMA((len(pieces),)),
            ],
        ),
        compiler_params=PARAMS,
        cost_estimate=cost(),
    )(scalars, hot, *in_hbm(*pieces))
    if feats % 128:
        out = out.transpose(1, 0, 2).reshape(tokens, 2 * feats)
    return out


def gate_up_kernel(scalar_ref, x_ref, wg_ref, wu_ref, *outs):
    width = wg_ref.shape[1]

    @pl.when((pl.program_id(0) == 0) & (pl.program_id(1) == 0))
    def _():
        outs[2][...] = x_ref[...].T

    for own in range(2):

        @pl.when(pl.program_id(1) == own)
        def _():
            outs[own][0, :, :width] = dot(x_ref[...], wg_ref[...]).astype(BF16)
            outs[own][0, :, width:] = dot(x_ref[...], wu_ref[...]).astype(BF16)


def gate_up(scalars, x, w_gate, w_up, count):
    slots, feats = x.shape
    width = w_gate.shape[1] // (2 * count)
    out = jax.ShapeDtypeStruct((count, slots, 2 * width), BF16)
    out_spec = pl.BlockSpec((1, slots, 2 * width), lambda i, own, c: (i, 0, 0))
    column = pl.BlockSpec(
        (feats, width), lambda i, own, c: (0, c[FIXED + 2 * count + own * count + i])
    )
    return pl.pallas_call(
        gate_up_kernel,
        out_shape=(out, out, jax.ShapeDtypeStruct((feats, slots), BF16)),
        grid_spec=pltpu.PrefetchScalarGridSpec(
            num_scalar_prefetch=1,
            grid=(count, 2),
            in_specs=[pl.BlockSpec((slots, feats), lambda i, own, c: (0, 0)), column, column],
            out_specs=(
                out_spec,
                out_spec,
                pl.BlockSpec((feats, slots), lambda i, own, c: (0, 0)),
            ),
        ),
        compiler_params=PARAMS,
        cost_estimate=cost(),
    )(scalars, x, *in_hbm(w_gate, w_up))


def back_kernel(scalar_ref, g_ref, wd_ref, *outs):
    for own in range(2):

        @pl.when(pl.program_id(1) == own)
        def _():
            outs[own][0] = dot(g_ref[...], wd_ref[...], LAST_DIMS).astype(BF16)


def back_rows(scalars, g, w_down, begin, size, count):
    slots, feats = g.shape
    width = w_down.shape[0] // (2 * count)
    out = jax.ShapeDtypeStruct((size, slots, width), BF16)
    out_spec = pl.BlockSpec((1, slots, width), lambda i, own, c: (i, 0, 0))
    row = pl.BlockSpec(
        (width, feats), lambda i, own, c: (c[FIXED + 2 * count + own * count + begin + i], 0)
    )
    return pl.pallas_call(
        back_kernel,
        out_shape=(out, out),
        grid_spec=pltpu.PrefetchScalarGridSpec(
            num_scalar_prefetch=1,
            grid=(size, 2),
            in_specs=[pl.BlockSpec((slots, feats), lambda i, own, c: (0, 0)), row],
            out_specs=(out_spec, out_spec),
        ),
        compiler_params=PARAMS,
        cost_estimate=cost(),
    )(scalars, g, *in_hbm(w_down))


def activate(gate, upper, back):
    sig = jax.nn.sigmoid(gate)
    gated = gate * sig
    return (
        (gated * upper).astype(BF16),
        (back * upper * sig * (1.0 + gate * (1.0 - sig))).astype(BF16),
        (back * gated).astype(BF16),
    )


def hop_kernel(plan, scalar_ref, *refs):
    slot, count, chips, came = plan
    own_gu, sib_gu, own_b, sib_b = refs[-5:-1]
    recv_ref = refs[0] if came else None
    send_ref = refs[-1]
    at = scalar_ref[0]
    width = send_ref.shape[1] // 3
    summing = (at <= slot) & (slot - at < count)

    def total(part):
        columns = slice(part * width, (part + 1) * width)
        if part < 2:
            value = own_gu[0, :, columns].astype(F32) + sib_gu[0, :, columns].astype(F32)
        else:
            value = own_b[0].astype(F32) + sib_b[0].astype(F32)
        if came:
            value += jnp.where(at > 0, recv_ref[:, columns].astype(F32), 0.0)
        return value

    @pl.when(summing & (at < chips - 1))
    def _():
        for part in range(3):
            send_ref[:, part * width : (part + 1) * width] = total(part).astype(BF16)

    @pl.when(summing & (at == chips - 1))
    def _():
        for part, value in enumerate(activate(total(0), total(1), total(2))):
            send_ref[:, part * width : (part + 1) * width] = value

    if came:

        @pl.when(jnp.logical_not(summing))
        def _():
            send_ref[...] = recv_ref[...]


def hop(scalars, slot, count, chips, recv, sums, part):
    rows = sums[0][0].shape[1] // PARTS
    cols = sums[0][0].shape[2] + sums[2][0].shape[2]
    message = pl.BlockSpec((rows, cols), lambda n, c: (0, 0))
    operands, in_specs = [], []
    if recv is not None:
        operands.append(recv)
        in_specs.append(message)
    for array, i in sums:
        operands.append(array)
        in_specs.append(
            pl.BlockSpec((1, rows, array.shape[2]), lambda n, c, i=i: (i, part, 0))
        )
    plan = (slot, count, chips, recv is not None)
    return pl.pallas_call(
        functools.partial(hop_kernel, plan),
        out_shape=jax.ShapeDtypeStruct((rows, cols), BF16),
        grid_spec=pltpu.PrefetchScalarGridSpec(
            num_scalar_prefetch=1,
            grid=(1,),
            in_specs=in_specs,
            out_specs=message,
        ),
        compiler_params=PARAMS,
        cost_estimate=cost(),
    )(scalars, *operands)


def choose_kernel(scalar_ref, *refs):
    *candidates, out_ref, sems = refs
    rows = candidates[0].shape[0]

    def copy(n, part):
        return pltpu.make_async_copy(
            candidates[n * PARTS + part], out_ref.at[pl.ds(part * rows, rows)], sems.at[part]
        )

    for n in range(len(candidates) // PARTS):

        @pl.when(scalar_ref[0] == n)
        def _():
            for part in range(PARTS):
                copy(n, part).start()

    for part in range(PARTS):
        copy(0, part).wait()


def choose(scalars, candidates):
    rows, cols = candidates[0].shape
    return pl.pallas_call(
        choose_kernel,
        out_shape=jax.ShapeDtypeStruct((rows * PARTS, cols), BF16),
        in_specs=[pl.BlockSpec(memory_space=pltpu.SMEM)]
        + [pl.BlockSpec(memory_space=pl.ANY)] * len(candidates),
        scratch_shapes=[pltpu.SemaphoreType.DMA((PARTS,))],
        compiler_params=PARAMS,
        cost_estimate=cost(),
    )(scalars, *candidates)


def gradients_kernel(scale, first, scalar_ref, xt_ref, g_ref, *refs):
    messages, refs = refs[:2], refs[2 if first else 5 :]
    gg_ref, gu_ref, gd_ref, token_ref = refs
    width = gg_ref.shape[1]
    pass_on(scalar_ref, token_ref)
    for u in range(2):

        @pl.when(pl.program_id(0) == u)
        def _():
            both = dot(xt_ref[...], messages[u][:, width:]) * scale
            gg_ref[...] = both[:, :width].astype(BF16)
            gu_ref[...] = both[:, width:].astype(BF16)
            scaled = messages[u][:, :width]
            gd_ref[...] = (dot(scaled, g_ref[...], ROWS_FIRST) * scale).astype(BF16)


def gradients(scalars, index, count, scale, x_t, g, messages, grads):
    slots, feats = g.shape
    width = messages[0].shape[1] // 3
    hidden = 2 * count * width
    message = pl.BlockSpec((slots, 3 * width), lambda d, c: (0, 0))

    def at(d, c):
        return c[FIXED + 2 * index + d]

    column = pl.BlockSpec((feats, width), lambda d, c: (0, at(d, c)))
    in_specs = [
        pl.BlockSpec((feats, slots), lambda d, c: (0, 0)),
        pl.BlockSpec((slots, feats), lambda d, c: (0, 0)),
        message,
        message,
    ]
    operands = [x_t, g, *messages]
    aliases = {}
    if grads is not None:
        aliases = {len(operands) + 1 + n: n for n in range(3)}
        operands += grads
        in_specs += [pl.BlockSpec(memory_space=pl.ANY)] * 3
    *grads, token = pl.pallas_call(
        functools.partial(gradients_kernel, scale, grads is None),
        out_shape=[
            jax.ShapeDtypeStruct((feats, hidden), BF16),
            jax.ShapeDtypeStruct((feats, hidden), BF16),
            jax.ShapeDtypeStruct((hidden, feats), BF16),
            jax.ShapeDtypeStruct(scalars.shape, jnp.int32),
        ],
        grid_spec=pltpu.PrefetchScalarGridSpec(
            num_scalar_prefetch=1,
            grid=(2,),
            in_specs=in_specs,
            out_specs=[
                column,
                column,
                pl.BlockSpec((width, feats), lambda d, c: (at(d, c), 0)),
                pl.BlockSpec(memory_space=pltpu.SMEM),
            ],
        ),
        input_output_aliases=aliases,
        compiler_params=PARAMS,
        cost_estimate=cost(),
    )(scalars, *operands)
    return grads, token


def sum_rows_kernel(units, first, scalar_ref, *refs):
    messages, (wg_ref, wu_ref, *refs) = refs[:units], refs[units:]
    acc_in = None if first else refs[0]
    out_ref, token_ref, acc = refs[-3:]
    width = wg_ref.shape[1]
    pass_on(scalar_ref, token_ref)
    for u in range(units):

        @pl.when(pl.program_id(0) == u)
        def _():
            both = jnp.concatenate([wg_ref[...], wu_ref[...]], axis=1)
            part = dot(messages[u][:, width:], both, LAST_DIMS)
            if u or not first:
                part += (acc if u else acc_in)[...]
            (acc if u < units - 1 else out_ref)[...] = part


def sum_rows(scalars, begin, messages, weights, acc):
    slots, width = messages[0].shape[0], messages[0].shape[1] // 3
    feats = weights[0].shape[0]
    units = len(messages)
    column = pl.BlockSpec((feats, width), lambda u, c: (0, c[FIXED + begin + u]))
    whole = pl.BlockSpec((slots, feats), lambda u, c: (0, 0))
    first = acc is None
    return pl.pallas_call(
        functools.partial(sum_rows_kernel, units, first),
        out_shape=(
            jax.ShapeDtypeStruct((slots, feats), F32),
            jax.ShapeDtypeStruct(scalars.shape, jnp.int32),
        ),
        grid_spec=pltpu.PrefetchScalarGridSpec(
            num_scalar_prefetch=1,
            grid=(units,),
            in_specs=[pl.BlockSpec((slots, 3 * width), lambda u, c: (0, 0))] * units
            + [column, column]
            + ([] if first else [whole]),
            out_specs=(whole, pl.BlockSpec(memory_space=pltpu.SMEM)),
            scratch_shapes=[pltpu.VMEM((slots, feats), F32)],
        ),
        compiler_params=PARAMS,
        cost_estimate=cost(),
    )(scalars, *messages, *in_hbm(*weights), *([] if first else [acc]))


def last_rows_kernel(scalar_ref, message_ref, wg_ref, wu_ref, acc_in, *refs):
    *pieces, acc = refs
    width = wg_ref.shape[1]
    both = jnp.concatenate([wg_ref[...], wu_ref[...]], axis=1)
    part = dot(message_ref[:, width:], both, LAST_DIMS)
    acc[...] = acc_in[...] + part
    size, each = pieces[0].shape[0], len(pieces) // 2
    for half in range(2):

        @pl.when(pl.program_id(0) == half)
        def _():
            for n in range(each):
                start = pl.multiple_of(((scalar_ref[1] % each) ^ n) * size, size)
                pieces[half * each + n][...] = acc[pl.ds(start, size), :].astype(BF16)


def last_rows(scalars, unit, message, weights, acc, groups):
    slots, feats = acc.shape
    width = message.shape[1] // 3
    size = slots // groups
    column = pl.BlockSpec((feats, width), lambda u, c: (0, c[FIXED + unit]))

    def rows(half, c):
        return ((c[1] // (groups // 2)) ^ half, 0)

    return pl.pallas_call(
        last_rows_kernel,
        out_shape=[jax.ShapeDtypeStruct((size, feats), BF16)] * groups,
        grid_spec=pltpu.PrefetchScalarGridSpec(
            num_scalar_prefetch=1,
            grid=(2,),
            in_specs=[
                pl.BlockSpec((slots // 2, 3 * width), rows),
                column,
                column,
                pl.BlockSpec((slots // 2, feats), rows),
            ],
            out_specs=[pl.BlockSpec((size, feats), lambda u, c: (0, 0))] * groups,
            scratch_shapes=[pltpu.VMEM((slots // 2, feats), F32)],
        ),
        compiler_params=PARAMS,
        cost_estimate=cost(),
    )(scalars, message, *in_hbm(*weights), acc)


def body(tokens, grad_out, expert_ids, route_weights, w_gate, w_up, w_down):
    experts = lax.axis_size("expert")
    groups = lax.axis_size("dp")
    tok_rows = tokens.shape[0]
    feats = w_gate.shape[1]
    capacity = tok_rows // 2
    chips = groups // 2
    count = chips
    assert groups == 2 * experts and tokens.shape[1] == 2 * feats
    inv_root = 1.0 / math.sqrt(tok_rows * groups)
    expert = lax.axis_index("expert").astype(jnp.int32)
    block = lax.axis_index("dp").astype(jnp.int32)
    chip, core = block // 2, block % 2
    along = jnp.where(core == 0, chip, chips - 1 - chip)
    w_gate, w_up, w_down = w_gate[0], w_up[0], w_down[0]
    ids, weights = expert_ids.T, route_weights.T

    swap = [(j, j ^ 1) for j in range(groups)]
    up = [2 * z for z in range(chips)]
    circle = up + [j + 1 for j in reversed(up)]
    ring = list(zip(circle, circle[1:] + circle[:1]))

    mixed = block ^ (2 * expert)
    scalars = [along, (expert + experts * core) ^ (2 * chip), mixed % experts, mixed // experts]
    scalars.append(expert)
    scalars += [(d ^ 1 ^ core) * count + k for k in range(count) for d in range(2)]
    scalars += [(1 - core) * count + (i - (chips - 1 - along)) % count for i in range(count)]
    scalars += [core * count + (i - along) % count for i in range(count)]
    scalars = jnp.stack(scalars).astype(jnp.int32)

    def exchange(messages):
        came = [messages[0]]
        for t in range(1, experts):
            came.append(lax.ppermute(messages[t], "expert", [(q, q ^ t) for q in range(experts)]))
        blocks = assemble(scalars, came).reshape(groups, capacity, feats)
        blocks = lax.all_to_all(blocks, "dp", split_axis=0, concat_axis=0, tiled=True)
        return blocks.reshape(groups * capacity, feats)

    x_messages, hot, token = dispatch_rows(scalars, ids, weights, tokens, experts, False)
    g_messages, _, _ = dispatch_rows(token, ids, weights, grad_out, experts, True)
    x = exchange(x_messages)
    g = exchange(g_messages)

    other_gu, own_gu, x_t = gate_up(scalars, x, w_gate, w_up, count)
    sib_gu = lax.ppermute(other_gu, "dp", swap)
    sums = []
    ahead = count // 2
    for begin, size in ((0, ahead), (ahead, count - ahead)):
        other_b, own_b = back_rows(scalars, g, w_down, begin, size, count)
        sib_b = lax.ppermute(other_b, "dp", swap)
        sums += [
            ((own_gu, begin + i), (sib_gu, begin + i), (own_b, i), (sib_b, i)) for i in range(size)
        ]

    slots = 2 * count + chips - 2
    first_back = chips - 1 + count
    recv, chunks = [], []
    grads, acc = None, None
    both = (w_gate, w_up)

    def gather(k, token):
        mine = choose(token, [r for n in range(chips) for r in recv[n - 1 + count + k]])
        chunks.append((mine, lax.ppermute(mine, "dp", swap)))

    def after(value, *things):
        return lax.optimization_barrier((value, *things))[0]

    def after(value, *things):
        return lax.optimization_barrier((value, *things))[0]

    token = scalars
    for s in range(slots):
        came = []
        k = s - first_back - 1
        for part in range(PARTS):
            if s < first_back:
                before = recv[s - 1][part] if s else None
                send = hop(scalars, s, count, chips, before, sums[s % count], part)
            else:
                send = recv[s - 1][part]
                if part == 1 and k >= 0:
                    placed = after(token, recv[s - 1][1])
                    grads, token = gradients(placed, k, count, inv_root, x_t, g, chunks[k], grads)
                    send = after(send, token)
            came.append(lax.ppermute(send, "dp", ring))
        recv.append(came)
        if s >= first_back:
            gather(s - first_back, after(token, came[0]))

    early = len(chunks)
    units = [message for chunk in chunks[: early - 1] for message in chunk]
    acc, token = sum_rows(after(token, recv[-1][0]), 0, units, both, None)
    grads, token = gradients(
        token, early - 1, count, inv_root, x_t, g, chunks[early - 1], grads
    )
    for k in range(early, count):
        gather(k, token)
    units = [message for chunk in chunks for message in chunk][2 * (early - 1) :]
    acc, _ = sum_rows(scalars, 2 * (early - 1), units[:-1], both, acc)
    pieces = last_rows(scalars, 2 * count - 1, units[-1], both, acc, groups)
    returned = []
    for r, piece in enumerate(pieces):
        pairs = []
        for q in range(experts):
            for b in range(groups):
                h, e = divmod(b ^ r ^ (2 * q), experts)
                pairs.append((e * groups + 2 * q + h, q * groups + b))
        returned.append(lax.ppermute(piece, ("expert", "dp"), pairs))
    for k in range(early, count):
        grads, _ = gradients(scalars, k, count, inv_root, x_t, g, chunks[k], grads)
    grad_tokens = combine_rows(scalars, hot, returned, experts)
    return (grad_tokens, grads[0][None], grads[1][None], grads[2][None])


def solution(mesh):
    in_specs = (
        P("dp", "expert"),
        P("dp", "expert"),
        P("dp", None),
        P("dp", None),
        P("expert", "dp", None),
        P("expert", "dp", None),
        P("expert", None, "dp"),
    )
    out_specs = (
        P("dp", "expert"),
        P("expert", "dp", None),
        P("expert", "dp", None),
        P("expert", None, "dp"),
    )
    return jax.shard_map(body, mesh=mesh, in_specs=in_specs, out_specs=out_specs, check_vma=False)
```

```python
import functools
import math

import jax
import jax.numpy as jnp
from jax import lax
from jax.experimental import pallas as pl
from jax.experimental.pallas import tpu as pltpu
from jax.sharding import PartitionSpec as P

F32 = jnp.float32
BF16 = jnp.bfloat16
LAST_DIMS = (((1,), (1,)), ((), ()))
ROWS_FIRST = (((0,), (0,)), ((), ()))
FIXED = 5
PARTS = 2
PARAMS = pltpu.CompilerParams(vmem_limit_bytes=28 * 1024 * 1024)


def dot(a, b, dims=None):
    if dims is None:
        return jnp.dot(a, b, preferred_element_type=F32)
    return lax.dot_general(a, b, dims, preferred_element_type=F32)


def cost():
    return pl.CostEstimate(flops=1024, bytes_accessed=1024, transcendentals=0)


def in_hbm(*arrays):
    return [pltpu.with_memory_space_constraint(a, pltpu.HBM) for a in arrays]


def pass_on(scalar_ref, out_ref):
    for n in range(out_ref.shape[0]):
        out_ref[n] = scalar_ref[n]


def slot_one_hot(ids_ref, experts, capacity):
    tokens = ids_ref.shape[1]
    first, second = ids_ref[0:1, :], ids_ref[1:2, :]
    expert = lax.broadcasted_iota(jnp.int32, (8 * (-(-experts // 8)), tokens), 0)
    chosen = (first == expert) | (second == expert)
    before = lax.broadcasted_iota(jnp.int32, (tokens, tokens), 0) < lax.broadcasted_iota(
        jnp.int32, (tokens, tokens), 1
    )
    place = dot(chosen.astype(F32).astype(BF16), before.astype(F32).astype(BF16))
    place = jnp.where(chosen, place, -1.0).astype(jnp.int32)
    slot = lax.broadcasted_iota(jnp.int32, (capacity, tokens), 0)
    return [slot == place[e : e + 1, :] for e in range(experts)]


def dispatch_kernel(experts, weighted, scalar_ref, ids_hbm, weights_hbm, rows_hbm, *refs):
    *messages, hot_ref, token_ref, ids_ref, weights_ref, rows_ref, scale_ref, sems = refs
    _, capacity, feats = messages[0].shape
    pass_on(scalar_ref, token_ref)
    pairs = [(ids_hbm, ids_ref), (weights_hbm, weights_ref)]
    for h in range(2):
        whole = len(rows_hbm.shape) == 3
        half = rows_hbm.at[h] if whole else rows_hbm.at[:, pl.ds(h * feats, feats)]
        pairs.append((half, rows_ref.at[h]))
    copies = [pltpu.make_async_copy(a, b, sems.at[n]) for n, (a, b) in enumerate(pairs)]
    for copy in copies:
        copy.start()
    copies[0].wait()
    copies[1].wait()
    for e, hit in enumerate(slot_one_hot(ids_ref, experts, capacity)):
        place = slice(e * capacity, (e + 1) * capacity)
        hot_ref[place, :] = hit.astype(F32).astype(BF16)
        if weighted:
            weight = jnp.where(ids_ref[0:1, :] == e, weights_ref[0:1, :], weights_ref[1:2, :])
            weight = jnp.sum(jnp.where(hit, weight, 0.0), axis=1, keepdims=True)
            scale_ref[place, :] = jnp.broadcast_to(weight, (capacity, scale_ref.shape[1]))
    places = [
        pl.ds(pl.multiple_of((scalar_ref[4] ^ t) * capacity, capacity), capacity)
        for t in range(experts)
    ]
    hot = jnp.concatenate([hot_ref[place, :] for place in places], axis=0)
    for h in range(2):
        copies[2 + h].wait()
        out = dot(hot, rows_ref[h])
        for t, place in enumerate(places):
            part = out[t * capacity : (t + 1) * capacity]
            if weighted:
                part = part * scale_ref[place, 0:1]
            messages[t][h] = part.astype(BF16)


def dispatch_rows(scalars, ids, weights, rows, experts, weighted):
    tokens, feats = rows.shape[0], rows.shape[1] // 2
    capacity = tokens // 2
    if feats % 128:
        rows = rows.reshape(tokens, 2, feats).transpose(1, 0, 2)
    *messages, hot, token = pl.pallas_call(
        functools.partial(dispatch_kernel, experts, weighted),
        out_shape=[jax.ShapeDtypeStruct((2, capacity, feats), BF16)] * experts
        + [
            jax.ShapeDtypeStruct((experts * capacity, tokens), BF16),
            jax.ShapeDtypeStruct(scalars.shape, jnp.int32),
        ],
        in_specs=[pl.BlockSpec(memory_space=pltpu.SMEM)]
        + [pl.BlockSpec(memory_space=pltpu.HBM)] * 3,
        out_specs=[pl.BlockSpec(memory_space=pltpu.VMEM)] * (experts + 1)
        + [pl.BlockSpec(memory_space=pltpu.SMEM)],
        scratch_shapes=[
            pltpu.VMEM((2, tokens), jnp.int32),
            pltpu.VMEM((2, tokens), F32),
            pltpu.VMEM((2, tokens, feats), BF16),
            pltpu.VMEM((experts * capacity, 128), F32),
            pltpu.SemaphoreType.DMA((4,)),
        ],
        compiler_params=PARAMS,
        cost_estimate=cost(),
    )(scalars, *in_hbm(ids, weights, rows))
    return messages, hot, token


def assemble_kernel(scalar_ref, *refs):
    *messages, out_ref, sems = refs

    def copy(t, message):
        return pltpu.make_async_copy(message, out_ref.at[t ^ scalar_ref[4]], sems.at[t])

    for t, message in enumerate(messages):
        copy(t, message).start()
    for t, message in enumerate(messages):
        copy(t, message).wait()


def assemble(scalars, messages):
    return pl.pallas_call(
        assemble_kernel,
        out_shape=jax.ShapeDtypeStruct((len(messages), *messages[0].shape), BF16),
        in_specs=[pl.BlockSpec(memory_space=pltpu.SMEM)]
        + [pl.BlockSpec(memory_space=pl.ANY)] * len(messages),
        scratch_shapes=[pltpu.SemaphoreType.DMA((len(messages),))],
        compiler_params=PARAMS,
        cost_estimate=cost(),
    )(scalars, *messages)


def combine_kernel(experts, scalar_ref, hot_ref, *refs):
    pieces, (out_ref, rows_ref, sems) = refs[:-3], refs[-3:]
    capacity = pieces[0].shape[0]
    at = pl.program_id(0)

    def copy(n):
        return pltpu.make_async_copy(
            pieces[n], rows_ref.at[pl.ds(n * capacity, capacity)], sems.at[n]
        )

    @pl.when(at == 0)
    def _():
        for n in range(len(pieces)):
            copy(n).start()

    hot = jnp.concatenate(
        [
            hot_ref[pl.ds(pl.multiple_of((scalar_ref[2] ^ n) * capacity, capacity), capacity), :]
            for n in range(experts)
        ],
        axis=0,
    )
    for half in range(2):

        @pl.when(at == half)
        def _():
            for n in range(half * experts, (half + 1) * experts):
                copy(n).wait()
            rows = rows_ref[half * experts * capacity : (half + 1) * experts * capacity, :]
            out = dot(hot, rows, ROWS_FIRST).astype(BF16)
            out_ref[...] = out.reshape(out_ref.shape)


def combine_rows(scalars, hot, pieces, experts):
    tokens = hot.shape[1]
    capacity, feats = pieces[0].shape
    if feats % 128:
        out_shape = jax.ShapeDtypeStruct((2, tokens, feats), BF16)
        out_spec = pl.BlockSpec((1, tokens, feats), lambda a, c: (a ^ c[3], 0, 0))
    else:
        out_shape = jax.ShapeDtypeStruct((tokens, 2 * feats), BF16)
        out_spec = pl.BlockSpec((tokens, feats), lambda a, c: (0, a ^ c[3]))
    out = pl.pallas_call(
        functools.partial(combine_kernel, experts),
        out_shape=out_shape,
        grid_spec=pltpu.PrefetchScalarGridSpec(
            num_scalar_prefetch=1,
            grid=(2,),
            in_specs=[pl.BlockSpec((experts * capacity, tokens), lambda a, c: (0, 0))]
            + [pl.BlockSpec(memory_space=pltpu.HBM)] * len(pieces),
            out_specs=out_spec,
            scratch_shapes=[
                pltpu.VMEM((len(pieces) * capacity, feats), BF16),
                pltpu.SemaphoreType.DMA((len(pieces),)),
            ],
        ),
        compiler_params=PARAMS,
        cost_estimate=cost(),
    )(scalars, hot, *in_hbm(*pieces))
    if feats % 128:
        out = out.transpose(1, 0, 2).reshape(tokens, 2 * feats)
    return out


def gate_up_kernel(scalar_ref, x_ref, wg_ref, wu_ref, *outs):
    width = wg_ref.shape[1]

    @pl.when((pl.program_id(0) == 0) & (pl.program_id(1) == 0))
    def _():
        outs[2][...] = x_ref[...].T

    for own in range(2):

        @pl.when(pl.program_id(1) == own)
        def _():
            outs[own][0, :, :width] = dot(x_ref[...], wg_ref[...]).astype(BF16)
            outs[own][0, :, width:] = dot(x_ref[...], wu_ref[...]).astype(BF16)


def gate_up(scalars, x, w_gate, w_up, count):
    slots, feats = x.shape
    width = w_gate.shape[1] // (2 * count)
    out = jax.ShapeDtypeStruct((count, slots, 2 * width), BF16)
    out_spec = pl.BlockSpec((1, slots, 2 * width), lambda i, own, c: (i, 0, 0))
    column = pl.BlockSpec(
        (feats, width), lambda i, own, c: (0, c[FIXED + 2 * count + own * count + i])
    )
    return pl.pallas_call(
        gate_up_kernel,
        out_shape=(out, out, jax.ShapeDtypeStruct((feats, slots), BF16)),
        grid_spec=pltpu.PrefetchScalarGridSpec(
            num_scalar_prefetch=1,
            grid=(count, 2),
            in_specs=[pl.BlockSpec((slots, feats), lambda i, own, c: (0, 0)), column, column],
            out_specs=(
                out_spec,
                out_spec,
                pl.BlockSpec((feats, slots), lambda i, own, c: (0, 0)),
            ),
        ),
        compiler_params=PARAMS,
        cost_estimate=cost(),
    )(scalars, x, *in_hbm(w_gate, w_up))


def back_kernel(scalar_ref, g_ref, wd_ref, *outs):
    pass_on(scalar_ref, outs[2])
    for own in range(2):

        @pl.when(pl.program_id(1) == own)
        def _():
            outs[own][0] = dot(g_ref[...], wd_ref[...], LAST_DIMS).astype(BF16)


def back_rows(scalars, g, w_down, begin, size, count):
    slots, feats = g.shape
    width = w_down.shape[0] // (2 * count)
    out = jax.ShapeDtypeStruct((size, slots, width), BF16)
    out_spec = pl.BlockSpec((1, slots, width), lambda i, own, c: (i, 0, 0))
    row = pl.BlockSpec(
        (width, feats), lambda i, own, c: (c[FIXED + 2 * count + own * count + begin + i], 0)
    )
    return pl.pallas_call(
        back_kernel,
        out_shape=(out, out, jax.ShapeDtypeStruct(scalars.shape, jnp.int32)),
        grid_spec=pltpu.PrefetchScalarGridSpec(
            num_scalar_prefetch=1,
            grid=(size, 2),
            in_specs=[pl.BlockSpec((slots, feats), lambda i, own, c: (0, 0)), row],
            out_specs=(out_spec, out_spec, pl.BlockSpec(memory_space=pltpu.SMEM)),
        ),
        compiler_params=PARAMS,
        cost_estimate=cost(),
    )(scalars, g, *in_hbm(w_down))


def activate(gate, upper, back):
    sig = jax.nn.sigmoid(gate)
    gated = gate * sig
    return (
        (gated * upper).astype(BF16),
        (back * upper * sig * (1.0 + gate * (1.0 - sig))).astype(BF16),
        (back * gated).astype(BF16),
    )


def hop_kernel(plan, scalar_ref, *refs):
    slot, count, chips, came = plan
    own_gu, sib_gu, own_b, sib_b = refs[-5:-1]
    recv_ref = refs[0] if came else None
    send_ref = refs[-1]
    at = scalar_ref[0]
    width = send_ref.shape[1] // 3
    summing = (at <= slot) & (slot - at < count)

    def total(part):
        columns = slice(part * width, (part + 1) * width)
        if part < 2:
            value = own_gu[0, :, columns].astype(F32) + sib_gu[0, :, columns].astype(F32)
        else:
            value = own_b[0].astype(F32) + sib_b[0].astype(F32)
        if came:
            value += jnp.where(at > 0, recv_ref[:, columns].astype(F32), 0.0)
        return value

    @pl.when(summing & (at < chips - 1))
    def _():
        for part in range(3):
            send_ref[:, part * width : (part + 1) * width] = total(part).astype(BF16)

    @pl.when(summing & (at == chips - 1))
    def _():
        for part, value in enumerate(activate(total(0), total(1), total(2))):
            send_ref[:, part * width : (part + 1) * width] = value

    if came:

        @pl.when(jnp.logical_not(summing))
        def _():
            send_ref[...] = recv_ref[...]


def hop(scalars, slot, count, chips, recv, sums, part):
    rows = sums[0][0].shape[1] // PARTS
    cols = sums[0][0].shape[2] + sums[2][0].shape[2]
    message = pl.BlockSpec((rows, cols), lambda n, c: (0, 0))
    operands, in_specs = [], []
    if recv is not None:
        operands.append(recv)
        in_specs.append(message)
    for array, i in sums:
        operands.append(array)
        in_specs.append(
            pl.BlockSpec((1, rows, array.shape[2]), lambda n, c, i=i: (i, part, 0))
        )
    plan = (slot, count, chips, recv is not None)
    return pl.pallas_call(
        functools.partial(hop_kernel, plan),
        out_shape=jax.ShapeDtypeStruct((rows, cols), BF16),
        grid_spec=pltpu.PrefetchScalarGridSpec(
            num_scalar_prefetch=1,
            grid=(1,),
            in_specs=in_specs,
            out_specs=message,
        ),
        compiler_params=PARAMS,
        cost_estimate=cost(),
    )(scalars, *operands)


def choose_kernel(scalar_ref, *refs):
    *candidates, out_ref, sems = refs
    rows = candidates[0].shape[0]

    def copy(n, part):
        return pltpu.make_async_copy(
            candidates[n * PARTS + part], out_ref.at[pl.ds(part * rows, rows)], sems.at[part]
        )

    for n in range(len(candidates) // PARTS):

        @pl.when(scalar_ref[0] == n)
        def _():
            for part in range(PARTS):
                copy(n, part).start()

    for part in range(PARTS):
        copy(0, part).wait()


def choose(scalars, candidates):
    rows, cols = candidates[0].shape
    return pl.pallas_call(
        choose_kernel,
        out_shape=jax.ShapeDtypeStruct((rows * PARTS, cols), BF16),
        in_specs=[pl.BlockSpec(memory_space=pltpu.SMEM)]
        + [pl.BlockSpec(memory_space=pl.ANY)] * len(candidates),
        scratch_shapes=[pltpu.SemaphoreType.DMA((PARTS,))],
        compiler_params=PARAMS,
        cost_estimate=cost(),
    )(scalars, *candidates)


def gradients_kernel(units, scale, first, scalar_ref, xt_ref, g_ref, *refs):
    messages, refs = refs[:units], refs[units if first else units + 3 :]
    gg_ref, gu_ref, gd_ref, token_ref = refs
    width = gg_ref.shape[1]
    pass_on(scalar_ref, token_ref)
    for u in range(units):

        @pl.when(pl.program_id(0) == u)
        def _():
            both = dot(xt_ref[...], messages[u][:, width:]) * scale
            gg_ref[...] = both[:, :width].astype(BF16)
            gu_ref[...] = both[:, width:].astype(BF16)
            scaled = messages[u][:, :width]
            gd_ref[...] = (dot(scaled, g_ref[...], ROWS_FIRST) * scale).astype(BF16)


def gradients(scalars, begin, count, scale, x_t, g, messages, grads):
    slots, feats = g.shape
    width = messages[0].shape[1] // 3
    hidden = 2 * count * width
    units = len(messages)

    def at(u, c):
        return c[FIXED + begin + u]

    column = pl.BlockSpec((feats, width), lambda u, c: (0, at(u, c)))
    in_specs = [
        pl.BlockSpec((feats, slots), lambda u, c: (0, 0)),
        pl.BlockSpec((slots, feats), lambda u, c: (0, 0)),
    ]
    in_specs += [pl.BlockSpec((slots, 3 * width), lambda u, c: (0, 0))] * units
    operands = [x_t, g, *messages]
    aliases = {}
    if grads is not None:
        aliases = {len(operands) + 1 + n: n for n in range(3)}
        operands += grads
        in_specs += [pl.BlockSpec(memory_space=pl.ANY)] * 3
    *grads, token = pl.pallas_call(
        functools.partial(gradients_kernel, units, scale, grads is None),
        out_shape=[
            jax.ShapeDtypeStruct((feats, hidden), BF16),
            jax.ShapeDtypeStruct((feats, hidden), BF16),
            jax.ShapeDtypeStruct((hidden, feats), BF16),
            jax.ShapeDtypeStruct(scalars.shape, jnp.int32),
        ],
        grid_spec=pltpu.PrefetchScalarGridSpec(
            num_scalar_prefetch=1,
            grid=(units,),
            in_specs=in_specs,
            out_specs=[
                column,
                column,
                pl.BlockSpec((width, feats), lambda u, c: (at(u, c), 0)),
                pl.BlockSpec(memory_space=pltpu.SMEM),
            ],
        ),
        input_output_aliases=aliases,
        compiler_params=PARAMS,
        cost_estimate=cost(),
    )(scalars, *operands)
    return grads, token


def sum_rows_kernel(units, pieces, scalar_ref, *refs):
    messages, weights, refs = refs[:units], refs[units : 3 * units], refs[3 * units :]
    width = weights[0].shape[1]
    both = jnp.concatenate([message[:, width:] for message in messages], axis=1)
    part = dot(both, jnp.concatenate([w[...] for w in weights], axis=1), LAST_DIMS)
    if not pieces:
        out_ref, token_ref = refs
        out_ref[...] = part
        pass_on(scalar_ref, token_ref)
        return
    acc_in, *outs, acc = refs
    acc[...] = acc_in[...] + part
    size, each = outs[0].shape[0], pieces // 2
    for half in range(2):

        @pl.when(pl.program_id(0) == half)
        def _():
            for n in range(each):
                start = pl.multiple_of(((scalar_ref[1] % each) ^ n) * size, size)
                outs[half * each + n][...] = acc[pl.ds(start, size), :].astype(BF16)


def sum_rows(scalars, begin, messages, weights, acc, pieces):
    slots, width = messages[0].shape[0], messages[0].shape[1] // 3
    feats = weights[0].shape[0]
    units = len(messages)

    def rows(half, c):
        return ((c[1] // (pieces // 2)) ^ half if pieces else half, 0)

    in_specs = [pl.BlockSpec((slots // 2, 3 * width), rows)] * units
    operands = list(messages)
    for u in range(units):
        column = pl.BlockSpec((feats, width), lambda half, c, u=u: (0, c[FIXED + begin + u]))
        operands += in_hbm(*weights)
        in_specs += [column, column]
    whole = pl.BlockSpec((slots // 2, feats), rows)
    if pieces:
        operands.append(acc)
        in_specs.append(whole)
        out_shape = [jax.ShapeDtypeStruct((slots // pieces, feats), BF16)] * pieces
        out_specs = [pl.BlockSpec((slots // pieces, feats), lambda half, c: (0, 0))] * pieces
        scratch = [pltpu.VMEM((slots // 2, feats), F32)]
    else:
        out_shape = [
            jax.ShapeDtypeStruct((slots, feats), F32),
            jax.ShapeDtypeStruct(scalars.shape, jnp.int32),
        ]
        out_specs = [whole, pl.BlockSpec(memory_space=pltpu.SMEM)]
        scratch = []
    return pl.pallas_call(
        functools.partial(sum_rows_kernel, units, pieces),
        out_shape=out_shape,
        grid_spec=pltpu.PrefetchScalarGridSpec(
            num_scalar_prefetch=1,
            grid=(2,),
            in_specs=in_specs,
            out_specs=out_specs,
            scratch_shapes=scratch,
        ),
        compiler_params=PARAMS,
        cost_estimate=cost(),
    )(scalars, *operands)


def body(tokens, grad_out, expert_ids, route_weights, w_gate, w_up, w_down):
    experts = lax.axis_size("expert")
    groups = lax.axis_size("dp")
    tok_rows = tokens.shape[0]
    feats = w_gate.shape[1]
    capacity = tok_rows // 2
    chips = groups // 2
    count = chips
    assert groups == 2 * experts and tokens.shape[1] == 2 * feats
    inv_root = 1.0 / math.sqrt(tok_rows * groups)
    expert = lax.axis_index("expert").astype(jnp.int32)
    block = lax.axis_index("dp").astype(jnp.int32)
    chip, core = block // 2, block % 2
    along = jnp.where(core == 0, chip, chips - 1 - chip)
    w_gate, w_up, w_down = w_gate[0], w_up[0], w_down[0]
    ids, weights = expert_ids.T, route_weights.T

    swap = [(j, j ^ 1) for j in range(groups)]
    up = [2 * z for z in range(chips)]
    circle = up + [j + 1 for j in reversed(up)]
    ring = list(zip(circle, circle[1:] + circle[:1]))

    mixed = block ^ (2 * expert)
    scalars = [along, (expert + experts * core) ^ (2 * chip), mixed % experts, mixed // experts]
    scalars.append(expert)
    scalars += [(d ^ 1 ^ core) * count + k for k in range(count) for d in range(2)]
    scalars += [(1 - core) * count + (i - (chips - 1 - along)) % count for i in range(count)]
    scalars += [core * count + (i - along) % count for i in range(count)]
    scalars = jnp.stack(scalars).astype(jnp.int32)

    def exchange(messages):
        came = [messages[0]]
        for t in range(1, experts):
            came.append(lax.ppermute(messages[t], "expert", [(q, q ^ t) for q in range(experts)]))
        blocks = assemble(scalars, came).reshape(groups, capacity, feats)
        blocks = lax.all_to_all(blocks, "dp", split_axis=0, concat_axis=0, tiled=True)
        return blocks.reshape(groups * capacity, feats)

    x_messages, hot, token = dispatch_rows(scalars, ids, weights, tokens, experts, False)
    g_messages, _, _ = dispatch_rows(token, ids, weights, grad_out, experts, True)
    x = exchange(x_messages)
    g = exchange(g_messages)

    other_gu, own_gu, x_t = gate_up(scalars, x, w_gate, w_up, count)
    sib_gu = lax.ppermute(other_gu, "dp", swap)
    sums = []
    ahead = count // 2
    for begin, size in ((0, ahead), (ahead, count - ahead)):
        other_b, own_b, token = back_rows(scalars, g, w_down, begin, size, count)
        sib_b = lax.ppermute(other_b, "dp", swap)
        sums += [
            ((own_gu, begin + i), (sib_gu, begin + i), (own_b, i), (sib_b, i)) for i in range(size)
        ]

    slots = 2 * count + chips - 2
    first_back = chips - 1 + count
    recv, chunks = [], []
    grads, acc = None, None
    both = (w_gate, w_up)

    def gather(k, token):
        mine = choose(token, [r for n in range(chips) for r in recv[n - 1 + count + k]])
        chunks.append((mine, lax.ppermute(mine, "dp", swap)))

    def after(value, *things):
        return lax.optimization_barrier((value, *things))[0]

    def after(value, *things):
        return lax.optimization_barrier((value, *things))[0]

    def after(value, *things):
        return lax.optimization_barrier((value, *things))[0]

    for s in range(slots):
        came = []
        for part in range(PARTS):
            if s < first_back:
                before = recv[s - 1][part] if s else None
                send = hop(token, s, count, chips, before, sums[s % count], part)
            else:
                send = recv[s - 1][part]
            came.append(lax.ppermute(send, "dp", ring))
        recv.append(came)

    early = count - 2
    for k in range(early):
        part = 1 if k == early - 1 else 0
        gather(k, after(scalars, recv[-2][part]))
    units = [message for chunk in chunks for message in chunk]
    grads, token = gradients(
        after(scalars, recv[-2][1]), 0, count, inv_root, x_t, g, units, None
    )
    acc, token = sum_rows(after(token, recv[-1][0]), 0, units, both, None, 0)
    for k in range(early, count):
        gather(k, token)
    units = [message for chunk in chunks[early:] for message in chunk]
    pieces = sum_rows(scalars, 2 * early, units, both, acc, groups)
    returned = []
    for r, piece in enumerate(pieces):
        pairs = []
        for q in range(experts):
            for b in range(groups):
                h, e = divmod(b ^ r ^ (2 * q), experts)
                pairs.append((e * groups + 2 * q + h, q * groups + b))
        returned.append(lax.ppermute(piece, ("expert", "dp"), pairs))
    grads, _ = gradients(scalars, 2 * early, count, inv_root, x_t, g, units, grads)
    grad_tokens = combine_rows(scalars, hot, returned, experts)
    return (grad_tokens, grads[0][None], grads[1][None], grads[2][None])


def solution(mesh):
    in_specs = (
        P("dp", "expert"),
        P("dp", "expert"),
        P("dp", None),
        P("dp", None),
        P("expert", "dp", None),
        P("expert", "dp", None),
        P("expert", None, "dp"),
    )
    out_specs = (
        P("dp", "expert"),
        P("expert", "dp", None),
        P("expert", "dp", None),
        P("expert", None, "dp"),
    )
    return jax.shard_map(body, mesh=mesh, in_specs=in_specs, out_specs=out_specs, check_vma=False)
```

```python
import functools
import math

import jax
import jax.numpy as jnp
from jax import lax
from jax.experimental import pallas as pl
from jax.experimental.pallas import tpu as pltpu
from jax.sharding import PartitionSpec as P

F32 = jnp.float32
BF16 = jnp.bfloat16
LAST_DIMS = (((1,), (1,)), ((), ()))
ROWS_FIRST = (((0,), (0,)), ((), ()))
FIXED = 5
PARTS = 2
PARAMS = pltpu.CompilerParams(vmem_limit_bytes=28 * 1024 * 1024)


def dot(a, b, dims=None):
    if dims is None:
        return jnp.dot(a, b, preferred_element_type=F32)
    return lax.dot_general(a, b, dims, preferred_element_type=F32)


def cost():
    return pl.CostEstimate(flops=1024, bytes_accessed=1024, transcendentals=0)


def in_hbm(*arrays):
    return [pltpu.with_memory_space_constraint(a, pltpu.HBM) for a in arrays]


def pass_on(scalar_ref, out_ref):
    for n in range(out_ref.shape[0]):
        out_ref[n] = scalar_ref[n]


def slot_one_hot(ids_ref, experts, capacity):
    tokens = ids_ref.shape[1]
    first, second = ids_ref[0:1, :], ids_ref[1:2, :]
    expert = lax.broadcasted_iota(jnp.int32, (8 * (-(-experts // 8)), tokens), 0)
    chosen = (first == expert) | (second == expert)
    before = lax.broadcasted_iota(jnp.int32, (tokens, tokens), 0) < lax.broadcasted_iota(
        jnp.int32, (tokens, tokens), 1
    )
    place = dot(chosen.astype(F32).astype(BF16), before.astype(F32).astype(BF16))
    place = jnp.where(chosen, place, -1.0).astype(jnp.int32)
    slot = lax.broadcasted_iota(jnp.int32, (capacity, tokens), 0)
    return [slot == place[e : e + 1, :] for e in range(experts)]


def dispatch_kernel(experts, weighted, scalar_ref, ids_hbm, weights_hbm, rows_hbm, *refs):
    *messages, hot_ref, token_ref, ids_ref, weights_ref, rows_ref, scale_ref, sems = refs
    _, capacity, feats = messages[0].shape
    pass_on(scalar_ref, token_ref)
    pairs = [(ids_hbm, ids_ref), (weights_hbm, weights_ref)]
    for h in range(2):
        whole = len(rows_hbm.shape) == 3
        half = rows_hbm.at[h] if whole else rows_hbm.at[:, pl.ds(h * feats, feats)]
        pairs.append((half, rows_ref.at[h]))
    copies = [pltpu.make_async_copy(a, b, sems.at[n]) for n, (a, b) in enumerate(pairs)]
    for copy in copies:
        copy.start()
    copies[0].wait()
    copies[1].wait()
    for e, hit in enumerate(slot_one_hot(ids_ref, experts, capacity)):
        place = slice(e * capacity, (e + 1) * capacity)
        hot_ref[place, :] = hit.astype(F32).astype(BF16)
        if weighted:
            weight = jnp.where(ids_ref[0:1, :] == e, weights_ref[0:1, :], weights_ref[1:2, :])
            weight = jnp.sum(jnp.where(hit, weight, 0.0), axis=1, keepdims=True)
            scale_ref[place, :] = jnp.broadcast_to(weight, (capacity, scale_ref.shape[1]))
    places = [
        pl.ds(pl.multiple_of((scalar_ref[4] ^ t) * capacity, capacity), capacity)
        for t in range(experts)
    ]
    hot = jnp.concatenate([hot_ref[place, :] for place in places], axis=0)
    for h in range(2):
        copies[2 + h].wait()
        out = dot(hot, rows_ref[h])
        for t, place in enumerate(places):
            part = out[t * capacity : (t + 1) * capacity]
            if weighted:
                part = part * scale_ref[place, 0:1]
            messages[t][h] = part.astype(BF16)


def dispatch_rows(scalars, ids, weights, rows, experts, weighted):
    tokens, feats = rows.shape[0], rows.shape[1] // 2
    capacity = tokens // 2
    if feats % 128:
        rows = rows.reshape(tokens, 2, feats).transpose(1, 0, 2)
    *messages, hot, token = pl.pallas_call(
        functools.partial(dispatch_kernel, experts, weighted),
        out_shape=[jax.ShapeDtypeStruct((2, capacity, feats), BF16)] * experts
        + [
            jax.ShapeDtypeStruct((experts * capacity, tokens), BF16),
            jax.ShapeDtypeStruct(scalars.shape, jnp.int32),
        ],
        in_specs=[pl.BlockSpec(memory_space=pltpu.SMEM)]
        + [pl.BlockSpec(memory_space=pltpu.HBM)] * 3,
        out_specs=[pl.BlockSpec(memory_space=pltpu.VMEM)] * (experts + 1)
        + [pl.BlockSpec(memory_space=pltpu.SMEM)],
        scratch_shapes=[
            pltpu.VMEM((2, tokens), jnp.int32),
            pltpu.VMEM((2, tokens), F32),
            pltpu.VMEM((2, tokens, feats), BF16),
            pltpu.VMEM((experts * capacity, 128), F32),
            pltpu.SemaphoreType.DMA((4,)),
        ],
        compiler_params=PARAMS,
        cost_estimate=cost(),
    )(scalars, *in_hbm(ids, weights, rows))
    return messages, hot, token


def assemble_kernel(scalar_ref, *refs):
    *messages, out_ref, sems = refs

    def copy(t, message):
        return pltpu.make_async_copy(message, out_ref.at[t ^ scalar_ref[4]], sems.at[t])

    for t, message in enumerate(messages):
        copy(t, message).start()
    for t, message in enumerate(messages):
        copy(t, message).wait()


def assemble(scalars, messages):
    return pl.pallas_call(
        assemble_kernel,
        out_shape=jax.ShapeDtypeStruct((len(messages), *messages[0].shape), BF16),
        in_specs=[pl.BlockSpec(memory_space=pltpu.SMEM)]
        + [pl.BlockSpec(memory_space=pl.ANY)] * len(messages),
        scratch_shapes=[pltpu.SemaphoreType.DMA((len(messages),))],
        compiler_params=PARAMS,
        cost_estimate=cost(),
    )(scalars, *messages)


def combine_kernel(experts, scalar_ref, hot_ref, *refs):
    pieces, (out_ref, rows_ref, sems) = refs[:-3], refs[-3:]
    capacity = pieces[0].shape[0]
    at = pl.program_id(0)

    def copy(n):
        return pltpu.make_async_copy(
            pieces[n], rows_ref.at[pl.ds(n * capacity, capacity)], sems.at[n]
        )

    @pl.when(at == 0)
    def _():
        for n in range(len(pieces)):
            copy(n).start()

    hot = jnp.concatenate(
        [
            hot_ref[pl.ds(pl.multiple_of((scalar_ref[2] ^ n) * capacity, capacity), capacity), :]
            for n in range(experts)
        ],
        axis=0,
    )
    for half in range(2):

        @pl.when(at == half)
        def _():
            for n in range(half * experts, (half + 1) * experts):
                copy(n).wait()
            rows = rows_ref[half * experts * capacity : (half + 1) * experts * capacity, :]
            out = dot(hot, rows, ROWS_FIRST).astype(BF16)
            out_ref[...] = out.reshape(out_ref.shape)


def combine_rows(scalars, hot, pieces, experts):
    tokens = hot.shape[1]
    capacity, feats = pieces[0].shape
    if feats % 128:
        out_shape = jax.ShapeDtypeStruct((2, tokens, feats), BF16)
        out_spec = pl.BlockSpec((1, tokens, feats), lambda a, c: (a ^ c[3], 0, 0))
    else:
        out_shape = jax.ShapeDtypeStruct((tokens, 2 * feats), BF16)
        out_spec = pl.BlockSpec((tokens, feats), lambda a, c: (0, a ^ c[3]))
    out = pl.pallas_call(
        functools.partial(combine_kernel, experts),
        out_shape=out_shape,
        grid_spec=pltpu.PrefetchScalarGridSpec(
            num_scalar_prefetch=1,
            grid=(2,),
            in_specs=[pl.BlockSpec((experts * capacity, tokens), lambda a, c: (0, 0))]
            + [pl.BlockSpec(memory_space=pltpu.HBM)] * len(pieces),
            out_specs=out_spec,
            scratch_shapes=[
                pltpu.VMEM((len(pieces) * capacity, feats), BF16),
                pltpu.SemaphoreType.DMA((len(pieces),)),
            ],
        ),
        compiler_params=PARAMS,
        cost_estimate=cost(),
    )(scalars, hot, *in_hbm(*pieces))
    if feats % 128:
        out = out.transpose(1, 0, 2).reshape(tokens, 2 * feats)
    return out


def gate_up_kernel(own, scalar_ref, x_ref, wg_ref, wu_ref, *refs):
    width = wg_ref.shape[1]
    gate = dot(x_ref[...], wg_ref[...])
    upper = dot(x_ref[...], wu_ref[...])
    if own:
        sib_ref, out_ref = refs
        gate += sib_ref[0, :, :width].astype(F32)
        upper += sib_ref[0, :, width:].astype(F32)
    else:
        out_ref, turned_ref = refs

        @pl.when(pl.program_id(0) == 0)
        def _():
            turned_ref[...] = x_ref[...].T

    out_ref[0, :, :width] = gate.astype(BF16)
    out_ref[0, :, width:] = upper.astype(BF16)


def gate_up(scalars, x, w_gate, w_up, count, sib):
    slots, feats = x.shape
    width = w_gate.shape[1] // (2 * count)
    own = sib is not None
    chunk_spec = pl.BlockSpec((1, slots, 2 * width), lambda i, c: (i, 0, 0))
    column = pl.BlockSpec(
        (feats, width), lambda i, c: (0, c[FIXED + 2 * count + own * count + i])
    )
    out_shape = [jax.ShapeDtypeStruct((count, slots, 2 * width), BF16)]
    out_specs = [chunk_spec]
    if not own:
        out_shape.append(jax.ShapeDtypeStruct((feats, slots), BF16))
        out_specs.append(pl.BlockSpec((feats, slots), lambda i, c: (0, 0)))
    return pl.pallas_call(
        functools.partial(gate_up_kernel, own),
        out_shape=out_shape,
        grid_spec=pltpu.PrefetchScalarGridSpec(
            num_scalar_prefetch=1,
            grid=(count,),
            in_specs=[pl.BlockSpec((slots, feats), lambda i, c: (0, 0)), column, column]
            + [chunk_spec] * own,
            out_specs=out_specs,
        ),
        compiler_params=PARAMS,
        cost_estimate=cost(),
    )(scalars, x, *in_hbm(w_gate, w_up), *([sib] if own else []))


def back_kernel(own, scalar_ref, g_ref, wd_ref, *refs):
    back = dot(g_ref[...], wd_ref[...], LAST_DIMS)
    if own:
        back += refs[0][0].astype(F32)
    refs[-1][0] = back.astype(BF16)


def back_rows(scalars, g, w_down, begin, size, count, sib):
    slots, feats = g.shape
    width = w_down.shape[0] // (2 * count)
    own = sib is not None
    chunk_spec = pl.BlockSpec((1, slots, width), lambda i, c: (i, 0, 0))
    row = pl.BlockSpec(
        (width, feats), lambda i, c: (c[FIXED + 2 * count + own * count + begin + i], 0)
    )
    return pl.pallas_call(
        functools.partial(back_kernel, own),
        out_shape=jax.ShapeDtypeStruct((size, slots, width), BF16),
        grid_spec=pltpu.PrefetchScalarGridSpec(
            num_scalar_prefetch=1,
            grid=(size,),
            in_specs=[pl.BlockSpec((slots, feats), lambda i, c: (0, 0)), row]
            + [chunk_spec] * own,
            out_specs=chunk_spec,
        ),
        compiler_params=PARAMS,
        cost_estimate=cost(),
    )(scalars, g, *in_hbm(w_down), *([sib] if own else []))


def activate(gate, upper, back):
    sig = jax.nn.sigmoid(gate)
    gated = gate * sig
    return (
        (gated * upper).astype(BF16),
        (back * upper * sig * (1.0 + gate * (1.0 - sig))).astype(BF16),
        (back * gated).astype(BF16),
    )


def hop_kernel(plan, scalar_ref, *refs):
    slot, count, chips, came = plan
    gate_up_ref, back_ref = refs[-3:-1]
    recv_ref = refs[0] if came else None
    send_ref = refs[-1]
    at = scalar_ref[0]
    width = send_ref.shape[1] // 3
    summing = (at <= slot) & (slot - at < count)

    def total(part):
        columns = slice(part * width, (part + 1) * width)
        value = (gate_up_ref[0, :, columns] if part < 2 else back_ref[0]).astype(F32)
        if came:
            value += jnp.where(at > 0, recv_ref[:, columns].astype(F32), 0.0)
        return value

    @pl.when(summing & (at < chips - 1))
    def _():
        for part in range(3):
            send_ref[:, part * width : (part + 1) * width] = total(part).astype(BF16)

    @pl.when(summing & (at == chips - 1))
    def _():
        for part, value in enumerate(activate(total(0), total(1), total(2))):
            send_ref[:, part * width : (part + 1) * width] = value

    if came:

        @pl.when(jnp.logical_not(summing))
        def _():
            send_ref[...] = recv_ref[...]


def hop(scalars, slot, count, chips, recv, sums, part):
    rows = sums[0][0].shape[1] // PARTS
    cols = sums[0][0].shape[2] + sums[1][0].shape[2]
    message = pl.BlockSpec((rows, cols), lambda n, c: (0, 0))
    operands, in_specs = [], []
    if recv is not None:
        operands.append(recv)
        in_specs.append(message)
    for array, i in sums:
        operands.append(array)
        in_specs.append(
            pl.BlockSpec((1, rows, array.shape[2]), lambda n, c, i=i: (i, part, 0))
        )
    plan = (slot, count, chips, recv is not None)
    return pl.pallas_call(
        functools.partial(hop_kernel, plan),
        out_shape=jax.ShapeDtypeStruct((rows, cols), BF16),
        grid_spec=pltpu.PrefetchScalarGridSpec(
            num_scalar_prefetch=1,
            grid=(1,),
            in_specs=in_specs,
            out_specs=message,
        ),
        compiler_params=PARAMS,
        cost_estimate=cost(),
    )(scalars, *operands)


def choose_kernel(scalar_ref, *refs):
    *candidates, out_ref, token_ref, sems = refs
    rows = candidates[0].shape[0]
    pass_on(scalar_ref, token_ref)

    def copy(n, part):
        return pltpu.make_async_copy(
            candidates[n * PARTS + part], out_ref.at[pl.ds(part * rows, rows)], sems.at[part]
        )

    for n in range(len(candidates) // PARTS):

        @pl.when(scalar_ref[0] == n)
        def _():
            for part in range(PARTS):
                copy(n, part).start()

    for part in range(PARTS):
        copy(0, part).wait()


def choose(scalars, candidates):
    rows, cols = candidates[0].shape
    return pl.pallas_call(
        choose_kernel,
        out_shape=(
            jax.ShapeDtypeStruct((rows * PARTS, cols), BF16),
            jax.ShapeDtypeStruct(scalars.shape, jnp.int32),
        ),
        in_specs=[pl.BlockSpec(memory_space=pltpu.SMEM)]
        + [pl.BlockSpec(memory_space=pl.ANY)] * len(candidates),
        out_specs=(pl.BlockSpec(memory_space=pltpu.VMEM), pl.BlockSpec(memory_space=pltpu.SMEM)),
        scratch_shapes=[pltpu.SemaphoreType.DMA((PARTS,))],
        compiler_params=PARAMS,
        cost_estimate=cost(),
    )(scalars, *candidates)


def gradients_kernel(units, scale, first, scalar_ref, xt_ref, g_ref, *refs):
    messages, refs = refs[:units], refs[units if first else units + 3 :]
    gg_ref, gu_ref, gd_ref, token_ref = refs
    width = gg_ref.shape[1]
    pass_on(scalar_ref, token_ref)
    for u in range(units):

        @pl.when(pl.program_id(0) == u)
        def _():
            both = dot(xt_ref[...], messages[u][:, width:]) * scale
            gg_ref[...] = both[:, :width].astype(BF16)
            gu_ref[...] = both[:, width:].astype(BF16)
            scaled = messages[u][:, :width]
            gd_ref[...] = (dot(scaled, g_ref[...], ROWS_FIRST) * scale).astype(BF16)


def gradients(scalars, begin, count, scale, x_t, g, messages, grads):
    slots, feats = g.shape
    width = messages[0].shape[1] // 3
    hidden = 2 * count * width
    units = len(messages)

    def at(u, c):
        return c[FIXED + begin + u]

    column = pl.BlockSpec((feats, width), lambda u, c: (0, at(u, c)))
    in_specs = [
        pl.BlockSpec((feats, slots), lambda u, c: (0, 0)),
        pl.BlockSpec((slots, feats), lambda u, c: (0, 0)),
    ]
    in_specs += [pl.BlockSpec((slots, 3 * width), lambda u, c: (0, 0))] * units
    operands = [x_t, g, *messages]
    aliases = {}
    if grads is not None:
        aliases = {len(operands) + 1 + n: n for n in range(3)}
        operands += grads
        in_specs += [pl.BlockSpec(memory_space=pl.ANY)] * 3
    *grads, token = pl.pallas_call(
        functools.partial(gradients_kernel, units, scale, grads is None),
        out_shape=[
            jax.ShapeDtypeStruct((feats, hidden), BF16),
            jax.ShapeDtypeStruct((feats, hidden), BF16),
            jax.ShapeDtypeStruct((hidden, feats), BF16),
            jax.ShapeDtypeStruct(scalars.shape, jnp.int32),
        ],
        grid_spec=pltpu.PrefetchScalarGridSpec(
            num_scalar_prefetch=1,
            grid=(units,),
            in_specs=in_specs,
            out_specs=[
                column,
                column,
                pl.BlockSpec((width, feats), lambda u, c: (at(u, c), 0)),
                pl.BlockSpec(memory_space=pltpu.SMEM),
            ],
        ),
        input_output_aliases=aliases,
        compiler_params=PARAMS,
        cost_estimate=cost(),
    )(scalars, *operands)
    return grads, token


def sum_rows_kernel(units, pieces, scalar_ref, *refs):
    messages, weights, refs = refs[:units], refs[units : 3 * units], refs[3 * units :]
    width = weights[0].shape[1]
    both = jnp.concatenate([message[:, width:] for message in messages], axis=1)
    part = dot(both, jnp.concatenate([w[...] for w in weights], axis=1), LAST_DIMS)
    if not pieces:
        out_ref, token_ref = refs
        out_ref[...] = part
        pass_on(scalar_ref, token_ref)
        return
    acc_in, *outs, acc = refs
    acc[...] = acc_in[...] + part
    size = outs[0].shape[0]
    for n, out in enumerate(outs):
        start = pl.multiple_of((scalar_ref[1] ^ n) * size, size)
        out[...] = acc[pl.ds(start, size), :].astype(BF16)


def sum_rows(scalars, begin, messages, weights, acc, pieces):
    slots, width = messages[0].shape[0], messages[0].shape[1] // 3
    feats = weights[0].shape[0]
    units = len(messages)
    in_specs = [pl.BlockSpec((slots, 3 * width), lambda n, c: (0, 0))] * units
    operands = list(messages)
    for u in range(units):
        column = pl.BlockSpec((feats, width), lambda n, c, u=u: (0, c[FIXED + begin + u]))
        operands += in_hbm(*weights)
        in_specs += [column, column]
    whole = pl.BlockSpec((slots, feats), lambda n, c: (0, 0))
    if pieces:
        operands.append(acc)
        in_specs.append(whole)
        out_shape = [jax.ShapeDtypeStruct((slots // pieces, feats), BF16)] * pieces
        out_specs = [pl.BlockSpec((slots // pieces, feats), lambda n, c: (0, 0))] * pieces
        scratch = [pltpu.VMEM((slots, feats), F32)]
    else:
        out_shape = [
            jax.ShapeDtypeStruct((slots, feats), F32),
            jax.ShapeDtypeStruct(scalars.shape, jnp.int32),
        ]
        out_specs = [whole, pl.BlockSpec(memory_space=pltpu.SMEM)]
        scratch = []
    return pl.pallas_call(
        functools.partial(sum_rows_kernel, units, pieces),
        out_shape=out_shape,
        grid_spec=pltpu.PrefetchScalarGridSpec(
            num_scalar_prefetch=1,
            grid=(1,),
            in_specs=in_specs,
            out_specs=out_specs,
            scratch_shapes=scratch,
        ),
        compiler_params=PARAMS,
        cost_estimate=cost(),
    )(scalars, *operands)


def body(tokens, grad_out, expert_ids, route_weights, w_gate, w_up, w_down):
    experts = lax.axis_size("expert")
    groups = lax.axis_size("dp")
    tok_rows = tokens.shape[0]
    feats = w_gate.shape[1]
    capacity = tok_rows // 2
    chips = groups // 2
    count = chips
    assert groups == 2 * experts and tokens.shape[1] == 2 * feats
    inv_root = 1.0 / math.sqrt(tok_rows * groups)
    expert = lax.axis_index("expert").astype(jnp.int32)
    block = lax.axis_index("dp").astype(jnp.int32)
    chip, core = block // 2, block % 2
    along = jnp.where(core == 0, chip, chips - 1 - chip)
    w_gate, w_up, w_down = w_gate[0], w_up[0], w_down[0]
    ids, weights = expert_ids.T, route_weights.T

    swap = [(j, j ^ 1) for j in range(groups)]
    up = [2 * z for z in range(chips)]
    circle = up + [j + 1 for j in reversed(up)]
    ring = list(zip(circle, circle[1:] + circle[:1]))

    scalars = [along, expert + experts * core, block % experts, block // experts, expert]
    scalars += [(d ^ 1 ^ core) * count + k for k in range(count) for d in range(2)]
    scalars += [(1 - core) * count + (i - (chips - 1 - along)) % count for i in range(count)]
    scalars += [core * count + (i - along) % count for i in range(count)]
    scalars = jnp.stack(scalars).astype(jnp.int32)

    def exchange(messages):
        came = [messages[0]]
        for t in range(1, experts):
            came.append(lax.ppermute(messages[t], "expert", [(q, q ^ t) for q in range(experts)]))
        blocks = assemble(scalars, came).reshape(groups, capacity, feats)
        blocks = lax.all_to_all(blocks, "dp", split_axis=0, concat_axis=0, tiled=True)
        return blocks.reshape(groups * capacity, feats)

    x_messages, hot, token = dispatch_rows(scalars, ids, weights, tokens, experts, False)
    g_messages, _, _ = dispatch_rows(token, ids, weights, grad_out, experts, True)
    x = exchange(x_messages)
    g = exchange(g_messages)

    other_gu, x_t = gate_up(scalars, x, w_gate, w_up, count, None)
    (both_gu,) = gate_up(scalars, x, w_gate, w_up, count, lax.ppermute(other_gu, "dp", swap))
    spans = ((0, count // 2), (count // 2, count - count // 2))
    others = [
        lax.ppermute(back_rows(scalars, g, w_down, begin, size, count, None), "dp", swap)
        for begin, size in spans
    ]
    sums = []
    for (begin, size), sib in zip(spans, others):
        both_b = back_rows(scalars, g, w_down, begin, size, count, sib)
        sums += [((both_gu, begin + i), (both_b, i)) for i in range(size)]

    slots = 2 * count + chips - 2
    first_back = chips - 1 + count
    recv, chunks = [], []
    grads, acc = None, None
    both = (w_gate, w_up)

    def gather(k, token):
        mine, token = choose(token, [r for n in range(chips) for r in recv[n - 1 + count + k]])
        chunks.append((mine, lax.ppermute(mine, "dp", swap)))
        return token

    def after(value, *things):
        return lax.optimization_barrier((value, *things))[0]

    early = count - 2
    place = along.astype(jnp.int32)[None]
    for s in range(slots):
        came = []
        for part in range(PARTS):
            if s < first_back:
                before = recv[s - 1][part] if s else None
                send = hop(place, s, count, chips, before, sums[s % count], part)
            else:
                send = recv[s - 1][part]
                if s == slots - 1:
                    some = range(early - 1) if part == 0 else range(early - 1, early)
                    for k in some:
                        token = gather(k, after(scalars, recv[s - 2][part]))
                        send = after(send, token)
            came.append(lax.ppermute(send, "dp", ring))
        recv.append(came)

    units = [message for chunk in chunks for message in chunk]
    grads, token = gradients(
        after(scalars, recv[-2][1]), 0, count, inv_root, x_t, g, units, None
    )
    acc, token = sum_rows(after(token, recv[-1][0]), 0, units, both, None, 0)
    for k in range(early, count):
        gather(k, token)
    units = [message for chunk in chunks[early:] for message in chunk]
    pieces = sum_rows(scalars, 2 * early, units, both, acc, groups)
    returned = []
    for r, piece in enumerate(pieces):
        pairs = []
        for q in range(experts):
            for b in range(groups):
                h, e = divmod(b ^ r, experts)
                pairs.append((e * groups + 2 * q + h, q * groups + b))
        returned.append(lax.ppermute(piece, ("expert", "dp"), pairs))
    grads, _ = gradients(scalars, 2 * early, count, inv_root, x_t, g, units, grads)
    grad_tokens = combine_rows(scalars, hot, returned, experts)
    return (grad_tokens, grads[0][None], grads[1][None], grads[2][None])


def solution(mesh):
    in_specs = (
        P("dp", "expert"),
        P("dp", "expert"),
        P("dp", None),
        P("dp", None),
        P("expert", "dp", None),
        P("expert", "dp", None),
        P("expert", None, "dp"),
    )
    out_specs = (
        P("dp", "expert"),
        P("expert", "dp", None),
        P("expert", "dp", None),
        P("expert", None, "dp"),
    )
    return jax.shard_map(body, mesh=mesh, in_specs=in_specs, out_specs=out_specs, check_vma=False)
```

```python
import functools
import math

import jax
import jax.numpy as jnp
from jax import lax
from jax.experimental import pallas as pl
from jax.experimental.pallas import tpu as pltpu
from jax.sharding import PartitionSpec as P

F32 = jnp.float32
BF16 = jnp.bfloat16
LAST_DIMS = (((1,), (1,)), ((), ()))
ROWS_FIRST = (((0,), (0,)), ((), ()))
FIXED = 5
PARTS = 2
PARAMS = pltpu.CompilerParams(vmem_limit_bytes=28 * 1024 * 1024)


def dot(a, b, dims=None):
    if dims is None:
        return jnp.dot(a, b, preferred_element_type=F32)
    return lax.dot_general(a, b, dims, preferred_element_type=F32)


def cost():
    return pl.CostEstimate(flops=1024, bytes_accessed=1024, transcendentals=0)


def in_hbm(*arrays):
    return [pltpu.with_memory_space_constraint(a, pltpu.HBM) for a in arrays]


def pass_on(scalar_ref, out_ref):
    for n in range(out_ref.shape[0]):
        out_ref[n] = scalar_ref[n]


def slot_one_hot(ids_ref, experts, capacity):
    tokens = ids_ref.shape[1]
    first, second = ids_ref[0:1, :], ids_ref[1:2, :]
    expert = lax.broadcasted_iota(jnp.int32, (8 * (-(-experts // 8)), tokens), 0)
    chosen = (first == expert) | (second == expert)
    before = lax.broadcasted_iota(jnp.int32, (tokens, tokens), 0) < lax.broadcasted_iota(
        jnp.int32, (tokens, tokens), 1
    )
    place = dot(chosen.astype(F32).astype(BF16), before.astype(F32).astype(BF16))
    place = jnp.where(chosen, place, -1.0).astype(jnp.int32)
    slot = lax.broadcasted_iota(jnp.int32, (capacity, tokens), 0)
    return [slot == place[e : e + 1, :] for e in range(experts)]


def dispatch_kernel(experts, weighted, scalar_ref, ids_hbm, weights_hbm, rows_hbm, *refs):
    *messages, hot_ref, token_ref, ids_ref, weights_ref, rows_ref, scale_ref, sems = refs
    _, capacity, feats = messages[0].shape
    pass_on(scalar_ref, token_ref)
    pairs = [(ids_hbm, ids_ref), (weights_hbm, weights_ref)]
    for h in range(2):
        whole = len(rows_hbm.shape) == 3
        half = rows_hbm.at[h] if whole else rows_hbm.at[:, pl.ds(h * feats, feats)]
        pairs.append((half, rows_ref.at[h]))
    copies = [pltpu.make_async_copy(a, b, sems.at[n]) for n, (a, b) in enumerate(pairs)]
    for copy in copies:
        copy.start()
    copies[0].wait()
    copies[1].wait()
    for e, hit in enumerate(slot_one_hot(ids_ref, experts, capacity)):
        place = slice(e * capacity, (e + 1) * capacity)
        hot_ref[place, :] = hit.astype(F32).astype(BF16)
        if weighted:
            weight = jnp.where(ids_ref[0:1, :] == e, weights_ref[0:1, :], weights_ref[1:2, :])
            weight = jnp.sum(jnp.where(hit, weight, 0.0), axis=1, keepdims=True)
            scale_ref[place, :] = jnp.broadcast_to(weight, (capacity, scale_ref.shape[1]))
    places = [
        pl.ds(pl.multiple_of((scalar_ref[4] ^ t) * capacity, capacity), capacity)
        for t in range(experts)
    ]
    hot = jnp.concatenate([hot_ref[place, :] for place in places], axis=0)
    for h in range(2):
        copies[2 + h].wait()
        out = dot(hot, rows_ref[h])
        for t, place in enumerate(places):
            part = out[t * capacity : (t + 1) * capacity]
            if weighted:
                part = part * scale_ref[place, 0:1]
            messages[t][h] = part.astype(BF16)


def dispatch_rows(scalars, ids, weights, rows, experts, weighted):
    tokens, feats = rows.shape[0], rows.shape[1] // 2
    capacity = tokens // 2
    if feats % 128:
        rows = rows.reshape(tokens, 2, feats).transpose(1, 0, 2)
    *messages, hot, token = pl.pallas_call(
        functools.partial(dispatch_kernel, experts, weighted),
        out_shape=[jax.ShapeDtypeStruct((2, capacity, feats), BF16)] * experts
        + [
            jax.ShapeDtypeStruct((experts * capacity, tokens), BF16),
            jax.ShapeDtypeStruct(scalars.shape, jnp.int32),
        ],
        in_specs=[pl.BlockSpec(memory_space=pltpu.SMEM)]
        + [pl.BlockSpec(memory_space=pltpu.HBM)] * 3,
        out_specs=[pl.BlockSpec(memory_space=pltpu.VMEM)] * (experts + 1)
        + [pl.BlockSpec(memory_space=pltpu.SMEM)],
        scratch_shapes=[
            pltpu.VMEM((2, tokens), jnp.int32),
            pltpu.VMEM((2, tokens), F32),
            pltpu.VMEM((2, tokens, feats), BF16),
            pltpu.VMEM((experts * capacity, 128), F32),
            pltpu.SemaphoreType.DMA((4,)),
        ],
        compiler_params=PARAMS,
        cost_estimate=cost(),
    )(scalars, *in_hbm(ids, weights, rows))
    return messages, hot, token


def assemble_kernel(scalar_ref, *refs):
    *messages, out_ref, sems = refs

    def copy(t, message):
        return pltpu.make_async_copy(message, out_ref.at[t ^ scalar_ref[4]], sems.at[t])

    for t, message in enumerate(messages):
        copy(t, message).start()
    for t, message in enumerate(messages):
        copy(t, message).wait()


def assemble(scalars, messages):
    return pl.pallas_call(
        assemble_kernel,
        out_shape=jax.ShapeDtypeStruct((len(messages), *messages[0].shape), BF16),
        in_specs=[pl.BlockSpec(memory_space=pltpu.SMEM)]
        + [pl.BlockSpec(memory_space=pl.ANY)] * len(messages),
        scratch_shapes=[pltpu.SemaphoreType.DMA((len(messages),))],
        compiler_params=PARAMS,
        cost_estimate=cost(),
    )(scalars, *messages)


def combine_kernel(experts, scalar_ref, hot_ref, *refs):
    pieces, (out_ref, rows_ref, sems) = refs[:-3], refs[-3:]
    capacity = pieces[0].shape[0]
    at = pl.program_id(0)

    def copy(n):
        return pltpu.make_async_copy(
            pieces[n], rows_ref.at[pl.ds(n * capacity, capacity)], sems.at[n]
        )

    @pl.when(at == 0)
    def _():
        for n in range(len(pieces)):
            copy(n).start()

    hot = jnp.concatenate(
        [
            hot_ref[pl.ds(pl.multiple_of((scalar_ref[2] ^ n) * capacity, capacity), capacity), :]
            for n in range(experts)
        ],
        axis=0,
    )
    for half in range(2):

        @pl.when(at == half)
        def _():
            for n in range(half * experts, (half + 1) * experts):
                copy(n).wait()
            rows = rows_ref[half * experts * capacity : (half + 1) * experts * capacity, :]
            out = dot(hot, rows, ROWS_FIRST).astype(BF16)
            out_ref[...] = out.reshape(out_ref.shape)


def combine_rows(scalars, hot, pieces, experts):
    tokens = hot.shape[1]
    capacity, feats = pieces[0].shape
    if feats % 128:
        out_shape = jax.ShapeDtypeStruct((2, tokens, feats), BF16)
        out_spec = pl.BlockSpec((1, tokens, feats), lambda a, c: (a ^ c[3], 0, 0))
    else:
        out_shape = jax.ShapeDtypeStruct((tokens, 2 * feats), BF16)
        out_spec = pl.BlockSpec((tokens, feats), lambda a, c: (0, a ^ c[3]))
    out = pl.pallas_call(
        functools.partial(combine_kernel, experts),
        out_shape=out_shape,
        grid_spec=pltpu.PrefetchScalarGridSpec(
            num_scalar_prefetch=1,
            grid=(2,),
            in_specs=[pl.BlockSpec((experts * capacity, tokens), lambda a, c: (0, 0))]
            + [pl.BlockSpec(memory_space=pltpu.HBM)] * len(pieces),
            out_specs=out_spec,
            scratch_shapes=[
                pltpu.VMEM((len(pieces) * capacity, feats), BF16),
                pltpu.SemaphoreType.DMA((len(pieces),)),
            ],
        ),
        compiler_params=PARAMS,
        cost_estimate=cost(),
    )(scalars, hot, *in_hbm(*pieces))
    if feats % 128:
        out = out.transpose(1, 0, 2).reshape(tokens, 2 * feats)
    return out


def turn_kernel(scalar_ref, *refs):
    *weights, out_ref, token_ref = refs
    pass_on(scalar_ref, token_ref)
    if len(weights) == 1:
        out_ref[...] = weights[0][...].T
        return
    width = out_ref.shape[0] // len(weights)
    for n, w_ref in enumerate(weights):
        out_ref[n * width : (n + 1) * width, :] = w_ref[...].T


def turn_down(scalars, w_down, chunks):
    hidden, feats = w_down.shape
    width = hidden // chunks
    return pl.pallas_call(
        turn_kernel,
        out_shape=(
            jax.ShapeDtypeStruct((feats, hidden), BF16),
            jax.ShapeDtypeStruct(scalars.shape, jnp.int32),
        ),
        grid_spec=pltpu.PrefetchScalarGridSpec(
            num_scalar_prefetch=1,
            grid=(chunks,),
            in_specs=[pl.BlockSpec((width, feats), lambda k, c: (k, 0))],
            out_specs=(
                pl.BlockSpec((feats, width), lambda k, c: (0, k)),
                pl.BlockSpec(memory_space=pltpu.SMEM),
            ),
        ),
        compiler_params=PARAMS,
        cost_estimate=cost(),
    )(scalars, *in_hbm(w_down))


def turn_gate_up(scalars, w_gate, w_up, chunks):
    feats, hidden = w_gate.shape
    width = hidden // chunks
    column = pl.BlockSpec((feats, width), lambda k, c: (0, k))
    return pl.pallas_call(
        turn_kernel,
        out_shape=(
            jax.ShapeDtypeStruct((2 * hidden, feats), BF16),
            jax.ShapeDtypeStruct(scalars.shape, jnp.int32),
        ),
        grid_spec=pltpu.PrefetchScalarGridSpec(
            num_scalar_prefetch=1,
            grid=(chunks,),
            in_specs=[column, column],
            out_specs=(
                pl.BlockSpec((2 * width, feats), lambda k, c: (k, 0)),
                pl.BlockSpec(memory_space=pltpu.SMEM),
            ),
        ),
        compiler_params=PARAMS,
        cost_estimate=cost(),
    )(scalars, *in_hbm(w_gate, w_up))


def gate_up_kernel(own, scalar_ref, x_ref, wg_ref, wu_ref, *refs):
    width = wg_ref.shape[1]
    gate = dot(x_ref[...], wg_ref[...])
    upper = dot(x_ref[...], wu_ref[...])
    *refs, token_ref = refs
    pass_on(scalar_ref, token_ref)
    if own:
        sib_ref, out_ref = refs
        gate += sib_ref[0, :, :width].astype(F32)
        upper += sib_ref[0, :, width:].astype(F32)
    else:
        out_ref, turned_ref = refs

        @pl.when(pl.program_id(0) == 0)
        def _():
            turned_ref[...] = x_ref[...].T

    out_ref[0, :, :width] = gate.astype(BF16)
    out_ref[0, :, width:] = upper.astype(BF16)


def gate_up(scalars, x, w_gate, w_up, count, sib):
    slots, feats = x.shape
    width = w_gate.shape[1] // (2 * count)
    own = sib is not None
    chunk_spec = pl.BlockSpec((1, slots, 2 * width), lambda i, c: (i, 0, 0))
    column = pl.BlockSpec(
        (feats, width), lambda i, c: (0, c[FIXED + 2 * count + own * count + i])
    )
    out_shape = [jax.ShapeDtypeStruct((count, slots, 2 * width), BF16)]
    out_specs = [chunk_spec]
    if not own:
        out_shape.append(jax.ShapeDtypeStruct((feats, slots), BF16))
        out_specs.append(pl.BlockSpec((feats, slots), lambda i, c: (0, 0)))
    out_shape.append(jax.ShapeDtypeStruct(scalars.shape, jnp.int32))
    out_specs.append(pl.BlockSpec(memory_space=pltpu.SMEM))
    return pl.pallas_call(
        functools.partial(gate_up_kernel, own),
        out_shape=out_shape,
        grid_spec=pltpu.PrefetchScalarGridSpec(
            num_scalar_prefetch=1,
            grid=(count,),
            in_specs=[pl.BlockSpec((slots, feats), lambda i, c: (0, 0)), column, column]
            + [chunk_spec] * own,
            out_specs=out_specs,
        ),
        compiler_params=PARAMS,
        cost_estimate=cost(),
    )(scalars, x, *in_hbm(w_gate, w_up), *([sib] if own else []))


def back_kernel(own, scalar_ref, g_ref, wd_ref, *refs):
    back = dot(g_ref[...], wd_ref[...])
    if own:
        back += refs[0][0].astype(F32)
    refs[-1][0] = back.astype(BF16)


def back_rows(scalars, g, turned, begin, size, count, sib):
    slots, feats = g.shape
    width = turned.shape[1] // (2 * count)
    own = sib is not None
    chunk_spec = pl.BlockSpec((1, slots, width), lambda i, c: (i, 0, 0))
    column = pl.BlockSpec(
        (feats, width), lambda i, c: (0, c[FIXED + 2 * count + own * count + begin + i])
    )
    return pl.pallas_call(
        functools.partial(back_kernel, own),
        out_shape=jax.ShapeDtypeStruct((size, slots, width), BF16),
        grid_spec=pltpu.PrefetchScalarGridSpec(
            num_scalar_prefetch=1,
            grid=(size,),
            in_specs=[pl.BlockSpec((slots, feats), lambda i, c: (0, 0)), column]
            + [chunk_spec] * own,
            out_specs=chunk_spec,
        ),
        compiler_params=PARAMS,
        cost_estimate=cost(),
    )(scalars, g, *in_hbm(turned), *([sib] if own else []))


def activate(gate, upper, back):
    sig = jax.nn.sigmoid(gate)
    gated = gate * sig
    return (
        (gated * upper).astype(BF16),
        (back * upper * sig * (1.0 + gate * (1.0 - sig))).astype(BF16),
        (back * gated).astype(BF16),
    )


def hop_kernel(plan, scalar_ref, *refs):
    slot, count, chips, came = plan
    gate_up_ref, back_ref = refs[-3:-1]
    recv_ref = refs[0] if came else None
    send_ref = refs[-1]
    at = scalar_ref[0]
    width = send_ref.shape[1] // 3
    summing = (at <= slot) & (slot - at < count)

    def total(part):
        columns = slice(part * width, (part + 1) * width)
        value = (gate_up_ref[0, :, columns] if part < 2 else back_ref[0]).astype(F32)
        if came:
            value += jnp.where(at > 0, recv_ref[:, columns].astype(F32), 0.0)
        return value

    @pl.when(summing & (at < chips - 1))
    def _():
        for part in range(3):
            send_ref[:, part * width : (part + 1) * width] = total(part).astype(BF16)

    @pl.when(summing & (at == chips - 1))
    def _():
        for part, value in enumerate(activate(total(0), total(1), total(2))):
            send_ref[:, part * width : (part + 1) * width] = value

    if came:

        @pl.when(jnp.logical_not(summing))
        def _():
            send_ref[...] = recv_ref[...]


def hop(scalars, slot, count, chips, recv, sums, part):
    rows = sums[0][0].shape[1] // PARTS
    cols = sums[0][0].shape[2] + sums[1][0].shape[2]
    message = pl.BlockSpec((rows, cols), lambda n, c: (0, 0))
    operands, in_specs = [], []
    if recv is not None:
        operands.append(recv)
        in_specs.append(message)
    for array, i in sums:
        operands.append(array)
        in_specs.append(
            pl.BlockSpec((1, rows, array.shape[2]), lambda n, c, i=i: (i, part, 0))
        )
    plan = (slot, count, chips, recv is not None)
    return pl.pallas_call(
        functools.partial(hop_kernel, plan),
        out_shape=jax.ShapeDtypeStruct((rows, cols), BF16),
        grid_spec=pltpu.PrefetchScalarGridSpec(
            num_scalar_prefetch=1,
            grid=(1,),
            in_specs=in_specs,
            out_specs=message,
        ),
        compiler_params=PARAMS,
        cost_estimate=cost(),
    )(scalars, *operands)


def choose_kernel(scalar_ref, *refs):
    *candidates, out_ref, token_ref, sems = refs
    rows = candidates[0].shape[0]
    pass_on(scalar_ref, token_ref)

    def copy(n, part):
        return pltpu.make_async_copy(
            candidates[n * PARTS + part], out_ref.at[pl.ds(part * rows, rows)], sems.at[part]
        )

    for n in range(len(candidates) // PARTS):

        @pl.when(scalar_ref[0] == n)
        def _():
            for part in range(PARTS):
                copy(n, part).start()

    for part in range(PARTS):
        copy(0, part).wait()


def choose(scalars, candidates):
    rows, cols = candidates[0].shape
    return pl.pallas_call(
        choose_kernel,
        out_shape=(
            jax.ShapeDtypeStruct((rows * PARTS, cols), BF16),
            jax.ShapeDtypeStruct(scalars.shape, jnp.int32),
        ),
        in_specs=[pl.BlockSpec(memory_space=pltpu.SMEM)]
        + [pl.BlockSpec(memory_space=pl.ANY)] * len(candidates),
        out_specs=(pl.BlockSpec(memory_space=pltpu.VMEM), pl.BlockSpec(memory_space=pltpu.SMEM)),
        scratch_shapes=[pltpu.SemaphoreType.DMA((PARTS,))],
        compiler_params=PARAMS,
        cost_estimate=cost(),
    )(scalars, *candidates)


def gradients_kernel(units, scale, first, scalar_ref, xt_ref, g_ref, *refs):
    messages, refs = refs[:units], refs[units if first else units + 3 :]
    gg_ref, gu_ref, gd_ref, token_ref = refs
    width = gg_ref.shape[1]
    pass_on(scalar_ref, token_ref)
    for u in range(units):

        @pl.when(pl.program_id(0) == u)
        def _():
            both = dot(xt_ref[...], messages[u][:, width:]) * scale
            gg_ref[...] = both[:, :width].astype(BF16)
            gu_ref[...] = both[:, width:].astype(BF16)
            scaled = messages[u][:, :width]
            gd_ref[...] = (dot(scaled, g_ref[...], ROWS_FIRST) * scale).astype(BF16)


def gradients(scalars, begin, count, scale, x_t, g, messages, grads):
    slots, feats = g.shape
    width = messages[0].shape[1] // 3
    hidden = 2 * count * width
    units = len(messages)

    def at(u, c):
        return c[FIXED + begin + u]

    column = pl.BlockSpec((feats, width), lambda u, c: (0, at(u, c)))
    in_specs = [
        pl.BlockSpec((feats, slots), lambda u, c: (0, 0)),
        pl.BlockSpec((slots, feats), lambda u, c: (0, 0)),
    ]
    in_specs += [pl.BlockSpec((slots, 3 * width), lambda u, c: (0, 0))] * units
    operands = [x_t, g, *messages]
    aliases = {}
    if grads is not None:
        aliases = {len(operands) + 1 + n: n for n in range(3)}
        operands += grads
        in_specs += [pl.BlockSpec(memory_space=pl.ANY)] * 3
    *grads, token = pl.pallas_call(
        functools.partial(gradients_kernel, units, scale, grads is None),
        out_shape=[
            jax.ShapeDtypeStruct((feats, hidden), BF16),
            jax.ShapeDtypeStruct((feats, hidden), BF16),
            jax.ShapeDtypeStruct((hidden, feats), BF16),
            jax.ShapeDtypeStruct(scalars.shape, jnp.int32),
        ],
        grid_spec=pltpu.PrefetchScalarGridSpec(
            num_scalar_prefetch=1,
            grid=(units,),
            in_specs=in_specs,
            out_specs=[
                column,
                column,
                pl.BlockSpec((width, feats), lambda u, c: (at(u, c), 0)),
                pl.BlockSpec(memory_space=pltpu.SMEM),
            ],
        ),
        input_output_aliases=aliases,
        compiler_params=PARAMS,
        cost_estimate=cost(),
    )(scalars, *operands)
    return grads, token


def sum_rows_kernel(units, pieces, scalar_ref, *refs):
    messages, weights, refs = refs[:units], refs[units : 2 * units], refs[2 * units :]
    width = weights[0].shape[0] // 2
    both = jnp.concatenate([message[:, width:] for message in messages], axis=1)
    part = dot(both, jnp.concatenate([w[...] for w in weights], axis=0))
    if not pieces:
        out_ref, token_ref = refs
        out_ref[...] = part
        pass_on(scalar_ref, token_ref)
        return
    acc_in, *outs, acc = refs
    acc[...] = acc_in[...] + part
    size = outs[0].shape[0]
    for n, out in enumerate(outs):
        start = pl.multiple_of((scalar_ref[1] ^ n) * size, size)
        out[...] = acc[pl.ds(start, size), :].astype(BF16)


def sum_rows(scalars, begin, messages, turned, acc, pieces):
    slots, width = messages[0].shape[0], messages[0].shape[1] // 3
    feats = turned.shape[1]
    units = len(messages)
    in_specs = [pl.BlockSpec((slots, 3 * width), lambda n, c: (0, 0))] * units
    operands = list(messages)
    for u in range(units):
        operands += in_hbm(turned)
        in_specs.append(
            pl.BlockSpec((2 * width, feats), lambda n, c, u=u: (c[FIXED + begin + u], 0))
        )
    whole = pl.BlockSpec((slots, feats), lambda n, c: (0, 0))
    if pieces:
        operands.append(acc)
        in_specs.append(whole)
        out_shape = [jax.ShapeDtypeStruct((slots // pieces, feats), BF16)] * pieces
        out_specs = [pl.BlockSpec((slots // pieces, feats), lambda n, c: (0, 0))] * pieces
        scratch = [pltpu.VMEM((slots, feats), F32)]
    else:
        out_shape = [
            jax.ShapeDtypeStruct((slots, feats), F32),
            jax.ShapeDtypeStruct(scalars.shape, jnp.int32),
        ]
        out_specs = [whole, pl.BlockSpec(memory_space=pltpu.SMEM)]
        scratch = []
    return pl.pallas_call(
        functools.partial(sum_rows_kernel, units, pieces),
        out_shape=out_shape,
        grid_spec=pltpu.PrefetchScalarGridSpec(
            num_scalar_prefetch=1,
            grid=(1,),
            in_specs=in_specs,
            out_specs=out_specs,
            scratch_shapes=scratch,
        ),
        compiler_params=PARAMS,
        cost_estimate=cost(),
    )(scalars, *operands)


def body(tokens, grad_out, expert_ids, route_weights, w_gate, w_up, w_down):
    experts = lax.axis_size("expert")
    groups = lax.axis_size("dp")
    tok_rows = tokens.shape[0]
    feats = w_gate.shape[1]
    capacity = tok_rows // 2
    chips = groups // 2
    count = chips
    assert groups == 2 * experts and tokens.shape[1] == 2 * feats
    inv_root = 1.0 / math.sqrt(tok_rows * groups)
    expert = lax.axis_index("expert").astype(jnp.int32)
    block = lax.axis_index("dp").astype(jnp.int32)
    chip, core = block // 2, block % 2
    along = jnp.where(core == 0, chip, chips - 1 - chip)
    w_gate, w_up, w_down = w_gate[0], w_up[0], w_down[0]
    ids, weights = expert_ids.T, route_weights.T

    swap = [(j, j ^ 1) for j in range(groups)]
    up = [2 * z for z in range(chips)]
    circle = up + [j + 1 for j in reversed(up)]
    ring = list(zip(circle, circle[1:] + circle[:1]))

    scalars = [along, expert + experts * core, block % experts, block // experts, expert]
    scalars += [(d ^ 1 ^ core) * count + k for k in range(count) for d in range(2)]
    scalars += [(1 - core) * count + (i - (chips - 1 - along)) % count for i in range(count)]
    scalars += [core * count + (i - along) % count for i in range(count)]
    scalars = jnp.stack(scalars).astype(jnp.int32)

    def exchange(messages, token):
        came = [messages[0]]
        for t in range(1, experts):
            came.append(lax.ppermute(messages[t], "expert", [(q, q ^ t) for q in range(experts)]))
        blocks = assemble(token, came).reshape(groups, capacity, feats)
        blocks = lax.all_to_all(blocks, "dp", split_axis=0, concat_axis=0, tiled=True)
        return blocks.reshape(groups * capacity, feats)

    x_messages, hot, token = dispatch_rows(scalars, ids, weights, tokens, experts, False)
    g_messages, _, token = dispatch_rows(token, ids, weights, grad_out, experts, True)
    x = exchange(x_messages, scalars)
    turned_down, token = turn_down(token, w_down, 2 * count)
    g = exchange(g_messages, token)

    other_gu, x_t, token = gate_up(scalars, x, w_gate, w_up, count, None)
    turned_gu, token = turn_gate_up(token, w_gate, w_up, 2 * count)
    both_gu, token = gate_up(token, x, w_gate, w_up, count, lax.ppermute(other_gu, "dp", swap))
    spans = ((0, count // 2), (count // 2, count - count // 2))
    others = [
        lax.ppermute(back_rows(token, g, turned_down, begin, size, count, None), "dp", swap)
        for begin, size in spans
    ]
    sums = []
    for (begin, size), sib in zip(spans, others):
        both_b = back_rows(scalars, g, turned_down, begin, size, count, sib)
        sums += [((both_gu, begin + i), (both_b, i)) for i in range(size)]

    slots = 2 * count + chips - 2
    first_back = chips - 1 + count
    recv, chunks = [], []
    grads, acc = None, None

    def gather(k, token):
        mine, token = choose(token, [r for n in range(chips) for r in recv[n - 1 + count + k]])
        chunks.append((mine, lax.ppermute(mine, "dp", swap)))
        return token

    def after(value, *things):
        return lax.optimization_barrier((value, *things))[0]

    early = count - 2
    place = along.astype(jnp.int32)[None]
    for s in range(slots):
        came = []
        for part in range(PARTS):
            if s < first_back:
                before = recv[s - 1][part] if s else None
                send = hop(place, s, count, chips, before, sums[s % count], part)
            else:
                send = recv[s - 1][part]
                if part == PARTS - 1:
                    token = gather(s - first_back, scalars)
                    send = after(send, token)
            came.append(lax.ppermute(send, "dp", ring))
        recv.append(came)

    units = [message for chunk in chunks[:early] for message in chunk]
    grads, token = gradients(
        after(token, recv[-2][1]), 0, count, inv_root, x_t, g, units, None
    )
    acc, token = sum_rows(after(token, recv[-1][0]), 0, units, turned_gu, None, 0)
    for k in range(len(chunks), count):
        gather(k, token)
    units = [message for chunk in chunks[early:] for message in chunk]
    pieces = sum_rows(scalars, 2 * early, units, turned_gu, acc, groups)
    returned = []
    for r, piece in enumerate(pieces):
        pairs = []
        for q in range(experts):
            for b in range(groups):
                h, e = divmod(b ^ r, experts)
                pairs.append((e * groups + 2 * q + h, q * groups + b))
        returned.append(lax.ppermute(piece, ("expert", "dp"), pairs))
    grads, _ = gradients(scalars, 2 * early, count, inv_root, x_t, g, units, grads)
    grad_tokens = combine_rows(scalars, hot, returned, experts)
    return (grad_tokens, grads[0][None], grads[1][None], grads[2][None])


def solution(mesh):
    in_specs = (
        P("dp", "expert"),
        P("dp", "expert"),
        P("dp", None),
        P("dp", None),
        P("expert", "dp", None),
        P("expert", "dp", None),
        P("expert", None, "dp"),
    )
    out_specs = (
        P("dp", "expert"),
        P("expert", "dp", None),
        P("expert", "dp", None),
        P("expert", None, "dp"),
    )
    return jax.shard_map(body, mesh=mesh, in_specs=in_specs, out_specs=out_specs, check_vma=False)
```

```python
import functools
import math

import jax
import jax.numpy as jnp
from jax import lax
from jax.experimental import pallas as pl
from jax.experimental.pallas import tpu as pltpu
from jax.sharding import PartitionSpec as P

F32 = jnp.float32
BF16 = jnp.bfloat16
LAST_DIMS = (((1,), (1,)), ((), ()))
ROWS_FIRST = (((0,), (0,)), ((), ()))
FIXED = 5
PARTS = 2
PARAMS = pltpu.CompilerParams(vmem_limit_bytes=28 * 1024 * 1024)


def dot(a, b, dims=None):
    if dims is None:
        return jnp.dot(a, b, preferred_element_type=F32)
    return lax.dot_general(a, b, dims, preferred_element_type=F32)


def cost():
    return pl.CostEstimate(flops=1024, bytes_accessed=1024, transcendentals=0)


def in_hbm(*arrays):
    return [pltpu.with_memory_space_constraint(a, pltpu.HBM) for a in arrays]


def pass_on(scalar_ref, out_ref):
    for n in range(out_ref.shape[0]):
        out_ref[n] = scalar_ref[n]


def slot_one_hot(ids_ref, experts, capacity):
    tokens = ids_ref.shape[1]
    first, second = ids_ref[0:1, :], ids_ref[1:2, :]
    expert = lax.broadcasted_iota(jnp.int32, (8 * (-(-experts // 8)), tokens), 0)
    chosen = (first == expert) | (second == expert)
    before = lax.broadcasted_iota(jnp.int32, (tokens, tokens), 0) < lax.broadcasted_iota(
        jnp.int32, (tokens, tokens), 1
    )
    place = dot(chosen.astype(F32).astype(BF16), before.astype(F32).astype(BF16))
    place = jnp.where(chosen, place, -1.0).astype(jnp.int32)
    slot = lax.broadcasted_iota(jnp.int32, (capacity, tokens), 0)
    return [slot == place[e : e + 1, :] for e in range(experts)]


def dispatch_kernel(experts, weighted, scalar_ref, ids_hbm, weights_hbm, rows_hbm, *refs):
    *messages, hot_ref, token_ref, ids_ref, weights_ref, rows_ref, scale_ref, sems = refs
    _, capacity, feats = messages[0].shape
    pass_on(scalar_ref, token_ref)
    pairs = [(ids_hbm, ids_ref), (weights_hbm, weights_ref)]
    for h in range(2):
        whole = len(rows_hbm.shape) == 3
        half = rows_hbm.at[h] if whole else rows_hbm.at[:, pl.ds(h * feats, feats)]
        pairs.append((half, rows_ref.at[h]))
    copies = [pltpu.make_async_copy(a, b, sems.at[n]) for n, (a, b) in enumerate(pairs)]
    for copy in copies:
        copy.start()
    copies[0].wait()
    copies[1].wait()
    for e, hit in enumerate(slot_one_hot(ids_ref, experts, capacity)):
        place = slice(e * capacity, (e + 1) * capacity)
        hot_ref[place, :] = hit.astype(F32).astype(BF16)
        if weighted:
            weight = jnp.where(ids_ref[0:1, :] == e, weights_ref[0:1, :], weights_ref[1:2, :])
            weight = jnp.sum(jnp.where(hit, weight, 0.0), axis=1, keepdims=True)
            scale_ref[place, :] = jnp.broadcast_to(weight, (capacity, scale_ref.shape[1]))
    places = [
        pl.ds(pl.multiple_of((scalar_ref[4] ^ t) * capacity, capacity), capacity)
        for t in range(experts)
    ]
    hot = jnp.concatenate([hot_ref[place, :] for place in places], axis=0)
    for h in range(2):
        copies[2 + h].wait()
        out = dot(hot, rows_ref[h])
        for t, place in enumerate(places):
            part = out[t * capacity : (t + 1) * capacity]
            if weighted:
                part = part * scale_ref[place, 0:1]
            messages[t][h] = part.astype(BF16)


def dispatch_rows(scalars, ids, weights, rows, experts, weighted):
    tokens, feats = rows.shape[0], rows.shape[1] // 2
    capacity = tokens // 2
    if feats % 128:
        rows = rows.reshape(tokens, 2, feats).transpose(1, 0, 2)
    *messages, hot, token = pl.pallas_call(
        functools.partial(dispatch_kernel, experts, weighted),
        out_shape=[jax.ShapeDtypeStruct((2, capacity, feats), BF16)] * experts
        + [
            jax.ShapeDtypeStruct((experts * capacity, tokens), BF16),
            jax.ShapeDtypeStruct(scalars.shape, jnp.int32),
        ],
        in_specs=[pl.BlockSpec(memory_space=pltpu.SMEM)]
        + [pl.BlockSpec(memory_space=pltpu.HBM)] * 3,
        out_specs=[pl.BlockSpec(memory_space=pltpu.VMEM)] * (experts + 1)
        + [pl.BlockSpec(memory_space=pltpu.SMEM)],
        scratch_shapes=[
            pltpu.VMEM((2, tokens), jnp.int32),
            pltpu.VMEM((2, tokens), F32),
            pltpu.VMEM((2, tokens, feats), BF16),
            pltpu.VMEM((experts * capacity, 128), F32),
            pltpu.SemaphoreType.DMA((4,)),
        ],
        compiler_params=PARAMS,
        cost_estimate=cost(),
    )(scalars, *in_hbm(ids, weights, rows))
    return messages, hot, token


def assemble_kernel(scalar_ref, *refs):
    *messages, out_ref, sems = refs

    def copy(t, message):
        return pltpu.make_async_copy(message, out_ref.at[t ^ scalar_ref[4]], sems.at[t])

    for t, message in enumerate(messages):
        copy(t, message).start()
    for t, message in enumerate(messages):
        copy(t, message).wait()


def assemble(scalars, messages):
    return pl.pallas_call(
        assemble_kernel,
        out_shape=jax.ShapeDtypeStruct((len(messages), *messages[0].shape), BF16),
        in_specs=[pl.BlockSpec(memory_space=pltpu.SMEM)]
        + [pl.BlockSpec(memory_space=pl.ANY)] * len(messages),
        scratch_shapes=[pltpu.SemaphoreType.DMA((len(messages),))],
        compiler_params=PARAMS,
        cost_estimate=cost(),
    )(scalars, *messages)


def combine_kernel(experts, scalar_ref, hot_ref, *refs):
    pieces, (out_ref, rows_ref, sems) = refs[:-3], refs[-3:]
    capacity = pieces[0].shape[0]
    at = pl.program_id(0)

    def copy(n):
        return pltpu.make_async_copy(
            pieces[n], rows_ref.at[pl.ds(n * capacity, capacity)], sems.at[n]
        )

    @pl.when(at == 0)
    def _():
        for n in range(len(pieces)):
            copy(n).start()

    hot = jnp.concatenate(
        [
            hot_ref[pl.ds(pl.multiple_of((scalar_ref[2] ^ n) * capacity, capacity), capacity), :]
            for n in range(experts)
        ],
        axis=0,
    )
    for half in range(2):

        @pl.when(at == half)
        def _():
            for n in range(half * experts, (half + 1) * experts):
                copy(n).wait()
            rows = rows_ref[half * experts * capacity : (half + 1) * experts * capacity, :]
            out = dot(hot, rows, ROWS_FIRST).astype(BF16)
            out_ref[...] = out.reshape(out_ref.shape)


def combine_rows(scalars, hot, pieces, experts):
    tokens = hot.shape[1]
    capacity, feats = pieces[0].shape
    if feats % 128:
        out_shape = jax.ShapeDtypeStruct((2, tokens, feats), BF16)
        out_spec = pl.BlockSpec((1, tokens, feats), lambda a, c: (a ^ c[3], 0, 0))
    else:
        out_shape = jax.ShapeDtypeStruct((tokens, 2 * feats), BF16)
        out_spec = pl.BlockSpec((tokens, feats), lambda a, c: (0, a ^ c[3]))
    out = pl.pallas_call(
        functools.partial(combine_kernel, experts),
        out_shape=out_shape,
        grid_spec=pltpu.PrefetchScalarGridSpec(
            num_scalar_prefetch=1,
            grid=(2,),
            in_specs=[pl.BlockSpec((experts * capacity, tokens), lambda a, c: (0, 0))]
            + [pl.BlockSpec(memory_space=pltpu.HBM)] * len(pieces),
            out_specs=out_spec,
            scratch_shapes=[
                pltpu.VMEM((len(pieces) * capacity, feats), BF16),
                pltpu.SemaphoreType.DMA((len(pieces),)),
            ],
        ),
        compiler_params=PARAMS,
        cost_estimate=cost(),
    )(scalars, hot, *in_hbm(*pieces))
    if feats % 128:
        out = out.transpose(1, 0, 2).reshape(tokens, 2 * feats)
    return out


def gate_up_kernel(own, scalar_ref, x_ref, wg_ref, wu_ref, *refs):
    width = wg_ref.shape[1]
    gate = dot(x_ref[...], wg_ref[...])
    upper = dot(x_ref[...], wu_ref[...])
    *refs, token_ref = refs
    pass_on(scalar_ref, token_ref)
    if own:
        sib_ref, out_ref = refs
        gate += sib_ref[0, :, :width].astype(F32)
        upper += sib_ref[0, :, width:].astype(F32)
    else:
        out_ref, turned_ref = refs

        @pl.when(pl.program_id(0) == 0)
        def _():
            turned_ref[...] = x_ref[...].T

    out_ref[0, :, :width] = gate.astype(BF16)
    out_ref[0, :, width:] = upper.astype(BF16)


def gate_up(scalars, x, w_gate, w_up, count, sib):
    slots, feats = x.shape
    width = w_gate.shape[1] // (2 * count)
    own = sib is not None
    chunk_spec = pl.BlockSpec((1, slots, 2 * width), lambda i, c: (i, 0, 0))
    column = pl.BlockSpec(
        (feats, width), lambda i, c: (0, c[FIXED + 2 * count + own * count + i])
    )
    out_shape = [jax.ShapeDtypeStruct((count, slots, 2 * width), BF16)]
    out_specs = [chunk_spec]
    if not own:
        out_shape.append(jax.ShapeDtypeStruct((feats, slots), BF16))
        out_specs.append(pl.BlockSpec((feats, slots), lambda i, c: (0, 0)))
    out_shape.append(jax.ShapeDtypeStruct(scalars.shape, jnp.int32))
    out_specs.append(pl.BlockSpec(memory_space=pltpu.SMEM))
    return pl.pallas_call(
        functools.partial(gate_up_kernel, own),
        out_shape=out_shape,
        grid_spec=pltpu.PrefetchScalarGridSpec(
            num_scalar_prefetch=1,
            grid=(count,),
            in_specs=[pl.BlockSpec((slots, feats), lambda i, c: (0, 0)), column, column]
            + [chunk_spec] * own,
            out_specs=out_specs,
        ),
        compiler_params=PARAMS,
        cost_estimate=cost(),
    )(scalars, x, *in_hbm(w_gate, w_up), *([sib] if own else []))


def back_kernel(own, scalar_ref, g_ref, wd_ref, *refs):
    back = dot(g_ref[...], wd_ref[...], LAST_DIMS)
    if own:
        back += refs[0][0].astype(F32)
    refs[-1][0] = back.astype(BF16)


def back_rows(scalars, g, w_down, begin, size, count, sib):
    slots, feats = g.shape
    width = w_down.shape[0] // (2 * count)
    own = sib is not None
    chunk_spec = pl.BlockSpec((1, slots, width), lambda i, c: (i, 0, 0))
    row = pl.BlockSpec(
        (width, feats), lambda i, c: (c[FIXED + 2 * count + own * count + begin + i], 0)
    )
    return pl.pallas_call(
        functools.partial(back_kernel, own),
        out_shape=jax.ShapeDtypeStruct((size, slots, width), BF16),
        grid_spec=pltpu.PrefetchScalarGridSpec(
            num_scalar_prefetch=1,
            grid=(size,),
            in_specs=[pl.BlockSpec((slots, feats), lambda i, c: (0, 0)), row]
            + [chunk_spec] * own,
            out_specs=chunk_spec,
        ),
        compiler_params=PARAMS,
        cost_estimate=cost(),
    )(scalars, g, *in_hbm(w_down), *([sib] if own else []))


def activate(gate, upper, back):
    sig = jax.nn.sigmoid(gate)
    gated = gate * sig
    return (
        (gated * upper).astype(BF16),
        (back * upper * sig * (1.0 + gate * (1.0 - sig))).astype(BF16),
        (back * gated).astype(BF16),
    )


def hop_kernel(plan, scalar_ref, *refs):
    slot, count, chips, came = plan
    gate_up_ref, back_ref = refs[-3:-1]
    recv_ref = refs[0] if came else None
    send_ref = refs[-1]
    at = scalar_ref[0]
    width = send_ref.shape[1] // 3
    summing = (at <= slot) & (slot - at < count)

    def total(part):
        columns = slice(part * width, (part + 1) * width)
        value = (gate_up_ref[0, :, columns] if part < 2 else back_ref[0]).astype(F32)
        if came:
            value += jnp.where(at > 0, recv_ref[:, columns].astype(F32), 0.0)
        return value

    @pl.when(summing & (at < chips - 1))
    def _():
        for part in range(3):
            send_ref[:, part * width : (part + 1) * width] = total(part).astype(BF16)

    @pl.when(summing & (at == chips - 1))
    def _():
        for part, value in enumerate(activate(total(0), total(1), total(2))):
            send_ref[:, part * width : (part + 1) * width] = value

    if came:

        @pl.when(jnp.logical_not(summing))
        def _():
            send_ref[...] = recv_ref[...]


def hop(scalars, slot, count, chips, recv, sums, part):
    rows = sums[0][0].shape[1] // PARTS
    cols = sums[0][0].shape[2] + sums[1][0].shape[2]
    message = pl.BlockSpec((rows, cols), lambda n, c: (0, 0))
    operands, in_specs = [], []
    if recv is not None:
        operands.append(recv)
        in_specs.append(message)
    for array, i in sums:
        operands.append(array)
        in_specs.append(
            pl.BlockSpec((1, rows, array.shape[2]), lambda n, c, i=i: (i, part, 0))
        )
    plan = (slot, count, chips, recv is not None)
    return pl.pallas_call(
        functools.partial(hop_kernel, plan),
        out_shape=jax.ShapeDtypeStruct((rows, cols), BF16),
        grid_spec=pltpu.PrefetchScalarGridSpec(
            num_scalar_prefetch=1,
            grid=(1,),
            in_specs=in_specs,
            out_specs=message,
        ),
        compiler_params=PARAMS,
        cost_estimate=cost(),
    )(scalars, *operands)


def choose_kernel(scalar_ref, *refs):
    *candidates, out_ref, token_ref, sems = refs
    rows = candidates[0].shape[0]
    pass_on(scalar_ref, token_ref)

    def copy(n, part):
        return pltpu.make_async_copy(
            candidates[n * PARTS + part], out_ref.at[pl.ds(part * rows, rows)], sems.at[part]
        )

    for n in range(len(candidates) // PARTS):

        @pl.when(scalar_ref[0] == n)
        def _():
            for part in range(PARTS):
                copy(n, part).start()

    for part in range(PARTS):
        copy(0, part).wait()


def choose(scalars, candidates):
    rows, cols = candidates[0].shape
    return pl.pallas_call(
        choose_kernel,
        out_shape=(
            jax.ShapeDtypeStruct((rows * PARTS, cols), BF16),
            jax.ShapeDtypeStruct(scalars.shape, jnp.int32),
        ),
        in_specs=[pl.BlockSpec(memory_space=pltpu.SMEM)]
        + [pl.BlockSpec(memory_space=pl.ANY)] * len(candidates),
        out_specs=(pl.BlockSpec(memory_space=pltpu.VMEM), pl.BlockSpec(memory_space=pltpu.SMEM)),
        scratch_shapes=[pltpu.SemaphoreType.DMA((PARTS,))],
        compiler_params=PARAMS,
        cost_estimate=cost(),
    )(scalars, *candidates)


def forward_on_kernel(scalar_ref, in_ref, out_ref):
    out_ref[...] = in_ref[...]


def forward_on(scalars, message):
    return pl.pallas_call(
        forward_on_kernel,
        out_shape=jax.ShapeDtypeStruct(message.shape, message.dtype),
        in_specs=[
            pl.BlockSpec(memory_space=pltpu.SMEM),
            pl.BlockSpec(memory_space=pltpu.VMEM),
        ],
        compiler_params=PARAMS,
        cost_estimate=cost(),
    )(scalars, message)


def gradients_kernel(units, scale, first, scalar_ref, xt_ref, g_ref, *refs):
    messages, refs = refs[:units], refs[units if first else units + 3 :]
    gg_ref, gu_ref, gd_ref, token_ref = refs
    width = gg_ref.shape[1]
    pass_on(scalar_ref, token_ref)
    for u in range(units):

        @pl.when(pl.program_id(0) == u)
        def _():
            both = dot(xt_ref[...], messages[u][:, width:]) * scale
            gg_ref[...] = both[:, :width].astype(BF16)
            gu_ref[...] = both[:, width:].astype(BF16)
            scaled = messages[u][:, :width]
            gd_ref[...] = (dot(scaled, g_ref[...], ROWS_FIRST) * scale).astype(BF16)


def gradients(scalars, begin, count, scale, x_t, g, messages, grads):
    slots, feats = g.shape
    width = messages[0].shape[1] // 3
    hidden = 2 * count * width
    units = len(messages)

    def at(u, c):
        return c[FIXED + begin + u]

    column = pl.BlockSpec((feats, width), lambda u, c: (0, at(u, c)))
    in_specs = [
        pl.BlockSpec((feats, slots), lambda u, c: (0, 0)),
        pl.BlockSpec((slots, feats), lambda u, c: (0, 0)),
    ]
    in_specs += [pl.BlockSpec((slots, 3 * width), lambda u, c: (0, 0))] * units
    operands = [x_t, g, *messages]
    aliases = {}
    if grads is not None:
        aliases = {len(operands) + 1 + n: n for n in range(3)}
        operands += grads
        in_specs += [pl.BlockSpec(memory_space=pl.ANY)] * 3
    *grads, token = pl.pallas_call(
        functools.partial(gradients_kernel, units, scale, grads is None),
        out_shape=[
            jax.ShapeDtypeStruct((feats, hidden), BF16),
            jax.ShapeDtypeStruct((feats, hidden), BF16),
            jax.ShapeDtypeStruct((hidden, feats), BF16),
            jax.ShapeDtypeStruct(scalars.shape, jnp.int32),
        ],
        grid_spec=pltpu.PrefetchScalarGridSpec(
            num_scalar_prefetch=1,
            grid=(units,),
            in_specs=in_specs,
            out_specs=[
                column,
                column,
                pl.BlockSpec((width, feats), lambda u, c: (at(u, c), 0)),
                pl.BlockSpec(memory_space=pltpu.SMEM),
            ],
        ),
        input_output_aliases=aliases,
        compiler_params=PARAMS,
        cost_estimate=cost(),
    )(scalars, *operands)
    return grads, token


def sum_rows_kernel(units, pieces, scalar_ref, *refs):
    messages, weights, refs = refs[:units], refs[units : 3 * units], refs[3 * units :]
    width = weights[0].shape[1]
    both = jnp.concatenate([message[:, width:] for message in messages], axis=1)
    part = dot(both, jnp.concatenate([w[...] for w in weights], axis=1), LAST_DIMS)
    if not pieces:
        out_ref, token_ref = refs
        out_ref[...] = part
        pass_on(scalar_ref, token_ref)
        return
    acc_in, *outs, acc = refs
    acc[...] = acc_in[...] + part
    size = outs[0].shape[0]
    for n, out in enumerate(outs):
        start = pl.multiple_of((scalar_ref[1] ^ n) * size, size)
        out[...] = acc[pl.ds(start, size), :].astype(BF16)


def sum_rows(scalars, begin, messages, weights, acc, pieces):
    slots, width = messages[0].shape[0], messages[0].shape[1] // 3
    feats = weights[0].shape[0]
    units = len(messages)
    in_specs = [pl.BlockSpec((slots, 3 * width), lambda n, c: (0, 0))] * units
    operands = list(messages)
    for u in range(units):
        column = pl.BlockSpec((feats, width), lambda n, c, u=u: (0, c[FIXED + begin + u]))
        operands += in_hbm(*weights)
        in_specs += [column, column]
    whole = pl.BlockSpec((slots, feats), lambda n, c: (0, 0))
    if pieces:
        operands.append(acc)
        in_specs.append(whole)
        out_shape = [jax.ShapeDtypeStruct((slots // pieces, feats), BF16)] * pieces
        out_specs = [pl.BlockSpec((slots // pieces, feats), lambda n, c: (0, 0))] * pieces
        scratch = [pltpu.VMEM((slots, feats), F32)]
    else:
        out_shape = [
            jax.ShapeDtypeStruct((slots, feats), F32),
            jax.ShapeDtypeStruct(scalars.shape, jnp.int32),
        ]
        out_specs = [whole, pl.BlockSpec(memory_space=pltpu.SMEM)]
        scratch = []
    return pl.pallas_call(
        functools.partial(sum_rows_kernel, units, pieces),
        out_shape=out_shape,
        grid_spec=pltpu.PrefetchScalarGridSpec(
            num_scalar_prefetch=1,
            grid=(1,),
            in_specs=in_specs,
            out_specs=out_specs,
            scratch_shapes=scratch,
        ),
        compiler_params=PARAMS,
        cost_estimate=cost(),
    )(scalars, *operands)


def body(tokens, grad_out, expert_ids, route_weights, w_gate, w_up, w_down):
    experts = lax.axis_size("expert")
    groups = lax.axis_size("dp")
    tok_rows = tokens.shape[0]
    feats = w_gate.shape[1]
    capacity = tok_rows // 2
    chips = groups // 2
    count = chips
    assert groups == 2 * experts and tokens.shape[1] == 2 * feats
    inv_root = 1.0 / math.sqrt(tok_rows * groups)
    expert = lax.axis_index("expert").astype(jnp.int32)
    block = lax.axis_index("dp").astype(jnp.int32)
    chip, core = block // 2, block % 2
    along = jnp.where(core == 0, chip, chips - 1 - chip)
    w_gate, w_up, w_down = w_gate[0], w_up[0], w_down[0]
    ids, weights = expert_ids.T, route_weights.T

    swap = [(j, j ^ 1) for j in range(groups)]
    up = [2 * z for z in range(chips)]
    circle = up + [j + 1 for j in reversed(up)]
    ring = list(zip(circle, circle[1:] + circle[:1]))

    scalars = [along, expert + experts * core, block % experts, block // experts, expert]
    scalars += [(d ^ 1 ^ core) * count + k for k in range(count) for d in range(2)]
    scalars += [(1 - core) * count + (i - (chips - 1 - along)) % count for i in range(count)]
    scalars += [core * count + (i - along) % count for i in range(count)]
    scalars = jnp.stack(scalars).astype(jnp.int32)

    def exchange(messages):
        came = [messages[0]]
        for t in range(1, experts):
            came.append(lax.ppermute(messages[t], "expert", [(q, q ^ t) for q in range(experts)]))
        blocks = assemble(scalars, came).reshape(groups, capacity, feats)
        blocks = lax.all_to_all(blocks, "dp", split_axis=0, concat_axis=0, tiled=True)
        return blocks.reshape(groups * capacity, feats)

    x_messages, hot, token = dispatch_rows(scalars, ids, weights, tokens, experts, False)
    g_messages, _, _ = dispatch_rows(token, ids, weights, grad_out, experts, True)
    x = exchange(x_messages)
    g = exchange(g_messages)

    other_gu, x_t, _ = gate_up(scalars, x, w_gate, w_up, count, None)
    sib_gu = lax.ppermute(other_gu, "dp", swap)
    both_gu, token = gate_up(scalars, x, w_gate, w_up, count, sib_gu)
    spans = ((0, count // 2), (count // 2, count - count // 2))
    others = [
        lax.ppermute(back_rows(token, g, w_down, begin, size, count, None), "dp", swap)
        for begin, size in spans
    ]
    sums = []
    for (begin, size), sib in zip(spans, others):
        both_b = back_rows(scalars, g, w_down, begin, size, count, sib)
        sums += [((both_gu, begin + i), (both_b, i)) for i in range(size)]

    slots = 2 * count + chips - 2
    first_back = chips - 1 + count
    recv, chunks = [], []
    grads, acc = None, None
    both = (w_gate, w_up)

    def gather(k, token):
        mine, token = choose(token, [r for n in range(chips) for r in recv[n - 1 + count + k]])
        chunks.append((mine, lax.ppermute(mine, "dp", swap)))
        return token

    early = count - 2
    place = along.astype(jnp.int32)[None]
    for s in range(slots):
        came = []
        for part in range(PARTS):
            if s < first_back:
                before = recv[s - 1][part] if s else None
                send = hop(place, s, count, chips, before, sums[s % count], part)
            else:
                send = recv[s - 1][part]
                if part == PARTS - 1:
                    token = gather(s - first_back, scalars)
                    send = forward_on(token, send)
            came.append(lax.ppermute(send, "dp", ring))
        recv.append(came)

    units = [message for chunk in chunks[:early] for message in chunk]
    grads, token = gradients(token, 0, count, inv_root, x_t, g, units, None)
    acc, token = sum_rows(token, 0, units, both, None, 0)
    for k in range(len(chunks), count):
        gather(k, token)
    units = [message for chunk in chunks[early:] for message in chunk]
    pieces = sum_rows(scalars, 2 * early, units, both, acc, groups)
    returned = []
    for r, piece in enumerate(pieces):
        pairs = []
        for q in range(experts):
            for b in range(groups):
                h, e = divmod(b ^ r, experts)
                pairs.append((e * groups + 2 * q + h, q * groups + b))
        returned.append(lax.ppermute(piece, ("expert", "dp"), pairs))
    grads, _ = gradients(scalars, 2 * early, count, inv_root, x_t, g, units, grads)
    grad_tokens = combine_rows(scalars, hot, returned, experts)
    return (grad_tokens, grads[0][None], grads[1][None], grads[2][None])


def solution(mesh):
    in_specs = (
        P("dp", "expert"),
        P("dp", "expert"),
        P("dp", None),
        P("dp", None),
        P("expert", "dp", None),
        P("expert", "dp", None),
        P("expert", None, "dp"),
    )
    out_specs = (
        P("dp", "expert"),
        P("expert", "dp", None),
        P("expert", "dp", None),
        P("expert", None, "dp"),
    )
    return jax.shard_map(body, mesh=mesh, in_specs=in_specs, out_specs=out_specs, check_vma=False)
```

```python
import functools
import math

import jax
import jax.numpy as jnp
from jax import lax
from jax.experimental import pallas as pl
from jax.experimental.pallas import tpu as pltpu
from jax.sharding import PartitionSpec as P

F32 = jnp.float32
BF16 = jnp.bfloat16
LAST_DIMS = (((1,), (1,)), ((), ()))
ROWS_FIRST = (((0,), (0,)), ((), ()))
FIXED = 5
PARTS = 2
PARAMS = pltpu.CompilerParams(vmem_limit_bytes=28 * 1024 * 1024)


def dot(a, b, dims=None):
    if dims is None:
        return jnp.dot(a, b, preferred_element_type=F32)
    return lax.dot_general(a, b, dims, preferred_element_type=F32)


def cost():
    return pl.CostEstimate(flops=1024, bytes_accessed=1024, transcendentals=0)


def in_hbm(*arrays):
    return [pltpu.with_memory_space_constraint(a, pltpu.HBM) for a in arrays]


def pass_on(scalar_ref, out_ref):
    for n in range(out_ref.shape[0]):
        out_ref[n] = scalar_ref[n]


def slot_one_hot(ids_ref, experts, capacity):
    tokens = ids_ref.shape[1]
    first, second = ids_ref[0:1, :], ids_ref[1:2, :]
    expert = lax.broadcasted_iota(jnp.int32, (8 * (-(-experts // 8)), tokens), 0)
    chosen = (first == expert) | (second == expert)
    before = lax.broadcasted_iota(jnp.int32, (tokens, tokens), 0) < lax.broadcasted_iota(
        jnp.int32, (tokens, tokens), 1
    )
    place = dot(chosen.astype(F32).astype(BF16), before.astype(F32).astype(BF16))
    place = jnp.where(chosen, place, -1.0).astype(jnp.int32)
    slot = lax.broadcasted_iota(jnp.int32, (capacity, tokens), 0)
    return [slot == place[e : e + 1, :] for e in range(experts)]


def dispatch_kernel(experts, weighted, scalar_ref, ids_hbm, weights_hbm, rows_hbm, *refs):
    *messages, hot_ref, token_ref, ids_ref, weights_ref, rows_ref, scale_ref, sems = refs
    _, capacity, feats = messages[0].shape
    pass_on(scalar_ref, token_ref)
    pairs = [(ids_hbm, ids_ref), (weights_hbm, weights_ref)]
    for h in range(2):
        whole = len(rows_hbm.shape) == 3
        half = rows_hbm.at[h] if whole else rows_hbm.at[:, pl.ds(h * feats, feats)]
        pairs.append((half, rows_ref.at[h]))
    copies = [pltpu.make_async_copy(a, b, sems.at[n]) for n, (a, b) in enumerate(pairs)]
    for copy in copies:
        copy.start()
    copies[0].wait()
    copies[1].wait()
    for e, hit in enumerate(slot_one_hot(ids_ref, experts, capacity)):
        place = slice(e * capacity, (e + 1) * capacity)
        hot_ref[place, :] = hit.astype(F32).astype(BF16)
        if weighted:
            weight = jnp.where(ids_ref[0:1, :] == e, weights_ref[0:1, :], weights_ref[1:2, :])
            weight = jnp.sum(jnp.where(hit, weight, 0.0), axis=1, keepdims=True)
            scale_ref[place, :] = jnp.broadcast_to(weight, (capacity, scale_ref.shape[1]))
    places = [
        pl.ds(pl.multiple_of((scalar_ref[4] ^ t) * capacity, capacity), capacity)
        for t in range(experts)
    ]
    hot = jnp.concatenate([hot_ref[place, :] for place in places], axis=0)
    for h in range(2):
        copies[2 + h].wait()
        out = dot(hot, rows_ref[h])
        for t, place in enumerate(places):
            part = out[t * capacity : (t + 1) * capacity]
            if weighted:
                part = part * scale_ref[place, 0:1]
            messages[t][h] = part.astype(BF16)


def dispatch_rows(scalars, ids, weights, rows, experts, weighted):
    tokens, feats = rows.shape[0], rows.shape[1] // 2
    capacity = tokens // 2
    if feats % 128:
        rows = rows.reshape(tokens, 2, feats).transpose(1, 0, 2)
    *messages, hot, token = pl.pallas_call(
        functools.partial(dispatch_kernel, experts, weighted),
        out_shape=[jax.ShapeDtypeStruct((2, capacity, feats), BF16)] * experts
        + [
            jax.ShapeDtypeStruct((experts * capacity, tokens), BF16),
            jax.ShapeDtypeStruct(scalars.shape, jnp.int32),
        ],
        in_specs=[pl.BlockSpec(memory_space=pltpu.SMEM)]
        + [pl.BlockSpec(memory_space=pltpu.HBM)] * 3,
        out_specs=[pl.BlockSpec(memory_space=pltpu.VMEM)] * (experts + 1)
        + [pl.BlockSpec(memory_space=pltpu.SMEM)],
        scratch_shapes=[
            pltpu.VMEM((2, tokens), jnp.int32),
            pltpu.VMEM((2, tokens), F32),
            pltpu.VMEM((2, tokens, feats), BF16),
            pltpu.VMEM((experts * capacity, 128), F32),
            pltpu.SemaphoreType.DMA((4,)),
        ],
        compiler_params=PARAMS,
        cost_estimate=cost(),
    )(scalars, *in_hbm(ids, weights, rows))
    return messages, hot, token


def assemble_kernel(scalar_ref, *refs):
    *messages, out_ref, token_ref, sems = refs
    pass_on(scalar_ref, token_ref)

    def copy(t, message):
        return pltpu.make_async_copy(message, out_ref.at[t ^ scalar_ref[4]], sems.at[t])

    for t, message in enumerate(messages):
        copy(t, message).start()
    for t, message in enumerate(messages):
        copy(t, message).wait()


def assemble(scalars, messages):
    return pl.pallas_call(
        assemble_kernel,
        out_shape=(
            jax.ShapeDtypeStruct((len(messages), *messages[0].shape), BF16),
            jax.ShapeDtypeStruct(scalars.shape, jnp.int32),
        ),
        in_specs=[pl.BlockSpec(memory_space=pltpu.SMEM)]
        + [pl.BlockSpec(memory_space=pl.ANY)] * len(messages),
        out_specs=(pl.BlockSpec(memory_space=pltpu.VMEM), pl.BlockSpec(memory_space=pltpu.SMEM)),
        scratch_shapes=[pltpu.SemaphoreType.DMA((len(messages),))],
        compiler_params=PARAMS,
        cost_estimate=cost(),
    )(scalars, *messages)


def combine_kernel(experts, scalar_ref, hot_ref, *refs):
    pieces, (out_ref, rows_ref, sems) = refs[:-3], refs[-3:]
    capacity = pieces[0].shape[0]
    at = pl.program_id(0)

    def copy(n):
        return pltpu.make_async_copy(
            pieces[n], rows_ref.at[pl.ds(n * capacity, capacity)], sems.at[n]
        )

    @pl.when(at == 0)
    def _():
        for n in range(len(pieces)):
            copy(n).start()

    hot = jnp.concatenate(
        [
            hot_ref[pl.ds(pl.multiple_of((scalar_ref[2] ^ n) * capacity, capacity), capacity), :]
            for n in range(experts)
        ],
        axis=0,
    )
    for half in range(2):

        @pl.when(at == half)
        def _():
            for n in range(half * experts, (half + 1) * experts):
                copy(n).wait()
            rows = rows_ref[half * experts * capacity : (half + 1) * experts * capacity, :]
            out = dot(hot, rows, ROWS_FIRST).astype(BF16)
            out_ref[...] = out.reshape(out_ref.shape)


def combine_rows(scalars, hot, pieces, experts):
    tokens = hot.shape[1]
    capacity, feats = pieces[0].shape
    if feats % 128:
        out_shape = jax.ShapeDtypeStruct((2, tokens, feats), BF16)
        out_spec = pl.BlockSpec((1, tokens, feats), lambda a, c: (a ^ c[3], 0, 0))
    else:
        out_shape = jax.ShapeDtypeStruct((tokens, 2 * feats), BF16)
        out_spec = pl.BlockSpec((tokens, feats), lambda a, c: (0, a ^ c[3]))
    out = pl.pallas_call(
        functools.partial(combine_kernel, experts),
        out_shape=out_shape,
        grid_spec=pltpu.PrefetchScalarGridSpec(
            num_scalar_prefetch=1,
            grid=(2,),
            in_specs=[pl.BlockSpec((experts * capacity, tokens), lambda a, c: (0, 0))]
            + [pl.BlockSpec(memory_space=pltpu.HBM)] * len(pieces),
            out_specs=out_spec,
            scratch_shapes=[
                pltpu.VMEM((len(pieces) * capacity, feats), BF16),
                pltpu.SemaphoreType.DMA((len(pieces),)),
            ],
        ),
        compiler_params=PARAMS,
        cost_estimate=cost(),
    )(scalars, hot, *in_hbm(*pieces))
    if feats % 128:
        out = out.transpose(1, 0, 2).reshape(tokens, 2 * feats)
    return out


def gate_up_kernel(own, scalar_ref, x_ref, wg_ref, wu_ref, *refs):
    width = wg_ref.shape[1]
    gate = dot(x_ref[...], wg_ref[...])
    upper = dot(x_ref[...], wu_ref[...])
    *refs, token_ref = refs
    pass_on(scalar_ref, token_ref)
    if own:
        sib_ref, out_ref = refs
        gate += sib_ref[0, :, :width].astype(F32)
        upper += sib_ref[0, :, width:].astype(F32)
    else:
        out_ref, turned_ref = refs

        @pl.when(pl.program_id(0) == 0)
        def _():
            turned_ref[...] = x_ref[...].T

    out_ref[0, :, :width] = gate.astype(BF16)
    out_ref[0, :, width:] = upper.astype(BF16)


def gate_up(scalars, x, w_gate, w_up, count, sib):
    slots, feats = x.shape
    width = w_gate.shape[1] // (2 * count)
    own = sib is not None
    chunk_spec = pl.BlockSpec((1, slots, 2 * width), lambda i, c: (i, 0, 0))
    column = pl.BlockSpec(
        (feats, width), lambda i, c: (0, c[FIXED + 2 * count + own * count + i])
    )
    out_shape = [jax.ShapeDtypeStruct((count, slots, 2 * width), BF16)]
    out_specs = [chunk_spec]
    if not own:
        out_shape.append(jax.ShapeDtypeStruct((feats, slots), BF16))
        out_specs.append(pl.BlockSpec((feats, slots), lambda i, c: (0, 0)))
    out_shape.append(jax.ShapeDtypeStruct(scalars.shape, jnp.int32))
    out_specs.append(pl.BlockSpec(memory_space=pltpu.SMEM))
    return pl.pallas_call(
        functools.partial(gate_up_kernel, own),
        out_shape=out_shape,
        grid_spec=pltpu.PrefetchScalarGridSpec(
            num_scalar_prefetch=1,
            grid=(count,),
            in_specs=[pl.BlockSpec((slots, feats), lambda i, c: (0, 0)), column, column]
            + [chunk_spec] * own,
            out_specs=out_specs,
        ),
        compiler_params=PARAMS,
        cost_estimate=cost(),
    )(scalars, x, *in_hbm(w_gate, w_up), *([sib] if own else []))


def back_kernel(own, scalar_ref, g_ref, wd_ref, *refs):
    back = dot(g_ref[...], wd_ref[...], LAST_DIMS)
    if own:
        back += refs[0][0].astype(F32)
    refs[-1][0] = back.astype(BF16)


def back_rows(scalars, g, w_down, begin, size, count, sib):
    slots, feats = g.shape
    width = w_down.shape[0] // (2 * count)
    own = sib is not None
    chunk_spec = pl.BlockSpec((1, slots, width), lambda i, c: (i, 0, 0))
    row = pl.BlockSpec(
        (width, feats), lambda i, c: (c[FIXED + 2 * count + own * count + begin + i], 0)
    )
    return pl.pallas_call(
        functools.partial(back_kernel, own),
        out_shape=jax.ShapeDtypeStruct((size, slots, width), BF16),
        grid_spec=pltpu.PrefetchScalarGridSpec(
            num_scalar_prefetch=1,
            grid=(size,),
            in_specs=[pl.BlockSpec((slots, feats), lambda i, c: (0, 0)), row]
            + [chunk_spec] * own,
            out_specs=chunk_spec,
        ),
        compiler_params=PARAMS,
        cost_estimate=cost(),
    )(scalars, g, *in_hbm(w_down), *([sib] if own else []))


def activate(gate, upper, back):
    sig = jax.nn.sigmoid(gate)
    gated = gate * sig
    return (
        (gated * upper).astype(BF16),
        (back * upper * sig * (1.0 + gate * (1.0 - sig))).astype(BF16),
        (back * gated).astype(BF16),
    )


def hop_kernel(plan, scalar_ref, *refs):
    slot, count, chips, came = plan
    gate_up_ref, back_ref = refs[-3:-1]
    recv_ref = refs[0] if came else None
    send_ref = refs[-1]
    at = scalar_ref[0]
    width = send_ref.shape[1] // 3
    summing = (at <= slot) & (slot - at < count)

    def total(part):
        columns = slice(part * width, (part + 1) * width)
        value = (gate_up_ref[0, :, columns] if part < 2 else back_ref[0]).astype(F32)
        if came:
            value += jnp.where(at > 0, recv_ref[:, columns].astype(F32), 0.0)
        return value

    @pl.when(summing & (at < chips - 1))
    def _():
        for part in range(3):
            send_ref[:, part * width : (part + 1) * width] = total(part).astype(BF16)

    @pl.when(summing & (at == chips - 1))
    def _():
        for part, value in enumerate(activate(total(0), total(1), total(2))):
            send_ref[:, part * width : (part + 1) * width] = value

    if came:

        @pl.when(jnp.logical_not(summing))
        def _():
            send_ref[...] = recv_ref[...]


def hop(scalars, slot, count, chips, recv, sums, part):
    rows = sums[0][0].shape[1] // PARTS
    cols = sums[0][0].shape[2] + sums[1][0].shape[2]
    message = pl.BlockSpec((rows, cols), lambda n, c: (0, 0))
    operands, in_specs = [], []
    if recv is not None:
        operands.append(recv)
        in_specs.append(message)
    for array, i in sums:
        operands.append(array)
        in_specs.append(
            pl.BlockSpec((1, rows, array.shape[2]), lambda n, c, i=i: (i, part, 0))
        )
    plan = (slot, count, chips, recv is not None)
    return pl.pallas_call(
        functools.partial(hop_kernel, plan),
        out_shape=jax.ShapeDtypeStruct((rows, cols), BF16),
        grid_spec=pltpu.PrefetchScalarGridSpec(
            num_scalar_prefetch=1,
            grid=(1,),
            in_specs=in_specs,
            out_specs=message,
        ),
        compiler_params=PARAMS,
        cost_estimate=cost(),
    )(scalars, *operands)


def choose_kernel(wanted, hops, scalar_ref, *refs):
    *candidates, sems = refs
    candidates, outs = candidates[:-wanted], candidates[-wanted:]
    rows = candidates[0].shape[0]

    def copy(k, n, part):
        return pltpu.make_async_copy(
            candidates[(k + n) * PARTS + part],
            outs[k].at[pl.ds(part * rows, rows)],
            sems.at[k, part],
        )

    for n in range(hops):

        @pl.when(scalar_ref[0] == n)
        def _():
            for k in range(wanted):
                for part in range(PARTS):
                    copy(k, n, part).start()

    for k in range(wanted):
        for part in range(PARTS):
            copy(k, 0, part).wait()


def choose(place, wanted, hops, candidates):
    rows, cols = candidates[0].shape
    return pl.pallas_call(
        functools.partial(choose_kernel, wanted, hops),
        out_shape=[jax.ShapeDtypeStruct((rows * PARTS, cols), BF16)] * wanted,
        in_specs=[pl.BlockSpec(memory_space=pltpu.SMEM)]
        + [pl.BlockSpec(memory_space=pl.ANY)] * len(candidates),
        scratch_shapes=[pltpu.SemaphoreType.DMA((wanted, PARTS))],
        compiler_params=PARAMS,
        cost_estimate=cost(),
    )(place, *candidates)


def gradients_kernel(units, scale, first, scalar_ref, xt_ref, g_ref, *refs):
    messages, refs = refs[:units], refs[units if first else units + 3 :]
    gg_ref, gu_ref, gd_ref, token_ref = refs
    width = gg_ref.shape[1]
    pass_on(scalar_ref, token_ref)
    for u in range(units):

        @pl.when(pl.program_id(0) == u)
        def _():
            both = dot(xt_ref[...], messages[u][:, width:]) * scale
            gg_ref[...] = both[:, :width].astype(BF16)
            gu_ref[...] = both[:, width:].astype(BF16)
            scaled = messages[u][:, :width]
            gd_ref[...] = (dot(scaled, g_ref[...], ROWS_FIRST) * scale).astype(BF16)


def gradients(scalars, begin, count, scale, x_t, g, messages, grads):
    slots, feats = g.shape
    width = messages[0].shape[1] // 3
    hidden = 2 * count * width
    units = len(messages)

    def at(u, c):
        return c[FIXED + begin + u]

    column = pl.BlockSpec((feats, width), lambda u, c: (0, at(u, c)))
    in_specs = [
        pl.BlockSpec((feats, slots), lambda u, c: (0, 0)),
        pl.BlockSpec((slots, feats), lambda u, c: (0, 0)),
    ]
    in_specs += [pl.BlockSpec((slots, 3 * width), lambda u, c: (0, 0))] * units
    operands = [x_t, g, *messages]
    aliases = {}
    if grads is not None:
        aliases = {len(operands) + 1 + n: n for n in range(3)}
        operands += grads
        in_specs += [pl.BlockSpec(memory_space=pl.ANY)] * 3
    *grads, token = pl.pallas_call(
        functools.partial(gradients_kernel, units, scale, grads is None),
        out_shape=[
            jax.ShapeDtypeStruct((feats, hidden), BF16),
            jax.ShapeDtypeStruct((feats, hidden), BF16),
            jax.ShapeDtypeStruct((hidden, feats), BF16),
            jax.ShapeDtypeStruct(scalars.shape, jnp.int32),
        ],
        grid_spec=pltpu.PrefetchScalarGridSpec(
            num_scalar_prefetch=1,
            grid=(units,),
            in_specs=in_specs,
            out_specs=[
                column,
                column,
                pl.BlockSpec((width, feats), lambda u, c: (at(u, c), 0)),
                pl.BlockSpec(memory_space=pltpu.SMEM),
            ],
        ),
        input_output_aliases=aliases,
        compiler_params=PARAMS,
        cost_estimate=cost(),
    )(scalars, *operands)
    return grads, token


def sum_rows_kernel(units, pieces, scalar_ref, *refs):
    messages, weights, refs = refs[:units], refs[units : 3 * units], refs[3 * units :]
    width = weights[0].shape[1]
    both = jnp.concatenate([message[:, width:] for message in messages], axis=1)
    part = dot(both, jnp.concatenate([w[...] for w in weights], axis=1), LAST_DIMS)
    if not pieces:
        out_ref, token_ref = refs
        out_ref[...] = part
        pass_on(scalar_ref, token_ref)
        return
    acc_in, *outs, acc = refs
    acc[...] = acc_in[...] + part
    size = outs[0].shape[0]
    for n, out in enumerate(outs):
        start = pl.multiple_of((scalar_ref[1] ^ n) * size, size)
        out[...] = acc[pl.ds(start, size), :].astype(BF16)


def sum_rows(scalars, begin, messages, weights, acc, pieces):
    slots, width = messages[0].shape[0], messages[0].shape[1] // 3
    feats = weights[0].shape[0]
    units = len(messages)
    in_specs = [pl.BlockSpec((slots, 3 * width), lambda n, c: (0, 0))] * units
    operands = list(messages)
    for u in range(units):
        column = pl.BlockSpec((feats, width), lambda n, c, u=u: (0, c[FIXED + begin + u]))
        operands += in_hbm(*weights)
        in_specs += [column, column]
    whole = pl.BlockSpec((slots, feats), lambda n, c: (0, 0))
    if pieces:
        operands.append(acc)
        in_specs.append(whole)
        out_shape = [jax.ShapeDtypeStruct((slots // pieces, feats), BF16)] * pieces
        out_specs = [pl.BlockSpec((slots // pieces, feats), lambda n, c: (0, 0))] * pieces
        scratch = [pltpu.VMEM((slots, feats), F32)]
    else:
        out_shape = [
            jax.ShapeDtypeStruct((slots, feats), F32),
            jax.ShapeDtypeStruct(scalars.shape, jnp.int32),
        ]
        out_specs = [whole, pl.BlockSpec(memory_space=pltpu.SMEM)]
        scratch = []
    return pl.pallas_call(
        functools.partial(sum_rows_kernel, units, pieces),
        out_shape=out_shape,
        grid_spec=pltpu.PrefetchScalarGridSpec(
            num_scalar_prefetch=1,
            grid=(1,),
            in_specs=in_specs,
            out_specs=out_specs,
            scratch_shapes=scratch,
        ),
        compiler_params=PARAMS,
        cost_estimate=cost(),
    )(scalars, *operands)


def body(tokens, grad_out, expert_ids, route_weights, w_gate, w_up, w_down):
    experts = lax.axis_size("expert")
    groups = lax.axis_size("dp")
    tok_rows = tokens.shape[0]
    feats = w_gate.shape[1]
    capacity = tok_rows // 2
    chips = groups // 2
    count = chips
    assert groups == 2 * experts and tokens.shape[1] == 2 * feats
    inv_root = 1.0 / math.sqrt(tok_rows * groups)
    expert = lax.axis_index("expert").astype(jnp.int32)
    block = lax.axis_index("dp").astype(jnp.int32)
    chip, core = block // 2, block % 2
    along = jnp.where(core == 0, chip, chips - 1 - chip)
    w_gate, w_up, w_down = w_gate[0], w_up[0], w_down[0]
    ids, weights = expert_ids.T, route_weights.T

    swap = [(j, j ^ 1) for j in range(groups)]
    up = [2 * z for z in range(chips)]
    circle = up + [j + 1 for j in reversed(up)]
    ring = list(zip(circle, circle[1:] + circle[:1]))

    scalars = [along, expert + experts * core, block % experts, block // experts, expert]
    scalars += [(d ^ 1 ^ core) * count + k for d in range(2) for k in range(count)]
    scalars += [(1 - core) * count + (i - (chips - 1 - along)) % count for i in range(count)]
    scalars += [core * count + (i - along) % count for i in range(count)]
    scalars = jnp.stack(scalars).astype(jnp.int32)

    def exchange(messages):
        came = [messages[0]]
        for t in range(1, experts):
            came.append(lax.ppermute(messages[t], "expert", [(q, q ^ t) for q in range(experts)]))
        blocks, token = assemble(scalars, came)
        blocks = blocks.reshape(groups, capacity, feats)
        blocks = lax.all_to_all(blocks, "dp", split_axis=0, concat_axis=0, tiled=True)
        return blocks.reshape(groups * capacity, feats), token

    x_messages, hot, token = dispatch_rows(scalars, ids, weights, tokens, experts, False)
    g_messages, _, _ = dispatch_rows(token, ids, weights, grad_out, experts, True)
    x, _ = exchange(x_messages)
    g, token = exchange(g_messages)

    other_gu, x_t, _ = gate_up(token, x, w_gate, w_up, count, None)
    sib_gu = lax.ppermute(other_gu, "dp", swap)
    both_gu, token = gate_up(scalars, x, w_gate, w_up, count, sib_gu)
    spans = ((0, count // 2), (count // 2, count - count // 2))
    others = [
        lax.ppermute(back_rows(token, g, w_down, begin, size, count, None), "dp", swap)
        for begin, size in spans
    ]
    sums = []
    for (begin, size), sib in zip(spans, others):
        both_b = back_rows(scalars, g, w_down, begin, size, count, sib)
        sums += [((both_gu, begin + i), (both_b, i)) for i in range(size)]

    slots = 2 * count + chips - 2
    first_back = chips - 1 + count
    recv = []
    both = (w_gate, w_up)
    place = along.astype(jnp.int32)[None]
    for s in range(slots):
        came = []
        for part in range(PARTS):
            send = recv[s - 1][part] if s else None
            if s < first_back:
                send = hop(place, s, count, chips, send, sums[s % count], part)
            came.append(lax.ppermute(send, "dp", ring))
        recv.append(came)

    def pick(begin, wanted):
        found = recv[count - 1 + begin : count - 1 + begin + chips + wanted - 1]
        return choose(place, wanted, chips, [part for came in found for part in came])

    early = count - 1
    mine = pick(0, early)
    others = [lax.ppermute(message, "dp", swap) for message in mine]
    grads, token = gradients(scalars, 0, count, inv_root, x_t, g, mine, None)
    acc, token = sum_rows(token, 0, mine, both, None, 0)
    mine = pick(early, count - early)
    others += [lax.ppermute(message, "dp", swap) for message in mine]
    units = [*mine, *others]
    pieces = sum_rows(scalars, early, units, both, acc, groups)
    returned = []
    for r, piece in enumerate(pieces):
        pairs = []
        for q in range(experts):
            for b in range(groups):
                h, e = divmod(b ^ r, experts)
                pairs.append((e * groups + 2 * q + h, q * groups + b))
        returned.append(lax.ppermute(piece, ("expert", "dp"), pairs))
    grads, _ = gradients(scalars, early, count, inv_root, x_t, g, units, grads)
    grad_tokens = combine_rows(scalars, hot, returned, experts)
    return (grad_tokens, grads[0][None], grads[1][None], grads[2][None])


def solution(mesh):
    in_specs = (
        P("dp", "expert"),
        P("dp", "expert"),
        P("dp", None),
        P("dp", None),
        P("expert", "dp", None),
        P("expert", "dp", None),
        P("expert", None, "dp"),
    )
    out_specs = (
        P("dp", "expert"),
        P("expert", "dp", None),
        P("expert", "dp", None),
        P("expert", None, "dp"),
    )
    return jax.shard_map(body, mesh=mesh, in_specs=in_specs, out_specs=out_specs, check_vma=False)
```

```python
import functools
import math

import jax
import jax.numpy as jnp
from jax import lax
from jax.experimental import pallas as pl
from jax.experimental.pallas import tpu as pltpu
from jax.sharding import PartitionSpec as P

F32 = jnp.float32
BF16 = jnp.bfloat16
LAST_DIMS = (((1,), (1,)), ((), ()))
ROWS_FIRST = (((0,), (0,)), ((), ()))
FIXED = 5
PARTS = 2
PARAMS = pltpu.CompilerParams(vmem_limit_bytes=28 * 1024 * 1024)


def dot(a, b, dims=None):
    if dims is None:
        return jnp.dot(a, b, preferred_element_type=F32)
    return lax.dot_general(a, b, dims, preferred_element_type=F32)


def cost():
    return pl.CostEstimate(flops=1024, bytes_accessed=1024, transcendentals=0)


def in_hbm(*arrays):
    return [pltpu.with_memory_space_constraint(a, pltpu.HBM) for a in arrays]


def pass_on(scalar_ref, out_ref):
    for n in range(out_ref.shape[0]):
        out_ref[n] = scalar_ref[n]


def slot_one_hot(ids_ref, experts, capacity):
    tokens = ids_ref.shape[1]
    first, second = ids_ref[0:1, :], ids_ref[1:2, :]
    expert = lax.broadcasted_iota(jnp.int32, (8 * (-(-experts // 8)), tokens), 0)
    chosen = (first == expert) | (second == expert)
    before = lax.broadcasted_iota(jnp.int32, (tokens, tokens), 0) < lax.broadcasted_iota(
        jnp.int32, (tokens, tokens), 1
    )
    place = dot(chosen.astype(F32).astype(BF16), before.astype(F32).astype(BF16))
    place = jnp.where(chosen, place, -1.0).astype(jnp.int32)
    slot = lax.broadcasted_iota(jnp.int32, (capacity, tokens), 0)
    return [slot == place[e : e + 1, :] for e in range(experts)]


def dispatch_kernel(experts, weighted, scalar_ref, ids_hbm, weights_hbm, rows_hbm, *refs):
    *messages, hot_ref, token_ref, ids_ref, weights_ref, rows_ref, scale_ref, sems = refs
    _, capacity, feats = messages[0].shape
    pass_on(scalar_ref, token_ref)
    pairs = [(ids_hbm, ids_ref), (weights_hbm, weights_ref)]
    for h in range(2):
        whole = len(rows_hbm.shape) == 3
        half = rows_hbm.at[h] if whole else rows_hbm.at[:, pl.ds(h * feats, feats)]
        pairs.append((half, rows_ref.at[h]))
    copies = [pltpu.make_async_copy(a, b, sems.at[n]) for n, (a, b) in enumerate(pairs)]
    for copy in copies:
        copy.start()
    copies[0].wait()
    copies[1].wait()
    for e, hit in enumerate(slot_one_hot(ids_ref, experts, capacity)):
        place = slice(e * capacity, (e + 1) * capacity)
        hot_ref[place, :] = hit.astype(F32).astype(BF16)
        if weighted:
            weight = jnp.where(ids_ref[0:1, :] == e, weights_ref[0:1, :], weights_ref[1:2, :])
            weight = jnp.sum(jnp.where(hit, weight, 0.0), axis=1, keepdims=True)
            scale_ref[place, :] = jnp.broadcast_to(weight, (capacity, scale_ref.shape[1]))
    places = [
        pl.ds(pl.multiple_of((scalar_ref[4] ^ t) * capacity, capacity), capacity)
        for t in range(experts)
    ]
    hot = jnp.concatenate([hot_ref[place, :] for place in places], axis=0)
    for h in range(2):
        copies[2 + h].wait()
        out = dot(hot, rows_ref[h])
        for t, place in enumerate(places):
            part = out[t * capacity : (t + 1) * capacity]
            if weighted:
                part = part * scale_ref[place, 0:1]
            messages[t][h] = part.astype(BF16)


def dispatch_rows(scalars, ids, weights, rows, experts, weighted):
    tokens, feats = rows.shape[0], rows.shape[1] // 2
    capacity = tokens // 2
    if feats % 128:
        rows = rows.reshape(tokens, 2, feats).transpose(1, 0, 2)
    *messages, hot, token = pl.pallas_call(
        functools.partial(dispatch_kernel, experts, weighted),
        out_shape=[jax.ShapeDtypeStruct((2, capacity, feats), BF16)] * experts
        + [
            jax.ShapeDtypeStruct((experts * capacity, tokens), BF16),
            jax.ShapeDtypeStruct(scalars.shape, jnp.int32),
        ],
        in_specs=[pl.BlockSpec(memory_space=pltpu.SMEM)]
        + [pl.BlockSpec(memory_space=pltpu.HBM)] * 3,
        out_specs=[pl.BlockSpec(memory_space=pltpu.VMEM)] * (experts + 1)
        + [pl.BlockSpec(memory_space=pltpu.SMEM)],
        scratch_shapes=[
            pltpu.VMEM((2, tokens), jnp.int32),
            pltpu.VMEM((2, tokens), F32),
            pltpu.VMEM((2, tokens, feats), BF16),
            pltpu.VMEM((experts * capacity, 128), F32),
            pltpu.SemaphoreType.DMA((4,)),
        ],
        compiler_params=PARAMS,
        cost_estimate=cost(),
    )(scalars, *in_hbm(ids, weights, rows))
    return messages, hot, token


def assemble_kernel(scalar_ref, *refs):
    *messages, out_ref, sems = refs

    def copy(t, message):
        return pltpu.make_async_copy(message, out_ref.at[t ^ scalar_ref[4]], sems.at[t])

    for t, message in enumerate(messages):
        copy(t, message).start()
    for t, message in enumerate(messages):
        copy(t, message).wait()


def assemble(scalars, messages):
    return pl.pallas_call(
        assemble_kernel,
        out_shape=jax.ShapeDtypeStruct((len(messages), *messages[0].shape), BF16),
        in_specs=[pl.BlockSpec(memory_space=pltpu.SMEM)]
        + [pl.BlockSpec(memory_space=pl.ANY)] * len(messages),
        scratch_shapes=[pltpu.SemaphoreType.DMA((len(messages),))],
        compiler_params=PARAMS,
        cost_estimate=cost(),
    )(scalars, *messages)


def combine_kernel(experts, scalar_ref, hot_ref, *refs):
    pieces, (out_ref, rows_ref, sems) = refs[:-3], refs[-3:]
    capacity = pieces[0].shape[0]
    at = pl.program_id(0)

    def copy(n):
        return pltpu.make_async_copy(
            pieces[n], rows_ref.at[pl.ds(n * capacity, capacity)], sems.at[n]
        )

    @pl.when(at == 0)
    def _():
        for n in range(len(pieces)):
            copy(n).start()

    hot = jnp.concatenate(
        [
            hot_ref[pl.ds(pl.multiple_of((scalar_ref[2] ^ n) * capacity, capacity), capacity), :]
            for n in range(experts)
        ],
        axis=0,
    )
    for half in range(2):

        @pl.when(at == half)
        def _():
            for n in range(half * experts, (half + 1) * experts):
                copy(n).wait()
            rows = rows_ref[half * experts * capacity : (half + 1) * experts * capacity, :]
            out = dot(hot, rows, ROWS_FIRST).astype(BF16)
            out_ref[...] = out.reshape(out_ref.shape)


def combine_rows(scalars, hot, pieces, experts):
    tokens = hot.shape[1]
    capacity, feats = pieces[0].shape
    if feats % 128:
        out_shape = jax.ShapeDtypeStruct((2, tokens, feats), BF16)
        out_spec = pl.BlockSpec((1, tokens, feats), lambda a, c: (a ^ c[3], 0, 0))
    else:
        out_shape = jax.ShapeDtypeStruct((tokens, 2 * feats), BF16)
        out_spec = pl.BlockSpec((tokens, feats), lambda a, c: (0, a ^ c[3]))
    out = pl.pallas_call(
        functools.partial(combine_kernel, experts),
        out_shape=out_shape,
        grid_spec=pltpu.PrefetchScalarGridSpec(
            num_scalar_prefetch=1,
            grid=(2,),
            in_specs=[pl.BlockSpec((experts * capacity, tokens), lambda a, c: (0, 0))]
            + [pl.BlockSpec(memory_space=pltpu.HBM)] * len(pieces),
            out_specs=out_spec,
            scratch_shapes=[
                pltpu.VMEM((len(pieces) * capacity, feats), BF16),
                pltpu.SemaphoreType.DMA((len(pieces),)),
            ],
        ),
        compiler_params=PARAMS,
        cost_estimate=cost(),
    )(scalars, hot, *in_hbm(*pieces))
    if feats % 128:
        out = out.transpose(1, 0, 2).reshape(tokens, 2 * feats)
    return out


def gate_up_kernel(scalar_ref, x_ref, wg_ref, wu_ref, *outs):
    width = wg_ref.shape[1]

    @pl.when((pl.program_id(0) == 0) & (pl.program_id(1) == 0))
    def _():
        outs[2][...] = x_ref[...].T

    for own in range(2):

        @pl.when(pl.program_id(1) == own)
        def _():
            outs[own][0, :, :width] = dot(x_ref[...], wg_ref[...]).astype(BF16)
            outs[own][0, :, width:] = dot(x_ref[...], wu_ref[...]).astype(BF16)


def gate_up(scalars, x, w_gate, w_up, count):
    slots, feats = x.shape
    width = w_gate.shape[1] // (2 * count)
    out = jax.ShapeDtypeStruct((count, slots, 2 * width), BF16)
    out_spec = pl.BlockSpec((1, slots, 2 * width), lambda i, own, c: (i, 0, 0))
    column = pl.BlockSpec(
        (feats, width), lambda i, own, c: (0, c[FIXED + 2 * count + own * count + i])
    )
    return pl.pallas_call(
        gate_up_kernel,
        out_shape=(out, out, jax.ShapeDtypeStruct((feats, slots), BF16)),
        grid_spec=pltpu.PrefetchScalarGridSpec(
            num_scalar_prefetch=1,
            grid=(count, 2),
            in_specs=[pl.BlockSpec((slots, feats), lambda i, own, c: (0, 0)), column, column],
            out_specs=(
                out_spec,
                out_spec,
                pl.BlockSpec((feats, slots), lambda i, own, c: (0, 0)),
            ),
        ),
        compiler_params=PARAMS,
        cost_estimate=cost(),
    )(scalars, x, *in_hbm(w_gate, w_up))


def back_kernel(scalar_ref, g_ref, wd_ref, *refs):
    *shares, out_ref = refs
    back = dot(g_ref[...], wd_ref[...], LAST_DIMS)
    if not shares:
        out_ref[0] = back.astype(BF16)
        return
    sib_b, own_gu, sib_gu = shares
    width = back.shape[1]
    both = own_gu[0].astype(F32) + sib_gu[0].astype(F32)
    out_ref[0, :, : 2 * width] = both.astype(BF16)
    out_ref[0, :, 2 * width :] = (back + sib_b[0].astype(F32)).astype(BF16)


def back_rows(scalars, g, w_down, begin, size, count, shares):
    slots, feats = g.shape
    width = w_down.shape[0] // (2 * count)
    own = bool(shares)
    row = pl.BlockSpec(
        (width, feats), lambda i, c: (c[FIXED + 2 * count + own * count + begin + i], 0)
    )
    in_specs = [pl.BlockSpec((slots, feats), lambda i, c: (0, 0)), row]
    if own:
        in_specs.append(pl.BlockSpec((1, slots, width), lambda i, c: (i, 0, 0)))
        in_specs += [pl.BlockSpec((1, slots, 2 * width), lambda i, c: (begin + i, 0, 0))] * 2
    cols = (3 if own else 1) * width
    return pl.pallas_call(
        back_kernel,
        out_shape=jax.ShapeDtypeStruct((size, slots, cols), BF16),
        grid_spec=pltpu.PrefetchScalarGridSpec(
            num_scalar_prefetch=1,
            grid=(size,),
            in_specs=in_specs,
            out_specs=pl.BlockSpec((1, slots, cols), lambda i, c: (i, 0, 0)),
        ),
        compiler_params=PARAMS,
        cost_estimate=cost(),
    )(scalars, g, *in_hbm(w_down), *shares)


def activate(gate, upper, back):
    sig = jax.nn.sigmoid(gate)
    gated = gate * sig
    return (
        (gated * upper).astype(BF16),
        (back * upper * sig * (1.0 + gate * (1.0 - sig))).astype(BF16),
        (back * gated).astype(BF16),
    )


def hop_kernel(plan, scalar_ref, *refs):
    slot, count, chips, came = plan
    sums_ref = refs[-2]
    recv_ref = refs[0] if came else None
    send_ref = refs[-1]
    at = scalar_ref[0]
    width = send_ref.shape[1] // 3
    summing = (at <= slot) & (slot - at < count)

    def total(part):
        columns = slice(part * width, (part + 1) * width)
        value = sums_ref[0, :, columns].astype(F32)
        if came:
            value += jnp.where(at > 0, recv_ref[:, columns].astype(F32), 0.0)
        return value

    @pl.when(summing & (at < chips - 1))
    def _():
        for part in range(3):
            send_ref[:, part * width : (part + 1) * width] = total(part).astype(BF16)

    @pl.when(summing & (at == chips - 1))
    def _():
        for part, value in enumerate(activate(total(0), total(1), total(2))):
            send_ref[:, part * width : (part + 1) * width] = value

    if came:

        @pl.when(jnp.logical_not(summing))
        def _():
            send_ref[...] = recv_ref[...]


def hop(scalars, slot, count, chips, recv, sums, part):
    array, i = sums
    rows, cols = array.shape[1] // PARTS, array.shape[2]
    message = pl.BlockSpec((rows, cols), lambda n, c: (0, 0))
    operands, in_specs = [], []
    if recv is not None:
        operands.append(recv)
        in_specs.append(message)
    operands.append(array)
    in_specs.append(pl.BlockSpec((1, rows, cols), lambda n, c: (i, part, 0)))
    plan = (slot, count, chips, recv is not None)
    return pl.pallas_call(
        functools.partial(hop_kernel, plan),
        out_shape=jax.ShapeDtypeStruct((rows, cols), BF16),
        grid_spec=pltpu.PrefetchScalarGridSpec(
            num_scalar_prefetch=1,
            grid=(1,),
            in_specs=in_specs,
            out_specs=message,
        ),
        compiler_params=PARAMS,
        cost_estimate=cost(),
    )(scalars, *operands)


def choose_kernel(wanted, hops, scalar_ref, *refs):
    *candidates, sems = refs
    candidates, outs = candidates[:-wanted], candidates[-wanted:]
    rows = candidates[0].shape[0]

    def copy(k, n, part):
        return pltpu.make_async_copy(
            candidates[(k + n) * PARTS + part],
            outs[k].at[pl.ds(part * rows, rows)],
            sems.at[k, part],
        )

    for n in range(hops):

        @pl.when(scalar_ref[0] == n)
        def _():
            for k in range(wanted):
                for part in range(PARTS):
                    copy(k, n, part).start()

    for k in range(wanted):
        for part in range(PARTS):
            copy(k, 0, part).wait()


def choose(place, wanted, hops, candidates):
    rows, cols = candidates[0].shape
    return pl.pallas_call(
        functools.partial(choose_kernel, wanted, hops),
        out_shape=[jax.ShapeDtypeStruct((rows * PARTS, cols), BF16)] * wanted,
        in_specs=[pl.BlockSpec(memory_space=pltpu.SMEM)]
        + [pl.BlockSpec(memory_space=pl.ANY)] * len(candidates),
        scratch_shapes=[pltpu.SemaphoreType.DMA((wanted, PARTS))],
        compiler_params=PARAMS,
        cost_estimate=cost(),
    )(place, *candidates)


def gradients_kernel(units, scale, first, scalar_ref, xt_ref, g_ref, *refs):
    messages, refs = refs[:units], refs[units if first else units + 3 :]
    gg_ref, gu_ref, gd_ref, token_ref = refs
    width = gg_ref.shape[1]
    pass_on(scalar_ref, token_ref)
    for u in range(units):

        @pl.when(pl.program_id(0) == u)
        def _():
            both = dot(xt_ref[...], messages[u][:, width:]) * scale
            gg_ref[...] = both[:, :width].astype(BF16)
            gu_ref[...] = both[:, width:].astype(BF16)
            scaled = messages[u][:, :width]
            gd_ref[...] = (dot(scaled, g_ref[...], ROWS_FIRST) * scale).astype(BF16)


def gradients(scalars, begin, count, scale, x_t, g, messages, grads):
    slots, feats = g.shape
    width = messages[0].shape[1] // 3
    hidden = 2 * count * width
    units = len(messages)

    def at(u, c):
        return c[FIXED + begin + u]

    column = pl.BlockSpec((feats, width), lambda u, c: (0, at(u, c)))
    in_specs = [
        pl.BlockSpec((feats, slots), lambda u, c: (0, 0)),
        pl.BlockSpec((slots, feats), lambda u, c: (0, 0)),
    ]
    in_specs += [pl.BlockSpec((slots, 3 * width), lambda u, c: (0, 0))] * units
    operands = [x_t, g, *messages]
    aliases = {}
    if grads is not None:
        aliases = {len(operands) + 1 + n: n for n in range(3)}
        operands += grads
        in_specs += [pl.BlockSpec(memory_space=pl.ANY)] * 3
    *grads, token = pl.pallas_call(
        functools.partial(gradients_kernel, units, scale, grads is None),
        out_shape=[
            jax.ShapeDtypeStruct((feats, hidden), BF16),
            jax.ShapeDtypeStruct((feats, hidden), BF16),
            jax.ShapeDtypeStruct((hidden, feats), BF16),
            jax.ShapeDtypeStruct(scalars.shape, jnp.int32),
        ],
        grid_spec=pltpu.PrefetchScalarGridSpec(
            num_scalar_prefetch=1,
            grid=(units,),
            in_specs=in_specs,
            out_specs=[
                column,
                column,
                pl.BlockSpec((width, feats), lambda u, c: (at(u, c), 0)),
                pl.BlockSpec(memory_space=pltpu.SMEM),
            ],
        ),
        input_output_aliases=aliases,
        compiler_params=PARAMS,
        cost_estimate=cost(),
    )(scalars, *operands)
    return grads, token


def sum_rows_kernel(units, pieces, scalar_ref, *refs):
    messages, weights, refs = refs[:units], refs[units : 3 * units], refs[3 * units :]
    width = weights[0].shape[1]
    both = jnp.concatenate([message[:, width:] for message in messages], axis=1)
    part = dot(both, jnp.concatenate([w[...] for w in weights], axis=1), LAST_DIMS)
    if not pieces:
        out_ref, token_ref = refs
        out_ref[...] = part
        pass_on(scalar_ref, token_ref)
        return
    acc_in, *outs, acc = refs
    acc[...] = acc_in[...] + part
    size = outs[0].shape[0]
    for n, out in enumerate(outs):
        start = pl.multiple_of((scalar_ref[1] ^ n) * size, size)
        out[...] = acc[pl.ds(start, size), :].astype(BF16)


def sum_rows(scalars, begin, messages, weights, acc, pieces):
    slots, width = messages[0].shape[0], messages[0].shape[1] // 3
    feats = weights[0].shape[0]
    units = len(messages)
    in_specs = [pl.BlockSpec((slots, 3 * width), lambda n, c: (0, 0))] * units
    operands = list(messages)
    for u in range(units):
        column = pl.BlockSpec((feats, width), lambda n, c, u=u: (0, c[FIXED + begin + u]))
        operands += in_hbm(*weights)
        in_specs += [column, column]
    whole = pl.BlockSpec((slots, feats), lambda n, c: (0, 0))
    if pieces:
        operands.append(acc)
        in_specs.append(whole)
        out_shape = [jax.ShapeDtypeStruct((slots // pieces, feats), BF16)] * pieces
        out_specs = [pl.BlockSpec((slots // pieces, feats), lambda n, c: (0, 0))] * pieces
        scratch = [pltpu.VMEM((slots, feats), F32)]
    else:
        out_shape = [
            jax.ShapeDtypeStruct((slots, feats), F32),
            jax.ShapeDtypeStruct(scalars.shape, jnp.int32),
        ]
        out_specs = [whole, pl.BlockSpec(memory_space=pltpu.SMEM)]
        scratch = []
    return pl.pallas_call(
        functools.partial(sum_rows_kernel, units, pieces),
        out_shape=out_shape,
        grid_spec=pltpu.PrefetchScalarGridSpec(
            num_scalar_prefetch=1,
            grid=(1,),
            in_specs=in_specs,
            out_specs=out_specs,
            scratch_shapes=scratch,
        ),
        compiler_params=PARAMS,
        cost_estimate=cost(),
    )(scalars, *operands)


def body(tokens, grad_out, expert_ids, route_weights, w_gate, w_up, w_down):
    experts = lax.axis_size("expert")
    groups = lax.axis_size("dp")
    tok_rows = tokens.shape[0]
    feats = w_gate.shape[1]
    capacity = tok_rows // 2
    chips = groups // 2
    count = chips
    assert groups == 2 * experts and tokens.shape[1] == 2 * feats
    inv_root = 1.0 / math.sqrt(tok_rows * groups)
    expert = lax.axis_index("expert").astype(jnp.int32)
    block = lax.axis_index("dp").astype(jnp.int32)
    chip, core = block // 2, block % 2
    along = jnp.where(core == 0, chip, chips - 1 - chip)
    w_gate, w_up, w_down = w_gate[0], w_up[0], w_down[0]
    ids, weights = expert_ids.T, route_weights.T

    swap = [(j, j ^ 1) for j in range(groups)]
    up = [2 * z for z in range(chips)]
    circle = up + [j + 1 for j in reversed(up)]
    ring = list(zip(circle, circle[1:] + circle[:1]))

    scalars = [along, expert + experts * core, block % experts, block // experts, expert]
    scalars += [(d ^ 1 ^ core) * count + k for d in range(2) for k in range(count)]
    scalars += [(1 - core) * count + (i - (chips - 1 - along)) % count for i in range(count)]
    scalars += [core * count + (i - along) % count for i in range(count)]
    scalars = jnp.stack(scalars).astype(jnp.int32)

    def exchange(messages):
        came = [messages[0]]
        for t in range(1, experts):
            came.append(lax.ppermute(messages[t], "expert", [(q, q ^ t) for q in range(experts)]))
        blocks = assemble(scalars, came).reshape(groups, capacity, feats)
        blocks = lax.all_to_all(blocks, "dp", split_axis=0, concat_axis=0, tiled=True)
        return blocks.reshape(groups * capacity, feats)

    x_messages, hot, token = dispatch_rows(scalars, ids, weights, tokens, experts, False)
    g_messages, _, _ = dispatch_rows(token, ids, weights, grad_out, experts, True)
    x = exchange(x_messages)
    g = exchange(g_messages)

    other_gu, own_gu, x_t = gate_up(scalars, x, w_gate, w_up, count)
    sib_gu = lax.ppermute(other_gu, "dp", swap)
    spans = ((0, count // 2), (count // 2, count - count // 2))
    others = [
        lax.ppermute(back_rows(scalars, g, w_down, begin, size, count, ()), "dp", swap)
        for begin, size in spans
    ]
    sums = []
    for (begin, size), sib_b in zip(spans, others):
        shares = (sib_b, own_gu, sib_gu)
        both = back_rows(scalars, g, w_down, begin, size, count, shares)
        sums += [(both, i) for i in range(size)]

    slots = 2 * count + chips - 2
    first_back = chips - 1 + count
    recv = []
    gate_and_up = (w_gate, w_up)
    place = along.astype(jnp.int32)[None]
    for s in range(slots):
        came = []
        for part in range(PARTS):
            send = recv[s - 1][part] if s else None
            if s < first_back:
                send = hop(place, s, count, chips, send, sums[s % count], part)
            came.append(lax.ppermute(send, "dp", ring))
        recv.append(came)

    def pick(token, begin, wanted):
        found = recv[count - 1 + begin : count - 1 + begin + chips + wanted - 1]
        return choose(token, wanted, chips, [part for came in found for part in came])

    early = count - 1
    mine = pick(place, 0, early)
    others = [lax.ppermute(message, "dp", swap) for message in mine]
    grads, token = gradients(scalars, 0, count, inv_root, x_t, g, mine, None)
    last = pick(token, early, count - early)
    acc, _ = sum_rows(token, 0, mine, gate_and_up, None, 0)
    mine = last
    others += [lax.ppermute(message, "dp", swap) for message in mine]
    units = [*mine, *others]
    pieces = sum_rows(scalars, early, units, gate_and_up, acc, groups)
    returned = []
    for r, piece in enumerate(pieces):
        pairs = []
        for q in range(experts):
            for b in range(groups):
                h, e = divmod(b ^ r, experts)
                pairs.append((e * groups + 2 * q + h, q * groups + b))
        returned.append(lax.ppermute(piece, ("expert", "dp"), pairs))
    grads, _ = gradients(scalars, early, count, inv_root, x_t, g, units, grads)
    grad_tokens = combine_rows(scalars, hot, returned, experts)
    return (grad_tokens, grads[0][None], grads[1][None], grads[2][None])


def solution(mesh):
    in_specs = (
        P("dp", "expert"),
        P("dp", "expert"),
        P("dp", None),
        P("dp", None),
        P("expert", "dp", None),
        P("expert", "dp", None),
        P("expert", None, "dp"),
    )
    out_specs = (
        P("dp", "expert"),
        P("expert", "dp", None),
        P("expert", "dp", None),
        P("expert", None, "dp"),
    )
    return jax.shard_map(body, mesh=mesh, in_specs=in_specs, out_specs=out_specs, check_vma=False)
```

```python
import functools
import math

import jax
import jax.numpy as jnp
from jax import lax
from jax.experimental import pallas as pl
from jax.experimental.pallas import tpu as pltpu
from jax.sharding import PartitionSpec as P

F32 = jnp.float32
BF16 = jnp.bfloat16
LAST_DIMS = (((1,), (1,)), ((), ()))
ROWS_FIRST = (((0,), (0,)), ((), ()))
FIXED = 5
PARTS = 2
PARAMS = pltpu.CompilerParams(vmem_limit_bytes=28 * 1024 * 1024)


def dot(a, b, dims=None):
    if dims is None:
        return jnp.dot(a, b, preferred_element_type=F32)
    return lax.dot_general(a, b, dims, preferred_element_type=F32)


def cost():
    return pl.CostEstimate(flops=1024, bytes_accessed=1024, transcendentals=0)


def in_hbm(*arrays):
    return [pltpu.with_memory_space_constraint(a, pltpu.HBM) for a in arrays]


def pass_on(scalar_ref, out_ref):
    for n in range(out_ref.shape[0]):
        out_ref[n] = scalar_ref[n]


def slot_one_hot(ids_ref, experts, capacity):
    tokens = ids_ref.shape[1]
    first, second = ids_ref[0:1, :], ids_ref[1:2, :]
    expert = lax.broadcasted_iota(jnp.int32, (8 * (-(-experts // 8)), tokens), 0)
    chosen = (first == expert) | (second == expert)
    before = lax.broadcasted_iota(jnp.int32, (tokens, tokens), 0) < lax.broadcasted_iota(
        jnp.int32, (tokens, tokens), 1
    )
    place = dot(chosen.astype(F32).astype(BF16), before.astype(F32).astype(BF16))
    place = jnp.where(chosen, place, -1.0).astype(jnp.int32)
    slot = lax.broadcasted_iota(jnp.int32, (capacity, tokens), 0)
    return [slot == place[e : e + 1, :] for e in range(experts)]


def dispatch_kernel(experts, weighted, scalar_ref, ids_hbm, weights_hbm, rows_hbm, *refs):
    *messages, hot_ref, token_ref, ids_ref, weights_ref, rows_ref, scale_ref, sems = refs
    _, capacity, feats = messages[0].shape
    pass_on(scalar_ref, token_ref)
    pairs = [(ids_hbm, ids_ref), (weights_hbm, weights_ref)]
    for h in range(2):
        whole = len(rows_hbm.shape) == 3
        half = rows_hbm.at[h] if whole else rows_hbm.at[:, pl.ds(h * feats, feats)]
        pairs.append((half, rows_ref.at[h]))
    copies = [pltpu.make_async_copy(a, b, sems.at[n]) for n, (a, b) in enumerate(pairs)]
    for copy in copies:
        copy.start()
    copies[0].wait()
    copies[1].wait()
    for e, hit in enumerate(slot_one_hot(ids_ref, experts, capacity)):
        place = slice(e * capacity, (e + 1) * capacity)
        hot_ref[place, :] = hit.astype(F32).astype(BF16)
        if weighted:
            weight = jnp.where(ids_ref[0:1, :] == e, weights_ref[0:1, :], weights_ref[1:2, :])
            weight = jnp.sum(jnp.where(hit, weight, 0.0), axis=1, keepdims=True)
            scale_ref[place, :] = jnp.broadcast_to(weight, (capacity, scale_ref.shape[1]))
    places = [
        pl.ds(pl.multiple_of((scalar_ref[4] ^ t) * capacity, capacity), capacity)
        for t in range(experts)
    ]
    hot = jnp.concatenate([hot_ref[place, :] for place in places], axis=0)
    for h in range(2):
        copies[2 + h].wait()
        out = dot(hot, rows_ref[h])
        for t, place in enumerate(places):
            part = out[t * capacity : (t + 1) * capacity]
            if weighted:
                part = part * scale_ref[place, 0:1]
            messages[t][h] = part.astype(BF16)


def dispatch_rows(scalars, ids, weights, rows, experts, weighted):
    tokens, feats = rows.shape[0], rows.shape[1] // 2
    capacity = tokens // 2
    if feats % 128:
        rows = rows.reshape(tokens, 2, feats).transpose(1, 0, 2)
    *messages, hot, token = pl.pallas_call(
        functools.partial(dispatch_kernel, experts, weighted),
        out_shape=[jax.ShapeDtypeStruct((2, capacity, feats), BF16)] * experts
        + [
            jax.ShapeDtypeStruct((experts * capacity, tokens), BF16),
            jax.ShapeDtypeStruct(scalars.shape, jnp.int32),
        ],
        in_specs=[pl.BlockSpec(memory_space=pltpu.SMEM)]
        + [pl.BlockSpec(memory_space=pltpu.HBM)] * 3,
        out_specs=[pl.BlockSpec(memory_space=pltpu.VMEM)] * (experts + 1)
        + [pl.BlockSpec(memory_space=pltpu.SMEM)],
        scratch_shapes=[
            pltpu.VMEM((2, tokens), jnp.int32),
            pltpu.VMEM((2, tokens), F32),
            pltpu.VMEM((2, tokens, feats), BF16),
            pltpu.VMEM((experts * capacity, 128), F32),
            pltpu.SemaphoreType.DMA((4,)),
        ],
        compiler_params=PARAMS,
        cost_estimate=cost(),
    )(scalars, *in_hbm(ids, weights, rows))
    return messages, hot, token


def assemble_kernel(scalar_ref, *refs):
    *messages, out_ref, sems = refs

    def copy(t, message):
        return pltpu.make_async_copy(message, out_ref.at[t ^ scalar_ref[4]], sems.at[t])

    for t, message in enumerate(messages):
        copy(t, message).start()
    for t, message in enumerate(messages):
        copy(t, message).wait()


def assemble(scalars, messages):
    return pl.pallas_call(
        assemble_kernel,
        out_shape=jax.ShapeDtypeStruct((len(messages), *messages[0].shape), BF16),
        in_specs=[pl.BlockSpec(memory_space=pltpu.SMEM)]
        + [pl.BlockSpec(memory_space=pl.ANY)] * len(messages),
        scratch_shapes=[pltpu.SemaphoreType.DMA((len(messages),))],
        compiler_params=PARAMS,
        cost_estimate=cost(),
    )(scalars, *messages)


def combine_kernel(experts, scalar_ref, hot_ref, *refs):
    pieces, (out_ref, rows_ref, sems) = refs[:-3], refs[-3:]
    capacity = pieces[0].shape[0]
    at = pl.program_id(0)

    def copy(n):
        return pltpu.make_async_copy(
            pieces[n], rows_ref.at[pl.ds(n * capacity, capacity)], sems.at[n]
        )

    @pl.when(at == 0)
    def _():
        for n in range(len(pieces)):
            copy(n).start()

    hot = jnp.concatenate(
        [
            hot_ref[pl.ds(pl.multiple_of((scalar_ref[2] ^ n) * capacity, capacity), capacity), :]
            for n in range(experts)
        ],
        axis=0,
    )
    for half in range(2):

        @pl.when(at == half)
        def _():
            for n in range(half * experts, (half + 1) * experts):
                copy(n).wait()
            rows = rows_ref[half * experts * capacity : (half + 1) * experts * capacity, :]
            out = dot(hot, rows, ROWS_FIRST).astype(BF16)
            out_ref[...] = out.reshape(out_ref.shape)


def combine_rows(scalars, hot, pieces, experts):
    tokens = hot.shape[1]
    capacity, feats = pieces[0].shape
    if feats % 128:
        out_shape = jax.ShapeDtypeStruct((2, tokens, feats), BF16)
        out_spec = pl.BlockSpec((1, tokens, feats), lambda a, c: (a ^ c[3], 0, 0))
    else:
        out_shape = jax.ShapeDtypeStruct((tokens, 2 * feats), BF16)
        out_spec = pl.BlockSpec((tokens, feats), lambda a, c: (0, a ^ c[3]))
    out = pl.pallas_call(
        functools.partial(combine_kernel, experts),
        out_shape=out_shape,
        grid_spec=pltpu.PrefetchScalarGridSpec(
            num_scalar_prefetch=1,
            grid=(2,),
            in_specs=[pl.BlockSpec((experts * capacity, tokens), lambda a, c: (0, 0))]
            + [pl.BlockSpec(memory_space=pltpu.HBM)] * len(pieces),
            out_specs=out_spec,
            scratch_shapes=[
                pltpu.VMEM((len(pieces) * capacity, feats), BF16),
                pltpu.SemaphoreType.DMA((len(pieces),)),
            ],
        ),
        compiler_params=PARAMS,
        cost_estimate=cost(),
    )(scalars, *in_hbm(hot, *pieces))
    if feats % 128:
        out = out.transpose(1, 0, 2).reshape(tokens, 2 * feats)
    return out


def gate_up_kernel(scalar_ref, x_ref, wg_ref, wu_ref, *outs):
    width = wg_ref.shape[1]

    @pl.when((pl.program_id(0) == 0) & (pl.program_id(1) == 0))
    def _():
        outs[2][...] = x_ref[...].T

    for own in range(2):

        @pl.when(pl.program_id(1) == own)
        def _():
            outs[own][0, :, :width] = dot(x_ref[...], wg_ref[...]).astype(BF16)
            outs[own][0, :, width:] = dot(x_ref[...], wu_ref[...]).astype(BF16)


def gate_up(scalars, x, w_gate, w_up, count):
    slots, feats = x.shape
    width = w_gate.shape[1] // (2 * count)
    out = jax.ShapeDtypeStruct((count, slots, 2 * width), BF16)
    out_spec = pl.BlockSpec((1, slots, 2 * width), lambda i, own, c: (i, 0, 0))
    column = pl.BlockSpec(
        (feats, width), lambda i, own, c: (0, c[FIXED + 2 * count + own * count + i])
    )
    return pl.pallas_call(
        gate_up_kernel,
        out_shape=(out, out, jax.ShapeDtypeStruct((feats, slots), BF16)),
        grid_spec=pltpu.PrefetchScalarGridSpec(
            num_scalar_prefetch=1,
            grid=(count, 2),
            in_specs=[pl.BlockSpec((slots, feats), lambda i, own, c: (0, 0)), column, column],
            out_specs=(
                out_spec,
                out_spec,
                pl.BlockSpec((feats, slots), lambda i, own, c: (0, 0)),
            ),
        ),
        compiler_params=PARAMS,
        cost_estimate=cost(),
    )(scalars, x, *in_hbm(w_gate, w_up))


def back_kernel(scalar_ref, g_ref, wd_ref, *refs):
    *shares, out_ref = refs
    back = dot(g_ref[...], wd_ref[...], LAST_DIMS)
    if not shares:
        out_ref[0] = back.astype(BF16)
        return
    sib_b, own_gu, sib_gu = shares
    width = back.shape[1]
    both = own_gu[0].astype(F32) + sib_gu[0].astype(F32)
    out_ref[0, :, : 2 * width] = both.astype(BF16)
    out_ref[0, :, 2 * width :] = (back + sib_b[0].astype(F32)).astype(BF16)


def back_rows(scalars, g, w_down, begin, size, count, shares):
    slots, feats = g.shape
    width = w_down.shape[0] // (2 * count)
    own = bool(shares)
    row = pl.BlockSpec(
        (width, feats), lambda i, c: (c[FIXED + 2 * count + own * count + begin + i], 0)
    )
    in_specs = [pl.BlockSpec((slots, feats), lambda i, c: (0, 0)), row]
    if own:
        in_specs.append(pl.BlockSpec((1, slots, width), lambda i, c: (i, 0, 0)))
        in_specs += [pl.BlockSpec((1, slots, 2 * width), lambda i, c: (begin + i, 0, 0))] * 2
    cols = (3 if own else 1) * width
    return pl.pallas_call(
        back_kernel,
        out_shape=jax.ShapeDtypeStruct((size, slots, cols), BF16),
        grid_spec=pltpu.PrefetchScalarGridSpec(
            num_scalar_prefetch=1,
            grid=(size,),
            in_specs=in_specs,
            out_specs=pl.BlockSpec((1, slots, cols), lambda i, c: (i, 0, 0)),
        ),
        compiler_params=PARAMS,
        cost_estimate=cost(),
    )(scalars, g, *in_hbm(w_down), *shares)


def activate(gate, upper, back):
    sig = jax.nn.sigmoid(gate)
    gated = gate * sig
    return (
        (gated * upper).astype(BF16),
        (back * upper * sig * (1.0 + gate * (1.0 - sig))).astype(BF16),
        (back * gated).astype(BF16),
    )


def hop_kernel(plan, scalar_ref, *refs):
    slot, count, chips, came = plan
    sums_ref = refs[-2]
    recv_ref = refs[0] if came else None
    send_ref = refs[-1]
    at = scalar_ref[0]
    width = send_ref.shape[1] // 3
    summing = (at <= slot) & (slot - at < count)

    def total(part):
        columns = slice(part * width, (part + 1) * width)
        value = sums_ref[0, :, columns].astype(F32)
        if came:
            value += jnp.where(at > 0, recv_ref[:, columns].astype(F32), 0.0)
        return value

    @pl.when(summing & (at < chips - 1))
    def _():
        for part in range(3):
            send_ref[:, part * width : (part + 1) * width] = total(part).astype(BF16)

    @pl.when(summing & (at == chips - 1))
    def _():
        for part, value in enumerate(activate(total(0), total(1), total(2))):
            send_ref[:, part * width : (part + 1) * width] = value

    if came:

        @pl.when(jnp.logical_not(summing))
        def _():
            send_ref[...] = recv_ref[...]


def hop(scalars, slot, count, chips, recv, sums, part):
    array, i = sums
    rows, cols = array.shape[1] // PARTS, array.shape[2]
    message = pl.BlockSpec((rows, cols), lambda n, c: (0, 0))
    operands, in_specs = [], []
    if recv is not None:
        operands.append(recv)
        in_specs.append(message)
    operands.append(array)
    in_specs.append(pl.BlockSpec((1, rows, cols), lambda n, c: (i, part, 0)))
    plan = (slot, count, chips, recv is not None)
    return pl.pallas_call(
        functools.partial(hop_kernel, plan),
        out_shape=jax.ShapeDtypeStruct((rows, cols), BF16),
        grid_spec=pltpu.PrefetchScalarGridSpec(
            num_scalar_prefetch=1,
            grid=(1,),
            in_specs=in_specs,
            out_specs=message,
        ),
        compiler_params=PARAMS,
        cost_estimate=cost(),
    )(scalars, *operands)


def choose_kernel(wanted, hops, scalar_ref, *refs):
    *candidates, sems = refs
    candidates, outs = candidates[:-wanted], candidates[-wanted:]
    rows = candidates[0].shape[0]

    def copy(k, n, part):
        return pltpu.make_async_copy(
            candidates[(k + n) * PARTS + part],
            outs[k].at[pl.ds(part * rows, rows)],
            sems.at[k, part],
        )

    for n in range(hops):

        @pl.when(scalar_ref[0] == n)
        def _():
            for k in range(wanted):
                for part in range(PARTS):
                    copy(k, n, part).start()

    for k in range(wanted):
        for part in range(PARTS):
            copy(k, 0, part).wait()


def choose(place, wanted, hops, candidates):
    rows, cols = candidates[0].shape
    return pl.pallas_call(
        functools.partial(choose_kernel, wanted, hops),
        out_shape=[jax.ShapeDtypeStruct((rows * PARTS, cols), BF16)] * wanted,
        in_specs=[pl.BlockSpec(memory_space=pltpu.SMEM)]
        + [pl.BlockSpec(memory_space=pl.ANY)] * len(candidates),
        scratch_shapes=[pltpu.SemaphoreType.DMA((wanted, PARTS))],
        compiler_params=PARAMS,
        cost_estimate=cost(),
    )(place, *candidates)


def gradients_kernel(units, scale, first, scalar_ref, xt_ref, g_ref, *refs):
    messages, refs = refs[:units], refs[units if first else units + 3 :]
    gg_ref, gu_ref, gd_ref, token_ref = refs
    width = gg_ref.shape[1]
    pass_on(scalar_ref, token_ref)
    for u in range(units):

        @pl.when(pl.program_id(0) == u)
        def _():
            both = dot(xt_ref[...], messages[u][:, width:]) * scale
            gg_ref[...] = both[:, :width].astype(BF16)
            gu_ref[...] = both[:, width:].astype(BF16)
            scaled = messages[u][:, :width]
            gd_ref[...] = (dot(scaled, g_ref[...], ROWS_FIRST) * scale).astype(BF16)


def gradients(scalars, begin, count, scale, x_t, g, messages, grads):
    slots, feats = g.shape
    width = messages[0].shape[1] // 3
    hidden = 2 * count * width
    units = len(messages)

    def at(u, c):
        return c[FIXED + begin + u]

    column = pl.BlockSpec((feats, width), lambda u, c: (0, at(u, c)))
    in_specs = [
        pl.BlockSpec((feats, slots), lambda u, c: (0, 0)),
        pl.BlockSpec((slots, feats), lambda u, c: (0, 0)),
    ]
    in_specs += [pl.BlockSpec((slots, 3 * width), lambda u, c: (0, 0))] * units
    operands = [x_t, g, *messages]
    aliases = {}
    if grads is not None:
        aliases = {len(operands) + 1 + n: n for n in range(3)}
        operands += grads
        in_specs += [pl.BlockSpec(memory_space=pl.ANY)] * 3
    *grads, token = pl.pallas_call(
        functools.partial(gradients_kernel, units, scale, grads is None),
        out_shape=[
            jax.ShapeDtypeStruct((feats, hidden), BF16),
            jax.ShapeDtypeStruct((feats, hidden), BF16),
            jax.ShapeDtypeStruct((hidden, feats), BF16),
            jax.ShapeDtypeStruct(scalars.shape, jnp.int32),
        ],
        grid_spec=pltpu.PrefetchScalarGridSpec(
            num_scalar_prefetch=1,
            grid=(units,),
            in_specs=in_specs,
            out_specs=[
                column,
                column,
                pl.BlockSpec((width, feats), lambda u, c: (at(u, c), 0)),
                pl.BlockSpec(memory_space=pltpu.SMEM),
            ],
        ),
        input_output_aliases=aliases,
        compiler_params=PARAMS,
        cost_estimate=cost(),
    )(scalars, *operands)
    return grads, token


def sum_rows_kernel(units, pieces, scalar_ref, *refs):
    messages, weights, refs = refs[:units], refs[units : 3 * units], refs[3 * units :]
    width = weights[0].shape[1]
    both = jnp.concatenate([message[:, width:] for message in messages], axis=1)
    part = dot(both, jnp.concatenate([w[...] for w in weights], axis=1), LAST_DIMS)
    if not pieces:
        out_ref, token_ref = refs
        out_ref[...] = part
        pass_on(scalar_ref, token_ref)
        return
    acc_in, *outs, acc = refs
    acc[...] = acc_in[...] + part
    size = outs[0].shape[0]
    for n, out in enumerate(outs):
        start = pl.multiple_of((scalar_ref[1] ^ n) * size, size)
        out[...] = acc[pl.ds(start, size), :].astype(BF16)


def sum_rows(scalars, begin, messages, weights, acc, pieces):
    slots, width = messages[0].shape[0], messages[0].shape[1] // 3
    feats = weights[0].shape[0]
    units = len(messages)
    in_specs = [pl.BlockSpec((slots, 3 * width), lambda n, c: (0, 0))] * units
    operands = list(messages)
    for u in range(units):
        column = pl.BlockSpec((feats, width), lambda n, c, u=u: (0, c[FIXED + begin + u]))
        operands += in_hbm(*weights)
        in_specs += [column, column]
    whole = pl.BlockSpec((slots, feats), lambda n, c: (0, 0))
    if pieces:
        operands.append(acc)
        in_specs.append(whole)
        out_shape = [jax.ShapeDtypeStruct((slots // pieces, feats), BF16)] * pieces
        out_specs = [pl.BlockSpec((slots // pieces, feats), lambda n, c: (0, 0))] * pieces
        scratch = [pltpu.VMEM((slots, feats), F32)]
    else:
        out_shape = [
            jax.ShapeDtypeStruct((slots, feats), F32),
            jax.ShapeDtypeStruct(scalars.shape, jnp.int32),
        ]
        out_specs = [whole, pl.BlockSpec(memory_space=pltpu.SMEM)]
        scratch = []
    return pl.pallas_call(
        functools.partial(sum_rows_kernel, units, pieces),
        out_shape=out_shape,
        grid_spec=pltpu.PrefetchScalarGridSpec(
            num_scalar_prefetch=1,
            grid=(1,),
            in_specs=in_specs,
            out_specs=out_specs,
            scratch_shapes=scratch,
        ),
        compiler_params=PARAMS,
        cost_estimate=cost(),
    )(scalars, *operands)


def body(tokens, grad_out, expert_ids, route_weights, w_gate, w_up, w_down):
    experts = lax.axis_size("expert")
    groups = lax.axis_size("dp")
    tok_rows = tokens.shape[0]
    feats = w_gate.shape[1]
    capacity = tok_rows // 2
    chips = groups // 2
    count = chips
    assert groups == 2 * experts and tokens.shape[1] == 2 * feats
    inv_root = 1.0 / math.sqrt(tok_rows * groups)
    expert = lax.axis_index("expert").astype(jnp.int32)
    block = lax.axis_index("dp").astype(jnp.int32)
    chip, core = block // 2, block % 2
    along = jnp.where(core == 0, chip, chips - 1 - chip)
    w_gate, w_up, w_down = w_gate[0], w_up[0], w_down[0]
    ids, weights = expert_ids.T, route_weights.T

    swap = [(j, j ^ 1) for j in range(groups)]
    up = [2 * z for z in range(chips)]
    circle = up + [j + 1 for j in reversed(up)]
    ring = list(zip(circle, circle[1:] + circle[:1]))

    scalars = [along, expert + experts * core, block % experts, block // experts, expert]
    scalars += [(d ^ 1 ^ core) * count + k for d in range(2) for k in range(count)]
    scalars += [(1 - core) * count + (i - (chips - 1 - along)) % count for i in range(count)]
    scalars += [core * count + (i - along) % count for i in range(count)]
    scalars = jnp.stack(scalars).astype(jnp.int32)

    def exchange(messages):
        came = [messages[0]]
        for t in range(1, experts):
            came.append(lax.ppermute(messages[t], "expert", [(q, q ^ t) for q in range(experts)]))
        blocks = assemble(scalars, came).reshape(groups, capacity, feats)
        blocks = lax.all_to_all(blocks, "dp", split_axis=0, concat_axis=0, tiled=True)
        return blocks.reshape(groups * capacity, feats)

    x_messages, hot, token = dispatch_rows(scalars, ids, weights, tokens, experts, False)
    g_messages, _, _ = dispatch_rows(token, ids, weights, grad_out, experts, True)
    x = exchange(x_messages)
    g = exchange(g_messages)

    other_gu, own_gu, x_t = gate_up(scalars, x, w_gate, w_up, count)
    sib_gu = lax.ppermute(other_gu, "dp", swap)
    spans = [(i, 1) for i in range(count)]
    others = [
        lax.ppermute(back_rows(scalars, g, w_down, begin, size, count, ()), "dp", swap)
        for begin, size in spans
    ]
    sums = []
    for (begin, size), sib_b in zip(spans, others):
        shares = (sib_b, own_gu, sib_gu)
        both = back_rows(scalars, g, w_down, begin, size, count, shares)
        sums += [(both, i) for i in range(size)]

    slots = 2 * count + chips - 2
    first_back = chips - 1 + count
    recv = []
    gate_and_up = (w_gate, w_up)
    place = along.astype(jnp.int32)[None]
    for s in range(slots):
        came = []
        for part in range(PARTS):
            send = recv[s - 1][part] if s else None
            if s < first_back:
                send = hop(place, s, count, chips, send, sums[s % count], part)
            came.append(lax.ppermute(send, "dp", ring))
        recv.append(came)

    def pick(token, begin, wanted):
        found = recv[count - 1 + begin : count - 1 + begin + chips + wanted - 1]
        return choose(token, wanted, chips, [part for came in found for part in came])

    early = count - 1
    mine = pick(place, 0, early)
    others = [lax.ppermute(message, "dp", swap) for message in mine]
    grads, token = gradients(scalars, 0, count, inv_root, x_t, g, mine, None)
    last = pick(token, early, count - early)
    acc, _ = sum_rows(token, 0, mine, gate_and_up, None, 0)
    mine = last
    others += [lax.ppermute(message, "dp", swap) for message in mine]
    units = [*mine, *others]
    pieces = sum_rows(scalars, early, units, gate_and_up, acc, groups)
    returned = []
    for r, piece in enumerate(pieces):
        pairs = []
        for q in range(experts):
            for b in range(groups):
                h, e = divmod(b ^ r, experts)
                pairs.append((e * groups + 2 * q + h, q * groups + b))
        returned.append(lax.ppermute(piece, ("expert", "dp"), pairs))
    grads, _ = gradients(scalars, early, count, inv_root, x_t, g, units, grads)
    grad_tokens = combine_rows(scalars, hot, returned, experts)
    return (grad_tokens, grads[0][None], grads[1][None], grads[2][None])


def solution(mesh):
    in_specs = (
        P("dp", "expert"),
        P("dp", "expert"),
        P("dp", None),
        P("dp", None),
        P("expert", "dp", None),
        P("expert", "dp", None),
        P("expert", None, "dp"),
    )
    out_specs = (
        P("dp", "expert"),
        P("expert", "dp", None),
        P("expert", "dp", None),
        P("expert", None, "dp"),
    )
    return jax.shard_map(body, mesh=mesh, in_specs=in_specs, out_specs=out_specs, check_vma=False)
```

```python
import functools
import math

import jax
import jax.numpy as jnp
from jax import lax
from jax.experimental import pallas as pl
from jax.experimental.pallas import tpu as pltpu
from jax.sharding import PartitionSpec as P

F32 = jnp.float32
BF16 = jnp.bfloat16
LAST_DIMS = (((1,), (1,)), ((), ()))
ROWS_FIRST = (((0,), (0,)), ((), ()))
FIXED = 5
PARTS = 2
PARAMS = pltpu.CompilerParams(vmem_limit_bytes=28 * 1024 * 1024)


def dot(a, b, dims=None):
    if dims is None:
        return jnp.dot(a, b, preferred_element_type=F32)
    return lax.dot_general(a, b, dims, preferred_element_type=F32)


def cost():
    return pl.CostEstimate(flops=1024, bytes_accessed=1024, transcendentals=0)


def in_hbm(*arrays):
    return [pltpu.with_memory_space_constraint(a, pltpu.HBM) for a in arrays]


def pass_on(scalar_ref, out_ref):
    for n in range(out_ref.shape[0]):
        out_ref[n] = scalar_ref[n]


def slot_one_hot(ids_ref, experts, capacity):
    tokens = ids_ref.shape[1]
    first, second = ids_ref[0:1, :], ids_ref[1:2, :]
    expert = lax.broadcasted_iota(jnp.int32, (8 * (-(-experts // 8)), tokens), 0)
    chosen = (first == expert) | (second == expert)
    before = lax.broadcasted_iota(jnp.int32, (tokens, tokens), 0) < lax.broadcasted_iota(
        jnp.int32, (tokens, tokens), 1
    )
    place = dot(chosen.astype(F32).astype(BF16), before.astype(F32).astype(BF16))
    place = jnp.where(chosen, place, -1.0).astype(jnp.int32)
    slot = lax.broadcasted_iota(jnp.int32, (capacity, tokens), 0)
    return [slot == place[e : e + 1, :] for e in range(experts)]


def dispatch_kernel(experts, weighted, scalar_ref, ids_hbm, weights_hbm, rows_hbm, *refs):
    *messages, hot_ref, token_ref, ids_ref, weights_ref, rows_ref, scale_ref, sems = refs
    _, capacity, feats = messages[0].shape
    pass_on(scalar_ref, token_ref)
    pairs = [(ids_hbm, ids_ref), (weights_hbm, weights_ref)]
    for h in range(2):
        whole = len(rows_hbm.shape) == 3
        half = rows_hbm.at[h] if whole else rows_hbm.at[:, pl.ds(h * feats, feats)]
        pairs.append((half, rows_ref.at[h]))
    copies = [pltpu.make_async_copy(a, b, sems.at[n]) for n, (a, b) in enumerate(pairs)]
    for copy in copies:
        copy.start()
    copies[0].wait()
    copies[1].wait()
    for e, hit in enumerate(slot_one_hot(ids_ref, experts, capacity)):
        place = slice(e * capacity, (e + 1) * capacity)
        hot_ref[place, :] = hit.astype(F32).astype(BF16)
        if weighted:
            weight = jnp.where(ids_ref[0:1, :] == e, weights_ref[0:1, :], weights_ref[1:2, :])
            weight = jnp.sum(jnp.where(hit, weight, 0.0), axis=1, keepdims=True)
            scale_ref[place, :] = jnp.broadcast_to(weight, (capacity, scale_ref.shape[1]))
    places = [
        pl.ds(pl.multiple_of((scalar_ref[4] ^ t) * capacity, capacity), capacity)
        for t in range(experts)
    ]
    hot = jnp.concatenate([hot_ref[place, :] for place in places], axis=0)
    for h in range(2):
        copies[2 + h].wait()
        out = dot(hot, rows_ref[h])
        for t, place in enumerate(places):
            part = out[t * capacity : (t + 1) * capacity]
            if weighted:
                part = part * scale_ref[place, 0:1]
            messages[t][h] = part.astype(BF16)


def dispatch_rows(scalars, ids, weights, rows, experts, weighted):
    tokens, feats = rows.shape[0], rows.shape[1] // 2
    capacity = tokens // 2
    if feats % 128:
        rows = rows.reshape(tokens, 2, feats).transpose(1, 0, 2)
    *messages, hot, token = pl.pallas_call(
        functools.partial(dispatch_kernel, experts, weighted),
        out_shape=[jax.ShapeDtypeStruct((2, capacity, feats), BF16)] * experts
        + [
            jax.ShapeDtypeStruct((experts * capacity, tokens), BF16),
            jax.ShapeDtypeStruct(scalars.shape, jnp.int32),
        ],
        in_specs=[pl.BlockSpec(memory_space=pltpu.SMEM)]
        + [pl.BlockSpec(memory_space=pltpu.HBM)] * 3,
        out_specs=[pl.BlockSpec(memory_space=pltpu.VMEM)] * (experts + 1)
        + [pl.BlockSpec(memory_space=pltpu.SMEM)],
        scratch_shapes=[
            pltpu.VMEM((2, tokens), jnp.int32),
            pltpu.VMEM((2, tokens), F32),
            pltpu.VMEM((2, tokens, feats), BF16),
            pltpu.VMEM((experts * capacity, 128), F32),
            pltpu.SemaphoreType.DMA((4,)),
        ],
        compiler_params=PARAMS,
        cost_estimate=cost(),
    )(scalars, *in_hbm(ids, weights, rows))
    return messages, hot, token


def assemble_kernel(scalar_ref, *refs):
    *messages, out_ref, sems = refs

    def copy(t, message):
        return pltpu.make_async_copy(message, out_ref.at[t ^ scalar_ref[4]], sems.at[t])

    for t, message in enumerate(messages):
        copy(t, message).start()
    for t, message in enumerate(messages):
        copy(t, message).wait()


def assemble(scalars, messages):
    return pl.pallas_call(
        assemble_kernel,
        out_shape=jax.ShapeDtypeStruct((len(messages), *messages[0].shape), BF16),
        in_specs=[pl.BlockSpec(memory_space=pltpu.SMEM)]
        + [pl.BlockSpec(memory_space=pl.ANY)] * len(messages),
        scratch_shapes=[pltpu.SemaphoreType.DMA((len(messages),))],
        compiler_params=PARAMS,
        cost_estimate=cost(),
    )(scalars, *messages)


def combine_kernel(experts, scalar_ref, hot_ref, *refs):
    pieces, (out_ref, rows_ref, sems) = refs[:-3], refs[-3:]
    capacity = pieces[0].shape[0]
    at = pl.program_id(0)

    def copy(n):
        return pltpu.make_async_copy(
            pieces[n], rows_ref.at[pl.ds(n * capacity, capacity)], sems.at[n]
        )

    @pl.when(at == 0)
    def _():
        for n in range(len(pieces)):
            copy(n).start()

    hot = jnp.concatenate(
        [
            hot_ref[pl.ds(pl.multiple_of((scalar_ref[2] ^ n) * capacity, capacity), capacity), :]
            for n in range(experts)
        ],
        axis=0,
    )
    for half in range(2):

        @pl.when(at == half)
        def _():
            for n in range(half * experts, (half + 1) * experts):
                copy(n).wait()
            rows = rows_ref[half * experts * capacity : (half + 1) * experts * capacity, :]
            out = dot(hot, rows, ROWS_FIRST).astype(BF16)
            out_ref[...] = out.reshape(out_ref.shape)


def combine_rows(scalars, hot, pieces, experts):
    tokens = hot.shape[1]
    capacity, feats = pieces[0].shape
    if feats % 128:
        out_shape = jax.ShapeDtypeStruct((2, tokens, feats), BF16)
        out_spec = pl.BlockSpec((1, tokens, feats), lambda a, c: (a ^ c[3], 0, 0))
    else:
        out_shape = jax.ShapeDtypeStruct((tokens, 2 * feats), BF16)
        out_spec = pl.BlockSpec((tokens, feats), lambda a, c: (0, a ^ c[3]))
    out = pl.pallas_call(
        functools.partial(combine_kernel, experts),
        out_shape=out_shape,
        grid_spec=pltpu.PrefetchScalarGridSpec(
            num_scalar_prefetch=1,
            grid=(2,),
            in_specs=[pl.BlockSpec((experts * capacity, tokens), lambda a, c: (0, 0))]
            + [pl.BlockSpec(memory_space=pltpu.HBM)] * len(pieces),
            out_specs=out_spec,
            scratch_shapes=[
                pltpu.VMEM((len(pieces) * capacity, feats), BF16),
                pltpu.SemaphoreType.DMA((len(pieces),)),
            ],
        ),
        compiler_params=PARAMS,
        cost_estimate=cost(),
    )(scalars, hot, *in_hbm(*pieces))
    if feats % 128:
        out = out.transpose(1, 0, 2).reshape(tokens, 2 * feats)
    return out


def gate_up_kernel(scalar_ref, x_ref, wg_ref, wu_ref, *outs):
    width = wg_ref.shape[1]

    @pl.when((pl.program_id(0) == 0) & (pl.program_id(1) == 0))
    def _():
        outs[2][...] = x_ref[...].T

    for own in range(2):

        @pl.when(pl.program_id(1) == own)
        def _():
            outs[own][0, :, :width] = dot(x_ref[...], wg_ref[...]).astype(BF16)
            outs[own][0, :, width:] = dot(x_ref[...], wu_ref[...]).astype(BF16)


def gate_up(scalars, x, w_gate, w_up, count):
    slots, feats = x.shape
    width = w_gate.shape[1] // (2 * count)
    out = jax.ShapeDtypeStruct((count, slots, 2 * width), BF16)
    out_spec = pl.BlockSpec((1, slots, 2 * width), lambda i, own, c: (i, 0, 0))
    column = pl.BlockSpec(
        (feats, width), lambda i, own, c: (0, c[FIXED + 2 * count + own * count + i])
    )
    return pl.pallas_call(
        gate_up_kernel,
        out_shape=(out, out, jax.ShapeDtypeStruct((feats, slots), BF16)),
        grid_spec=pltpu.PrefetchScalarGridSpec(
            num_scalar_prefetch=1,
            grid=(count, 2),
            in_specs=[pl.BlockSpec((slots, feats), lambda i, own, c: (0, 0)), column, column],
            out_specs=(
                out_spec,
                out_spec,
                pl.BlockSpec((feats, slots), lambda i, own, c: (0, 0)),
            ),
        ),
        compiler_params=PARAMS,
        cost_estimate=pl.CostEstimate(
            flops=8 * count * slots * feats * width,
            bytes_accessed=8 * count * width * (feats + slots),
            transcendentals=0,
        ),
    )(scalars, x, *in_hbm(w_gate, w_up))


def back_kernel(scalar_ref, g_ref, wd_ref, *refs):
    *shares, out_ref = refs
    back = dot(g_ref[...], wd_ref[...], LAST_DIMS)
    if not shares:
        out_ref[0] = back.astype(BF16)
        return
    sib_b, own_gu, sib_gu = shares
    width = back.shape[1]
    both = own_gu[0].astype(F32) + sib_gu[0].astype(F32)
    out_ref[0, :, : 2 * width] = both.astype(BF16)
    out_ref[0, :, 2 * width :] = (back + sib_b[0].astype(F32)).astype(BF16)


def back_rows(scalars, g, w_down, begin, size, count, shares):
    slots, feats = g.shape
    width = w_down.shape[0] // (2 * count)
    own = bool(shares)
    row = pl.BlockSpec(
        (width, feats), lambda i, c: (c[FIXED + 2 * count + own * count + begin + i], 0)
    )
    in_specs = [pl.BlockSpec((slots, feats), lambda i, c: (0, 0)), row]
    if own:
        in_specs.append(pl.BlockSpec((1, slots, width), lambda i, c: (i, 0, 0)))
        in_specs += [pl.BlockSpec((1, slots, 2 * width), lambda i, c: (begin + i, 0, 0))] * 2
    cols = (3 if own else 1) * width
    return pl.pallas_call(
        back_kernel,
        out_shape=jax.ShapeDtypeStruct((size, slots, cols), BF16),
        grid_spec=pltpu.PrefetchScalarGridSpec(
            num_scalar_prefetch=1,
            grid=(size,),
            in_specs=in_specs,
            out_specs=pl.BlockSpec((1, slots, cols), lambda i, c: (i, 0, 0)),
        ),
        compiler_params=PARAMS,
        cost_estimate=cost(),
    )(scalars, g, *in_hbm(w_down), *shares)


def activate(gate, upper, back):
    sig = jax.nn.sigmoid(gate)
    gated = gate * sig
    return (
        (gated * upper).astype(BF16),
        (back * upper * sig * (1.0 + gate * (1.0 - sig))).astype(BF16),
        (back * gated).astype(BF16),
    )


def hop_kernel(plan, scalar_ref, *refs):
    slot, count, chips, came = plan
    sums_ref = refs[-2]
    recv_ref = refs[0] if came else None
    send_ref = refs[-1]
    at = scalar_ref[0]
    width = send_ref.shape[1] // 3
    summing = (at <= slot) & (slot - at < count)

    def total(part):
        columns = slice(part * width, (part + 1) * width)
        value = sums_ref[0, :, columns].astype(F32)
        if came:
            value += jnp.where(at > 0, recv_ref[:, columns].astype(F32), 0.0)
        return value

    @pl.when(summing & (at < chips - 1))
    def _():
        for part in range(3):
            send_ref[:, part * width : (part + 1) * width] = total(part).astype(BF16)

    @pl.when(summing & (at == chips - 1))
    def _():
        for part, value in enumerate(activate(total(0), total(1), total(2))):
            send_ref[:, part * width : (part + 1) * width] = value

    if came:

        @pl.when(jnp.logical_not(summing))
        def _():
            send_ref[...] = recv_ref[...]


def hop(scalars, slot, count, chips, recv, sums, part):
    array, i = sums
    rows, cols = array.shape[1] // PARTS, array.shape[2]
    message = pl.BlockSpec((rows, cols), lambda n, c: (0, 0))
    operands, in_specs = [], []
    if recv is not None:
        operands.append(recv)
        in_specs.append(message)
    operands.append(array)
    in_specs.append(pl.BlockSpec((1, rows, cols), lambda n, c: (i, part, 0)))
    plan = (slot, count, chips, recv is not None)
    return pl.pallas_call(
        functools.partial(hop_kernel, plan),
        out_shape=jax.ShapeDtypeStruct((rows, cols), BF16),
        grid_spec=pltpu.PrefetchScalarGridSpec(
            num_scalar_prefetch=1,
            grid=(1,),
            in_specs=in_specs,
            out_specs=message,
        ),
        compiler_params=PARAMS,
        cost_estimate=cost(),
    )(scalars, *operands)


def choose_kernel(wanted, hops, scalar_ref, *refs):
    *candidates, sems = refs
    candidates, outs = candidates[:-wanted], candidates[-wanted:]
    rows = candidates[0].shape[0]

    def copy(k, n, part):
        return pltpu.make_async_copy(
            candidates[(k + n) * PARTS + part],
            outs[k].at[pl.ds(part * rows, rows)],
            sems.at[k, part],
        )

    for n in range(hops):

        @pl.when(scalar_ref[0] == n)
        def _():
            for k in range(wanted):
                for part in range(PARTS):
                    copy(k, n, part).start()

    for k in range(wanted):
        for part in range(PARTS):
            copy(k, 0, part).wait()


def choose(place, wanted, hops, candidates):
    rows, cols = candidates[0].shape
    return pl.pallas_call(
        functools.partial(choose_kernel, wanted, hops),
        out_shape=[jax.ShapeDtypeStruct((rows * PARTS, cols), BF16)] * wanted,
        in_specs=[pl.BlockSpec(memory_space=pltpu.SMEM)]
        + [pl.BlockSpec(memory_space=pl.ANY)] * len(candidates),
        scratch_shapes=[pltpu.SemaphoreType.DMA((wanted, PARTS))],
        compiler_params=PARAMS,
        cost_estimate=cost(),
    )(place, *candidates)


def gradients_kernel(units, scale, first, scalar_ref, xt_ref, g_ref, *refs):
    messages, refs = refs[:units], refs[units if first else units + 3 :]
    gg_ref, gu_ref, gd_ref, token_ref = refs
    width = gg_ref.shape[1]
    pass_on(scalar_ref, token_ref)
    for u in range(units):

        @pl.when(pl.program_id(0) == u)
        def _():
            both = dot(xt_ref[...], messages[u][:, width:]) * scale
            gg_ref[...] = both[:, :width].astype(BF16)
            gu_ref[...] = both[:, width:].astype(BF16)
            scaled = messages[u][:, :width]
            gd_ref[...] = (dot(scaled, g_ref[...], ROWS_FIRST) * scale).astype(BF16)


def gradients(scalars, begin, count, scale, x_t, g, messages, grads):
    slots, feats = g.shape
    width = messages[0].shape[1] // 3
    hidden = 2 * count * width
    units = len(messages)

    def at(u, c):
        return c[FIXED + begin + u]

    column = pl.BlockSpec((feats, width), lambda u, c: (0, at(u, c)))
    in_specs = [
        pl.BlockSpec((feats, slots), lambda u, c: (0, 0)),
        pl.BlockSpec((slots, feats), lambda u, c: (0, 0)),
    ]
    in_specs += [pl.BlockSpec((slots, 3 * width), lambda u, c: (0, 0))] * units
    operands = [x_t, g, *messages]
    aliases = {}
    if grads is not None:
        aliases = {len(operands) + 1 + n: n for n in range(3)}
        operands += grads
        in_specs += [pl.BlockSpec(memory_space=pl.ANY)] * 3
    *grads, token = pl.pallas_call(
        functools.partial(gradients_kernel, units, scale, grads is None),
        out_shape=[
            jax.ShapeDtypeStruct((feats, hidden), BF16),
            jax.ShapeDtypeStruct((feats, hidden), BF16),
            jax.ShapeDtypeStruct((hidden, feats), BF16),
            jax.ShapeDtypeStruct(scalars.shape, jnp.int32),
        ],
        grid_spec=pltpu.PrefetchScalarGridSpec(
            num_scalar_prefetch=1,
            grid=(units,),
            in_specs=in_specs,
            out_specs=[
                column,
                column,
                pl.BlockSpec((width, feats), lambda u, c: (at(u, c), 0)),
                pl.BlockSpec(memory_space=pltpu.SMEM),
            ],
        ),
        input_output_aliases=aliases,
        compiler_params=PARAMS,
        cost_estimate=cost(),
    )(scalars, *operands)
    return grads, token


def sum_rows_kernel(units, pieces, scalar_ref, *refs):
    messages, weights, refs = refs[:units], refs[units : 3 * units], refs[3 * units :]
    width = weights[0].shape[1]
    both = jnp.concatenate([message[:, width:] for message in messages], axis=1)
    part = dot(both, jnp.concatenate([w[...] for w in weights], axis=1), LAST_DIMS)
    if not pieces:
        out_ref, token_ref = refs
        out_ref[...] = part
        pass_on(scalar_ref, token_ref)
        return
    acc_in, *outs, acc = refs
    acc[...] = acc_in[...] + part
    size = outs[0].shape[0]
    for n, out in enumerate(outs):
        start = pl.multiple_of((scalar_ref[1] ^ n) * size, size)
        out[...] = acc[pl.ds(start, size), :].astype(BF16)


def sum_rows(scalars, begin, messages, weights, acc, pieces):
    slots, width = messages[0].shape[0], messages[0].shape[1] // 3
    feats = weights[0].shape[0]
    units = len(messages)
    in_specs = [pl.BlockSpec((slots, 3 * width), lambda n, c: (0, 0))] * units
    operands = list(messages)
    for u in range(units):
        column = pl.BlockSpec((feats, width), lambda n, c, u=u: (0, c[FIXED + begin + u]))
        operands += in_hbm(*weights)
        in_specs += [column, column]
    whole = pl.BlockSpec((slots, feats), lambda n, c: (0, 0))
    if pieces:
        operands.append(acc)
        in_specs.append(whole)
        out_shape = [jax.ShapeDtypeStruct((slots // pieces, feats), BF16)] * pieces
        out_specs = [pl.BlockSpec((slots // pieces, feats), lambda n, c: (0, 0))] * pieces
        scratch = [pltpu.VMEM((slots, feats), F32)]
    else:
        out_shape = [
            jax.ShapeDtypeStruct((slots, feats), F32),
            jax.ShapeDtypeStruct(scalars.shape, jnp.int32),
        ]
        out_specs = [whole, pl.BlockSpec(memory_space=pltpu.SMEM)]
        scratch = []
    return pl.pallas_call(
        functools.partial(sum_rows_kernel, units, pieces),
        out_shape=out_shape,
        grid_spec=pltpu.PrefetchScalarGridSpec(
            num_scalar_prefetch=1,
            grid=(1,),
            in_specs=in_specs,
            out_specs=out_specs,
            scratch_shapes=scratch,
        ),
        compiler_params=PARAMS,
        cost_estimate=cost(),
    )(scalars, *operands)


def body(tokens, grad_out, expert_ids, route_weights, w_gate, w_up, w_down):
    experts = lax.axis_size("expert")
    groups = lax.axis_size("dp")
    tok_rows = tokens.shape[0]
    feats = w_gate.shape[1]
    capacity = tok_rows // 2
    chips = groups // 2
    count = chips
    assert groups == 2 * experts and tokens.shape[1] == 2 * feats
    inv_root = 1.0 / math.sqrt(tok_rows * groups)
    expert = lax.axis_index("expert").astype(jnp.int32)
    block = lax.axis_index("dp").astype(jnp.int32)
    chip, core = block // 2, block % 2
    along = jnp.where(core == 0, chip, chips - 1 - chip)
    w_gate, w_up, w_down = w_gate[0], w_up[0], w_down[0]
    ids, weights = expert_ids.T, route_weights.T

    swap = [(j, j ^ 1) for j in range(groups)]
    up = [2 * z for z in range(chips)]
    circle = up + [j + 1 for j in reversed(up)]
    ring = list(zip(circle, circle[1:] + circle[:1]))

    scalars = [along, expert + experts * core, block % experts, block // experts, expert]
    scalars += [(d ^ 1 ^ core) * count + k for d in range(2) for k in range(count)]
    scalars += [(1 - core) * count + (i - (chips - 1 - along)) % count for i in range(count)]
    scalars += [core * count + (i - along) % count for i in range(count)]
    scalars = jnp.stack(scalars).astype(jnp.int32)

    def exchange(messages):
        came = [messages[0]]
        for t in range(1, experts):
            came.append(lax.ppermute(messages[t], "expert", [(q, q ^ t) for q in range(experts)]))
        blocks = assemble(scalars, came).reshape(groups, capacity, feats)
        blocks = lax.all_to_all(blocks, "dp", split_axis=0, concat_axis=0, tiled=True)
        return blocks.reshape(groups * capacity, feats)

    x_messages, hot, token = dispatch_rows(scalars, ids, weights, tokens, experts, False)
    g_messages, _, _ = dispatch_rows(token, ids, weights, grad_out, experts, True)
    x = exchange(x_messages)
    g = exchange(g_messages)

    other_gu, own_gu, x_t = gate_up(scalars, x, w_gate, w_up, count)
    sib_gu = lax.ppermute(other_gu, "dp", swap)
    spans = [(i, 1) for i in range(count)]
    others = [
        lax.ppermute(back_rows(scalars, g, w_down, begin, size, count, ()), "dp", swap)
        for begin, size in spans
    ]
    sums = []
    for (begin, size), sib_b in zip(spans, others):
        shares = (sib_b, own_gu, sib_gu)
        both = back_rows(scalars, g, w_down, begin, size, count, shares)
        sums += [(both, i) for i in range(size)]

    slots = 2 * count + chips - 2
    first_back = chips - 1 + count
    recv = []
    gate_and_up = (w_gate, w_up)
    place = along.astype(jnp.int32)[None]
    for s in range(slots):
        came = []
        for part in range(PARTS):
            send = recv[s - 1][part] if s else None
            if s < first_back:
                send = hop(place, s, count, chips, send, sums[s % count], part)
            came.append(lax.ppermute(send, "dp", ring))
        recv.append(came)

    def pick(token, begin, wanted):
        found = recv[count - 1 + begin : count - 1 + begin + chips + wanted - 1]
        return choose(token, wanted, chips, [part for came in found for part in came])

    early = count - 1
    mine = pick(place, 0, early)
    others = [lax.ppermute(message, "dp", swap) for message in mine]
    grads, token = gradients(scalars, 0, count, inv_root, x_t, g, mine, None)
    last = pick(token, early, count - early)
    acc, _ = sum_rows(token, 0, mine, gate_and_up, None, 0)
    mine = last
    others += [lax.ppermute(message, "dp", swap) for message in mine]
    units = [*mine, *others]
    pieces = sum_rows(scalars, early, units, gate_and_up, acc, groups)
    returned = []
    for r, piece in enumerate(pieces):
        pairs = []
        for q in range(experts):
            for b in range(groups):
                h, e = divmod(b ^ r, experts)
                pairs.append((e * groups + 2 * q + h, q * groups + b))
        returned.append(lax.ppermute(piece, ("expert", "dp"), pairs))
    grads, _ = gradients(scalars, early, count, inv_root, x_t, g, units, grads)
    grad_tokens = combine_rows(scalars, hot, returned, experts)
    return (grad_tokens, grads[0][None], grads[1][None], grads[2][None])


def solution(mesh):
    in_specs = (
        P("dp", "expert"),
        P("dp", "expert"),
        P("dp", None),
        P("dp", None),
        P("expert", "dp", None),
        P("expert", "dp", None),
        P("expert", None, "dp"),
    )
    out_specs = (
        P("dp", "expert"),
        P("expert", "dp", None),
        P("expert", "dp", None),
        P("expert", None, "dp"),
    )
    return jax.shard_map(body, mesh=mesh, in_specs=in_specs, out_specs=out_specs, check_vma=False)
```

```python
import functools
import math

import jax
import jax.numpy as jnp
from jax import lax
from jax.experimental import pallas as pl
from jax.experimental.pallas import tpu as pltpu
from jax.sharding import PartitionSpec as P

F32 = jnp.float32
BF16 = jnp.bfloat16
LAST_DIMS = (((1,), (1,)), ((), ()))
ROWS_FIRST = (((0,), (0,)), ((), ()))
FIXED = 5
PARTS = 2
PARAMS = pltpu.CompilerParams(vmem_limit_bytes=28 * 1024 * 1024)


def dot(a, b, dims=None):
    if dims is None:
        return jnp.dot(a, b, preferred_element_type=F32)
    return lax.dot_general(a, b, dims, preferred_element_type=F32)


def cost():
    return pl.CostEstimate(flops=1024, bytes_accessed=1024, transcendentals=0)


def in_hbm(*arrays):
    return [pltpu.with_memory_space_constraint(a, pltpu.HBM) for a in arrays]


def pass_on(scalar_ref, out_ref):
    for n in range(out_ref.shape[0]):
        out_ref[n] = scalar_ref[n]


def slot_one_hot(ids_ref, experts, capacity):
    tokens = ids_ref.shape[1]
    first, second = ids_ref[0:1, :], ids_ref[1:2, :]
    expert = lax.broadcasted_iota(jnp.int32, (8 * (-(-experts // 8)), tokens), 0)
    chosen = (first == expert) | (second == expert)
    before = lax.broadcasted_iota(jnp.int32, (tokens, tokens), 0) < lax.broadcasted_iota(
        jnp.int32, (tokens, tokens), 1
    )
    place = dot(chosen.astype(F32).astype(BF16), before.astype(F32).astype(BF16))
    place = jnp.where(chosen, place, -1.0).astype(jnp.int32)
    slot = lax.broadcasted_iota(jnp.int32, (capacity, tokens), 0)
    return [slot == place[e : e + 1, :] for e in range(experts)]


def dispatch_kernel(experts, weighted, scalar_ref, ids_hbm, weights_hbm, rows_hbm, *refs):
    *messages, hot_ref, token_ref, ids_ref, weights_ref, rows_ref, scale_ref, sems = refs
    _, capacity, feats = messages[0].shape
    pass_on(scalar_ref, token_ref)
    pairs = [(ids_hbm, ids_ref), (weights_hbm, weights_ref)]
    for h in range(2):
        whole = len(rows_hbm.shape) == 3
        half = rows_hbm.at[h] if whole else rows_hbm.at[:, pl.ds(h * feats, feats)]
        pairs.append((half, rows_ref.at[h]))
    copies = [pltpu.make_async_copy(a, b, sems.at[n]) for n, (a, b) in enumerate(pairs)]
    for copy in copies:
        copy.start()
    copies[0].wait()
    copies[1].wait()
    for e, hit in enumerate(slot_one_hot(ids_ref, experts, capacity)):
        place = slice(e * capacity, (e + 1) * capacity)
        hot_ref[place, :] = hit.astype(F32).astype(BF16)
        if weighted:
            weight = jnp.where(ids_ref[0:1, :] == e, weights_ref[0:1, :], weights_ref[1:2, :])
            weight = jnp.sum(jnp.where(hit, weight, 0.0), axis=1, keepdims=True)
            scale_ref[place, :] = jnp.broadcast_to(weight, (capacity, scale_ref.shape[1]))
    places = [
        pl.ds(pl.multiple_of((scalar_ref[4] ^ t) * capacity, capacity), capacity)
        for t in range(experts)
    ]
    hot = jnp.concatenate([hot_ref[place, :] for place in places], axis=0)
    for h in range(2):
        copies[2 + h].wait()
        out = dot(hot, rows_ref[h])
        for t, place in enumerate(places):
            part = out[t * capacity : (t + 1) * capacity]
            if weighted:
                part = part * scale_ref[place, 0:1]
            messages[t][h] = part.astype(BF16)


def dispatch_rows(scalars, ids, weights, rows, experts, weighted):
    tokens, feats = rows.shape[0], rows.shape[1] // 2
    capacity = tokens // 2
    if feats % 128:
        rows = rows.reshape(tokens, 2, feats).transpose(1, 0, 2)
    *messages, hot, token = pl.pallas_call(
        functools.partial(dispatch_kernel, experts, weighted),
        out_shape=[jax.ShapeDtypeStruct((2, capacity, feats), BF16)] * experts
        + [
            jax.ShapeDtypeStruct((experts * capacity, tokens), BF16),
            jax.ShapeDtypeStruct(scalars.shape, jnp.int32),
        ],
        in_specs=[pl.BlockSpec(memory_space=pltpu.SMEM)]
        + [pl.BlockSpec(memory_space=pltpu.HBM)] * 3,
        out_specs=[pl.BlockSpec(memory_space=pltpu.VMEM)] * (experts + 1)
        + [pl.BlockSpec(memory_space=pltpu.SMEM)],
        scratch_shapes=[
            pltpu.VMEM((2, tokens), jnp.int32),
            pltpu.VMEM((2, tokens), F32),
            pltpu.VMEM((2, tokens, feats), BF16),
            pltpu.VMEM((experts * capacity, 128), F32),
            pltpu.SemaphoreType.DMA((4,)),
        ],
        compiler_params=PARAMS,
        cost_estimate=cost(),
    )(scalars, *in_hbm(ids, weights, rows))
    return messages, hot, token


def assemble_kernel(scalar_ref, *refs):
    *messages, out_ref, sems = refs

    def copy(t, message):
        return pltpu.make_async_copy(message, out_ref.at[t ^ scalar_ref[4]], sems.at[t])

    for t, message in enumerate(messages):
        copy(t, message).start()
    for t, message in enumerate(messages):
        copy(t, message).wait()


def assemble(scalars, messages):
    return pl.pallas_call(
        assemble_kernel,
        out_shape=jax.ShapeDtypeStruct((len(messages), *messages[0].shape), BF16),
        in_specs=[pl.BlockSpec(memory_space=pltpu.SMEM)]
        + [pl.BlockSpec(memory_space=pl.ANY)] * len(messages),
        scratch_shapes=[pltpu.SemaphoreType.DMA((len(messages),))],
        compiler_params=PARAMS,
        cost_estimate=cost(),
    )(scalars, *messages)


def combine_kernel(experts, scalar_ref, hot_ref, *refs):
    pieces, (out_ref, rows_ref, sems) = refs[:-3], refs[-3:]
    capacity = pieces[0].shape[0]
    at = pl.program_id(0)

    def copy(n):
        return pltpu.make_async_copy(
            pieces[n], rows_ref.at[pl.ds(n * capacity, capacity)], sems.at[n]
        )

    @pl.when(at == 0)
    def _():
        for n in range(len(pieces)):
            copy(n).start()

    hot = jnp.concatenate(
        [
            hot_ref[pl.ds(pl.multiple_of((scalar_ref[2] ^ n) * capacity, capacity), capacity), :]
            for n in range(experts)
        ],
        axis=0,
    )
    for half in range(2):

        @pl.when(at == half)
        def _():
            for n in range(half * experts, (half + 1) * experts):
                copy(n).wait()
            rows = rows_ref[half * experts * capacity : (half + 1) * experts * capacity, :]
            out = dot(hot, rows, ROWS_FIRST).astype(BF16)
            out_ref[...] = out.reshape(out_ref.shape)


def combine_rows(scalars, hot, pieces, experts):
    tokens = hot.shape[1]
    capacity, feats = pieces[0].shape
    if feats % 128:
        out_shape = jax.ShapeDtypeStruct((2, tokens, feats), BF16)
        out_spec = pl.BlockSpec((1, tokens, feats), lambda a, c: (a ^ c[3], 0, 0))
    else:
        out_shape = jax.ShapeDtypeStruct((tokens, 2 * feats), BF16)
        out_spec = pl.BlockSpec((tokens, feats), lambda a, c: (0, a ^ c[3]))
    out = pl.pallas_call(
        functools.partial(combine_kernel, experts),
        out_shape=out_shape,
        grid_spec=pltpu.PrefetchScalarGridSpec(
            num_scalar_prefetch=1,
            grid=(2,),
            in_specs=[pl.BlockSpec((experts * capacity, tokens), lambda a, c: (0, 0))]
            + [pl.BlockSpec(memory_space=pltpu.HBM)] * len(pieces),
            out_specs=out_spec,
            scratch_shapes=[
                pltpu.VMEM((len(pieces) * capacity, feats), BF16),
                pltpu.SemaphoreType.DMA((len(pieces),)),
            ],
        ),
        compiler_params=PARAMS,
        cost_estimate=cost(),
    )(scalars, hot, *in_hbm(*pieces))
    if feats % 128:
        out = out.transpose(1, 0, 2).reshape(tokens, 2 * feats)
    return out


def gate_up_kernel(count, scalar_ref, x_ref, wg_ref, wu_ref, *outs):
    others, (own_ref, turned_ref) = outs[:count], outs[count:]
    width = wg_ref.shape[1]
    chunk, own = pl.program_id(0), pl.program_id(1)

    @pl.when((chunk == 0) & (own == 0))
    def _():
        turned_ref[...] = x_ref[...].T

    def write(out_ref):
        out_ref[0, :, :width] = dot(x_ref[...], wg_ref[...]).astype(BF16)
        out_ref[0, :, width:] = dot(x_ref[...], wu_ref[...]).astype(BF16)

    @pl.when(own == 1)
    def _():
        write(own_ref)

    for n, out_ref in enumerate(others):

        @pl.when((own == 0) & (chunk == n))
        def _():
            write(out_ref)


def gate_up(scalars, x, w_gate, w_up, count):
    slots, feats = x.shape
    width = w_gate.shape[1] // (2 * count)
    column = pl.BlockSpec(
        (feats, width), lambda i, own, c: (0, c[FIXED + 2 * count + own * count + i])
    )
    *others, own, turned = pl.pallas_call(
        functools.partial(gate_up_kernel, count),
        out_shape=[jax.ShapeDtypeStruct((1, slots, 2 * width), BF16)] * count
        + [
            jax.ShapeDtypeStruct((count, slots, 2 * width), BF16),
            jax.ShapeDtypeStruct((feats, slots), BF16),
        ],
        grid_spec=pltpu.PrefetchScalarGridSpec(
            num_scalar_prefetch=1,
            grid=(count, 2),
            in_specs=[pl.BlockSpec((slots, feats), lambda i, own, c: (0, 0)), column, column],
            out_specs=[pl.BlockSpec((1, slots, 2 * width), lambda i, own, c: (0, 0, 0))] * count
            + [
                pl.BlockSpec((1, slots, 2 * width), lambda i, own, c: (i, 0, 0)),
                pl.BlockSpec((feats, slots), lambda i, own, c: (0, 0)),
            ],
        ),
        compiler_params=PARAMS,
        cost_estimate=cost(),
    )(scalars, x, *in_hbm(w_gate, w_up))
    return others, own, turned


def back_kernel(scalar_ref, g_ref, wd_ref, *refs):
    *shares, out_ref = refs
    back = dot(g_ref[...], wd_ref[...], LAST_DIMS)
    if not shares:
        out_ref[0] = back.astype(BF16)
        return
    sib_b, own_gu, sib_gu = shares
    width = back.shape[1]
    both = own_gu[0].astype(F32) + sib_gu[0].astype(F32)
    out_ref[0, :, : 2 * width] = both.astype(BF16)
    out_ref[0, :, 2 * width :] = (back + sib_b[0].astype(F32)).astype(BF16)


def back_rows(scalars, g, w_down, begin, size, count, shares):
    slots, feats = g.shape
    width = w_down.shape[0] // (2 * count)
    own = bool(shares)
    row = pl.BlockSpec(
        (width, feats), lambda i, c: (c[FIXED + 2 * count + own * count + begin + i], 0)
    )
    in_specs = [pl.BlockSpec((slots, feats), lambda i, c: (0, 0)), row]
    if own:
        in_specs.append(pl.BlockSpec((1, slots, width), lambda i, c: (i, 0, 0)))
        in_specs.append(pl.BlockSpec((1, slots, 2 * width), lambda i, c: (begin + i, 0, 0)))
        in_specs.append(pl.BlockSpec((1, slots, 2 * width), lambda i, c: (0, 0, 0)))
    cols = (3 if own else 1) * width
    return pl.pallas_call(
        back_kernel,
        out_shape=jax.ShapeDtypeStruct((size, slots, cols), BF16),
        grid_spec=pltpu.PrefetchScalarGridSpec(
            num_scalar_prefetch=1,
            grid=(size,),
            in_specs=in_specs,
            out_specs=pl.BlockSpec((1, slots, cols), lambda i, c: (i, 0, 0)),
        ),
        compiler_params=PARAMS,
        cost_estimate=cost(),
    )(scalars, g, *in_hbm(w_down), *shares)


def activate(gate, upper, back):
    sig = jax.nn.sigmoid(gate)
    gated = gate * sig
    return (
        (gated * upper).astype(BF16),
        (back * upper * sig * (1.0 + gate * (1.0 - sig))).astype(BF16),
        (back * gated).astype(BF16),
    )


def hop_kernel(plan, scalar_ref, *refs):
    slot, count, chips, came = plan
    sums_ref = refs[-2]
    recv_ref = refs[0] if came else None
    send_ref = refs[-1]
    at = scalar_ref[0]
    width = send_ref.shape[1] // 3
    summing = (at <= slot) & (slot - at < count)

    def total(part):
        columns = slice(part * width, (part + 1) * width)
        value = sums_ref[0, :, columns].astype(F32)
        if came:
            value += jnp.where(at > 0, recv_ref[:, columns].astype(F32), 0.0)
        return value

    @pl.when(summing & (at < chips - 1))
    def _():
        for part in range(3):
            send_ref[:, part * width : (part + 1) * width] = total(part).astype(BF16)

    @pl.when(summing & (at == chips - 1))
    def _():
        for part, value in enumerate(activate(total(0), total(1), total(2))):
            send_ref[:, part * width : (part + 1) * width] = value

    if came:

        @pl.when(jnp.logical_not(summing))
        def _():
            send_ref[...] = recv_ref[...]


def hop(scalars, slot, count, chips, recv, sums, part):
    array, i = sums
    rows, cols = array.shape[1] // PARTS, array.shape[2]
    message = pl.BlockSpec((rows, cols), lambda n, c: (0, 0))
    operands, in_specs = [], []
    if recv is not None:
        operands.append(recv)
        in_specs.append(message)
    operands.append(array)
    in_specs.append(pl.BlockSpec((1, rows, cols), lambda n, c: (i, part, 0)))
    plan = (slot, count, chips, recv is not None)
    return pl.pallas_call(
        functools.partial(hop_kernel, plan),
        out_shape=jax.ShapeDtypeStruct((rows, cols), BF16),
        grid_spec=pltpu.PrefetchScalarGridSpec(
            num_scalar_prefetch=1,
            grid=(1,),
            in_specs=in_specs,
            out_specs=message,
        ),
        compiler_params=PARAMS,
        cost_estimate=cost(),
    )(scalars, *operands)


def choose_kernel(wanted, hops, scalar_ref, *refs):
    *candidates, sems = refs
    candidates, outs = candidates[:-wanted], candidates[-wanted:]
    rows = candidates[0].shape[0]

    def copy(k, n, part):
        return pltpu.make_async_copy(
            candidates[(k + n) * PARTS + part],
            outs[k].at[pl.ds(part * rows, rows)],
            sems.at[k, part],
        )

    for n in range(hops):

        @pl.when(scalar_ref[0] == n)
        def _():
            for k in range(wanted):
                for part in range(PARTS):
                    copy(k, n, part).start()

    for k in range(wanted):
        for part in range(PARTS):
            copy(k, 0, part).wait()


def choose(place, wanted, hops, candidates):
    rows, cols = candidates[0].shape
    return pl.pallas_call(
        functools.partial(choose_kernel, wanted, hops),
        out_shape=[jax.ShapeDtypeStruct((rows * PARTS, cols), BF16)] * wanted,
        in_specs=[pl.BlockSpec(memory_space=pltpu.SMEM)]
        + [pl.BlockSpec(memory_space=pl.ANY)] * len(candidates),
        scratch_shapes=[pltpu.SemaphoreType.DMA((wanted, PARTS))],
        compiler_params=PARAMS,
        cost_estimate=cost(),
    )(place, *candidates)


def gradients_kernel(units, scale, first, scalar_ref, xt_ref, g_ref, *refs):
    messages, refs = refs[:units], refs[units if first else units + 3 :]
    gg_ref, gu_ref, gd_ref, token_ref = refs
    width = gg_ref.shape[1]
    pass_on(scalar_ref, token_ref)
    for u in range(units):

        @pl.when(pl.program_id(0) == u)
        def _():
            both = dot(xt_ref[...], messages[u][:, width:]) * scale
            gg_ref[...] = both[:, :width].astype(BF16)
            gu_ref[...] = both[:, width:].astype(BF16)
            scaled = messages[u][:, :width]
            gd_ref[...] = (dot(scaled, g_ref[...], ROWS_FIRST) * scale).astype(BF16)


def gradients(scalars, begin, count, scale, x_t, g, messages, grads):
    slots, feats = g.shape
    width = messages[0].shape[1] // 3
    hidden = 2 * count * width
    units = len(messages)

    def at(u, c):
        return c[FIXED + begin + u]

    column = pl.BlockSpec((feats, width), lambda u, c: (0, at(u, c)))
    in_specs = [
        pl.BlockSpec((feats, slots), lambda u, c: (0, 0)),
        pl.BlockSpec((slots, feats), lambda u, c: (0, 0)),
    ]
    in_specs += [pl.BlockSpec((slots, 3 * width), lambda u, c: (0, 0))] * units
    operands = [x_t, g, *messages]
    aliases = {}
    if grads is not None:
        aliases = {len(operands) + 1 + n: n for n in range(3)}
        operands += grads
        in_specs += [pl.BlockSpec(memory_space=pl.ANY)] * 3
    *grads, token = pl.pallas_call(
        functools.partial(gradients_kernel, units, scale, grads is None),
        out_shape=[
            jax.ShapeDtypeStruct((feats, hidden), BF16),
            jax.ShapeDtypeStruct((feats, hidden), BF16),
            jax.ShapeDtypeStruct((hidden, feats), BF16),
            jax.ShapeDtypeStruct(scalars.shape, jnp.int32),
        ],
        grid_spec=pltpu.PrefetchScalarGridSpec(
            num_scalar_prefetch=1,
            grid=(units,),
            in_specs=in_specs,
            out_specs=[
                column,
                column,
                pl.BlockSpec((width, feats), lambda u, c: (at(u, c), 0)),
                pl.BlockSpec(memory_space=pltpu.SMEM),
            ],
        ),
        input_output_aliases=aliases,
        compiler_params=PARAMS,
        cost_estimate=cost(),
    )(scalars, *operands)
    return grads, token


def sum_rows_kernel(units, pieces, scalar_ref, *refs):
    messages, weights, refs = refs[:units], refs[units : 3 * units], refs[3 * units :]
    width = weights[0].shape[1]
    both = jnp.concatenate([message[:, width:] for message in messages], axis=1)
    part = dot(both, jnp.concatenate([w[...] for w in weights], axis=1), LAST_DIMS)
    if not pieces:
        out_ref, token_ref = refs
        out_ref[...] = part
        pass_on(scalar_ref, token_ref)
        return
    acc_in, *outs, acc = refs
    acc[...] = acc_in[...] + part
    size = outs[0].shape[0]
    for n, out in enumerate(outs):
        start = pl.multiple_of((scalar_ref[1] ^ n) * size, size)
        out[...] = acc[pl.ds(start, size), :].astype(BF16)


def sum_rows(scalars, begin, messages, weights, acc, pieces):
    slots, width = messages[0].shape[0], messages[0].shape[1] // 3
    feats = weights[0].shape[0]
    units = len(messages)
    in_specs = [pl.BlockSpec((slots, 3 * width), lambda n, c: (0, 0))] * units
    operands = list(messages)
    for u in range(units):
        column = pl.BlockSpec((feats, width), lambda n, c, u=u: (0, c[FIXED + begin + u]))
        operands += in_hbm(*weights)
        in_specs += [column, column]
    whole = pl.BlockSpec((slots, feats), lambda n, c: (0, 0))
    if pieces:
        operands.append(acc)
        in_specs.append(whole)
        out_shape = [jax.ShapeDtypeStruct((slots // pieces, feats), BF16)] * pieces
        out_specs = [pl.BlockSpec((slots // pieces, feats), lambda n, c: (0, 0))] * pieces
        scratch = [pltpu.VMEM((slots, feats), F32)]
    else:
        out_shape = [
            jax.ShapeDtypeStruct((slots, feats), F32),
            jax.ShapeDtypeStruct(scalars.shape, jnp.int32),
        ]
        out_specs = [whole, pl.BlockSpec(memory_space=pltpu.SMEM)]
        scratch = []
    return pl.pallas_call(
        functools.partial(sum_rows_kernel, units, pieces),
        out_shape=out_shape,
        grid_spec=pltpu.PrefetchScalarGridSpec(
            num_scalar_prefetch=1,
            grid=(1,),
            in_specs=in_specs,
            out_specs=out_specs,
            scratch_shapes=scratch,
        ),
        compiler_params=PARAMS,
        cost_estimate=cost(),
    )(scalars, *operands)


def body(tokens, grad_out, expert_ids, route_weights, w_gate, w_up, w_down):
    experts = lax.axis_size("expert")
    groups = lax.axis_size("dp")
    tok_rows = tokens.shape[0]
    feats = w_gate.shape[1]
    capacity = tok_rows // 2
    chips = groups // 2
    count = chips
    assert groups == 2 * experts and tokens.shape[1] == 2 * feats
    inv_root = 1.0 / math.sqrt(tok_rows * groups)
    expert = lax.axis_index("expert").astype(jnp.int32)
    block = lax.axis_index("dp").astype(jnp.int32)
    chip, core = block // 2, block % 2
    along = jnp.where(core == 0, chip, chips - 1 - chip)
    w_gate, w_up, w_down = w_gate[0], w_up[0], w_down[0]
    ids, weights = expert_ids.T, route_weights.T

    swap = [(j, j ^ 1) for j in range(groups)]
    up = [2 * z for z in range(chips)]
    circle = up + [j + 1 for j in reversed(up)]
    ring = list(zip(circle, circle[1:] + circle[:1]))

    scalars = [along, expert + experts * core, block % experts, block // experts, expert]
    scalars += [(d ^ 1 ^ core) * count + k for d in range(2) for k in range(count)]
    scalars += [(1 - core) * count + (i - (chips - 1 - along)) % count for i in range(count)]
    scalars += [core * count + (i - along) % count for i in range(count)]
    scalars = jnp.stack(scalars).astype(jnp.int32)

    def exchange(messages):
        came = [messages[0]]
        for t in range(1, experts):
            came.append(lax.ppermute(messages[t], "expert", [(q, q ^ t) for q in range(experts)]))
        blocks = assemble(scalars, came).reshape(groups, capacity, feats)
        blocks = lax.all_to_all(blocks, "dp", split_axis=0, concat_axis=0, tiled=True)
        return blocks.reshape(groups * capacity, feats)

    x_messages, hot, token = dispatch_rows(scalars, ids, weights, tokens, experts, False)
    g_messages, _, _ = dispatch_rows(token, ids, weights, grad_out, experts, True)
    x = exchange(x_messages)
    g = exchange(g_messages)

    other_gu, own_gu, x_t = gate_up(scalars, x, w_gate, w_up, count)
    sums = []
    for i in range(count):
        other_b = back_rows(scalars, g, w_down, i, 1, count, ())
        shares = (
            lax.ppermute(other_b, "dp", swap),
            own_gu,
            lax.ppermute(other_gu[i], "dp", swap),
        )
        sums.append((back_rows(scalars, g, w_down, i, 1, count, shares), 0))

    slots = 2 * count + chips - 2
    first_back = chips - 1 + count
    recv = []
    gate_and_up = (w_gate, w_up)
    place = along.astype(jnp.int32)[None]
    for s in range(slots):
        came = []
        for part in range(PARTS):
            send = recv[s - 1][part] if s else None
            if s < first_back:
                send = hop(place, s, count, chips, send, sums[s % count], part)
            came.append(lax.ppermute(send, "dp", ring))
        recv.append(came)

    def pick(token, begin, wanted):
        found = recv[count - 1 + begin : count - 1 + begin + chips + wanted - 1]
        return choose(token, wanted, chips, [part for came in found for part in came])

    early = count - 1
    mine = pick(place, 0, early)
    others = [lax.ppermute(message, "dp", swap) for message in mine]
    grads, token = gradients(scalars, 0, count, inv_root, x_t, g, mine, None)
    last = pick(token, early, count - early)
    acc, _ = sum_rows(token, 0, mine, gate_and_up, None, 0)
    mine = last
    others += [lax.ppermute(message, "dp", swap) for message in mine]
    units = [*mine, *others]
    pieces = sum_rows(scalars, early, units, gate_and_up, acc, groups)
    returned = []
    for r, piece in enumerate(pieces):
        pairs = []
        for q in range(experts):
            for b in range(groups):
                h, e = divmod(b ^ r, experts)
                pairs.append((e * groups + 2 * q + h, q * groups + b))
        returned.append(lax.ppermute(piece, ("expert", "dp"), pairs))
    grads, _ = gradients(scalars, early, count, inv_root, x_t, g, units, grads)
    grad_tokens = combine_rows(scalars, hot, returned, experts)
    return (grad_tokens, grads[0][None], grads[1][None], grads[2][None])


def solution(mesh):
    in_specs = (
        P("dp", "expert"),
        P("dp", "expert"),
        P("dp", None),
        P("dp", None),
        P("expert", "dp", None),
        P("expert", "dp", None),
        P("expert", None, "dp"),
    )
    out_specs = (
        P("dp", "expert"),
        P("expert", "dp", None),
        P("expert", "dp", None),
        P("expert", None, "dp"),
    )
    return jax.shard_map(body, mesh=mesh, in_specs=in_specs, out_specs=out_specs, check_vma=False)
```

```python
import functools
import math

import jax
import jax.numpy as jnp
from jax import lax
from jax.experimental import pallas as pl
from jax.experimental.pallas import tpu as pltpu
from jax.sharding import PartitionSpec as P

F32 = jnp.float32
BF16 = jnp.bfloat16
LAST_DIMS = (((1,), (1,)), ((), ()))
ROWS_FIRST = (((0,), (0,)), ((), ()))
FIXED = 5
PARTS = 2
PARAMS = pltpu.CompilerParams(vmem_limit_bytes=28 * 1024 * 1024)


def dot(a, b, dims=None):
    if dims is None:
        return jnp.dot(a, b, preferred_element_type=F32)
    return lax.dot_general(a, b, dims, preferred_element_type=F32)


def cost():
    return pl.CostEstimate(flops=1024, bytes_accessed=1024, transcendentals=0)


def in_hbm(*arrays):
    return [pltpu.with_memory_space_constraint(a, pltpu.HBM) for a in arrays]


def pass_on(scalar_ref, out_ref):
    for n in range(out_ref.shape[0]):
        out_ref[n] = scalar_ref[n]


def slot_one_hot(ids_ref, experts, capacity):
    tokens = ids_ref.shape[1]
    first, second = ids_ref[0:1, :], ids_ref[1:2, :]
    expert = lax.broadcasted_iota(jnp.int32, (8 * (-(-experts // 8)), tokens), 0)
    chosen = (first == expert) | (second == expert)
    before = lax.broadcasted_iota(jnp.int32, (tokens, tokens), 0) < lax.broadcasted_iota(
        jnp.int32, (tokens, tokens), 1
    )
    place = dot(chosen.astype(F32).astype(BF16), before.astype(F32).astype(BF16))
    place = jnp.where(chosen, place, -1.0).astype(jnp.int32)
    slot = lax.broadcasted_iota(jnp.int32, (capacity, tokens), 0)
    return [slot == place[e : e + 1, :] for e in range(experts)]


def dispatch_kernel(experts, weighted, scalar_ref, ids_hbm, weights_hbm, rows_hbm, *refs):
    *messages, hot_ref, token_ref, ids_ref, weights_ref, rows_ref, scale_ref, sems = refs
    _, capacity, feats = messages[0].shape
    pass_on(scalar_ref, token_ref)
    pairs = [(ids_hbm, ids_ref), (weights_hbm, weights_ref)]
    for h in range(2):
        whole = len(rows_hbm.shape) == 3
        half = rows_hbm.at[h] if whole else rows_hbm.at[:, pl.ds(h * feats, feats)]
        pairs.append((half, rows_ref.at[h]))
    copies = [pltpu.make_async_copy(a, b, sems.at[n]) for n, (a, b) in enumerate(pairs)]
    for copy in copies:
        copy.start()
    copies[0].wait()
    copies[1].wait()
    for e, hit in enumerate(slot_one_hot(ids_ref, experts, capacity)):
        place = slice(e * capacity, (e + 1) * capacity)
        hot_ref[place, :] = hit.astype(F32).astype(BF16)
        if weighted:
            weight = jnp.where(ids_ref[0:1, :] == e, weights_ref[0:1, :], weights_ref[1:2, :])
            weight = jnp.sum(jnp.where(hit, weight, 0.0), axis=1, keepdims=True)
            scale_ref[place, :] = jnp.broadcast_to(weight, (capacity, scale_ref.shape[1]))
    places = [
        pl.ds(pl.multiple_of((scalar_ref[4] ^ t) * capacity, capacity), capacity)
        for t in range(experts)
    ]
    hot = jnp.concatenate([hot_ref[place, :] for place in places], axis=0)
    for h in range(2):
        copies[2 + h].wait()
        out = dot(hot, rows_ref[h])
        for t, place in enumerate(places):
            part = out[t * capacity : (t + 1) * capacity]
            if weighted:
                part = part * scale_ref[place, 0:1]
            messages[t][h] = part.astype(BF16)


def dispatch_rows(scalars, ids, weights, rows, experts, weighted):
    tokens, feats = rows.shape[0], rows.shape[1] // 2
    capacity = tokens // 2
    if feats % 128:
        rows = rows.reshape(tokens, 2, feats).transpose(1, 0, 2)
    *messages, hot, token = pl.pallas_call(
        functools.partial(dispatch_kernel, experts, weighted),
        out_shape=[jax.ShapeDtypeStruct((2, capacity, feats), BF16)] * experts
        + [
            jax.ShapeDtypeStruct((experts * capacity, tokens), BF16),
            jax.ShapeDtypeStruct(scalars.shape, jnp.int32),
        ],
        in_specs=[pl.BlockSpec(memory_space=pltpu.SMEM)]
        + [pl.BlockSpec(memory_space=pltpu.HBM)] * 3,
        out_specs=[pl.BlockSpec(memory_space=pltpu.VMEM)] * (experts + 1)
        + [pl.BlockSpec(memory_space=pltpu.SMEM)],
        scratch_shapes=[
            pltpu.VMEM((2, tokens), jnp.int32),
            pltpu.VMEM((2, tokens), F32),
            pltpu.VMEM((2, tokens, feats), BF16),
            pltpu.VMEM((experts * capacity, 128), F32),
            pltpu.SemaphoreType.DMA((4,)),
        ],
        compiler_params=PARAMS,
        cost_estimate=cost(),
    )(scalars, *in_hbm(ids, weights, rows))
    return messages, hot, token


def assemble_kernel(scalar_ref, *refs):
    *messages, out_ref, sems = refs

    def copy(t, message):
        return pltpu.make_async_copy(message, out_ref.at[t ^ scalar_ref[4]], sems.at[t])

    for t, message in enumerate(messages):
        copy(t, message).start()
    for t, message in enumerate(messages):
        copy(t, message).wait()


def assemble(scalars, messages):
    return pl.pallas_call(
        assemble_kernel,
        out_shape=jax.ShapeDtypeStruct((len(messages), *messages[0].shape), BF16),
        in_specs=[pl.BlockSpec(memory_space=pltpu.SMEM)]
        + [pl.BlockSpec(memory_space=pl.ANY)] * len(messages),
        scratch_shapes=[pltpu.SemaphoreType.DMA((len(messages),))],
        compiler_params=PARAMS,
        cost_estimate=cost(),
    )(scalars, *messages)


def combine_kernel(experts, scalar_ref, hot_ref, *refs):
    pieces, (out_ref, rows_ref, sems) = refs[:-3], refs[-3:]
    capacity = pieces[0].shape[0]
    at = pl.program_id(0)

    def copy(n):
        return pltpu.make_async_copy(
            pieces[n], rows_ref.at[pl.ds(n * capacity, capacity)], sems.at[n]
        )

    @pl.when(at == 0)
    def _():
        for n in range(len(pieces)):
            copy(n).start()

    hot = jnp.concatenate(
        [
            hot_ref[pl.ds(pl.multiple_of((scalar_ref[2] ^ n) * capacity, capacity), capacity), :]
            for n in range(experts)
        ],
        axis=0,
    )
    for half in range(2):

        @pl.when(at == half)
        def _():
            for n in range(half * experts, (half + 1) * experts):
                copy(n).wait()
            rows = rows_ref[half * experts * capacity : (half + 1) * experts * capacity, :]
            out = dot(hot, rows, ROWS_FIRST).astype(BF16)
            out_ref[...] = out.reshape(out_ref.shape)


def combine_rows(scalars, hot, pieces, experts):
    tokens = hot.shape[1]
    capacity, feats = pieces[0].shape
    if feats % 128:
        out_shape = jax.ShapeDtypeStruct((2, tokens, feats), BF16)
        out_spec = pl.BlockSpec((1, tokens, feats), lambda a, c: (a ^ c[3], 0, 0))
    else:
        out_shape = jax.ShapeDtypeStruct((tokens, 2 * feats), BF16)
        out_spec = pl.BlockSpec((tokens, feats), lambda a, c: (0, a ^ c[3]))
    out = pl.pallas_call(
        functools.partial(combine_kernel, experts),
        out_shape=out_shape,
        grid_spec=pltpu.PrefetchScalarGridSpec(
            num_scalar_prefetch=1,
            grid=(2,),
            in_specs=[pl.BlockSpec((experts * capacity, tokens), lambda a, c: (0, 0))]
            + [pl.BlockSpec(memory_space=pltpu.HBM)] * len(pieces),
            out_specs=out_spec,
            scratch_shapes=[
                pltpu.VMEM((len(pieces) * capacity, feats), BF16),
                pltpu.SemaphoreType.DMA((len(pieces),)),
            ],
        ),
        compiler_params=PARAMS,
        cost_estimate=cost(),
    )(scalars, *in_hbm(hot, *pieces))
    if feats % 128:
        out = out.transpose(1, 0, 2).reshape(tokens, 2 * feats)
    return out


def gate_up_kernel(scalar_ref, x_ref, wg_ref, wu_ref, *outs):
    width = wg_ref.shape[1]

    @pl.when((pl.program_id(0) == 0) & (pl.program_id(1) == 0))
    def _():
        outs[2][...] = x_ref[...].T

    for own in range(2):

        @pl.when(pl.program_id(1) == own)
        def _():
            outs[own][0, :, :width] = dot(x_ref[...], wg_ref[...]).astype(BF16)
            outs[own][0, :, width:] = dot(x_ref[...], wu_ref[...]).astype(BF16)


def gate_up(scalars, x, w_gate, w_up, count):
    slots, feats = x.shape
    width = w_gate.shape[1] // (2 * count)
    out = jax.ShapeDtypeStruct((count, slots, 2 * width), BF16)
    out_spec = pl.BlockSpec((1, slots, 2 * width), lambda i, own, c: (i, 0, 0))
    column = pl.BlockSpec(
        (feats, width), lambda i, own, c: (0, c[FIXED + 2 * count + own * count + i])
    )
    return pl.pallas_call(
        gate_up_kernel,
        out_shape=(out, out, jax.ShapeDtypeStruct((feats, slots), BF16)),
        grid_spec=pltpu.PrefetchScalarGridSpec(
            num_scalar_prefetch=1,
            grid=(count, 2),
            in_specs=[pl.BlockSpec((slots, feats), lambda i, own, c: (0, 0)), column, column],
            out_specs=(
                out_spec,
                out_spec,
                pl.BlockSpec((feats, slots), lambda i, own, c: (0, 0)),
            ),
        ),
        compiler_params=PARAMS,
        cost_estimate=cost(),
    )(scalars, x, *in_hbm(w_gate, w_up))


def back_kernel(scalar_ref, g_ref, wd_ref, *refs):
    *shares, out_ref = refs
    back = dot(g_ref[...], wd_ref[...], LAST_DIMS)
    if not shares:
        out_ref[0] = back.astype(BF16)
        return
    sib_b, own_gu, sib_gu = shares
    width = back.shape[1]
    both = own_gu[0].astype(F32) + sib_gu[0].astype(F32)
    out_ref[0, :, : 2 * width] = both.astype(BF16)
    out_ref[0, :, 2 * width :] = (back + sib_b[0].astype(F32)).astype(BF16)


def back_rows(scalars, g, w_down, begin, size, count, shares):
    slots, feats = g.shape
    width = w_down.shape[0] // (2 * count)
    own = bool(shares)
    row = pl.BlockSpec(
        (width, feats), lambda i, c: (c[FIXED + 2 * count + own * count + begin + i], 0)
    )
    in_specs = [pl.BlockSpec((slots, feats), lambda i, c: (0, 0)), row]
    if own:
        in_specs.append(pl.BlockSpec((1, slots, width), lambda i, c: (i, 0, 0)))
        in_specs += [pl.BlockSpec((1, slots, 2 * width), lambda i, c: (begin + i, 0, 0))] * 2
    cols = (3 if own else 1) * width
    return pl.pallas_call(
        back_kernel,
        out_shape=jax.ShapeDtypeStruct((size, slots, cols), BF16),
        grid_spec=pltpu.PrefetchScalarGridSpec(
            num_scalar_prefetch=1,
            grid=(size,),
            in_specs=in_specs,
            out_specs=pl.BlockSpec((1, slots, cols), lambda i, c: (i, 0, 0)),
        ),
        compiler_params=PARAMS,
        cost_estimate=cost(),
    )(scalars, g, *in_hbm(w_down), *shares)


def activate(gate, upper, back):
    sig = jax.nn.sigmoid(gate)
    gated = gate * sig
    return (
        (gated * upper).astype(BF16),
        (back * upper * sig * (1.0 + gate * (1.0 - sig))).astype(BF16),
        (back * gated).astype(BF16),
    )


def hop_kernel(plan, scalar_ref, *refs):
    slot, count, chips, came = plan
    sums_ref = refs[-2]
    recv_ref = refs[0] if came else None
    send_ref = refs[-1]
    at = scalar_ref[0]
    width = send_ref.shape[1] // 3
    summing = (at <= slot) & (slot - at < count)

    def total(part):
        columns = slice(part * width, (part + 1) * width)
        value = sums_ref[0, :, columns].astype(F32)
        if came:
            value += jnp.where(at > 0, recv_ref[:, columns].astype(F32), 0.0)
        return value

    @pl.when(summing & (at < chips - 1))
    def _():
        for part in range(3):
            send_ref[:, part * width : (part + 1) * width] = total(part).astype(BF16)

    @pl.when(summing & (at == chips - 1))
    def _():
        for part, value in enumerate(activate(total(0), total(1), total(2))):
            send_ref[:, part * width : (part + 1) * width] = value

    if came:

        @pl.when(jnp.logical_not(summing))
        def _():
            send_ref[...] = recv_ref[...]


def hop(scalars, slot, count, chips, recv, sums, part):
    array, i = sums
    rows, cols = array.shape[1] // PARTS, array.shape[2]
    message = pl.BlockSpec((rows, cols), lambda n, c: (0, 0))
    operands, in_specs = [], []
    if recv is not None:
        operands.append(recv)
        in_specs.append(message)
    operands.append(array)
    in_specs.append(pl.BlockSpec((1, rows, cols), lambda n, c: (i, part, 0)))
    plan = (slot, count, chips, recv is not None)
    return pl.pallas_call(
        functools.partial(hop_kernel, plan),
        out_shape=jax.ShapeDtypeStruct((rows, cols), BF16),
        grid_spec=pltpu.PrefetchScalarGridSpec(
            num_scalar_prefetch=1,
            grid=(1,),
            in_specs=in_specs,
            out_specs=message,
        ),
        compiler_params=PARAMS,
        cost_estimate=cost(),
    )(scalars, *operands)


def choose_kernel(wanted, hops, scalar_ref, *refs):
    *candidates, sems = refs
    candidates, outs = candidates[:-wanted], candidates[-wanted:]
    rows = candidates[0].shape[0]

    def copy(k, n, part):
        return pltpu.make_async_copy(
            candidates[(k + n) * PARTS + part],
            outs[k].at[pl.ds(part * rows, rows)],
            sems.at[k, part],
        )

    for n in range(hops):

        @pl.when(scalar_ref[0] == n)
        def _():
            for k in range(wanted):
                for part in range(PARTS):
                    copy(k, n, part).start()

    for k in range(wanted):
        for part in range(PARTS):
            copy(k, 0, part).wait()


def choose(place, wanted, hops, candidates):
    rows, cols = candidates[0].shape
    return pl.pallas_call(
        functools.partial(choose_kernel, wanted, hops),
        out_shape=[jax.ShapeDtypeStruct((rows * PARTS, cols), BF16)] * wanted,
        in_specs=[pl.BlockSpec(memory_space=pltpu.SMEM)]
        + [pl.BlockSpec(memory_space=pl.ANY)] * len(candidates),
        scratch_shapes=[pltpu.SemaphoreType.DMA((wanted, PARTS))],
        compiler_params=PARAMS,
        cost_estimate=cost(),
    )(place, *candidates)


def forward_on_kernel(scalar_ref, in_ref, out_ref):
    out_ref[...] = in_ref[...]


def forward_on(scalars, message):
    return pl.pallas_call(
        forward_on_kernel,
        out_shape=jax.ShapeDtypeStruct(message.shape, message.dtype),
        in_specs=[
            pl.BlockSpec(memory_space=pltpu.SMEM),
            pl.BlockSpec(memory_space=pltpu.VMEM),
        ],
        compiler_params=PARAMS,
        cost_estimate=cost(),
    )(scalars, message)


def gradients_kernel(units, scale, first, scalar_ref, xt_ref, g_ref, *refs):
    messages, refs = refs[:units], refs[units if first else units + 3 :]
    gg_ref, gu_ref, gd_ref, token_ref = refs
    width = gg_ref.shape[1]
    pass_on(scalar_ref, token_ref)
    for u in range(units):

        @pl.when(pl.program_id(0) == u)
        def _():
            both = dot(xt_ref[...], messages[u][:, width:]) * scale
            gg_ref[...] = both[:, :width].astype(BF16)
            gu_ref[...] = both[:, width:].astype(BF16)
            scaled = messages[u][:, :width]
            gd_ref[...] = (dot(scaled, g_ref[...], ROWS_FIRST) * scale).astype(BF16)


def gradients(scalars, begin, count, scale, x_t, g, messages, grads):
    slots, feats = g.shape
    width = messages[0].shape[1] // 3
    hidden = 2 * count * width
    units = len(messages)

    def at(u, c):
        return c[FIXED + begin + u]

    column = pl.BlockSpec((feats, width), lambda u, c: (0, at(u, c)))
    in_specs = [
        pl.BlockSpec((feats, slots), lambda u, c: (0, 0)),
        pl.BlockSpec((slots, feats), lambda u, c: (0, 0)),
    ]
    in_specs += [pl.BlockSpec((slots, 3 * width), lambda u, c: (0, 0))] * units
    operands = [x_t, g, *messages]
    aliases = {}
    if grads is not None:
        aliases = {len(operands) + 1 + n: n for n in range(3)}
        operands += grads
        in_specs += [pl.BlockSpec(memory_space=pl.ANY)] * 3
    *grads, token = pl.pallas_call(
        functools.partial(gradients_kernel, units, scale, grads is None),
        out_shape=[
            jax.ShapeDtypeStruct((feats, hidden), BF16),
            jax.ShapeDtypeStruct((feats, hidden), BF16),
            jax.ShapeDtypeStruct((hidden, feats), BF16),
            jax.ShapeDtypeStruct(scalars.shape, jnp.int32),
        ],
        grid_spec=pltpu.PrefetchScalarGridSpec(
            num_scalar_prefetch=1,
            grid=(units,),
            in_specs=in_specs,
            out_specs=[
                column,
                column,
                pl.BlockSpec((width, feats), lambda u, c: (at(u, c), 0)),
                pl.BlockSpec(memory_space=pltpu.SMEM),
            ],
        ),
        input_output_aliases=aliases,
        compiler_params=PARAMS,
        cost_estimate=cost(),
    )(scalars, *operands)
    return grads, token


def sum_rows_kernel(units, pieces, scalar_ref, *refs):
    messages, weights, refs = refs[:units], refs[units : 3 * units], refs[3 * units :]
    width = weights[0].shape[1]
    both = jnp.concatenate([message[:, width:] for message in messages], axis=1)
    part = dot(both, jnp.concatenate([w[...] for w in weights], axis=1), LAST_DIMS)
    if not pieces:
        out_ref, token_ref = refs
        out_ref[...] = part
        pass_on(scalar_ref, token_ref)
        return
    acc_in, *outs, acc = refs
    acc[...] = acc_in[...] + part
    size = outs[0].shape[0]
    for n, out in enumerate(outs):
        start = pl.multiple_of((scalar_ref[1] ^ n) * size, size)
        out[...] = acc[pl.ds(start, size), :].astype(BF16)


def sum_rows(scalars, begin, messages, weights, acc, pieces):
    slots, width = messages[0].shape[0], messages[0].shape[1] // 3
    feats = weights[0].shape[0]
    units = len(messages)
    in_specs = [pl.BlockSpec((slots, 3 * width), lambda n, c: (0, 0))] * units
    operands = list(messages)
    for u in range(units):
        column = pl.BlockSpec((feats, width), lambda n, c, u=u: (0, c[FIXED + begin + u]))
        operands += in_hbm(*weights)
        in_specs += [column, column]
    whole = pl.BlockSpec((slots, feats), lambda n, c: (0, 0))
    if pieces:
        operands.append(acc)
        in_specs.append(whole)
        out_shape = [jax.ShapeDtypeStruct((slots // pieces, feats), BF16)] * pieces
        out_specs = [pl.BlockSpec((slots // pieces, feats), lambda n, c: (0, 0))] * pieces
        scratch = [pltpu.VMEM((slots, feats), F32)]
    else:
        out_shape = [
            jax.ShapeDtypeStruct((slots, feats), F32),
            jax.ShapeDtypeStruct(scalars.shape, jnp.int32),
        ]
        out_specs = [whole, pl.BlockSpec(memory_space=pltpu.SMEM)]
        scratch = []
    return pl.pallas_call(
        functools.partial(sum_rows_kernel, units, pieces),
        out_shape=out_shape,
        grid_spec=pltpu.PrefetchScalarGridSpec(
            num_scalar_prefetch=1,
            grid=(1,),
            in_specs=in_specs,
            out_specs=out_specs,
            scratch_shapes=scratch,
        ),
        compiler_params=PARAMS,
        cost_estimate=cost(),
    )(scalars, *operands)


def body(tokens, grad_out, expert_ids, route_weights, w_gate, w_up, w_down):
    experts = lax.axis_size("expert")
    groups = lax.axis_size("dp")
    tok_rows = tokens.shape[0]
    feats = w_gate.shape[1]
    capacity = tok_rows // 2
    chips = groups // 2
    count = chips
    assert groups == 2 * experts and tokens.shape[1] == 2 * feats
    inv_root = 1.0 / math.sqrt(tok_rows * groups)
    expert = lax.axis_index("expert").astype(jnp.int32)
    block = lax.axis_index("dp").astype(jnp.int32)
    chip, core = block // 2, block % 2
    along = jnp.where(core == 0, chip, chips - 1 - chip)
    w_gate, w_up, w_down = w_gate[0], w_up[0], w_down[0]
    ids, weights = expert_ids.T, route_weights.T

    swap = [(j, j ^ 1) for j in range(groups)]
    up = [2 * z for z in range(chips)]
    circle = up + [j + 1 for j in reversed(up)]
    ring = list(zip(circle, circle[1:] + circle[:1]))

    scalars = [along, expert + experts * core, block % experts, block // experts, expert]
    scalars += [(d ^ 1 ^ core) * count + k for d in range(2) for k in range(count)]
    scalars += [(1 - core) * count + (i - (chips - 1 - along)) % count for i in range(count)]
    scalars += [core * count + (i - along) % count for i in range(count)]
    scalars = jnp.stack(scalars).astype(jnp.int32)

    def exchange(messages):
        came = [messages[0]]
        for t in range(1, experts):
            came.append(lax.ppermute(messages[t], "expert", [(q, q ^ t) for q in range(experts)]))
        blocks = assemble(scalars, came).reshape(groups, capacity, feats)
        blocks = lax.all_to_all(blocks, "dp", split_axis=0, concat_axis=0, tiled=True)
        return blocks.reshape(groups * capacity, feats)

    x_messages, _, token = dispatch_rows(scalars, ids, weights, tokens, experts, False)
    g_messages, hot, _ = dispatch_rows(token, ids, weights, grad_out, experts, True)
    x = exchange(x_messages)
    g = exchange(g_messages)

    other_gu, own_gu, x_t = gate_up(scalars, x, w_gate, w_up, count)
    sib_gu = lax.ppermute(other_gu, "dp", swap)
    spans = ((0, count // 2), (count // 2, count - count // 2))
    others = [
        lax.ppermute(back_rows(scalars, g, w_down, begin, size, count, ()), "dp", swap)
        for begin, size in spans
    ]
    sums = []
    for (begin, size), sib_b in zip(spans, others):
        shares = (sib_b, own_gu, sib_gu)
        both = back_rows(scalars, g, w_down, begin, size, count, shares)
        sums += [(both, i) for i in range(size)]

    slots = 2 * count + chips - 2
    first_back = chips - 1 + count
    recv = []
    gate_and_up = (w_gate, w_up)
    place = along.astype(jnp.int32)[None]

    def pick(token, begin, wanted):
        found = recv[count - 1 + begin : count - 1 + begin + chips + wanted - 1]
        return choose(token, wanted, chips, [part for came in found for part in came])

    early = count - 1
    mine, grads = [], None
    for s in range(slots):
        came = []
        for part in range(PARTS):
            send = recv[s - 1][part] if s else None
            if s < first_back:
                send = hop(place, s, count, chips, send, sums[s % count], part)
            elif s > first_back and part == 0:
                k = len(mine)
                mine += pick(place, k, 1)
                grads, token = gradients(
                    scalars, k, count, inv_root, x_t, g, mine[-1:], grads
                )
                send = forward_on(token, send)
            came.append(lax.ppermute(send, "dp", ring))
        recv.append(came)

    ready = len(mine)
    mine += pick(place, ready, early - ready)
    others = [lax.ppermute(message, "dp", swap) for message in mine]
    acc, token = sum_rows(scalars, 0, mine, gate_and_up, None, 0)
    last = pick(token, early, count - early)
    grads, _ = gradients(
        token, ready, count, inv_root, x_t, g, mine[ready:], grads
    )
    mine = last
    others += [lax.ppermute(message, "dp", swap) for message in mine]
    units = [*mine, *others]
    pieces = sum_rows(scalars, early, units, gate_and_up, acc, groups)
    returned = []
    for r, piece in enumerate(pieces):
        pairs = []
        for q in range(experts):
            for b in range(groups):
                h, e = divmod(b ^ r, experts)
                pairs.append((e * groups + 2 * q + h, q * groups + b))
        returned.append(lax.ppermute(piece, ("expert", "dp"), pairs))
    grads, _ = gradients(scalars, early, count, inv_root, x_t, g, units, grads)
    grad_tokens = combine_rows(scalars, hot, returned, experts)
    return (grad_tokens, grads[0][None], grads[1][None], grads[2][None])


def solution(mesh):
    in_specs = (
        P("dp", "expert"),
        P("dp", "expert"),
        P("dp", None),
        P("dp", None),
        P("expert", "dp", None),
        P("expert", "dp", None),
        P("expert", None, "dp"),
    )
    out_specs = (
        P("dp", "expert"),
        P("expert", "dp", None),
        P("expert", "dp", None),
        P("expert", None, "dp"),
    )
    return jax.shard_map(body, mesh=mesh, in_specs=in_specs, out_specs=out_specs, check_vma=False)
```

```python
import functools
import math

import jax
import jax.numpy as jnp
from jax import lax
from jax.experimental import pallas as pl
from jax.experimental.pallas import tpu as pltpu
from jax.sharding import PartitionSpec as P

F32 = jnp.float32
BF16 = jnp.bfloat16
LAST_DIMS = (((1,), (1,)), ((), ()))
ROWS_FIRST = (((0,), (0,)), ((), ()))
FIXED = 5
PARTS = 2
PARAMS = pltpu.CompilerParams(vmem_limit_bytes=28 * 1024 * 1024)


def dot(a, b, dims=None):
    if dims is None:
        return jnp.dot(a, b, preferred_element_type=F32)
    return lax.dot_general(a, b, dims, preferred_element_type=F32)


def cost():
    return pl.CostEstimate(flops=1024, bytes_accessed=1024, transcendentals=0)


def in_hbm(*arrays):
    return [pltpu.with_memory_space_constraint(a, pltpu.HBM) for a in arrays]


def pass_on(scalar_ref, out_ref):
    for n in range(out_ref.shape[0]):
        out_ref[n] = scalar_ref[n]


def slot_one_hot(ids_ref, experts, capacity):
    tokens = ids_ref.shape[1]
    first, second = ids_ref[0:1, :], ids_ref[1:2, :]
    expert = lax.broadcasted_iota(jnp.int32, (8 * (-(-experts // 8)), tokens), 0)
    chosen = (first == expert) | (second == expert)
    before = lax.broadcasted_iota(jnp.int32, (tokens, tokens), 0) < lax.broadcasted_iota(
        jnp.int32, (tokens, tokens), 1
    )
    place = dot(chosen.astype(F32).astype(BF16), before.astype(F32).astype(BF16))
    place = jnp.where(chosen, place, -1.0).astype(jnp.int32)
    slot = lax.broadcasted_iota(jnp.int32, (capacity, tokens), 0)
    return [slot == place[e : e + 1, :] for e in range(experts)]


def dispatch_kernel(experts, weighted, scalar_ref, ids_hbm, weights_hbm, rows_hbm, *refs):
    *messages, hot_ref, token_ref, ids_ref, weights_ref, rows_ref, scale_ref, sems = refs
    _, capacity, feats = messages[0].shape
    pass_on(scalar_ref, token_ref)
    pairs = [(ids_hbm, ids_ref), (weights_hbm, weights_ref)]
    for h in range(2):
        whole = len(rows_hbm.shape) == 3
        half = rows_hbm.at[h] if whole else rows_hbm.at[:, pl.ds(h * feats, feats)]
        pairs.append((half, rows_ref.at[h]))
    copies = [pltpu.make_async_copy(a, b, sems.at[n]) for n, (a, b) in enumerate(pairs)]
    for copy in copies:
        copy.start()
    copies[0].wait()
    copies[1].wait()
    for e, hit in enumerate(slot_one_hot(ids_ref, experts, capacity)):
        place = slice(e * capacity, (e + 1) * capacity)
        hot_ref[place, :] = hit.astype(F32).astype(BF16)
        if weighted:
            weight = jnp.where(ids_ref[0:1, :] == e, weights_ref[0:1, :], weights_ref[1:2, :])
            weight = jnp.sum(jnp.where(hit, weight, 0.0), axis=1, keepdims=True)
            scale_ref[place, :] = jnp.broadcast_to(weight, (capacity, scale_ref.shape[1]))
    places = [
        pl.ds(pl.multiple_of((scalar_ref[4] ^ t) * capacity, capacity), capacity)
        for t in range(experts)
    ]
    hot = jnp.concatenate([hot_ref[place, :] for place in places], axis=0)
    for h in range(2):
        copies[2 + h].wait()
        out = dot(hot, rows_ref[h])
        for t, place in enumerate(places):
            part = out[t * capacity : (t + 1) * capacity]
            if weighted:
                part = part * scale_ref[place, 0:1]
            messages[t][h] = part.astype(BF16)


def dispatch_rows(scalars, ids, weights, rows, experts, weighted):
    tokens, feats = rows.shape[0], rows.shape[1] // 2
    capacity = tokens // 2
    if feats % 128:
        rows = rows.reshape(tokens, 2, feats).transpose(1, 0, 2)
    *messages, hot, token = pl.pallas_call(
        functools.partial(dispatch_kernel, experts, weighted),
        out_shape=[jax.ShapeDtypeStruct((2, capacity, feats), BF16)] * experts
        + [
            jax.ShapeDtypeStruct((experts * capacity, tokens), BF16),
            jax.ShapeDtypeStruct(scalars.shape, jnp.int32),
        ],
        in_specs=[pl.BlockSpec(memory_space=pltpu.SMEM)]
        + [pl.BlockSpec(memory_space=pltpu.HBM)] * 3,
        out_specs=[pl.BlockSpec(memory_space=pltpu.VMEM)] * (experts + 1)
        + [pl.BlockSpec(memory_space=pltpu.SMEM)],
        scratch_shapes=[
            pltpu.VMEM((2, tokens), jnp.int32),
            pltpu.VMEM((2, tokens), F32),
            pltpu.VMEM((2, tokens, feats), BF16),
            pltpu.VMEM((experts * capacity, 128), F32),
            pltpu.SemaphoreType.DMA((4,)),
        ],
        compiler_params=PARAMS,
        cost_estimate=cost(),
    )(scalars, *in_hbm(ids, weights, rows))
    return messages, hot, token


def assemble_kernel(scalar_ref, *refs):
    *messages, out_ref, sems = refs

    def copy(t, message):
        return pltpu.make_async_copy(message, out_ref.at[t ^ scalar_ref[4]], sems.at[t])

    for t, message in enumerate(messages):
        copy(t, message).start()
    for t, message in enumerate(messages):
        copy(t, message).wait()


def assemble(scalars, messages):
    return pl.pallas_call(
        assemble_kernel,
        out_shape=jax.ShapeDtypeStruct((len(messages), *messages[0].shape), BF16),
        in_specs=[pl.BlockSpec(memory_space=pltpu.SMEM)]
        + [pl.BlockSpec(memory_space=pl.ANY)] * len(messages),
        scratch_shapes=[pltpu.SemaphoreType.DMA((len(messages),))],
        compiler_params=PARAMS,
        cost_estimate=cost(),
    )(scalars, *messages)


def combine_kernel(experts, scalar_ref, hot_ref, *refs):
    pieces, (out_ref, rows_ref, sems) = refs[:-3], refs[-3:]
    capacity = pieces[0].shape[0]
    at = pl.program_id(0)

    def copy(n):
        return pltpu.make_async_copy(
            pieces[n], rows_ref.at[pl.ds(n * capacity, capacity)], sems.at[n]
        )

    @pl.when(at == 0)
    def _():
        for n in range(len(pieces)):
            copy(n).start()

    hot = jnp.concatenate(
        [
            hot_ref[pl.ds(pl.multiple_of((scalar_ref[2] ^ n) * capacity, capacity), capacity), :]
            for n in range(experts)
        ],
        axis=0,
    )
    for half in range(2):

        @pl.when(at == half)
        def _():
            for n in range(half * experts, (half + 1) * experts):
                copy(n).wait()
            rows = rows_ref[half * experts * capacity : (half + 1) * experts * capacity, :]
            out = dot(hot, rows, ROWS_FIRST).astype(BF16)
            out_ref[...] = out.reshape(out_ref.shape)


def combine_rows(scalars, hot, pieces, experts):
    tokens = hot.shape[1]
    capacity, feats = pieces[0].shape
    if feats % 128:
        out_shape = jax.ShapeDtypeStruct((2, tokens, feats), BF16)
        out_spec = pl.BlockSpec((1, tokens, feats), lambda a, c: (a ^ c[3], 0, 0))
    else:
        out_shape = jax.ShapeDtypeStruct((tokens, 2 * feats), BF16)
        out_spec = pl.BlockSpec((tokens, feats), lambda a, c: (0, a ^ c[3]))
    out = pl.pallas_call(
        functools.partial(combine_kernel, experts),
        out_shape=out_shape,
        grid_spec=pltpu.PrefetchScalarGridSpec(
            num_scalar_prefetch=1,
            grid=(2,),
            in_specs=[pl.BlockSpec((experts * capacity, tokens), lambda a, c: (0, 0))]
            + [pl.BlockSpec(memory_space=pltpu.HBM)] * len(pieces),
            out_specs=out_spec,
            scratch_shapes=[
                pltpu.VMEM((len(pieces) * capacity, feats), BF16),
                pltpu.SemaphoreType.DMA((len(pieces),)),
            ],
        ),
        compiler_params=PARAMS,
        cost_estimate=cost(),
    )(scalars, hot, *in_hbm(*pieces))
    if feats % 128:
        out = out.transpose(1, 0, 2).reshape(tokens, 2 * feats)
    return out


def gate_up_kernel(scalar_ref, x_ref, wg_ref, wu_ref, *outs):
    width = wg_ref.shape[1]

    @pl.when((pl.program_id(0) == 0) & (pl.program_id(1) == 0))
    def _():
        outs[2][...] = x_ref[...].T

    for own in range(2):

        @pl.when(pl.program_id(1) == own)
        def _():
            outs[own][0, :, :width] = dot(x_ref[...], wg_ref[...]).astype(BF16)
            outs[own][0, :, width:] = dot(x_ref[...], wu_ref[...]).astype(BF16)


def gate_up(scalars, x, w_gate, w_up, count):
    slots, feats = x.shape
    width = w_gate.shape[1] // (2 * count)
    out = jax.ShapeDtypeStruct((count, slots, 2 * width), BF16)
    out_spec = pl.BlockSpec((1, slots, 2 * width), lambda i, own, c: (i, 0, 0))
    column = pl.BlockSpec(
        (feats, width), lambda i, own, c: (0, c[FIXED + 2 * count + own * count + i])
    )
    return pl.pallas_call(
        gate_up_kernel,
        out_shape=(out, out, jax.ShapeDtypeStruct((feats, slots), BF16)),
        grid_spec=pltpu.PrefetchScalarGridSpec(
            num_scalar_prefetch=1,
            grid=(count, 2),
            in_specs=[pl.BlockSpec((slots, feats), lambda i, own, c: (0, 0)), column, column],
            out_specs=(
                out_spec,
                out_spec,
                pl.BlockSpec((feats, slots), lambda i, own, c: (0, 0)),
            ),
        ),
        compiler_params=PARAMS,
        cost_estimate=cost(),
    )(scalars, x, *in_hbm(w_gate, w_up))


def back_kernel(scalar_ref, g_ref, wd_ref, *refs):
    *shares, out_ref = refs
    back = dot(g_ref[...], wd_ref[...], LAST_DIMS)
    if not shares:
        out_ref[0] = back.astype(BF16)
        return
    sib_b, own_gu, sib_gu = shares
    width = back.shape[1]
    both = own_gu[0].astype(F32) + sib_gu[0].astype(F32)
    out_ref[0, :, : 2 * width] = both.astype(BF16)
    out_ref[0, :, 2 * width :] = (back + sib_b[0].astype(F32)).astype(BF16)


def back_rows(scalars, g, w_down, begin, size, count, shares):
    slots, feats = g.shape
    width = w_down.shape[0] // (2 * count)
    own = bool(shares)
    row = pl.BlockSpec(
        (width, feats), lambda i, c: (c[FIXED + 2 * count + own * count + begin + i], 0)
    )
    in_specs = [pl.BlockSpec((slots, feats), lambda i, c: (0, 0)), row]
    if own:
        in_specs.append(pl.BlockSpec((1, slots, width), lambda i, c: (i, 0, 0)))
        in_specs += [pl.BlockSpec((1, slots, 2 * width), lambda i, c: (begin + i, 0, 0))] * 2
    cols = (3 if own else 1) * width
    return pl.pallas_call(
        back_kernel,
        out_shape=jax.ShapeDtypeStruct((size, slots, cols), BF16),
        grid_spec=pltpu.PrefetchScalarGridSpec(
            num_scalar_prefetch=1,
            grid=(size,),
            in_specs=in_specs,
            out_specs=pl.BlockSpec((1, slots, cols), lambda i, c: (i, 0, 0)),
        ),
        compiler_params=PARAMS,
        cost_estimate=cost(),
    )(scalars, g, *in_hbm(w_down), *shares)


def activate(gate, upper, back):
    sig = jax.nn.sigmoid(gate)
    gated = gate * sig
    return (
        (gated * upper).astype(BF16),
        (back * upper * sig * (1.0 + gate * (1.0 - sig))).astype(BF16),
        (back * gated).astype(BF16),
    )


def hop_kernel(plan, scalar_ref, *refs):
    slot, count, chips, came = plan
    sums_ref = refs[-2]
    recv_ref = refs[0] if came else None
    send_ref = refs[-1]
    at = scalar_ref[0]
    width = send_ref.shape[1] // 3
    summing = (at <= slot) & (slot - at < count)

    def total(part):
        columns = slice(part * width, (part + 1) * width)
        value = sums_ref[0, :, columns].astype(F32)
        if came:
            value += jnp.where(at > 0, recv_ref[:, columns].astype(F32), 0.0)
        return value

    @pl.when(summing & (at < chips - 1))
    def _():
        for part in range(3):
            send_ref[:, part * width : (part + 1) * width] = total(part).astype(BF16)

    @pl.when(summing & (at == chips - 1))
    def _():
        for part, value in enumerate(activate(total(0), total(1), total(2))):
            send_ref[:, part * width : (part + 1) * width] = value

    if came:

        @pl.when(jnp.logical_not(summing))
        def _():
            send_ref[...] = recv_ref[...]


def hop(scalars, slot, count, chips, recv, sums, part):
    array, i = sums
    rows, cols = array.shape[1] // PARTS, array.shape[2]
    message = pl.BlockSpec((rows, cols), lambda n, c: (0, 0))
    operands, in_specs = [], []
    if recv is not None:
        operands.append(recv)
        in_specs.append(message)
    operands.append(array)
    in_specs.append(pl.BlockSpec((1, rows, cols), lambda n, c: (i, part, 0)))
    plan = (slot, count, chips, recv is not None)
    return pl.pallas_call(
        functools.partial(hop_kernel, plan),
        out_shape=jax.ShapeDtypeStruct((rows, cols), BF16),
        grid_spec=pltpu.PrefetchScalarGridSpec(
            num_scalar_prefetch=1,
            grid=(1,),
            in_specs=in_specs,
            out_specs=message,
        ),
        compiler_params=PARAMS,
        cost_estimate=cost(),
    )(scalars, *operands)


def choose_kernel(wanted, hops, scalar_ref, *refs):
    *candidates, sems = refs
    candidates, outs = candidates[:-wanted], candidates[-wanted:]
    rows = candidates[0].shape[0]

    def copy(k, n, part):
        return pltpu.make_async_copy(
            candidates[(k + n) * PARTS + part],
            outs[k].at[pl.ds(part * rows, rows)],
            sems.at[k, part],
        )

    for n in range(hops):

        @pl.when(scalar_ref[0] == n)
        def _():
            for k in range(wanted):
                for part in range(PARTS):
                    copy(k, n, part).start()

    for k in range(wanted):
        for part in range(PARTS):
            copy(k, 0, part).wait()


def choose(place, wanted, hops, candidates):
    rows, cols = candidates[0].shape
    return pl.pallas_call(
        functools.partial(choose_kernel, wanted, hops),
        out_shape=[jax.ShapeDtypeStruct((rows * PARTS, cols), BF16)] * wanted,
        in_specs=[pl.BlockSpec(memory_space=pltpu.SMEM)]
        + [pl.BlockSpec(memory_space=pl.ANY)] * len(candidates),
        scratch_shapes=[pltpu.SemaphoreType.DMA((wanted, PARTS))],
        compiler_params=PARAMS,
        cost_estimate=cost(),
    )(place, *candidates)


def forward_on_kernel(scalar_ref, in_ref, out_ref):
    out_ref[...] = in_ref[...]


def forward_on(scalars, message):
    return pl.pallas_call(
        forward_on_kernel,
        out_shape=jax.ShapeDtypeStruct(message.shape, message.dtype),
        in_specs=[
            pl.BlockSpec(memory_space=pltpu.SMEM),
            pl.BlockSpec(memory_space=pltpu.VMEM),
        ],
        compiler_params=PARAMS,
        cost_estimate=cost(),
    )(scalars, message)


def gradients_kernel(units, scale, first, scalar_ref, xt_ref, g_ref, *refs):
    messages, refs = refs[:units], refs[units if first else units + 3 :]
    gg_ref, gu_ref, gd_ref, token_ref = refs
    width = gg_ref.shape[1]
    pass_on(scalar_ref, token_ref)
    for u in range(units):

        @pl.when(pl.program_id(0) == u)
        def _():
            both = dot(xt_ref[...], messages[u][:, width:]) * scale
            gg_ref[...] = both[:, :width].astype(BF16)
            gu_ref[...] = both[:, width:].astype(BF16)
            scaled = messages[u][:, :width]
            gd_ref[...] = (dot(scaled, g_ref[...], ROWS_FIRST) * scale).astype(BF16)


def gradients(scalars, begin, count, scale, x_t, g, messages, grads):
    slots, feats = g.shape
    width = messages[0].shape[1] // 3
    hidden = 2 * count * width
    units = len(messages)

    def at(u, c):
        return c[FIXED + begin + u]

    column = pl.BlockSpec((feats, width), lambda u, c: (0, at(u, c)))
    in_specs = [
        pl.BlockSpec((feats, slots), lambda u, c: (0, 0)),
        pl.BlockSpec((slots, feats), lambda u, c: (0, 0)),
    ]
    in_specs += [pl.BlockSpec((slots, 3 * width), lambda u, c: (0, 0))] * units
    operands = [x_t, g, *messages]
    aliases = {}
    if grads is not None:
        aliases = {len(operands) + 1 + n: n for n in range(3)}
        operands += grads
        in_specs += [pl.BlockSpec(memory_space=pl.ANY)] * 3
    *grads, token = pl.pallas_call(
        functools.partial(gradients_kernel, units, scale, grads is None),
        out_shape=[
            jax.ShapeDtypeStruct((feats, hidden), BF16),
            jax.ShapeDtypeStruct((feats, hidden), BF16),
            jax.ShapeDtypeStruct((hidden, feats), BF16),
            jax.ShapeDtypeStruct(scalars.shape, jnp.int32),
        ],
        grid_spec=pltpu.PrefetchScalarGridSpec(
            num_scalar_prefetch=1,
            grid=(units,),
            in_specs=in_specs,
            out_specs=[
                column,
                column,
                pl.BlockSpec((width, feats), lambda u, c: (at(u, c), 0)),
                pl.BlockSpec(memory_space=pltpu.SMEM),
            ],
        ),
        input_output_aliases=aliases,
        compiler_params=PARAMS,
        cost_estimate=cost(),
    )(scalars, *operands)
    return grads, token


def sum_rows_kernel(units, pieces, scalar_ref, *refs):
    messages, weights, refs = refs[:units], refs[units : 3 * units], refs[3 * units :]
    width = weights[0].shape[1]
    both = jnp.concatenate([message[:, width:] for message in messages], axis=1)
    part = dot(both, jnp.concatenate([w[...] for w in weights], axis=1), LAST_DIMS)
    if not pieces:
        out_ref, token_ref = refs
        out_ref[...] = part
        pass_on(scalar_ref, token_ref)
        return
    acc_in, *outs, acc = refs
    acc[...] = acc_in[...] + part
    size = outs[0].shape[0]
    for n, out in enumerate(outs):
        start = pl.multiple_of((scalar_ref[1] ^ n) * size, size)
        out[...] = acc[pl.ds(start, size), :].astype(BF16)


def sum_rows(scalars, begin, messages, weights, acc, pieces):
    slots, width = messages[0].shape[0], messages[0].shape[1] // 3
    feats = weights[0].shape[0]
    units = len(messages)
    in_specs = [pl.BlockSpec((slots, 3 * width), lambda n, c: (0, 0))] * units
    operands = list(messages)
    for u in range(units):
        column = pl.BlockSpec((feats, width), lambda n, c, u=u: (0, c[FIXED + begin + u]))
        operands += in_hbm(*weights)
        in_specs += [column, column]
    whole = pl.BlockSpec((slots, feats), lambda n, c: (0, 0))
    if pieces:
        operands.append(acc)
        in_specs.append(whole)
        out_shape = [jax.ShapeDtypeStruct((slots // pieces, feats), BF16)] * pieces
        out_specs = [pl.BlockSpec((slots // pieces, feats), lambda n, c: (0, 0))] * pieces
        scratch = [pltpu.VMEM((slots, feats), F32)]
    else:
        out_shape = [
            jax.ShapeDtypeStruct((slots, feats), F32),
            jax.ShapeDtypeStruct(scalars.shape, jnp.int32),
        ]
        out_specs = [whole, pl.BlockSpec(memory_space=pltpu.SMEM)]
        scratch = []
    return pl.pallas_call(
        functools.partial(sum_rows_kernel, units, pieces),
        out_shape=out_shape,
        grid_spec=pltpu.PrefetchScalarGridSpec(
            num_scalar_prefetch=1,
            grid=(1,),
            in_specs=in_specs,
            out_specs=out_specs,
            scratch_shapes=scratch,
        ),
        compiler_params=PARAMS,
        cost_estimate=cost(),
    )(scalars, *operands)


def body(tokens, grad_out, expert_ids, route_weights, w_gate, w_up, w_down):
    experts = lax.axis_size("expert")
    groups = lax.axis_size("dp")
    tok_rows = tokens.shape[0]
    feats = w_gate.shape[1]
    capacity = tok_rows // 2
    chips = groups // 2
    count = chips
    assert groups == 2 * experts and tokens.shape[1] == 2 * feats
    inv_root = 1.0 / math.sqrt(tok_rows * groups)
    expert = lax.axis_index("expert").astype(jnp.int32)
    block = lax.axis_index("dp").astype(jnp.int32)
    chip, core = block // 2, block % 2
    along = jnp.where(core == 0, chip, chips - 1 - chip)
    w_gate, w_up, w_down = w_gate[0], w_up[0], w_down[0]
    ids, weights = expert_ids.T, route_weights.T

    swap = [(j, j ^ 1) for j in range(groups)]
    up = [2 * z for z in range(chips)]
    circle = up + [j + 1 for j in reversed(up)]
    ring = list(zip(circle, circle[1:] + circle[:1]))

    scalars = [along, expert + experts * core, block % experts, block // experts, expert]
    scalars += [(d ^ 1 ^ core) * count + k for d in range(2) for k in range(count)]
    scalars += [(1 - core) * count + (i - (chips - 1 - along)) % count for i in range(count)]
    scalars += [core * count + (i - along) % count for i in range(count)]
    scalars = jnp.stack(scalars).astype(jnp.int32)

    def exchange(messages):
        came = [messages[0]]
        for t in range(1, experts):
            came.append(lax.ppermute(messages[t], "expert", [(q, q ^ t) for q in range(experts)]))
        blocks = assemble(scalars, came).reshape(groups, capacity, feats)
        blocks = lax.all_to_all(blocks, "dp", split_axis=0, concat_axis=0, tiled=True)
        return blocks.reshape(groups * capacity, feats)

    x_messages, _, token = dispatch_rows(scalars, ids, weights, tokens, experts, False)
    g_messages, hot, _ = dispatch_rows(token, ids, weights, grad_out, experts, True)
    x = exchange(x_messages)
    g = exchange(g_messages)

    other_gu, own_gu, x_t = gate_up(scalars, x, w_gate, w_up, count)
    sib_gu = lax.ppermute(other_gu, "dp", swap)
    spans = ((0, count // 2), (count // 2, count - count // 2))
    others = [
        lax.ppermute(back_rows(scalars, g, w_down, begin, size, count, ()), "dp", swap)
        for begin, size in spans
    ]
    sums = []
    for (begin, size), sib_b in zip(spans, others):
        shares = (sib_b, own_gu, sib_gu)
        both = back_rows(scalars, g, w_down, begin, size, count, shares)
        sums += [(both, i) for i in range(size)]

    slots = 2 * count + chips - 2
    first_back = chips - 1 + count
    recv = []
    gate_and_up = (w_gate, w_up)
    place = along.astype(jnp.int32)[None]

    def pick(token, begin, wanted):
        found = recv[count - 1 + begin : count - 1 + begin + chips + wanted - 1]
        return choose(token, wanted, chips, [part for came in found for part in came])

    early = count - 1
    mine, grads = [], None
    for s in range(slots):
        came = []
        for part in range(PARTS):
            send = recv[s - 1][part] if s else None
            if s < first_back:
                send = hop(place, s, count, chips, send, sums[s % count], part)
            elif s > first_back and part == 0:
                k = len(mine)
                mine += pick(place, k, 1)
                grads, token = gradients(
                    scalars, k, count, inv_root, x_t, g, mine[-1:], grads
                )
                send = forward_on(token, send)
            came.append(lax.ppermute(send, "dp", ring))
        recv.append(came)

    ready = len(mine)
    mine += pick(place, ready, early - ready)
    others = [lax.ppermute(message, "dp", swap) for message in mine]
    acc, token = sum_rows(scalars, 0, mine, gate_and_up, None, 0)
    last = pick(token, early, count - early)
    mine += last
    others += [lax.ppermute(message, "dp", swap) for message in last]
    grads, token = gradients(token, ready, count, inv_root, x_t, g, mine[ready:], grads)
    units = [*last, *others]
    pieces = sum_rows(token, early, units, gate_and_up, acc, groups)
    returned = []
    for r, piece in enumerate(pieces):
        pairs = []
        for q in range(experts):
            for b in range(groups):
                h, e = divmod(b ^ r, experts)
                pairs.append((e * groups + 2 * q + h, q * groups + b))
        returned.append(lax.ppermute(piece, ("expert", "dp"), pairs))
    grads, _ = gradients(scalars, count, count, inv_root, x_t, g, others, grads)
    grad_tokens = combine_rows(scalars, hot, returned, experts)
    return (grad_tokens, grads[0][None], grads[1][None], grads[2][None])


def solution(mesh):
    in_specs = (
        P("dp", "expert"),
        P("dp", "expert"),
        P("dp", None),
        P("dp", None),
        P("expert", "dp", None),
        P("expert", "dp", None),
        P("expert", None, "dp"),
    )
    out_specs = (
        P("dp", "expert"),
        P("expert", "dp", None),
        P("expert", "dp", None),
        P("expert", None, "dp"),
    )
    return jax.shard_map(body, mesh=mesh, in_specs=in_specs, out_specs=out_specs, check_vma=False)
```

```python
import functools
import math

import jax
import jax.numpy as jnp
from jax import lax
from jax.experimental import pallas as pl
from jax.experimental.pallas import tpu as pltpu
from jax.sharding import PartitionSpec as P

F32 = jnp.float32
BF16 = jnp.bfloat16
LAST_DIMS = (((1,), (1,)), ((), ()))
ROWS_FIRST = (((0,), (0,)), ((), ()))
FIXED = 5
PARTS = 2
PARAMS = pltpu.CompilerParams(vmem_limit_bytes=28 * 1024 * 1024)


def dot(a, b, dims=None):
    if dims is None:
        return jnp.dot(a, b, preferred_element_type=F32)
    return lax.dot_general(a, b, dims, preferred_element_type=F32)


def cost():
    return pl.CostEstimate(flops=1024, bytes_accessed=1024, transcendentals=0)


def in_hbm(*arrays):
    return [pltpu.with_memory_space_constraint(a, pltpu.HBM) for a in arrays]


def pass_on(scalar_ref, out_ref):
    for n in range(out_ref.shape[0]):
        out_ref[n] = scalar_ref[n]


def slot_one_hot(ids_ref, experts, capacity):
    tokens = ids_ref.shape[1]
    first, second = ids_ref[0:1, :], ids_ref[1:2, :]
    expert = lax.broadcasted_iota(jnp.int32, (8 * (-(-experts // 8)), tokens), 0)
    chosen = (first == expert) | (second == expert)
    before = lax.broadcasted_iota(jnp.int32, (tokens, tokens), 0) < lax.broadcasted_iota(
        jnp.int32, (tokens, tokens), 1
    )
    place = dot(chosen.astype(F32).astype(BF16), before.astype(F32).astype(BF16))
    place = jnp.where(chosen, place, -1.0).astype(jnp.int32)
    slot = lax.broadcasted_iota(jnp.int32, (capacity, tokens), 0)
    return [slot == place[e : e + 1, :] for e in range(experts)]


def dispatch_kernel(experts, weighted, scalar_ref, ids_hbm, weights_hbm, rows_hbm, *refs):
    *messages, hot_ref, token_ref, ids_ref, weights_ref, rows_ref, scale_ref, sems = refs
    _, capacity, feats = messages[0].shape
    pass_on(scalar_ref, token_ref)
    pairs = [(ids_hbm, ids_ref), (weights_hbm, weights_ref)]
    for h in range(2):
        whole = len(rows_hbm.shape) == 3
        half = rows_hbm.at[h] if whole else rows_hbm.at[:, pl.ds(h * feats, feats)]
        pairs.append((half, rows_ref.at[h]))
    copies = [pltpu.make_async_copy(a, b, sems.at[n]) for n, (a, b) in enumerate(pairs)]
    for copy in copies:
        copy.start()
    copies[0].wait()
    copies[1].wait()
    for e, hit in enumerate(slot_one_hot(ids_ref, experts, capacity)):
        place = slice(e * capacity, (e + 1) * capacity)
        hot_ref[place, :] = hit.astype(F32).astype(BF16)
        if weighted:
            weight = jnp.where(ids_ref[0:1, :] == e, weights_ref[0:1, :], weights_ref[1:2, :])
            weight = jnp.sum(jnp.where(hit, weight, 0.0), axis=1, keepdims=True)
            scale_ref[place, :] = jnp.broadcast_to(weight, (capacity, scale_ref.shape[1]))
    places = [
        pl.ds(pl.multiple_of((scalar_ref[4] ^ t) * capacity, capacity), capacity)
        for t in range(experts)
    ]
    hot = jnp.concatenate([hot_ref[place, :] for place in places], axis=0)
    for h in range(2):
        copies[2 + h].wait()
        out = dot(hot, rows_ref[h])
        for t, place in enumerate(places):
            part = out[t * capacity : (t + 1) * capacity]
            if weighted:
                part = part * scale_ref[place, 0:1]
            messages[t][h] = part.astype(BF16)


def dispatch_rows(scalars, ids, weights, rows, experts, weighted):
    tokens, feats = rows.shape[0], rows.shape[1] // 2
    capacity = tokens // 2
    if feats % 128:
        rows = rows.reshape(tokens, 2, feats).transpose(1, 0, 2)
    *messages, hot, token = pl.pallas_call(
        functools.partial(dispatch_kernel, experts, weighted),
        out_shape=[jax.ShapeDtypeStruct((2, capacity, feats), BF16)] * experts
        + [
            jax.ShapeDtypeStruct((experts * capacity, tokens), BF16),
            jax.ShapeDtypeStruct(scalars.shape, jnp.int32),
        ],
        in_specs=[pl.BlockSpec(memory_space=pltpu.SMEM)]
        + [pl.BlockSpec(memory_space=pltpu.HBM)] * 3,
        out_specs=[pl.BlockSpec(memory_space=pltpu.VMEM)] * (experts + 1)
        + [pl.BlockSpec(memory_space=pltpu.SMEM)],
        scratch_shapes=[
            pltpu.VMEM((2, tokens), jnp.int32),
            pltpu.VMEM((2, tokens), F32),
            pltpu.VMEM((2, tokens, feats), BF16),
            pltpu.VMEM((experts * capacity, 128), F32),
            pltpu.SemaphoreType.DMA((4,)),
        ],
        compiler_params=PARAMS,
        cost_estimate=cost(),
    )(scalars, *in_hbm(ids, weights, rows))
    return messages, hot, token


def assemble_kernel(scalar_ref, *refs):
    *messages, out_ref, sems = refs

    def copy(t, message):
        return pltpu.make_async_copy(message, out_ref.at[t ^ scalar_ref[4]], sems.at[t])

    for t, message in enumerate(messages):
        copy(t, message).start()
    for t, message in enumerate(messages):
        copy(t, message).wait()


def assemble(scalars, messages):
    return pl.pallas_call(
        assemble_kernel,
        out_shape=jax.ShapeDtypeStruct((len(messages), *messages[0].shape), BF16),
        in_specs=[pl.BlockSpec(memory_space=pltpu.SMEM)]
        + [pl.BlockSpec(memory_space=pl.ANY)] * len(messages),
        scratch_shapes=[pltpu.SemaphoreType.DMA((len(messages),))],
        compiler_params=PARAMS,
        cost_estimate=cost(),
    )(scalars, *messages)


def combine_kernel(experts, scalar_ref, hot_ref, *refs):
    pieces, (out_ref, rows_ref, sems) = refs[:-3], refs[-3:]
    capacity = pieces[0].shape[0]
    at = pl.program_id(0)

    def copy(n):
        return pltpu.make_async_copy(
            pieces[n], rows_ref.at[pl.ds(n * capacity, capacity)], sems.at[n]
        )

    @pl.when(at == 0)
    def _():
        for n in range(len(pieces)):
            copy(n).start()

    hot = jnp.concatenate(
        [
            hot_ref[pl.ds(pl.multiple_of((scalar_ref[2] ^ n) * capacity, capacity), capacity), :]
            for n in range(experts)
        ],
        axis=0,
    )
    for half in range(2):

        @pl.when(at == half)
        def _():
            for n in range(half * experts, (half + 1) * experts):
                copy(n).wait()
            rows = rows_ref[half * experts * capacity : (half + 1) * experts * capacity, :]
            out = dot(hot, rows, ROWS_FIRST).astype(BF16)
            out_ref[...] = out.reshape(out_ref.shape)


def combine_rows(scalars, hot, pieces, experts):
    tokens = hot.shape[1]
    capacity, feats = pieces[0].shape
    if feats % 128:
        out_shape = jax.ShapeDtypeStruct((2, tokens, feats), BF16)
        out_spec = pl.BlockSpec((1, tokens, feats), lambda a, c: (a ^ c[3], 0, 0))
    else:
        out_shape = jax.ShapeDtypeStruct((tokens, 2 * feats), BF16)
        out_spec = pl.BlockSpec((tokens, feats), lambda a, c: (0, a ^ c[3]))
    out = pl.pallas_call(
        functools.partial(combine_kernel, experts),
        out_shape=out_shape,
        grid_spec=pltpu.PrefetchScalarGridSpec(
            num_scalar_prefetch=1,
            grid=(2,),
            in_specs=[pl.BlockSpec((experts * capacity, tokens), lambda a, c: (0, 0))]
            + [pl.BlockSpec(memory_space=pltpu.HBM)] * len(pieces),
            out_specs=out_spec,
            scratch_shapes=[
                pltpu.VMEM((len(pieces) * capacity, feats), BF16),
                pltpu.SemaphoreType.DMA((len(pieces),)),
            ],
        ),
        compiler_params=PARAMS,
        cost_estimate=cost(),
    )(scalars, hot, *in_hbm(*pieces))
    if feats % 128:
        out = out.transpose(1, 0, 2).reshape(tokens, 2 * feats)
    return out


def gate_up_kernel(scalar_ref, x_ref, wg_ref, wu_ref, *outs):
    width = wg_ref.shape[1]

    @pl.when((pl.program_id(0) == 0) & (pl.program_id(1) == 0))
    def _():
        outs[2][...] = x_ref[...].T

    for own in range(2):

        @pl.when(pl.program_id(1) == own)
        def _():
            outs[own][0, :, :width] = dot(x_ref[...], wg_ref[...]).astype(BF16)
            outs[own][0, :, width:] = dot(x_ref[...], wu_ref[...]).astype(BF16)


def gate_up(scalars, x, w_gate, w_up, count):
    slots, feats = x.shape
    width = w_gate.shape[1] // (2 * count)
    out = jax.ShapeDtypeStruct((count, slots, 2 * width), BF16)
    out_spec = pl.BlockSpec((1, slots, 2 * width), lambda i, own, c: (i, 0, 0))
    column = pl.BlockSpec(
        (feats, width), lambda i, own, c: (0, c[FIXED + 2 * count + own * count + i])
    )
    return pl.pallas_call(
        gate_up_kernel,
        out_shape=(out, out, jax.ShapeDtypeStruct((feats, slots), BF16)),
        grid_spec=pltpu.PrefetchScalarGridSpec(
            num_scalar_prefetch=1,
            grid=(count, 2),
            in_specs=[pl.BlockSpec((slots, feats), lambda i, own, c: (0, 0)), column, column],
            out_specs=(
                out_spec,
                out_spec,
                pl.BlockSpec((feats, slots), lambda i, own, c: (0, 0)),
            ),
        ),
        compiler_params=PARAMS,
        cost_estimate=cost(),
    )(scalars, x, *in_hbm(w_gate, w_up))


def back_kernel(scalar_ref, g_ref, wd_ref, *refs):
    *shares, out_ref = refs
    back = dot(g_ref[...], wd_ref[...], LAST_DIMS)
    if not shares:
        out_ref[0] = back.astype(BF16)
        return
    sib_b, own_gu, sib_gu = shares
    width = back.shape[1]
    both = own_gu[0].astype(F32) + sib_gu[0].astype(F32)
    out_ref[0, :, : 2 * width] = both.astype(BF16)
    out_ref[0, :, 2 * width :] = (back + sib_b[0].astype(F32)).astype(BF16)


def back_rows(scalars, g, w_down, begin, size, count, shares):
    slots, feats = g.shape
    width = w_down.shape[0] // (2 * count)
    own = bool(shares)
    row = pl.BlockSpec(
        (width, feats), lambda i, c: (c[FIXED + 2 * count + own * count + begin + i], 0)
    )
    in_specs = [pl.BlockSpec((slots, feats), lambda i, c: (0, 0)), row]
    if own:
        in_specs.append(pl.BlockSpec((1, slots, width), lambda i, c: (i, 0, 0)))
        in_specs += [pl.BlockSpec((1, slots, 2 * width), lambda i, c: (begin + i, 0, 0))] * 2
    cols = (3 if own else 1) * width
    return pl.pallas_call(
        back_kernel,
        out_shape=jax.ShapeDtypeStruct((size, slots, cols), BF16),
        grid_spec=pltpu.PrefetchScalarGridSpec(
            num_scalar_prefetch=1,
            grid=(size,),
            in_specs=in_specs,
            out_specs=pl.BlockSpec((1, slots, cols), lambda i, c: (i, 0, 0)),
        ),
        compiler_params=PARAMS,
        cost_estimate=cost(),
    )(scalars, g, *in_hbm(w_down), *shares)


def activate(gate, upper, back):
    sig = jax.nn.sigmoid(gate)
    gated = gate * sig
    return (
        (gated * upper).astype(BF16),
        (back * upper * sig * (1.0 + gate * (1.0 - sig))).astype(BF16),
        (back * gated).astype(BF16),
    )


def hop_kernel(plan, scalar_ref, *refs):
    slot, count, chips, came = plan
    sums_ref = refs[-2]
    recv_ref = refs[0] if came else None
    send_ref = refs[-1]
    at = scalar_ref[0]
    width = send_ref.shape[1] // 3
    summing = (at <= slot) & (slot - at < count)

    def total(part):
        columns = slice(part * width, (part + 1) * width)
        value = sums_ref[0, :, columns].astype(F32)
        if came:
            value += jnp.where(at > 0, recv_ref[:, columns].astype(F32), 0.0)
        return value

    @pl.when(summing & (at < chips - 1))
    def _():
        for part in range(3):
            send_ref[:, part * width : (part + 1) * width] = total(part).astype(BF16)

    @pl.when(summing & (at == chips - 1))
    def _():
        for part, value in enumerate(activate(total(0), total(1), total(2))):
            send_ref[:, part * width : (part + 1) * width] = value

    if came:

        @pl.when(jnp.logical_not(summing))
        def _():
            send_ref[...] = recv_ref[...]


def hop(scalars, slot, count, chips, recv, sums, part):
    array, i = sums
    rows, cols = array.shape[1] // PARTS, array.shape[2]
    message = pl.BlockSpec((rows, cols), lambda n, c: (0, 0))
    operands, in_specs = [], []
    if recv is not None:
        operands.append(recv)
        in_specs.append(message)
    operands.append(array)
    in_specs.append(pl.BlockSpec((1, rows, cols), lambda n, c: (i, part, 0)))
    plan = (slot, count, chips, recv is not None)
    return pl.pallas_call(
        functools.partial(hop_kernel, plan),
        out_shape=jax.ShapeDtypeStruct((rows, cols), BF16),
        grid_spec=pltpu.PrefetchScalarGridSpec(
            num_scalar_prefetch=1,
            grid=(1,),
            in_specs=in_specs,
            out_specs=message,
        ),
        compiler_params=PARAMS,
        cost_estimate=cost(),
    )(scalars, *operands)


def choose_kernel(wanted, hops, scalar_ref, *refs):
    *candidates, sems = refs
    candidates, outs = candidates[:-wanted], candidates[-wanted:]
    rows = candidates[0].shape[0]

    def copy(k, n, part):
        return pltpu.make_async_copy(
            candidates[(k + n) * PARTS + part],
            outs[k].at[pl.ds(part * rows, rows)],
            sems.at[k, part],
        )

    for n in range(hops):

        @pl.when(scalar_ref[0] == n)
        def _():
            for k in range(wanted):
                for part in range(PARTS):
                    copy(k, n, part).start()

    for k in range(wanted):
        for part in range(PARTS):
            copy(k, 0, part).wait()


def choose(place, wanted, hops, candidates):
    rows, cols = candidates[0].shape
    return pl.pallas_call(
        functools.partial(choose_kernel, wanted, hops),
        out_shape=[jax.ShapeDtypeStruct((rows * PARTS, cols), BF16)] * wanted,
        in_specs=[pl.BlockSpec(memory_space=pltpu.SMEM)]
        + [pl.BlockSpec(memory_space=pl.ANY)] * len(candidates),
        scratch_shapes=[pltpu.SemaphoreType.DMA((wanted, PARTS))],
        compiler_params=PARAMS,
        cost_estimate=cost(),
    )(place, *candidates)


def forward_on_kernel(scalar_ref, in_ref, out_ref):
    out_ref[...] = in_ref[...]


def forward_on(scalars, message):
    return pl.pallas_call(
        forward_on_kernel,
        out_shape=jax.ShapeDtypeStruct(message.shape, message.dtype),
        in_specs=[
            pl.BlockSpec(memory_space=pltpu.SMEM),
            pl.BlockSpec(memory_space=pltpu.VMEM),
        ],
        compiler_params=PARAMS,
        cost_estimate=cost(),
    )(scalars, message)


def gradients_kernel(units, scale, first, scalar_ref, xt_ref, g_ref, *refs):
    messages, refs = refs[:units], refs[units if first else units + 3 :]
    gg_ref, gu_ref, gd_ref, token_ref = refs
    width = gg_ref.shape[1]
    pass_on(scalar_ref, token_ref)
    for u in range(units):

        @pl.when(pl.program_id(0) == u)
        def _():
            both = dot(xt_ref[...], messages[u][:, width:]) * scale
            gg_ref[...] = both[:, :width].astype(BF16)
            gu_ref[...] = both[:, width:].astype(BF16)
            scaled = messages[u][:, :width]
            gd_ref[...] = (dot(scaled, g_ref[...], ROWS_FIRST) * scale).astype(BF16)


def gradients(scalars, begin, count, scale, x_t, g, messages, grads):
    slots, feats = g.shape
    width = messages[0].shape[1] // 3
    hidden = 2 * count * width
    units = len(messages)

    def at(u, c):
        return c[FIXED + begin + u]

    column = pl.BlockSpec((feats, width), lambda u, c: (0, at(u, c)))
    in_specs = [
        pl.BlockSpec((feats, slots), lambda u, c: (0, 0)),
        pl.BlockSpec((slots, feats), lambda u, c: (0, 0)),
    ]
    in_specs += [pl.BlockSpec((slots, 3 * width), lambda u, c: (0, 0))] * units
    operands = [x_t, g, *messages]
    aliases = {}
    if grads is not None:
        aliases = {len(operands) + 1 + n: n for n in range(3)}
        operands += grads
        in_specs += [pl.BlockSpec(memory_space=pl.ANY)] * 3
    *grads, token = pl.pallas_call(
        functools.partial(gradients_kernel, units, scale, grads is None),
        out_shape=[
            jax.ShapeDtypeStruct((feats, hidden), BF16),
            jax.ShapeDtypeStruct((feats, hidden), BF16),
            jax.ShapeDtypeStruct((hidden, feats), BF16),
            jax.ShapeDtypeStruct(scalars.shape, jnp.int32),
        ],
        grid_spec=pltpu.PrefetchScalarGridSpec(
            num_scalar_prefetch=1,
            grid=(units,),
            in_specs=in_specs,
            out_specs=[
                column,
                column,
                pl.BlockSpec((width, feats), lambda u, c: (at(u, c), 0)),
                pl.BlockSpec(memory_space=pltpu.SMEM),
            ],
        ),
        input_output_aliases=aliases,
        compiler_params=PARAMS,
        cost_estimate=cost(),
    )(scalars, *operands)
    return grads, token


def sum_rows_kernel(units, pieces, scalar_ref, *refs):
    messages, weights, refs = refs[:units], refs[units : 3 * units], refs[3 * units :]
    width = weights[0].shape[1]
    both = jnp.concatenate([message[:, width:] for message in messages], axis=1)
    part = dot(both, jnp.concatenate([w[...] for w in weights], axis=1), LAST_DIMS)
    if not pieces:
        out_ref, token_ref = refs
        out_ref[...] = part
        pass_on(scalar_ref, token_ref)
        return
    acc_in, *outs, acc = refs
    acc[...] = acc_in[...] + part
    size = outs[0].shape[0]
    for n, out in enumerate(outs):
        start = pl.multiple_of((scalar_ref[1] ^ n) * size, size)
        out[...] = acc[pl.ds(start, size), :].astype(BF16)


def sum_rows(scalars, begin, messages, weights, acc, pieces):
    slots, width = messages[0].shape[0], messages[0].shape[1] // 3
    feats = weights[0].shape[0]
    units = len(messages)
    in_specs = [pl.BlockSpec((slots, 3 * width), lambda n, c: (0, 0))] * units
    operands = list(messages)
    for u in range(units):
        column = pl.BlockSpec((feats, width), lambda n, c, u=u: (0, c[FIXED + begin + u]))
        operands += in_hbm(*weights)
        in_specs += [column, column]
    whole = pl.BlockSpec((slots, feats), lambda n, c: (0, 0))
    if pieces:
        operands.append(acc)
        in_specs.append(whole)
        out_shape = [jax.ShapeDtypeStruct((slots // pieces, feats), BF16)] * pieces
        out_specs = [pl.BlockSpec((slots // pieces, feats), lambda n, c: (0, 0))] * pieces
        scratch = [pltpu.VMEM((slots, feats), F32)]
    else:
        out_shape = [
            jax.ShapeDtypeStruct((slots, feats), F32),
            jax.ShapeDtypeStruct(scalars.shape, jnp.int32),
        ]
        out_specs = [whole, pl.BlockSpec(memory_space=pltpu.SMEM)]
        scratch = []
    return pl.pallas_call(
        functools.partial(sum_rows_kernel, units, pieces),
        out_shape=out_shape,
        grid_spec=pltpu.PrefetchScalarGridSpec(
            num_scalar_prefetch=1,
            grid=(1,),
            in_specs=in_specs,
            out_specs=out_specs,
            scratch_shapes=scratch,
        ),
        compiler_params=PARAMS,
        cost_estimate=cost(),
    )(scalars, *operands)


def body(tokens, grad_out, expert_ids, route_weights, w_gate, w_up, w_down):
    experts = lax.axis_size("expert")
    groups = lax.axis_size("dp")
    tok_rows = tokens.shape[0]
    feats = w_gate.shape[1]
    capacity = tok_rows // 2
    chips = groups // 2
    count = chips
    assert groups == 2 * experts and tokens.shape[1] == 2 * feats
    inv_root = 1.0 / math.sqrt(tok_rows * groups)
    expert = lax.axis_index("expert").astype(jnp.int32)
    block = lax.axis_index("dp").astype(jnp.int32)
    chip, core = block // 2, block % 2
    along = jnp.where(core == 0, chip, chips - 1 - chip)
    w_gate, w_up, w_down = w_gate[0], w_up[0], w_down[0]
    ids, weights = expert_ids.T, route_weights.T

    swap = [(j, j ^ 1) for j in range(groups)]
    up = [2 * z for z in range(chips)]
    circle = up + [j + 1 for j in reversed(up)]
    ring = list(zip(circle, circle[1:] + circle[:1]))

    scalars = [along, expert + experts * core, block % experts, block // experts, expert]
    scalars += [(d ^ 1 ^ core) * count + k for d in range(2) for k in range(count)]
    scalars += [(1 - core) * count + (i - (chips - 1 - along)) % count for i in range(count)]
    scalars += [core * count + (i - along) % count for i in range(count)]
    scalars = jnp.stack(scalars).astype(jnp.int32)

    def exchange(messages):
        came = [messages[0]]
        for t in range(1, experts):
            came.append(lax.ppermute(messages[t], "expert", [(q, q ^ t) for q in range(experts)]))
        blocks = assemble(scalars, came).reshape(groups, capacity, feats)
        blocks = lax.all_to_all(blocks, "dp", split_axis=0, concat_axis=0, tiled=True)
        return blocks.reshape(groups * capacity, feats)

    x_messages, _, token = dispatch_rows(scalars, ids, weights, tokens, experts, False)
    g_messages, hot, _ = dispatch_rows(token, ids, weights, grad_out, experts, True)
    x = exchange(x_messages)
    g = exchange(g_messages)

    other_gu, own_gu, x_t = gate_up(scalars, x, w_gate, w_up, count)
    sib_gu = lax.ppermute(other_gu, "dp", swap)
    spans = ((0, count // 2), (count // 2, count - count // 2))
    others = [
        lax.ppermute(back_rows(scalars, g, w_down, begin, size, count, ()), "dp", swap)
        for begin, size in spans
    ]
    sums = []
    for (begin, size), sib_b in zip(spans, others):
        shares = (sib_b, own_gu, sib_gu)
        both = back_rows(scalars, g, w_down, begin, size, count, shares)
        sums += [(both, i) for i in range(size)]

    slots = 2 * count + chips - 2
    first_back = chips - 1 + count
    recv = []
    gate_and_up = (w_gate, w_up)
    place = along.astype(jnp.int32)[None]

    def pick(token, begin, wanted):
        found = recv[count - 1 + begin : count - 1 + begin + chips + wanted - 1]
        return choose(token, wanted, chips, [part for came in found for part in came])

    early = count - 1
    mine, grads = [], None
    for s in range(slots):
        came = []
        for part in range(PARTS):
            send = recv[s - 1][part] if s else None
            if s < first_back:
                send = hop(place, s, count, chips, send, sums[s % count], part)
            elif s > first_back and (part == 0 or s == slots - 1):
                k = len(mine)
                mine += pick(place, k, 1)
                grads, token = gradients(
                    scalars, k, count, inv_root, x_t, g, mine[-1:], grads
                )
                send = forward_on(token, send)
            came.append(lax.ppermute(send, "dp", ring))
        recv.append(came)

    assert len(mine) == early
    others = [lax.ppermute(message, "dp", swap) for message in mine]
    acc, token = sum_rows(scalars, 0, mine, gate_and_up, None, 0)
    last = pick(token, early, count - early)
    others += [lax.ppermute(message, "dp", swap) for message in last]
    grads, token = gradients(token, early, count, inv_root, x_t, g, last, grads)
    units = [*last, *others]
    pieces = sum_rows(token, early, units, gate_and_up, acc, groups)
    returned = []
    for r, piece in enumerate(pieces):
        pairs = []
        for q in range(experts):
            for b in range(groups):
                h, e = divmod(b ^ r, experts)
                pairs.append((e * groups + 2 * q + h, q * groups + b))
        returned.append(lax.ppermute(piece, ("expert", "dp"), pairs))
    grads, _ = gradients(scalars, count, count, inv_root, x_t, g, others, grads)
    grad_tokens = combine_rows(scalars, hot, returned, experts)
    return (grad_tokens, grads[0][None], grads[1][None], grads[2][None])


def solution(mesh):
    in_specs = (
        P("dp", "expert"),
        P("dp", "expert"),
        P("dp", None),
        P("dp", None),
        P("expert", "dp", None),
        P("expert", "dp", None),
        P("expert", None, "dp"),
    )
    out_specs = (
        P("dp", "expert"),
        P("expert", "dp", None),
        P("expert", "dp", None),
        P("expert", None, "dp"),
    )
    return jax.shard_map(body, mesh=mesh, in_specs=in_specs, out_specs=out_specs, check_vma=False)
```

```python
import functools
import math

import jax
import jax.numpy as jnp
from jax import lax
from jax.experimental import pallas as pl
from jax.experimental.pallas import tpu as pltpu
from jax.sharding import PartitionSpec as P

F32 = jnp.float32
BF16 = jnp.bfloat16
LAST_DIMS = (((1,), (1,)), ((), ()))
ROWS_FIRST = (((0,), (0,)), ((), ()))
FIXED = 5
PARTS = 2
PARAMS = pltpu.CompilerParams(vmem_limit_bytes=28 * 1024 * 1024)


def dot(a, b, dims=None):
    if dims is None:
        return jnp.dot(a, b, preferred_element_type=F32)
    return lax.dot_general(a, b, dims, preferred_element_type=F32)


def cost():
    return pl.CostEstimate(flops=1024, bytes_accessed=1024, transcendentals=0)


def in_hbm(*arrays):
    return [pltpu.with_memory_space_constraint(a, pltpu.HBM) for a in arrays]


def pass_on(scalar_ref, out_ref):
    for n in range(out_ref.shape[0]):
        out_ref[n] = scalar_ref[n]


def slot_one_hot(ids_ref, experts, capacity):
    tokens = ids_ref.shape[1]
    first, second = ids_ref[0:1, :], ids_ref[1:2, :]
    expert = lax.broadcasted_iota(jnp.int32, (8 * (-(-experts // 8)), tokens), 0)
    chosen = (first == expert) | (second == expert)
    before = lax.broadcasted_iota(jnp.int32, (tokens, tokens), 0) < lax.broadcasted_iota(
        jnp.int32, (tokens, tokens), 1
    )
    place = dot(chosen.astype(F32).astype(BF16), before.astype(F32).astype(BF16))
    place = jnp.where(chosen, place, -1.0).astype(jnp.int32)
    slot = lax.broadcasted_iota(jnp.int32, (capacity, tokens), 0)
    return [slot == place[e : e + 1, :] for e in range(experts)]


def dispatch_kernel(experts, weighted, scalar_ref, ids_hbm, weights_hbm, rows_hbm, *refs):
    *messages, hot_ref, token_ref, ids_ref, weights_ref, rows_ref, scale_ref, sems = refs
    _, capacity, feats = messages[0].shape
    pass_on(scalar_ref, token_ref)
    pairs = [(ids_hbm, ids_ref), (weights_hbm, weights_ref)]
    for h in range(2):
        whole = len(rows_hbm.shape) == 3
        half = rows_hbm.at[h] if whole else rows_hbm.at[:, pl.ds(h * feats, feats)]
        pairs.append((half, rows_ref.at[h]))
    copies = [pltpu.make_async_copy(a, b, sems.at[n]) for n, (a, b) in enumerate(pairs)]
    for copy in copies:
        copy.start()
    copies[0].wait()
    copies[1].wait()
    for e, hit in enumerate(slot_one_hot(ids_ref, experts, capacity)):
        place = slice(e * capacity, (e + 1) * capacity)
        hot_ref[place, :] = hit.astype(F32).astype(BF16)
        if weighted:
            weight = jnp.where(ids_ref[0:1, :] == e, weights_ref[0:1, :], weights_ref[1:2, :])
            weight = jnp.sum(jnp.where(hit, weight, 0.0), axis=1, keepdims=True)
            scale_ref[place, :] = jnp.broadcast_to(weight, (capacity, scale_ref.shape[1]))
    places = [
        pl.ds(pl.multiple_of((scalar_ref[4] ^ t) * capacity, capacity), capacity)
        for t in range(experts)
    ]
    hot = jnp.concatenate([hot_ref[place, :] for place in places], axis=0)
    for h in range(2):
        copies[2 + h].wait()
        out = dot(hot, rows_ref[h])
        for t, place in enumerate(places):
            part = out[t * capacity : (t + 1) * capacity]
            if weighted:
                part = part * scale_ref[place, 0:1]
            messages[t][h] = part.astype(BF16)


def dispatch_rows(scalars, ids, weights, rows, experts, weighted):
    tokens, feats = rows.shape[0], rows.shape[1] // 2
    capacity = tokens // 2
    if feats % 128:
        rows = rows.reshape(tokens, 2, feats).transpose(1, 0, 2)
    *messages, hot, token = pl.pallas_call(
        functools.partial(dispatch_kernel, experts, weighted),
        out_shape=[jax.ShapeDtypeStruct((2, capacity, feats), BF16)] * experts
        + [
            jax.ShapeDtypeStruct((experts * capacity, tokens), BF16),
            jax.ShapeDtypeStruct(scalars.shape, jnp.int32),
        ],
        in_specs=[pl.BlockSpec(memory_space=pltpu.SMEM)]
        + [pl.BlockSpec(memory_space=pltpu.HBM)] * 3,
        out_specs=[pl.BlockSpec(memory_space=pltpu.VMEM)] * (experts + 1)
        + [pl.BlockSpec(memory_space=pltpu.SMEM)],
        scratch_shapes=[
            pltpu.VMEM((2, tokens), jnp.int32),
            pltpu.VMEM((2, tokens), F32),
            pltpu.VMEM((2, tokens, feats), BF16),
            pltpu.VMEM((experts * capacity, 128), F32),
            pltpu.SemaphoreType.DMA((4,)),
        ],
        compiler_params=PARAMS,
        cost_estimate=cost(),
    )(scalars, *in_hbm(ids, weights, rows))
    return messages, hot, token


def assemble_kernel(scalar_ref, *refs):
    *messages, out_ref, sems = refs

    def copy(t, message):
        return pltpu.make_async_copy(message, out_ref.at[t ^ scalar_ref[4]], sems.at[t])

    for t, message in enumerate(messages):
        copy(t, message).start()
    for t, message in enumerate(messages):
        copy(t, message).wait()


def assemble(scalars, messages):
    return pl.pallas_call(
        assemble_kernel,
        out_shape=jax.ShapeDtypeStruct((len(messages), *messages[0].shape), BF16),
        in_specs=[pl.BlockSpec(memory_space=pltpu.SMEM)]
        + [pl.BlockSpec(memory_space=pl.ANY)] * len(messages),
        scratch_shapes=[pltpu.SemaphoreType.DMA((len(messages),))],
        compiler_params=PARAMS,
        cost_estimate=cost(),
    )(scalars, *messages)


def combine_kernel(experts, scalar_ref, hot_ref, *refs):
    pieces, (out_ref, rows_ref, sems) = refs[:-3], refs[-3:]
    capacity = pieces[0].shape[0]
    at = pl.program_id(0)

    def copy(n):
        return pltpu.make_async_copy(
            pieces[n], rows_ref.at[pl.ds(n * capacity, capacity)], sems.at[n]
        )

    @pl.when(at == 0)
    def _():
        for n in range(len(pieces)):
            copy(n).start()

    hot = jnp.concatenate(
        [
            hot_ref[pl.ds(pl.multiple_of((scalar_ref[2] ^ n) * capacity, capacity), capacity), :]
            for n in range(experts)
        ],
        axis=0,
    )
    for half in range(2):

        @pl.when(at == half)
        def _():
            for n in range(half * experts, (half + 1) * experts):
                copy(n).wait()
            rows = rows_ref[half * experts * capacity : (half + 1) * experts * capacity, :]
            out = dot(hot, rows, ROWS_FIRST).astype(BF16)
            out_ref[...] = out.reshape(out_ref.shape)


def combine_rows(scalars, hot, pieces, experts):
    tokens = hot.shape[1]
    capacity, feats = pieces[0].shape
    if feats % 128:
        out_shape = jax.ShapeDtypeStruct((2, tokens, feats), BF16)
        out_spec = pl.BlockSpec((1, tokens, feats), lambda a, c: (a ^ c[3], 0, 0))
    else:
        out_shape = jax.ShapeDtypeStruct((tokens, 2 * feats), BF16)
        out_spec = pl.BlockSpec((tokens, feats), lambda a, c: (0, a ^ c[3]))
    out = pl.pallas_call(
        functools.partial(combine_kernel, experts),
        out_shape=out_shape,
        grid_spec=pltpu.PrefetchScalarGridSpec(
            num_scalar_prefetch=1,
            grid=(2,),
            in_specs=[pl.BlockSpec((experts * capacity, tokens), lambda a, c: (0, 0))]
            + [pl.BlockSpec(memory_space=pltpu.HBM)] * len(pieces),
            out_specs=out_spec,
            scratch_shapes=[
                pltpu.VMEM((len(pieces) * capacity, feats), BF16),
                pltpu.SemaphoreType.DMA((len(pieces),)),
            ],
        ),
        compiler_params=PARAMS,
        cost_estimate=cost(),
    )(scalars, hot, *in_hbm(*pieces))
    if feats % 128:
        out = out.transpose(1, 0, 2).reshape(tokens, 2 * feats)
    return out


def gate_up_kernel(scalar_ref, x_ref, wg_ref, wu_ref, *outs):
    width = wg_ref.shape[1]

    @pl.when((pl.program_id(0) == 0) & (pl.program_id(1) == 0))
    def _():
        outs[2][...] = x_ref[...].T

    for own in range(2):

        @pl.when(pl.program_id(1) == own)
        def _():
            outs[own][0, :, :width] = dot(x_ref[...], wg_ref[...]).astype(BF16)
            outs[own][0, :, width:] = dot(x_ref[...], wu_ref[...]).astype(BF16)


def gate_up(scalars, x, w_gate, w_up, count):
    slots, feats = x.shape
    width = w_gate.shape[1] // (2 * count)
    out = jax.ShapeDtypeStruct((count, slots, 2 * width), BF16)
    out_spec = pl.BlockSpec((1, slots, 2 * width), lambda i, own, c: (i, 0, 0))
    column = pl.BlockSpec(
        (feats, width), lambda i, own, c: (0, c[FIXED + 2 * count + own * count + i])
    )
    return pl.pallas_call(
        gate_up_kernel,
        out_shape=(out, out, jax.ShapeDtypeStruct((feats, slots), BF16)),
        grid_spec=pltpu.PrefetchScalarGridSpec(
            num_scalar_prefetch=1,
            grid=(count, 2),
            in_specs=[pl.BlockSpec((slots, feats), lambda i, own, c: (0, 0)), column, column],
            out_specs=(
                out_spec,
                out_spec,
                pl.BlockSpec((feats, slots), lambda i, own, c: (0, 0)),
            ),
        ),
        compiler_params=PARAMS,
        cost_estimate=cost(),
    )(scalars, x, *in_hbm(w_gate, w_up))


def back_kernel(scalar_ref, g_ref, wd_ref, *refs):
    *shares, out_ref = refs
    back = dot(g_ref[...], wd_ref[...], LAST_DIMS)
    if not shares:
        out_ref[0] = back.astype(BF16)
        return
    sib_b, own_gu, sib_gu = shares
    width = back.shape[1]
    both = own_gu[0].astype(F32) + sib_gu[0].astype(F32)
    out_ref[0, :, : 2 * width] = both.astype(BF16)
    out_ref[0, :, 2 * width :] = (back + sib_b[0].astype(F32)).astype(BF16)


def back_rows(scalars, g, w_down, begin, size, count, shares):
    slots, feats = g.shape
    width = w_down.shape[0] // (2 * count)
    own = bool(shares)
    row = pl.BlockSpec(
        (width, feats), lambda i, c: (c[FIXED + 2 * count + own * count + begin + i], 0)
    )
    in_specs = [pl.BlockSpec((slots, feats), lambda i, c: (0, 0)), row]
    if own:
        in_specs.append(pl.BlockSpec((1, slots, width), lambda i, c: (i, 0, 0)))
        in_specs += [pl.BlockSpec((1, slots, 2 * width), lambda i, c: (begin + i, 0, 0))] * 2
    cols = (3 if own else 1) * width
    return pl.pallas_call(
        back_kernel,
        out_shape=jax.ShapeDtypeStruct((size, slots, cols), BF16),
        grid_spec=pltpu.PrefetchScalarGridSpec(
            num_scalar_prefetch=1,
            grid=(size,),
            in_specs=in_specs,
            out_specs=pl.BlockSpec((1, slots, cols), lambda i, c: (i, 0, 0)),
        ),
        compiler_params=PARAMS,
        cost_estimate=cost(),
    )(scalars, g, *in_hbm(w_down), *shares)


def activate(gate, upper, back):
    sig = jax.nn.sigmoid(gate)
    gated = gate * sig
    return (
        (gated * upper).astype(BF16),
        (back * upper * sig * (1.0 + gate * (1.0 - sig))).astype(BF16),
        (back * gated).astype(BF16),
    )


def hop_kernel(plan, scalar_ref, *refs):
    slot, count, chips, came = plan
    sums_ref = refs[-2]
    recv_ref = refs[0] if came else None
    send_ref = refs[-1]
    at = scalar_ref[0]
    width = send_ref.shape[1] // 3
    summing = (at <= slot) & (slot - at < count)

    def total(part):
        columns = slice(part * width, (part + 1) * width)
        value = sums_ref[0, :, columns].astype(F32)
        if came:
            value += jnp.where(at > 0, recv_ref[:, columns].astype(F32), 0.0)
        return value

    @pl.when(summing & (at < chips - 1))
    def _():
        for part in range(3):
            send_ref[:, part * width : (part + 1) * width] = total(part).astype(BF16)

    @pl.when(summing & (at == chips - 1))
    def _():
        for part, value in enumerate(activate(total(0), total(1), total(2))):
            send_ref[:, part * width : (part + 1) * width] = value

    if came:

        @pl.when(jnp.logical_not(summing))
        def _():
            send_ref[...] = recv_ref[...]


def hop(scalars, slot, count, chips, recv, sums, part):
    array, i = sums
    rows, cols = array.shape[1] // PARTS, array.shape[2]
    message = pl.BlockSpec((rows, cols), lambda n, c: (0, 0))
    operands, in_specs = [], []
    if recv is not None:
        operands.append(recv)
        in_specs.append(message)
    operands.append(array)
    in_specs.append(pl.BlockSpec((1, rows, cols), lambda n, c: (i, part, 0)))
    plan = (slot, count, chips, recv is not None)
    return pl.pallas_call(
        functools.partial(hop_kernel, plan),
        out_shape=jax.ShapeDtypeStruct((rows, cols), BF16),
        grid_spec=pltpu.PrefetchScalarGridSpec(
            num_scalar_prefetch=1,
            grid=(1,),
            in_specs=in_specs,
            out_specs=message,
        ),
        compiler_params=PARAMS,
        cost_estimate=cost(),
    )(scalars, *operands)


def choose_kernel(wanted, hops, scalar_ref, *refs):
    *candidates, sems = refs
    candidates, outs = candidates[:-wanted], candidates[-wanted:]
    rows = candidates[0].shape[0]

    def copy(k, n, part):
        return pltpu.make_async_copy(
            candidates[(k + n) * PARTS + part],
            outs[k].at[pl.ds(part * rows, rows)],
            sems.at[k, part],
        )

    for n in range(hops):

        @pl.when(scalar_ref[0] == n)
        def _():
            for k in range(wanted):
                for part in range(PARTS):
                    copy(k, n, part).start()

    for k in range(wanted):
        for part in range(PARTS):
            copy(k, 0, part).wait()


def choose(place, wanted, hops, candidates):
    rows, cols = candidates[0].shape
    return pl.pallas_call(
        functools.partial(choose_kernel, wanted, hops),
        out_shape=[jax.ShapeDtypeStruct((rows * PARTS, cols), BF16)] * wanted,
        in_specs=[pl.BlockSpec(memory_space=pltpu.SMEM)]
        + [pl.BlockSpec(memory_space=pl.ANY)] * len(candidates),
        scratch_shapes=[pltpu.SemaphoreType.DMA((wanted, PARTS))],
        compiler_params=PARAMS,
        cost_estimate=cost(),
    )(place, *candidates)


def forward_on_kernel(scalar_ref, in_ref, out_ref):
    out_ref[...] = in_ref[...]


def forward_on(scalars, message):
    return pl.pallas_call(
        forward_on_kernel,
        out_shape=jax.ShapeDtypeStruct(message.shape, message.dtype),
        in_specs=[
            pl.BlockSpec(memory_space=pltpu.SMEM),
            pl.BlockSpec(memory_space=pltpu.VMEM),
        ],
        compiler_params=PARAMS,
        cost_estimate=cost(),
    )(scalars, message)


def gradients_kernel(units, scale, first, scalar_ref, xt_ref, g_ref, *refs):
    messages, refs = refs[:units], refs[units if first else units + 3 :]
    gg_ref, gu_ref, gd_ref, token_ref = refs
    width = gg_ref.shape[1]
    pass_on(scalar_ref, token_ref)
    for u in range(units):

        @pl.when(pl.program_id(0) == u)
        def _():
            both = dot(xt_ref[...], messages[u][:, width:]) * scale
            gg_ref[...] = both[:, :width].astype(BF16)
            gu_ref[...] = both[:, width:].astype(BF16)
            scaled = messages[u][:, :width]
            gd_ref[...] = (dot(scaled, g_ref[...], ROWS_FIRST) * scale).astype(BF16)


def gradients(scalars, begin, count, scale, x_t, g, messages, grads):
    slots, feats = g.shape
    width = messages[0].shape[1] // 3
    hidden = 2 * count * width
    units = len(messages)

    def at(u, c):
        return c[FIXED + begin + u]

    column = pl.BlockSpec((feats, width), lambda u, c: (0, at(u, c)))
    in_specs = [
        pl.BlockSpec((feats, slots), lambda u, c: (0, 0)),
        pl.BlockSpec((slots, feats), lambda u, c: (0, 0)),
    ]
    in_specs += [pl.BlockSpec((slots, 3 * width), lambda u, c: (0, 0))] * units
    operands = [x_t, g, *messages]
    aliases = {}
    if grads is not None:
        aliases = {len(operands) + 1 + n: n for n in range(3)}
        operands += grads
        in_specs += [pl.BlockSpec(memory_space=pl.ANY)] * 3
    *grads, token = pl.pallas_call(
        functools.partial(gradients_kernel, units, scale, grads is None),
        out_shape=[
            jax.ShapeDtypeStruct((feats, hidden), BF16),
            jax.ShapeDtypeStruct((feats, hidden), BF16),
            jax.ShapeDtypeStruct((hidden, feats), BF16),
            jax.ShapeDtypeStruct(scalars.shape, jnp.int32),
        ],
        grid_spec=pltpu.PrefetchScalarGridSpec(
            num_scalar_prefetch=1,
            grid=(units,),
            in_specs=in_specs,
            out_specs=[
                column,
                column,
                pl.BlockSpec((width, feats), lambda u, c: (at(u, c), 0)),
                pl.BlockSpec(memory_space=pltpu.SMEM),
            ],
        ),
        input_output_aliases=aliases,
        compiler_params=PARAMS,
        cost_estimate=cost(),
    )(scalars, *operands)
    return grads, token


def sum_rows_kernel(units, pieces, scalar_ref, *refs):
    messages, weights, refs = refs[:units], refs[units : 3 * units], refs[3 * units :]
    width = weights[0].shape[1]
    both = jnp.concatenate([message[:, width:] for message in messages], axis=1)
    part = dot(both, jnp.concatenate([w[...] for w in weights], axis=1), LAST_DIMS)
    if not pieces:
        out_ref, token_ref = refs
        out_ref[...] = part
        pass_on(scalar_ref, token_ref)
        return
    acc_in, *outs, acc = refs
    acc[...] = acc_in[...] + part
    size = outs[0].shape[0]
    for n, out in enumerate(outs):
        start = pl.multiple_of((scalar_ref[1] ^ n) * size, size)
        out[...] = acc[pl.ds(start, size), :].astype(BF16)


def sum_rows(scalars, begin, messages, weights, acc, pieces):
    slots, width = messages[0].shape[0], messages[0].shape[1] // 3
    feats = weights[0].shape[0]
    units = len(messages)
    in_specs = [pl.BlockSpec((slots, 3 * width), lambda n, c: (0, 0))] * units
    operands = list(messages)
    for u in range(units):
        column = pl.BlockSpec((feats, width), lambda n, c, u=u: (0, c[FIXED + begin + u]))
        operands += in_hbm(*weights)
        in_specs += [column, column]
    whole = pl.BlockSpec((slots, feats), lambda n, c: (0, 0))
    if pieces:
        operands.append(acc)
        in_specs.append(whole)
        out_shape = [jax.ShapeDtypeStruct((slots // pieces, feats), BF16)] * pieces
        out_specs = [pl.BlockSpec((slots // pieces, feats), lambda n, c: (0, 0))] * pieces
        scratch = [pltpu.VMEM((slots, feats), F32)]
    else:
        out_shape = [
            jax.ShapeDtypeStruct((slots, feats), F32),
            jax.ShapeDtypeStruct(scalars.shape, jnp.int32),
        ]
        out_specs = [whole, pl.BlockSpec(memory_space=pltpu.SMEM)]
        scratch = []
    return pl.pallas_call(
        functools.partial(sum_rows_kernel, units, pieces),
        out_shape=out_shape,
        grid_spec=pltpu.PrefetchScalarGridSpec(
            num_scalar_prefetch=1,
            grid=(1,),
            in_specs=in_specs,
            out_specs=out_specs,
            scratch_shapes=scratch,
        ),
        compiler_params=PARAMS,
        cost_estimate=cost(),
    )(scalars, *operands)


def body(tokens, grad_out, expert_ids, route_weights, w_gate, w_up, w_down):
    experts = lax.axis_size("expert")
    groups = lax.axis_size("dp")
    tok_rows = tokens.shape[0]
    feats = w_gate.shape[1]
    capacity = tok_rows // 2
    chips = groups // 2
    count = chips
    assert groups == 2 * experts and tokens.shape[1] == 2 * feats
    inv_root = 1.0 / math.sqrt(tok_rows * groups)
    expert = lax.axis_index("expert").astype(jnp.int32)
    block = lax.axis_index("dp").astype(jnp.int32)
    chip, core = block // 2, block % 2
    along = jnp.where(core == 0, chip, chips - 1 - chip)
    w_gate, w_up, w_down = w_gate[0], w_up[0], w_down[0]
    ids, weights = expert_ids.T, route_weights.T

    swap = [(j, j ^ 1) for j in range(groups)]
    up = [2 * z for z in range(chips)]
    circle = up + [j + 1 for j in reversed(up)]
    ring = list(zip(circle, circle[1:] + circle[:1]))

    scalars = [along, expert + experts * core, block % experts, block // experts, expert]
    scalars += [(d ^ 1 ^ core) * count + k for d in range(2) for k in range(count)]
    scalars += [(1 - core) * count + (i - (chips - 1 - along)) % count for i in range(count)]
    scalars += [core * count + (i - along) % count for i in range(count)]
    scalars = jnp.stack(scalars).astype(jnp.int32)

    def exchange(messages):
        came = [messages[0]]
        for t in range(1, experts):
            came.append(lax.ppermute(messages[t], "expert", [(q, q ^ t) for q in range(experts)]))
        blocks = assemble(scalars, came).reshape(groups, capacity, feats)
        blocks = lax.all_to_all(blocks, "dp", split_axis=0, concat_axis=0, tiled=True)
        return blocks.reshape(groups * capacity, feats)

    x_messages, _, token = dispatch_rows(scalars, ids, weights, tokens, experts, False)
    g_messages, hot, _ = dispatch_rows(token, ids, weights, grad_out, experts, True)
    x = exchange(x_messages)
    g = exchange(g_messages)

    other_gu, own_gu, x_t = gate_up(scalars, x, w_gate, w_up, count)
    sib_gu = lax.ppermute(other_gu, "dp", swap)
    spans = ((0, count // 2), (count // 2, count - count // 2))
    others = [
        lax.ppermute(back_rows(scalars, g, w_down, begin, size, count, ()), "dp", swap)
        for begin, size in spans
    ]
    sums = []
    for (begin, size), sib_b in zip(spans, others):
        shares = (sib_b, own_gu, sib_gu)
        both = back_rows(scalars, g, w_down, begin, size, count, shares)
        sums += [(both, i) for i in range(size)]

    slots = 2 * count + chips - 2
    first_back = chips - 1 + count
    recv = []
    gate_and_up = (w_gate, w_up)
    place = along.astype(jnp.int32)[None]

    def pick(token, begin, wanted):
        found = recv[count - 1 + begin : count - 1 + begin + chips + wanted - 1]
        return choose(token, wanted, chips, [part for came in found for part in came])

    early = count - 1
    mine, grads = [], None
    for s in range(slots):
        came = []
        for part in range(PARTS):
            send = recv[s - 1][part] if s else None
            if s < first_back:
                send = hop(place, s, count, chips, send, sums[s % count], part)
            elif s > first_back and part == 0:
                k = len(mine)
                mine += pick(place, k, 1)
                grads, token = gradients(
                    scalars, k, count, inv_root, x_t, g, mine[-1:], grads
                )
                send = forward_on(token, send)
            came.append(lax.ppermute(send, "dp", ring))
        recv.append(came)

    ready = len(mine)
    mine += pick(place, ready, early - ready)
    others = [lax.ppermute(message, "dp", swap) for message in mine]
    acc, token = sum_rows(scalars, 0, mine, gate_and_up, None, 0)
    last = pick(token, early, count - early)
    others += [lax.ppermute(message, "dp", swap) for message in last]
    grads, token = gradients(token, ready, count, inv_root, x_t, g, mine[ready:], grads)
    units = [*last, *others]
    pieces = sum_rows(token, early, units, gate_and_up, acc, groups)
    returned = []
    for r, piece in enumerate(pieces):
        pairs = []
        for q in range(experts):
            for b in range(groups):
                h, e = divmod(b ^ r, experts)
                pairs.append((e * groups + 2 * q + h, q * groups + b))
        returned.append(lax.ppermute(piece, ("expert", "dp"), pairs))
    grads, _ = gradients(scalars, early, count, inv_root, x_t, g, units, grads)
    grad_tokens = combine_rows(scalars, hot, returned, experts)
    return (grad_tokens, grads[0][None], grads[1][None], grads[2][None])


def solution(mesh):
    in_specs = (
        P("dp", "expert"),
        P("dp", "expert"),
        P("dp", None),
        P("dp", None),
        P("expert", "dp", None),
        P("expert", "dp", None),
        P("expert", None, "dp"),
    )
    out_specs = (
        P("dp", "expert"),
        P("expert", "dp", None),
        P("expert", "dp", None),
        P("expert", None, "dp"),
    )
    return jax.shard_map(body, mesh=mesh, in_specs=in_specs, out_specs=out_specs, check_vma=False)
```
